32 devices in a mesh: shard: 4 (over x, core), ctx: 4 (over z), tp: 2 (over y).
Axes of the slice: x: 2, y: 2, z: 4, core: 2. Of those that a mesh axis runs over, the one named last changes fastest.
Arguments:
- tokens: bfloat16 [8, 1024, 2048], P('shard', 'ctx'), may hold values from -6 to 6
- cotangent: bfloat16 [8, 1024, 2048], P('shard', 'ctx'), may hold values from -6 to 6
- buckets: int32 [1024, 1024], P('ctx'), may hold values from 0 to 31, as said below
- query_weight: bfloat16 [2048, 2048], P('shard', 'tp'), may hold values from -0.03125 to 0.03125
- key_weight: bfloat16 [2048, 2048], P('shard', 'tp'), may hold values from -0.125 to 0.125
- value_weight: bfloat16 [2048, 2048], P('shard', 'tp'), may hold values from -0.125 to 0.125
- output_weight: bfloat16 [2048, 2048], P('shard', 'tp'), may hold values from -0.375 to 0.375
- gate_weight: bfloat16 [2048, 5120], P('shard', 'tp'), may hold values from -0.125 to 0.125
- up_weight: bfloat16 [2048, 5120], P('shard', 'tp'), may hold values from -0.125 to 0.125
- down_weight: bfloat16 [2048, 5120], P('shard', 'tp'), may hold values from -0.078125 to 0.078125
- norm_gain: bfloat16 [2048], replicated, may hold values from 0.25 to 1.75
- ffn_gain: bfloat16 [2048], replicated, may hold values from 0.25 to 1.75
- bucket_bias_table: bfloat16 [32, 32], P(None, 'tp'), may hold values from -4 to 4
Outputs:
- layer_output: bfloat16 [8, 1024, 2048], P('shard', 'ctx')
- input_grad: float32 [8, 1024, 2048], P('shard', 'ctx')
- query_grad: float32 [2048, 2048], P('shard', 'tp')
- key_grad: float32 [2048, 2048], P('shard', 'tp')
- value_grad: float32 [2048, 2048], P('shard', 'tp')
- output_grad: float32 [2048, 2048], P('shard', 'tp')
- gate_grad: float32 [2048, 5120], P('shard', 'tp')
- up_grad: float32 [2048, 5120], P('shard', 'tp')
- down_grad: float32 [2048, 5120], P('shard', 'tp')
- norm_gain_grad: float32 [2048], replicated
- ffn_gain_grad: float32 [2048], replicated
- table_grad: float32 [32, 32], P(None, 'tp')
The draws below stay inside these ranges and needn't reach their ends.
Inputs may be any that keep to these rules, and one draw needn't show every extreme that they name: buckets[i, j] is T5's bidirectional relative position bucket of the offset j - i (32 buckets, maximum distance 128), its bucket number relabelled by one permutation of the 32 buckets; it depends only on j - i, and one table serves every sequence.
All inputs are finite; a program needn't handle non-finite values.
Results may differ from the reference program's by a relative error of at most 0.023.
Values may be sent and summed in bfloat16 or wider, within the bound.
A program may use at most 256 MiB of HBM per device.

```python
import math
import jax
import jax.numpy as jnp
from jax import lax

D = 2048
H = 32
DK = 64
FF = 5120
NB = 32
LEN = 1024
SEQS = 8


def draw_buckets(key, part):
    key = jax.random.fold_in(key, 7)
    half = NB // 2
    exact = half // 2
    limits = [int(math.ceil(exact * (128.0 / exact) ** (step / (half - exact)) - 1e-06)) for step in range(1, half - exact)]
    rows = jnp.arange(LEN, dtype=jnp.int32)
    offset = rows[None, :] - rows[:, None]
    distance = jnp.abs(offset)
    bucket = jnp.minimum(distance, exact)
    for limit in limits:
        bucket = bucket + (distance >= limit).astype(jnp.int32)
    bucket = bucket + half * (offset > 0).astype(jnp.int32)
    relabel = jax.random.permutation(key, jnp.arange(NB, dtype=jnp.int32))
    return relabel[bucket].astype(jnp.int32)


def steps_of(key, shape, shards, least, top_value):
    level, own = 1.0, jax.random.fold_in(key, 6)
    for dim, parts in shards:
        steps = jnp.exp(jax.random.uniform(jax.random.fold_in(own, dim), (parts,), jnp.float32, least / len(shards), top_value / len(shards)))
        level = level * jnp.repeat(steps, shape[dim] // parts).reshape([-1 if axis == dim else 1 for axis in range(len(shape))])
    return level


def scatter_about(rng, extent, deviation, most, cuts=(), kind=jnp.bfloat16):
    values = deviation * jax.random.normal(rng, extent, jnp.float32)
    if cuts:
        values = values * steps_of(rng, extent, cuts, -0.22, 0.18)
    return jnp.clip(values, -most, most).astype(kind)


def setup_inputs(seed: int = 0) -> dict:
    keys = jax.random.split(jax.random.key(seed), 14)
    return {
        "tokens": scatter_about(keys[0], (SEQS, LEN, D), 1.0, 6.0, ((0, 4), (1, 4))),
        "cotangent": scatter_about(keys[1], (SEQS, LEN, D), 1.0, 6.0, ((0, 4), (1, 4))),
        "buckets": draw_buckets(jax.random.fold_in(keys[13], 71), 0),
        "query_weight": scatter_about(keys[3], (D, H * DK), (16 * D) ** -0.5, 0.03125, ((0, 4), (1, 2))),
        "key_weight": scatter_about(keys[4], (D, H * DK), D ** -0.5, 0.125, ((0, 4), (1, 2))),
        "value_weight": scatter_about(keys[5], (D, H * DK), D ** -0.5, 0.125, ((0, 4), (1, 2))),
        "output_weight": scatter_about(keys[6], (D, H * DK), (H * DK // 8) ** -0.5, 0.375, ((0, 4), (1, 2))),
        "gate_weight": scatter_about(keys[7], (D, FF), D ** -0.5, 0.125, ((0, 4), (1, 2))),
        "up_weight": scatter_about(keys[8], (D, FF), D ** -0.5, 0.125, ((0, 4), (1, 2))),
        "down_weight": scatter_about(keys[9], (D, FF), FF ** -0.5, 0.078125, ((0, 4), (1, 2))),
        "norm_gain": jnp.clip(1.0 + 0.15 * jax.random.normal(keys[10], (D,), jnp.float32), 0.25, 1.75).astype(jnp.bfloat16),
        "ffn_gain": jnp.clip(1.0 + 0.15 * jax.random.normal(keys[11], (D,), jnp.float32), 0.25, 1.75).astype(jnp.bfloat16),
        "bucket_bias_table": scatter_about(keys[12], (NB, H), 1.0, 4.0, ((1, 2),)),
    }


@jax.custom_vjp
def low(v):
    return lax.optimization_barrier(v.astype(jnp.bfloat16)).astype(jnp.float32)

@jax.custom_vjp
def low_back(v):
    return v

def low_keep(v):
    return (low(v), None)

def low_pass(kept, grad):
    return (grad,)

def back_keep(v):
    return (v, None)

def back_low(kept, grad):
    return (low(grad),)
low.defvjp(low_keep, low_pass)
low_back.defvjp(back_keep, back_low)

def matmul(left, right):
    return jnp.dot(left, right, preferred_element_type=jnp.float32, precision=lax.Precision.HIGHEST)

def rms_norm(values, gain):
    scale = lax.rsqrt(lax.optimization_barrier(jnp.mean(values * values, axis=-1, keepdims=True)) + 1e-06)
    return values * scale * gain

def geglu(gate, up):
    return jax.nn.gelu(gate, approximate=True) * up

def layer(params, seq, buckets):
    wq, wk, wv, wo, wi0, wi1, wff, gain_one, gain_two, bias_lookup_table = params
    length = seq.shape[0]
    normed = low(rms_norm(seq, gain_one))
    query = low(low_back(matmul(normed, wq))).reshape(length, H, DK)
    key = low(low_back(matmul(normed, wk))).reshape(length, H, DK)
    value = low(low_back(matmul(normed, wv))).reshape(length, H, DK)
    bucket_indicator = (buckets[None, :, :] == jnp.arange(NB, dtype=jnp.int32)[:, None, None]).astype(jnp.float32)
    position_bias = jnp.einsum('lev,lr->rev', bucket_indicator, bias_lookup_table, precision=lax.Precision.HIGHEST)
    scores = jnp.einsum('qhd,khd->hqk', query, key, precision=lax.Precision.HIGHEST) + position_bias
    scores = low_back(scores)
    probs = jax.nn.softmax(scores, axis=-1)
    mixed = jnp.einsum('hqk,khd->qhd', low(probs), value, precision=lax.Precision.HIGHEST)
    attended = low(low_back(mixed.reshape(length, H * DK)))
    branch = low_back(matmul(attended, wo.T))
    hidden = seq + branch
    normed_two = low(rms_norm(hidden, gain_two))
    gate = low_back(matmul(normed_two, wi0))
    up = low_back(matmul(normed_two, wi1))
    inner = low(geglu(gate, up))
    return hidden + low_back(matmul(inner, wff.T))

def reference(tokens, cotangent, buckets, query_weight, key_weight, value_weight, output_weight, gate_weight, up_weight, down_weight, norm_gain, ffn_gain, bucket_bias_table):
    params = tuple((w.astype(jnp.float32) for w in (query_weight, key_weight, value_weight, output_weight, gate_weight, up_weight, down_weight, norm_gain, ffn_gain, bucket_bias_table)))

    def one_sequence(totals, pair):
        seq, seq_grad = pair
        result, pull = jax.vjp(lambda weights, inputs: layer(weights, inputs, buckets), params, seq.astype(jnp.float32))
        weight_grads, input_grad = pull(seq_grad.astype(jnp.float32))
        totals = tuple((total + grad for total, grad in zip(totals, weight_grads)))
        return (totals, (result.astype(jnp.bfloat16), input_grad))
    zeros = tuple((jnp.zeros_like(w) for w in params))
    totals, (outputs, input_grads) = lax.scan(one_sequence, zeros, (tokens, cotangent))
    return (outputs, input_grads, totals[0], totals[1], totals[2], totals[3], totals[4], totals[5], totals[6], totals[7], totals[8], totals[9])
```

```python
import functools

import jax
import jax.numpy as jnp
from jax import lax
from jax.experimental import pallas as pl
from jax.experimental.pallas import tpu as pltpu
from jax.sharding import PartitionSpec as P

F32 = jnp.float32
BF16 = jnp.bfloat16
VMEM_LIMIT = 48 * 2**20


def contract_rows(left, right):
    return lax.dot_general(left, right, (((0,), (0,)), ((), ())), preferred_element_type=F32)


def contract_cols(left, right):
    return lax.dot_general(left, right, (((1,), (1,)), ((), ())), preferred_element_type=F32)


def dot(left, right):
    return jnp.dot(left, right, preferred_element_type=F32)


def rms_scale(values):
    return lax.rsqrt(jnp.mean(values * values, axis=-1, keepdims=True) + 1e-06)


def rms_back(values, scale, gain, upstream):
    weighted = upstream * gain
    inner_average = jnp.mean(values * weighted, axis=-1, keepdims=True)
    return scale * weighted - values * scale * scale * scale * inner_average


def geglu(gate, up):
    return jax.nn.gelu(gate, approximate=True) * up


def bias_rows(table_row, out):
    span = out.shape[1]
    out[0:1, :] = table_row
    done = 1
    while done < out.shape[0]:
        out[done : 2 * done, :] = pltpu.roll(out[0:done, :], done, 1)
        done *= 2
    del span


def diagonal_sums(acc):
    rows, span = acc.shape
    total = acc[...]
    while rows > 1:
        rows //= 2
        total = total[:rows] + pltpu.roll(total[rows:], span - rows, 1)
    return total


def head_mask(shape, head, head_dim):
    lane = lax.broadcasted_iota(jnp.int32, shape, 1)
    return (lane >= head * head_dim) & (lane < (head + 1) * head_dim)


def window(me, n, part, query, key):
    q_at = lax.rem(me - query + n, n)
    k_at = lax.rem(me - key + n, n)
    return pl.multiple_of((n + k_at - q_at) * part, part)


def attend_kernel(n, head_dim, me_ref, table_ref, *refs):
    pieces, outs, lse_ref, bias, keys, values = (
        refs[:n], refs[n : 2 * n], refs[2 * n], refs[2 * n + 1], refs[2 * n + 2], refs[2 * n + 3],
    )
    part, lanes = pieces[0].shape[2:]
    per = lanes // head_dim
    me = me_ref[0]

    @pl.when(pl.program_id(1) == 0)
    def _():
        for head in range(per):
            bias_rows(table_ref[0, head : head + 1, :], bias.at[head])

    for b in range(n):
        keys[b * part : (b + 1) * part, :] = pieces[b][1, 0]
        values[b * part : (b + 1) * part, :] = pieces[b][2, 0]
    for a in range(n):
        lse = jnp.zeros((part, lanes), F32)
        mixed = jnp.zeros((part, lanes), F32)
        lane = lax.broadcasted_iota(jnp.int32, (part, lanes), 1)
        for head in range(per):
            mask = head_mask((part, lanes), head, head_dim)
            query = jnp.where(mask, pieces[a][0, 0], 0)
            scores = contract_cols(query, keys[...])
            scores = scores + jnp.concatenate(
                [bias[head, :, pl.ds(window(me, n, part, a, b), part)] for b in range(n)], axis=1
            )
            peak = jnp.max(scores, axis=1, keepdims=True)
            expo = jnp.exp(scores - peak)
            total = jnp.sum(expo, axis=1, keepdims=True)
            probs = (expo * (1.0 / total)).astype(BF16)
            mixed = jnp.where(mask, dot(probs, values[...]), mixed)
            lse = jnp.where(lane == head, peak + jnp.log(total), lse)
        outs[a][0] = mixed.astype(BF16)
        lse_ref[0, 0, a] = lse


def attend_back_kernel(n, head_dim, me_ref, table_ref, *refs):
    pieces, grads, lse_ref = refs[:n], refs[n : 2 * n], refs[2 * n]
    outs, table_out = refs[2 * n + 1 : 3 * n + 1], refs[3 * n + 1]
    bias, sums, keys, values, grad_k, grad_v = refs[3 * n + 2 :]
    part, lanes = pieces[0].shape[2:]
    per = lanes // head_dim
    me = me_ref[0]

    @pl.when(pl.program_id(1) == 0)
    def _():
        for head in range(per):
            bias_rows(table_ref[0, head : head + 1, :], bias.at[head])
        sums[...] = jnp.zeros_like(sums)

    for b in range(n):
        keys[b * part : (b + 1) * part, :] = pieces[b][1, 0]
        values[b * part : (b + 1) * part, :] = pieces[b][2, 0]
    grad_k[...] = jnp.zeros_like(grad_k)
    grad_v[...] = jnp.zeros_like(grad_v)
    for a in range(n):
        grad_q = jnp.zeros((part, lanes), F32)
        for head in range(per):
            mask = head_mask((part, lanes), head, head_dim)
            query = jnp.where(mask, pieces[a][0, 0], 0)
            upstream = jnp.where(mask, grads[a][0], 0)
            starts = [window(me, n, part, a, b) for b in range(n)]
            scores = contract_cols(query, keys[...])
            scores = scores + jnp.concatenate(
                [bias[head, :, pl.ds(start, part)] for start in starts], axis=1
            )
            probs = jnp.exp(scores - lse_ref[0, 0, a][:, head : head + 1])
            grad_probs = contract_cols(upstream, values[...])
            delta = jnp.sum(grad_probs * probs, axis=1, keepdims=True)
            grad_scores = (probs * (grad_probs - delta)).astype(BF16)
            for b, start in enumerate(starts):
                sums[head, :, pl.ds(start, part)] += grad_scores[:, b * part : (b + 1) * part].astype(F32)
            grad_q = jnp.where(mask, dot(grad_scores, keys[...]), grad_q)
            grad_k[...] += contract_rows(grad_scores, query)
            grad_v[...] += contract_rows(probs.astype(BF16), upstream)
        outs[a][0, 0] = grad_q.astype(BF16)
    for b in range(n):
        outs[b][1, 0] = grad_k[b * part : (b + 1) * part, :].astype(BF16)
        outs[b][2, 0] = grad_v[b * part : (b + 1) * part, :].astype(BF16)

    @pl.when(pl.program_id(1) == pl.num_programs(1) - 1)
    def _():
        for head in range(per):
            table_out[0, head : head + 1, :] = diagonal_sums(sums.at[head])


def attention_calls(n, seqs, part, cols, head_dim):
    lanes = 2 * head_dim
    groups, per, span = cols // lanes, lanes // head_dim, 2 * n * part
    smem = pl.BlockSpec(memory_space=pltpu.SMEM)
    table_spec = pl.BlockSpec((1, per, span), lambda g, s: (g, 0, 0))
    three = pl.BlockSpec((3, 1, part, lanes), lambda g, s: (0, s, 0, g))
    one = pl.BlockSpec((1, part, lanes), lambda g, s: (s, 0, g))
    lse_spec = pl.BlockSpec((1, 1, n, part, lanes), lambda g, s: (g, s, 0, 0, 0))
    piece = jax.ShapeDtypeStruct((3, seqs, part, cols), BF16)
    single = jax.ShapeDtypeStruct((seqs, part, cols), BF16)
    lse = jax.ShapeDtypeStruct((groups, seqs, n, part, lanes), F32)
    table = jax.ShapeDtypeStruct((groups, per, span), F32)
    length = n * part
    pairs = seqs * (cols // head_dim) * length * length
    forward = pl.pallas_call(
        functools.partial(attend_kernel, n, head_dim),
        grid=(groups, seqs),
        in_specs=[smem, table_spec] + [three] * n,
        out_specs=[one] * n + [lse_spec],
        out_shape=[single] * n + [lse],
        scratch_shapes=[
            pltpu.VMEM((per, part, span), F32),
            pltpu.VMEM((length, lanes), BF16),
            pltpu.VMEM((length, lanes), BF16),
        ],
        compiler_params=pltpu.CompilerParams(vmem_limit_bytes=VMEM_LIMIT),
        cost_estimate=pl.CostEstimate(
            flops=4 * pairs * 256, bytes_accessed=2**23, transcendentals=pairs
        ),
        name="attend",
    )
    backward = pl.pallas_call(
        functools.partial(attend_back_kernel, n, head_dim),
        grid=(groups, seqs),
        in_specs=[smem, table_spec] + [three] * n + [one] * n + [lse_spec],
        out_specs=[three] * n + [table_spec],
        out_shape=[piece] * n + [table],
        scratch_shapes=[
            pltpu.VMEM((per, part, span), F32),
            pltpu.VMEM((per, part, span), F32),
            pltpu.VMEM((length, lanes), BF16),
            pltpu.VMEM((length, lanes), BF16),
            pltpu.VMEM((length, lanes), F32),
            pltpu.VMEM((length, lanes), F32),
        ],
        compiler_params=pltpu.CompilerParams(vmem_limit_bytes=VMEM_LIMIT),
        cost_estimate=pl.CostEstimate(
            flops=10 * pairs * 256, bytes_accessed=2**24, transcendentals=pairs
        ),
        name="attend_back",
    )
    return forward, backward


def ring(n, d):
    return [(i, (i + d) % n) for i in range(n)]


class Links:
    def __init__(self, mesh):
        self.shard, self.ctx, self.tp = mesh.shape["shard"], mesh.shape["ctx"], mesh.shape["tp"]
        self.chips = self.shard // 2

    def to_core(self, value):
        return lax.ppermute(value, "shard", [(i, i ^ 1) for i in range(self.shard)])

    def to_chip(self, value, d):
        n = self.shard
        return lax.ppermute(value, "shard", [(i, (i + 2 * d) % n) for i in range(n)])

    def tp_sum(self, value):
        if self.tp != 2:
            return lax.psum(value, "tp").astype(F32)
        other = lax.ppermute(value, "tp", ring(2, 1))
        return value.astype(F32) + other.astype(F32)

    def ctx_sum(self, value):
        low = value.astype(BF16)
        if self.ctx != 4:
            return lax.psum(low, "ctx").astype(F32)
        inward = lax.ppermute(low, "ctx", [(0, 1), (3, 2)])
        half = (low.astype(F32) + inward.astype(F32)).astype(BF16)
        across = lax.ppermute(half, "ctx", [(1, 2), (2, 1)])
        whole = (half.astype(F32) + across.astype(F32)).astype(BF16)
        outward = lax.ppermute(whole, "ctx", [(1, 0), (2, 3)])
        me = lax.axis_index("ctx")
        middle = (me == 1) | (me == 2)
        return jnp.where(middle, whole, outward).astype(F32)

    def shard_sums(self, left, right):
        n, chips = self.shard, self.chips
        rows = left.shape[1] // n
        me = lax.axis_index("shard")
        chip, core = me // 2, me % 2

        def term(chip_at, core_at):
            at = (2 * chip_at + core_at) * rows
            return contract_rows(lax.dynamic_slice_in_dim(left, at, rows, 1), right)

        def chip_of(d):
            return lax.rem(chip + d, chips)

        order = list(range(1, chips)) + [0]
        got = {d: self.to_core(term(chip_of(d), 1 - core).astype(BF16)) for d in order}
        total = None
        arrived = []
        for d in order:
            pair = term(chip_of(d), core) + got[d].astype(F32)
            if d:
                arrived.append(self.to_chip(pair.astype(BF16), d))
            else:
                total = pair
        for value in arrived:
            total = total + value.astype(F32)
        return total

    def small_sum(self, value):
        for axis, n in (("shard", self.shard), ("ctx", self.ctx)):
            step = 1
            while step < n:
                value = value + lax.ppermute(value, axis, [(i, i ^ step) for i in range(n)])
                step *= 2
        return value


def per_device(
    links,
    tokens,
    cotangent,
    buckets,
    query_weight,
    key_weight,
    value_weight,
    output_weight,
    gate_weight,
    up_weight,
    down_weight,
    norm_gain,
    ffn_gain,
    bucket_bias_table,
):
    seqs, part, width = tokens.shape
    rows = seqs * part
    slots, heads = bucket_bias_table.shape
    inner_width = query_weight.shape[1]
    head_dim = inner_width // heads
    n = links.ctx
    cols = inner_width // n
    own_heads = heads // n
    me = lax.axis_index("ctx")
    gain_one = norm_gain.astype(F32)
    gain_two = ffn_gain.astype(F32)

    def gathered(weight):
        return lax.all_gather(weight, "shard", axis=0, tiled=True)

    def at_ctx(d):
        return lax.rem(me + d + n, n)

    corner = lax.dynamic_slice(buckets, (0, me * part), (part, part))
    later, earlier = corner[0, :], corner[:, 0]
    reach = n * part
    by_offset = jnp.concatenate(
        [
            jnp.broadcast_to(earlier[part - 1 :], (reach - part + 1,)),
            earlier[:0:-1],
            later,
            jnp.broadcast_to(later[part - 1 :], (reach - part,)),
        ]
    )
    indicator = by_offset[None, :] == jnp.arange(slots, dtype=jnp.int32)[:, None]
    own_table = lax.dynamic_slice(bucket_bias_table, (0, me * own_heads), (slots, own_heads))
    offset_bias = lax.dot_general(
        own_table, indicator.astype(BF16), (((0,), (0,)), ((), ())), preferred_element_type=F32
    )
    groups = cols // (2 * head_dim)
    offset_bias = offset_bias.reshape(groups, 2, 2 * reach)
    where_am_i = me.astype(jnp.int32).reshape(1)
    attend, attend_back = attention_calls(n, seqs, part, cols, head_dim)

    wq, wk, wv = gathered(query_weight), gathered(key_weight), gathered(value_weight)
    inputs = tokens.reshape(rows, width).astype(F32)
    scale_one = rms_scale(inputs)
    normed = (inputs * scale_one * gain_one).astype(BF16)
    projected = [dot(normed, w).astype(BF16) for w in (wq, wk, wv)]

    def heads_of(values, d):
        start = at_ctx(d) * cols
        return [lax.dynamic_slice_in_dim(v, start, cols, 1).reshape(seqs, part, cols) for v in values]

    pieces = [jnp.stack(heads_of(projected, d)) for d in range(n)]
    pieces = [pieces[0]] + [lax.ppermute(pieces[d], "ctx", ring(n, d)) for d in range(1, n)]
    *mixed, lse = attend(where_am_i, offset_bias, *pieces)

    def heads_back(blocks):
        blocks = [blocks[0]] + [lax.ppermute(blocks[d], "ctx", ring(n, n - d)) for d in range(1, n)]
        around = jnp.concatenate(blocks, axis=-1)
        twice = jnp.concatenate([around, around], axis=-1)
        return lax.dynamic_slice_in_dim(twice, (n - me) * cols, n * cols, around.ndim - 1)

    attended = heads_back(mixed).reshape(rows, inner_width)
    wo = gathered(output_weight)
    branch = links.tp_sum(contract_cols(attended, wo).astype(BF16))
    hidden = inputs + branch
    wi0, wi1, wff = gathered(gate_weight), gathered(up_weight), gathered(down_weight)
    scale_two = rms_scale(hidden)
    normed_two = (hidden * scale_two * gain_two).astype(BF16)
    gate = dot(normed_two, wi0)
    up = dot(normed_two, wi1)
    inner = geglu(gate, up).astype(BF16)
    ffn_out = links.tp_sum(contract_cols(inner, wff).astype(BF16))
    result = (hidden + ffn_out).astype(BF16).reshape(seqs, part, width)

    upstream = cotangent.reshape(rows, width).astype(F32)
    upstream_low = cotangent.reshape(rows, width)
    grad_down_w = links.ctx_sum(links.shard_sums(upstream_low, inner))
    grad_inner = dot(upstream_low, wff)
    unused, geglu_backward_pull = jax.vjp(geglu, gate, up)
    grad_gate, grad_up = geglu_backward_pull(grad_inner)
    grad_gate = grad_gate.astype(BF16)
    grad_up = grad_up.astype(BF16)
    grad_normed_two = links.tp_sum(
        (contract_cols(grad_gate, wi0) + contract_cols(grad_up, wi1)).astype(BF16)
    )
    grad_gate_w = links.ctx_sum(links.shard_sums(normed_two, grad_gate))
    grad_up_w = links.ctx_sum(links.shard_sums(normed_two, grad_up))
    grad_ffn_gain = jnp.sum(grad_normed_two * hidden * scale_two, axis=0)
    grad_hidden = upstream + rms_back(hidden, scale_two, gain_two, grad_normed_two)
    branch_low = grad_hidden.astype(BF16)
    grad_attended = dot(branch_low, wo).astype(BF16)
    grad_output_w = links.ctx_sum(links.shard_sums(branch_low, attended))

    upstreams = [heads_of([grad_attended], d)[0] for d in range(n)]
    upstreams = [upstreams[0]] + [lax.ppermute(upstreams[d], "ctx", ring(n, d)) for d in range(1, n)]
    *grad_pieces, offset_grad = attend_back(where_am_i, offset_bias, *pieces, *upstreams, lse)
    grad_projected = heads_back(grad_pieces).reshape(3, rows, inner_width)
    grad_query, grad_key, grad_value = grad_projected[0], grad_projected[1], grad_projected[2]
    offset_grad = offset_grad.reshape(own_heads, 2 * reach)
    table_part = jnp.sum(jnp.where(indicator[:, None, :], offset_grad[None], 0.0), axis=-1)
    grad_table = lax.dynamic_update_slice(
        jnp.zeros((slots, heads), F32), table_part, (0, me * own_heads)
    )

    grad_normed = links.tp_sum(
        (contract_cols(grad_query, wq) + contract_cols(grad_key, wk) + contract_cols(grad_value, wv)).astype(BF16)
    )
    grad_query_w = links.ctx_sum(links.shard_sums(normed, grad_query))
    grad_key_w = links.ctx_sum(links.shard_sums(normed, grad_key))
    grad_value_w = links.ctx_sum(links.shard_sums(normed, grad_value))
    grad_norm_gain = jnp.sum(grad_normed * inputs * scale_one, axis=0)
    grad_inputs = grad_hidden + rms_back(inputs, scale_one, gain_one, grad_normed)
    small = links.small_sum(jnp.concatenate([grad_norm_gain, grad_ffn_gain, grad_table.reshape(-1)]))
    return (
        result,
        grad_inputs.reshape(seqs, part, width),
        grad_query_w,
        grad_key_w,
        grad_value_w,
        grad_output_w,
        grad_gate_w,
        grad_up_w,
        grad_down_w,
        small[:width],
        small[width : 2 * width],
        small[2 * width :].reshape(slots, heads),
    )


def solution(mesh):
    rows, weights = P("shard", "ctx", None), P("shard", "tp")
    return jax.shard_map(
        functools.partial(per_device, Links(mesh)),
        mesh=mesh,
        in_specs=(rows, rows, P("ctx", None)) + (weights,) * 7 + (P(), P(), P(None, "tp")),
        out_specs=(rows, rows) + (weights,) * 7 + (P(), P(), P(None, "tp")),
        check_vma=False,
    )
```

```python
import functools

import jax
import jax.numpy as jnp
from jax import lax
from jax.experimental import pallas as pl
from jax.experimental.pallas import tpu as pltpu
from jax.sharding import PartitionSpec as P

F32 = jnp.float32
BF16 = jnp.bfloat16
VMEM_LIMIT = 48 * 2**20


def contract_rows(left, right):
    return lax.dot_general(left, right, (((0,), (0,)), ((), ())), preferred_element_type=F32)


def contract_cols(left, right):
    return lax.dot_general(left, right, (((1,), (1,)), ((), ())), preferred_element_type=F32)


def dot(left, right):
    return jnp.dot(left, right, preferred_element_type=F32)


def rms_scale(values):
    return lax.rsqrt(jnp.mean(values * values, axis=-1, keepdims=True) + 1e-06)


def rms_back(values, scale, gain, upstream):
    weighted = upstream * gain
    inner_average = jnp.mean(values * weighted, axis=-1, keepdims=True)
    return scale * weighted - values * scale * scale * scale * inner_average


def geglu(gate, up):
    return jax.nn.gelu(gate, approximate=True) * up


def bias_rows(table_row, out):
    span = out.shape[1]
    out[0:1, :] = table_row
    done = 1
    while done < out.shape[0]:
        out[done : 2 * done, :] = pltpu.roll(out[0:done, :], done, 1)
        done *= 2
    del span


def diagonal_sums(acc):
    rows, span = acc.shape
    total = acc[...]
    while rows > 1:
        rows //= 2
        total = total[:rows] + pltpu.roll(total[rows:], span - rows, 1)
    return total


def head_mask(shape, head, head_dim):
    lane = lax.broadcasted_iota(jnp.int32, shape, 1)
    return (lane >= head * head_dim) & (lane < (head + 1) * head_dim)


def window(me, n, part, query, key):
    q_at = lax.rem(me - query + n, n)
    k_at = lax.rem(me - key + n, n)
    return pl.multiple_of((n + k_at - q_at) * part, part)


def attend_kernel(n, head_dim, me_ref, table_ref, *refs):
    pieces, outs, lse_ref, bias, keys, values = (
        refs[:n], refs[n : 2 * n], refs[2 * n], refs[2 * n + 1], refs[2 * n + 2], refs[2 * n + 3],
    )
    part, lanes = pieces[0].shape[2:]
    per = lanes // head_dim
    me = me_ref[0]

    @pl.when(pl.program_id(1) == 0)
    def _():
        for head in range(per):
            bias_rows(table_ref[0, head : head + 1, :], bias.at[head])

    for b in range(n):
        keys[b * part : (b + 1) * part, :] = pieces[b][1, 0]
        values[b * part : (b + 1) * part, :] = pieces[b][2, 0]
    for a in range(n):
        lse = jnp.zeros((part, lanes), F32)
        mixed = jnp.zeros((part, lanes), F32)
        lane = lax.broadcasted_iota(jnp.int32, (part, lanes), 1)
        for head in range(per):
            mask = head_mask((part, lanes), head, head_dim)
            query = jnp.where(mask, pieces[a][0, 0], 0)
            scores = contract_cols(query, keys[...])
            scores = scores + jnp.concatenate(
                [bias[head, :, pl.ds(window(me, n, part, a, b), part)] for b in range(n)], axis=1
            )
            peak = jnp.max(scores, axis=1, keepdims=True)
            expo = jnp.exp(scores - peak)
            total = jnp.sum(expo, axis=1, keepdims=True)
            probs = (expo * (1.0 / total)).astype(BF16)
            mixed = jnp.where(mask, dot(probs, values[...]), mixed)
            lse = jnp.where(lane == head, peak + jnp.log(total), lse)
        outs[a][0] = mixed.astype(BF16)
        lse_ref[0, 0, a] = lse


def attend_back_kernel(n, head_dim, me_ref, table_ref, *refs):
    pieces, grads, lse_ref = refs[:n], refs[n : 2 * n], refs[2 * n]
    outs, table_out = refs[2 * n + 1 : 3 * n + 1], refs[3 * n + 1]
    bias, sums, keys, values, grad_k, grad_v = refs[3 * n + 2 :]
    part, lanes = pieces[0].shape[2:]
    per = lanes // head_dim
    me = me_ref[0]

    @pl.when(pl.program_id(1) == 0)
    def _():
        for head in range(per):
            bias_rows(table_ref[0, head : head + 1, :], bias.at[head])
        sums[...] = jnp.zeros_like(sums)

    for b in range(n):
        keys[b * part : (b + 1) * part, :] = pieces[b][1, 0]
        values[b * part : (b + 1) * part, :] = pieces[b][2, 0]
    grad_k[...] = jnp.zeros_like(grad_k)
    grad_v[...] = jnp.zeros_like(grad_v)
    for a in range(n):
        grad_q = jnp.zeros((part, lanes), F32)
        for head in range(per):
            mask = head_mask((part, lanes), head, head_dim)
            query = jnp.where(mask, pieces[a][0, 0], 0)
            upstream = jnp.where(mask, grads[a][0], 0)
            starts = [window(me, n, part, a, b) for b in range(n)]
            scores = contract_cols(query, keys[...])
            scores = scores + jnp.concatenate(
                [bias[head, :, pl.ds(start, part)] for start in starts], axis=1
            )
            probs = jnp.exp(scores - lse_ref[0, 0, a][:, head : head + 1])
            grad_probs = contract_cols(upstream, values[...])
            delta = jnp.sum(grad_probs * probs, axis=1, keepdims=True)
            grad_scores = (probs * (grad_probs - delta)).astype(BF16)
            for b, start in enumerate(starts):
                sums[head, :, pl.ds(start, part)] += grad_scores[:, b * part : (b + 1) * part].astype(F32)
            grad_q = jnp.where(mask, dot(grad_scores, keys[...]), grad_q)
            grad_k[...] += contract_rows(grad_scores, query)
            grad_v[...] += contract_rows(probs.astype(BF16), upstream)
        outs[a][0, 0] = grad_q.astype(BF16)
    for b in range(n):
        outs[b][1, 0] = grad_k[b * part : (b + 1) * part, :].astype(BF16)
        outs[b][2, 0] = grad_v[b * part : (b + 1) * part, :].astype(BF16)

    @pl.when(pl.program_id(1) == pl.num_programs(1) - 1)
    def _():
        for head in range(per):
            table_out[0, head : head + 1, :] = diagonal_sums(sums.at[head])


def attention_calls(n, seqs, part, cols, head_dim):
    lanes = 2 * head_dim
    groups, per, span = cols // lanes, lanes // head_dim, 2 * n * part
    smem = pl.BlockSpec(memory_space=pltpu.SMEM)
    table_spec = pl.BlockSpec((1, per, span), lambda g, s: (g, 0, 0))
    three = pl.BlockSpec((3, 1, part, lanes), lambda g, s: (0, s, 0, g))
    one = pl.BlockSpec((1, part, lanes), lambda g, s: (s, 0, g))
    lse_spec = pl.BlockSpec((1, 1, n, part, lanes), lambda g, s: (g, s, 0, 0, 0))
    piece = jax.ShapeDtypeStruct((3, seqs, part, cols), BF16)
    single = jax.ShapeDtypeStruct((seqs, part, cols), BF16)
    lse = jax.ShapeDtypeStruct((groups, seqs, n, part, lanes), F32)
    table = jax.ShapeDtypeStruct((groups, per, span), F32)
    length = n * part
    pairs = seqs * (cols // head_dim) * length * length
    forward = pl.pallas_call(
        functools.partial(attend_kernel, n, head_dim),
        grid=(groups, seqs),
        in_specs=[smem, table_spec] + [three] * n,
        out_specs=[one] * n + [lse_spec],
        out_shape=[single] * n + [lse],
        scratch_shapes=[
            pltpu.VMEM((per, part, span), F32),
            pltpu.VMEM((length, lanes), BF16),
            pltpu.VMEM((length, lanes), BF16),
        ],
        compiler_params=pltpu.CompilerParams(vmem_limit_bytes=VMEM_LIMIT),
        cost_estimate=pl.CostEstimate(
            flops=4 * pairs * 256, bytes_accessed=2**23, transcendentals=pairs
        ),
        name="attend",
    )
    backward = pl.pallas_call(
        functools.partial(attend_back_kernel, n, head_dim),
        grid=(groups, seqs),
        in_specs=[smem, table_spec] + [three] * n + [one] * n + [lse_spec],
        out_specs=[three] * n + [table_spec],
        out_shape=[piece] * n + [table],
        scratch_shapes=[
            pltpu.VMEM((per, part, span), F32),
            pltpu.VMEM((per, part, span), F32),
            pltpu.VMEM((length, lanes), BF16),
            pltpu.VMEM((length, lanes), BF16),
            pltpu.VMEM((length, lanes), F32),
            pltpu.VMEM((length, lanes), F32),
        ],
        compiler_params=pltpu.CompilerParams(vmem_limit_bytes=VMEM_LIMIT),
        cost_estimate=pl.CostEstimate(
            flops=10 * pairs * 256, bytes_accessed=2**24, transcendentals=pairs
        ),
        name="attend_back",
    )
    return forward, backward


MESH = pl.DeviceIdType.MESH


class Spot:
    def __init__(self, shards, ctx, tp):
        self.shards, self.chips, self.n, self.tps = shards, shards // 2, ctx, tp
        self.shard, self.me, self.half = (lax.axis_index(a) for a in ("shard", "ctx", "tp"))
        self.chip, self.core = self.shard // 2, lax.rem(self.shard, 2)
        self.mate = 2 * self.chip + 1 - self.core

    def away(self, d):
        return lax.rem(self.shard + 2 * d, self.shards)

    def barrier(self):
        peers = [{"shard": self.mate}] + [{"shard": self.away(d)} for d in range(1, self.chips)]
        peers += [{"ctx": lax.rem(self.me + d, self.n)} for d in range(1, self.n)]
        peers += [{"tp": 1 - self.half}]
        semaphore = pltpu.get_barrier_semaphore()
        for peer in peers:
            pl.semaphore_signal(semaphore, inc=1, device_id=peer, device_id_type=MESH)
        pl.semaphore_wait(semaphore, len(peers))


def remote(src, dst, send, recv, peer):
    return pltpu.make_async_remote_copy(
        src_ref=src, dst_ref=dst, send_sem=send, recv_sem=recv, device_id=peer, device_id_type=MESH
    )


class Gather:
    def __init__(self, spot, own, full, sems):
        self.spot, self.own, self.full = spot, own, full
        self.local, self.send, self.recv, self.on_send, self.on_recv = sems
        spot_shard = spot.shard
        self.keep = pltpu.make_async_copy(own, full.at[spot_shard], self.local)
        self.far = [
            remote(own, full.at[spot_shard], self.send.at[d], self.recv.at[d], {"shard": spot.away(d)})
            for d in range(1, spot.chips)
        ]
        mate = {"shard": spot.mate}
        self.near = [remote(own, full.at[spot_shard], self.on_send.at[0], self.on_recv.at[0], mate)]
        for d in range(1, spot.chips):
            at = full.at[lax.rem(spot.shard - 2 * d + spot.shards, spot.shards)]
            self.near.append(remote(at, at, self.on_send.at[d], self.on_recv.at[d], mate))

    def start_far(self):
        for copy in self.far:
            copy.start()

    def start_near(self):
        self.keep.start()
        self.near[0].start()

    def pass_on(self):
        for d, copy in enumerate(self.far, 1):
            copy.wait_recv()
            self.near[d].start()

    def wait_own(self):
        self.keep.wait()
        self.near[0].wait_recv()

    def wait_near(self):
        for copy in self.near[1:]:
            copy.wait_recv()

    def wait_sent(self):
        for copy in self.far + self.near:
            copy.wait_send()


def forward_kernel(
    dims, tokens, gains, table, wq, wk, wv, wo, wi0, wi1, wff,
    normed, hidden, normed_two, attended, lse, pieces_out, full_q, full_k, full_v, full_o, full_0, full_1, full_2,
    weights, acc, bias, staged, pieces, mixed, heads_in, branch, branch_in,
    local_sem, far_send, far_recv, near_send, near_recv, head_send, head_recv, back_send, back_recv,
    swap_send, swap_recv, out_sem,
):
    spot = Spot(*dims.mesh)
    n, seqs, part, cols, head_dim = dims.n, dims.seqs, dims.part, dims.cols, dims.head_dim
    me, shards = spot.me, spot.shards
    shard_rows = weights.shape[2]
    rows = seqs * part
    lanes = 2 * head_dim
    per = 2
    spot.barrier()

    def gather(i, own, full):
        sems = [local_sem.at[i], far_send.at[i], far_recv.at[i], near_send.at[i], near_recv.at[i]]
        return Gather(spot, own, full, sems)

    loads = [gather(i, w, weights.at[i]) for i, w in enumerate((wq, wk, wv, wo))]
    loads += [gather(4 + i, w, f) for i, (w, f) in enumerate(((wi0, full_0), (wi1, full_1), (wff, full_2)))]
    for load in loads[:3]:
        load.start_far()
    for load in loads[:3]:
        load.start_near()

    @pl.loop(0, rows // 64)
    def _(i):
        at = pl.ds(pl.multiple_of(i * 64, 64), 64)
        values = tokens[at, :].astype(F32)
        normed[at, :] = (values * rms_scale(values) * gains[0:1, :]).astype(BF16)

    for head in range(dims.own_heads):
        bias_rows(table[head : head + 1, :], bias.at[head])

    def term(i, shard):
        at = pl.ds(pl.multiple_of(shard * shard_rows, 128), shard_rows)
        return dot(normed[:, at], weights[i, shard])

    moves = []
    for i, load in enumerate(loads[:3]):
        load.wait_own()
        acc[...] = term(i, spot.shard)
        acc[...] += term(i, spot.mate)
        load.pass_on()
        if i == 2:
            for later in loads[3:]:
                later.start_far()
            for later in loads[3:]:
                later.start_near()
        for d in range(1, spot.chips):
            acc[...] += term(i, lax.rem(spot.shard - 2 * d + shards, shards))
        load.wait_near()
        for d in range(1, spot.chips):
            acc[...] += term(i, lax.rem(spot.mate - 2 * d + shards, shards))
        for k in range(n):
            for s in range(seqs):
                staged[i, k, s] = acc[s * part : (s + 1) * part, k * cols : (k + 1) * cols].astype(BF16)
        for d in range(1, n):
            peer = lax.rem(me + d, n)
            move = remote(
                staged.at[i, peer], pieces.at[i, me], head_send.at[i, d], head_recv.at[i, d], {"ctx": peer}
            )
            move.start()
            moves.append(move)
        pieces[i, me] = staged[i, me]
    outs = [
        pltpu.make_async_copy(weights.at[i], full, out_sem.at[i])
        for i, full in enumerate((full_q, full_k, full_v, full_o))
    ]
    for copy in outs[:3]:
        copy.start()
    for move in moves:
        move.wait_recv()
    loads[3].wait_own()
    loads[3].pass_on()
    outs.append(pltpu.make_async_copy(pieces, pieces_out, out_sem.at[4]))
    outs[4].start()

    def back(s, at, to):
        return remote(mixed.at[s, at], heads_in.at[me, s], back_send.at[s, at], back_recv.at[s, me], {"ctx": to})

    @pl.loop(0, seqs * n)
    def _(step):
        s, a = step // n, lax.rem(step, n)
        lane = lax.broadcasted_iota(jnp.int32, (part, lanes), 1)
        log_total = jnp.zeros((part, lanes), F32)
        for group in range(cols // lanes):
            span = slice(group * lanes, (group + 1) * lanes)
            result = jnp.zeros((part, lanes), F32)
            for j in range(per):
                head = group * per + j
                mask = (lane >= j * head_dim) & (lane < (j + 1) * head_dim)
                query = jnp.where(mask, pieces[0, a, s, :, span], 0)
                scores = jnp.concatenate(
                    [
                        contract_cols(query, pieces[1, b, s, :, span])
                        + bias[head, :, pl.ds(pl.multiple_of((n + b - a) * part, part), part)]
                        for b in range(n)
                    ],
                    axis=1,
                )
                peak = jnp.max(scores, axis=1, keepdims=True)
                expo = jnp.exp(scores - peak)
                total = jnp.sum(expo, axis=1, keepdims=True)
                probs = (expo * (1.0 / total)).astype(BF16)
                summed = sum(
                    dot(probs[:, b * part : (b + 1) * part], pieces[2, b, s, :, span]) for b in range(n)
                )
                result = jnp.where(mask, summed, result)
                log_total = jnp.where(lane == head, peak + jnp.log(total), log_total)
            mixed[s, a, :, span] = result.astype(BF16)
        lse[s, a] = log_total

        @pl.when(a != me)
        def _():
            back(s, a, a).start()

        @pl.when(a == me)
        def _():
            heads_in[a, s] = mixed[s, a]

    loads[3].wait_near()
    outs[3].start()
    swaps = []
    for s in range(seqs):
        at = slice(s * part, (s + 1) * part)
        for d in range(1, n):
            peer = lax.rem(me + d, n)
            remote(
                mixed.at[s, 0], heads_in.at[peer, s], back_send.at[s, peer], back_recv.at[s, peer], {"ctx": peer}
            ).wait_recv()
        for k in range(n):
            attended[at, k * cols : (k + 1) * cols] = heads_in[k, s]
        for j in range(shards):
            branch[s, :, j * shard_rows : (j + 1) * shard_rows] = contract_cols(
                attended[at, :], weights[3, j]
            ).astype(BF16)
        swap = remote(branch.at[s], branch_in.at[s], swap_send.at[s], swap_recv.at[s], {"tp": 1 - spot.half})
        swap.start()
        swaps.append(swap)
    loads[4].wait_own()
    loads[4].pass_on()
    for s in range(seqs):
        swaps[s].wait_recv()

        @pl.loop(0, part // 64)
        def _(i):
            here = pl.ds(pl.multiple_of(i * 64, 64), 64)
            at = pl.ds(pl.multiple_of(s * part + i * 64, 64), 64)
            values = tokens[at, :].astype(F32) + (
                branch[s, here, :].astype(F32) + branch_in[s, here, :].astype(F32)
            )
            hidden[at, :] = values
            normed_two[at, :] = (values * rms_scale(values) * gains[1:2, :]).astype(BF16)

    for load in loads[5:]:
        load.wait_own()
        load.pass_on()
    for load in loads[4:]:
        load.wait_near()
    for load in loads:
        load.wait_sent()
    for move in moves + swaps:
        move.wait_send()
    for s in range(seqs):
        for d in range(1, n):
            peer = lax.rem(me + d, n)
            back(s, peer, peer).wait_send()
    for copy in outs:
        copy.wait()


class Dims:
    def __init__(self, links, seqs, part, width, inner_width, units, heads):
        self.mesh = (links.shard, links.ctx, links.tp)
        self.n, self.seqs, self.part, self.width = links.ctx, seqs, part, width
        self.inner_width, self.units = inner_width, units
        self.head_dim = inner_width // heads
        self.cols, self.own_heads = inner_width // links.ctx, heads // links.ctx
        self.shards, self.shard_rows = links.shard, width // links.shard


def forward_call(dims):
    rows, width, n, part, seqs = dims.seqs * dims.part, dims.width, dims.n, dims.part, dims.seqs
    shards, shard_rows, inner, units = dims.shards, dims.shard_rows, dims.inner_width, dims.units
    lanes, span = 2 * dims.head_dim, 2 * n * part
    vmem, anywhere = pl.BlockSpec(memory_space=pltpu.VMEM), pl.BlockSpec(memory_space=pl.ANY)
    shape = jax.ShapeDtypeStruct
    dma = pltpu.SemaphoreType.DMA
    chips = shards // 2
    block = (seqs, part, dims.cols)
    return pl.pallas_call(
        functools.partial(forward_kernel, dims),
        in_specs=[vmem] * 3 + [anywhere] * 7,
        out_specs=[vmem] * 5 + [anywhere] * 8,
        out_shape=[
            shape((rows, width), BF16),
            shape((rows, width), F32),
            shape((rows, width), BF16),
            shape((rows, inner), BF16),
            shape((seqs, n, part, lanes), F32),
            shape((3, n) + block, BF16),
        ]
        + [shape((shards, shard_rows, inner), BF16)] * 4
        + [shape((shards, shard_rows, units), BF16)] * 3,
        scratch_shapes=[
            pltpu.VMEM((4, shards, shard_rows, inner), BF16),
            pltpu.VMEM((rows, inner), F32),
            pltpu.VMEM((dims.own_heads, part, span), F32),
            pltpu.VMEM((3, n) + block, BF16),
            pltpu.VMEM((3, n) + block, BF16),
            pltpu.VMEM((seqs, n, part, dims.cols), BF16),
            pltpu.VMEM((n,) + block, BF16),
            pltpu.VMEM((seqs, part, width), BF16),
            pltpu.VMEM((seqs, part, width), BF16),
            dma((7,)),
            dma((7, chips)),
            dma((7, chips)),
            dma((7, chips)),
            dma((7, chips)),
            dma((3, n)),
            dma((3, n)),
            dma((seqs, n)),
            dma((seqs, n)),
            dma((seqs,)),
            dma((seqs,)),
            dma((5,)),
        ],
        compiler_params=pltpu.CompilerParams(
            vmem_limit_bytes=60 * 2**20, collective_id=0, has_side_effects=True
        ),
        name="forward",
    )


def ring(n, d):
    return [(i, (i + d) % n) for i in range(n)]


class Links:
    def __init__(self, mesh):
        self.shard, self.ctx, self.tp = mesh.shape["shard"], mesh.shape["ctx"], mesh.shape["tp"]
        self.chips = self.shard // 2

    def to_core(self, value):
        return lax.ppermute(value, "shard", [(i, i ^ 1) for i in range(self.shard)])

    def to_chip(self, value, d):
        n = self.shard
        return lax.ppermute(value, "shard", [(i, (i + 2 * d) % n) for i in range(n)])

    def tp_sum(self, value):
        if self.tp != 2:
            return lax.psum(value, "tp").astype(F32)
        other = lax.ppermute(value, "tp", ring(2, 1))
        return value.astype(F32) + other.astype(F32)

    def ctx_sum(self, value):
        low = value.astype(BF16)
        if self.ctx != 4:
            return lax.psum(low, "ctx").astype(F32)
        inward = lax.ppermute(low, "ctx", [(0, 1), (3, 2)])
        half = (low.astype(F32) + inward.astype(F32)).astype(BF16)
        across = lax.ppermute(half, "ctx", [(1, 2), (2, 1)])
        whole = (half.astype(F32) + across.astype(F32)).astype(BF16)
        outward = lax.ppermute(whole, "ctx", [(1, 0), (2, 3)])
        me = lax.axis_index("ctx")
        middle = (me == 1) | (me == 2)
        return jnp.where(middle, whole, outward).astype(F32)

    def shard_sums(self, left, right):
        n, chips = self.shard, self.chips
        rows = left.shape[1] // n
        me = lax.axis_index("shard")
        chip, core = me // 2, me % 2

        def term(chip_at, core_at):
            at = (2 * chip_at + core_at) * rows
            return contract_rows(lax.dynamic_slice_in_dim(left, at, rows, 1), right)

        def chip_of(d):
            return lax.rem(chip + d, chips)

        order = list(range(1, chips)) + [0]
        got = {d: self.to_core(term(chip_of(d), 1 - core).astype(BF16)) for d in order}
        total = None
        arrived = []
        for d in order:
            pair = term(chip_of(d), core) + got[d].astype(F32)
            if d:
                arrived.append(self.to_chip(pair.astype(BF16), d))
            else:
                total = pair
        for value in arrived:
            total = total + value.astype(F32)
        return total

    def small_sum(self, value):
        for axis, n in (("shard", self.shard), ("ctx", self.ctx)):
            step = 1
            while step < n:
                value = value + lax.ppermute(value, axis, [(i, i ^ step) for i in range(n)])
                step *= 2
        return value


def per_device(
    links,
    tokens,
    cotangent,
    buckets,
    query_weight,
    key_weight,
    value_weight,
    output_weight,
    gate_weight,
    up_weight,
    down_weight,
    norm_gain,
    ffn_gain,
    bucket_bias_table,
):
    seqs, part, width = tokens.shape
    rows = seqs * part
    slots, heads = bucket_bias_table.shape
    inner_width = query_weight.shape[1]
    head_dim = inner_width // heads
    n = links.ctx
    cols = inner_width // n
    own_heads = heads // n
    me = lax.axis_index("ctx")
    gain_one = norm_gain.astype(F32)
    gain_two = ffn_gain.astype(F32)

    def gathered(weight):
        return lax.all_gather(weight, "shard", axis=0, tiled=True)

    def at_ctx(d):
        return lax.rem(me + d + n, n)

    corner = lax.dynamic_slice(buckets, (0, me * part), (part, part))
    later, earlier = corner[0, :], corner[:, 0]
    reach = n * part
    by_offset = jnp.concatenate(
        [
            jnp.broadcast_to(earlier[part - 1 :], (reach - part + 1,)),
            earlier[:0:-1],
            later,
            jnp.broadcast_to(later[part - 1 :], (reach - part,)),
        ]
    )
    indicator = by_offset[None, :] == jnp.arange(slots, dtype=jnp.int32)[:, None]
    own_table = lax.dynamic_slice(bucket_bias_table, (0, me * own_heads), (slots, own_heads))
    offset_bias = lax.dot_general(
        own_table, indicator.astype(BF16), (((0,), (0,)), ((), ())), preferred_element_type=F32
    )
    groups = cols // (2 * head_dim)
    offset_bias = offset_bias.reshape(groups, 2, 2 * reach)
    where_am_i = me.astype(jnp.int32).reshape(1)
    unused_attend, attend_back = attention_calls(n, seqs, part, cols, head_dim)

    dims = Dims(links, seqs, part, width, inner_width, gate_weight.shape[1], heads)
    normed, hidden, normed_two, attended, lse, pieces, *full = forward_call(dims)(
        tokens.reshape(rows, width),
        jnp.stack([gain_one, gain_two]),
        offset_bias.reshape(own_heads, 2 * reach),
        query_weight, key_weight, value_weight, output_weight, gate_weight, up_weight, down_weight,
    )
    wq, wk, wv, wo, wi0, wi1, wff = (w.reshape(width, w.shape[2]) for w in full)
    inputs = tokens.reshape(rows, width).astype(F32)
    scale_one, scale_two = rms_scale(inputs), rms_scale(hidden)

    def heads_of(values, d):
        start = at_ctx(d) * cols
        return [lax.dynamic_slice_in_dim(v, start, cols, 1).reshape(seqs, part, cols) for v in values]

    def heads_back(blocks):
        blocks = [blocks[0]] + [lax.ppermute(blocks[d], "ctx", ring(n, n - d)) for d in range(1, n)]
        around = jnp.concatenate(blocks, axis=-1)
        twice = jnp.concatenate([around, around], axis=-1)
        return lax.dynamic_slice_in_dim(twice, (n - me) * cols, n * cols, around.ndim - 1)

    pieces = [lax.dynamic_index_in_dim(pieces, at_ctx(-d), 1, keepdims=False) for d in range(n)]
    lse = jnp.stack([lax.dynamic_index_in_dim(lse, at_ctx(-d), 1, keepdims=False) for d in range(n)], axis=1)
    lse = jnp.stack([lse[..., 2 * g : 2 * g + 2] for g in range(groups)])
    lse = jnp.pad(lse, ((0, 0),) * 4 + ((0, 2 * head_dim - 2),))
    gate = dot(normed_two, wi0)
    up = dot(normed_two, wi1)
    inner = geglu(gate, up).astype(BF16)
    ffn_out = links.tp_sum(contract_cols(inner, wff).astype(BF16))
    result = (hidden + ffn_out).astype(BF16).reshape(seqs, part, width)

    upstream = cotangent.reshape(rows, width).astype(F32)
    upstream_low = cotangent.reshape(rows, width)
    grad_down_w = links.ctx_sum(links.shard_sums(upstream_low, inner))
    grad_inner = dot(upstream_low, wff)
    unused, geglu_backward_pull = jax.vjp(geglu, gate, up)
    grad_gate, grad_up = geglu_backward_pull(grad_inner)
    grad_gate = grad_gate.astype(BF16)
    grad_up = grad_up.astype(BF16)
    grad_normed_two = links.tp_sum(
        (contract_cols(grad_gate, wi0) + contract_cols(grad_up, wi1)).astype(BF16)
    )
    grad_gate_w = links.ctx_sum(links.shard_sums(normed_two, grad_gate))
    grad_up_w = links.ctx_sum(links.shard_sums(normed_two, grad_up))
    grad_ffn_gain = jnp.sum(grad_normed_two * hidden * scale_two, axis=0)
    grad_hidden = upstream + rms_back(hidden, scale_two, gain_two, grad_normed_two)
    branch_low = grad_hidden.astype(BF16)
    grad_attended = dot(branch_low, wo).astype(BF16)
    grad_output_w = links.ctx_sum(links.shard_sums(branch_low, attended))

    upstreams = [heads_of([grad_attended], d)[0] for d in range(n)]
    upstreams = [upstreams[0]] + [lax.ppermute(upstreams[d], "ctx", ring(n, d)) for d in range(1, n)]
    *grad_pieces, offset_grad = attend_back(where_am_i, offset_bias, *pieces, *upstreams, lse)
    grad_projected = heads_back(grad_pieces).reshape(3, rows, inner_width)
    grad_query, grad_key, grad_value = grad_projected[0], grad_projected[1], grad_projected[2]
    offset_grad = offset_grad.reshape(own_heads, 2 * reach)
    table_part = jnp.sum(jnp.where(indicator[:, None, :], offset_grad[None], 0.0), axis=-1)
    grad_table = lax.dynamic_update_slice(
        jnp.zeros((slots, heads), F32), table_part, (0, me * own_heads)
    )

    grad_normed = links.tp_sum(
        (contract_cols(grad_query, wq) + contract_cols(grad_key, wk) + contract_cols(grad_value, wv)).astype(BF16)
    )
    grad_query_w = links.ctx_sum(links.shard_sums(normed, grad_query))
    grad_key_w = links.ctx_sum(links.shard_sums(normed, grad_key))
    grad_value_w = links.ctx_sum(links.shard_sums(normed, grad_value))
    grad_norm_gain = jnp.sum(grad_normed * inputs * scale_one, axis=0)
    grad_inputs = grad_hidden + rms_back(inputs, scale_one, gain_one, grad_normed)
    small = links.small_sum(jnp.concatenate([grad_norm_gain, grad_ffn_gain, grad_table.reshape(-1)]))
    return (
        result,
        grad_inputs.reshape(seqs, part, width),
        grad_query_w,
        grad_key_w,
        grad_value_w,
        grad_output_w,
        grad_gate_w,
        grad_up_w,
        grad_down_w,
        small[:width],
        small[width : 2 * width],
        small[2 * width :].reshape(slots, heads),
    )


def solution(mesh):
    rows, weights = P("shard", "ctx", None), P("shard", "tp")
    return jax.shard_map(
        functools.partial(per_device, Links(mesh)),
        mesh=mesh,
        in_specs=(rows, rows, P("ctx", None)) + (weights,) * 7 + (P(), P(), P(None, "tp")),
        out_specs=(rows, rows) + (weights,) * 7 + (P(), P(), P(None, "tp")),
        check_vma=False,
    )
```

```python
import functools

import jax
import jax.numpy as jnp
from jax import lax
from jax.experimental import pallas as pl
from jax.experimental.pallas import tpu as pltpu
from jax.sharding import PartitionSpec as P

F32 = jnp.float32
BF16 = jnp.bfloat16
VMEM_LIMIT = 48 * 2**20


def contract_rows(left, right):
    return lax.dot_general(left, right, (((0,), (0,)), ((), ())), preferred_element_type=F32)


def contract_cols(left, right):
    return lax.dot_general(left, right, (((1,), (1,)), ((), ())), preferred_element_type=F32)


def dot(left, right):
    return jnp.dot(left, right, preferred_element_type=F32)


def rms_scale(values):
    return lax.rsqrt(jnp.mean(values * values, axis=-1, keepdims=True) + 1e-06)


def rms_back(values, scale, gain, upstream):
    weighted = upstream * gain
    inner_average = jnp.mean(values * weighted, axis=-1, keepdims=True)
    return scale * weighted - values * scale * scale * scale * inner_average


def geglu(gate, up):
    return jax.nn.gelu(gate, approximate=True) * up


def bias_rows(table_row, out):
    span = out.shape[1]
    out[0:1, :] = table_row
    done = 1
    while done < out.shape[0]:
        out[done : 2 * done, :] = pltpu.roll(out[0:done, :], done, 1)
        done *= 2
    del span


def diagonal_sums(acc):
    rows, span = acc.shape
    total = acc[...]
    while rows > 1:
        rows //= 2
        total = total[:rows] + pltpu.roll(total[rows:], span - rows, 1)
    return total


MESH = pl.DeviceIdType.MESH


class Spot:
    def __init__(self, shards, ctx, tp):
        self.shards, self.chips, self.n, self.tps = shards, shards // 2, ctx, tp
        self.shard, self.me, self.half = (lax.axis_index(a) for a in ("shard", "ctx", "tp"))
        self.chip, self.core = self.shard // 2, lax.rem(self.shard, 2)
        self.mate = 2 * self.chip + 1 - self.core

    def away(self, d):
        return lax.rem(self.shard + 2 * d, self.shards)

    def barrier(self):
        peers = [{"shard": self.mate}] + [{"shard": self.away(d)} for d in range(1, self.chips)]
        peers += [{"ctx": lax.rem(self.me + d, self.n)} for d in range(1, self.n)]
        peers += [{"tp": 1 - self.half}]
        semaphore = pltpu.get_barrier_semaphore()
        for peer in peers:
            pl.semaphore_signal(semaphore, inc=1, device_id=peer, device_id_type=MESH)
        pl.semaphore_wait(semaphore, len(peers))


def remote(src, dst, send, recv, peer):
    return pltpu.make_async_remote_copy(
        src_ref=src, dst_ref=dst, send_sem=send, recv_sem=recv, device_id=peer, device_id_type=MESH
    )


class Gather:
    def __init__(self, spot, own, full, sems):
        self.spot, self.own, self.full = spot, own, full
        self.local, self.send, self.recv, self.on_send, self.on_recv = sems
        spot_shard = spot.shard
        self.keep = pltpu.make_async_copy(own, full.at[spot_shard], self.local)
        self.far = [
            remote(own, full.at[spot_shard], self.send.at[d], self.recv.at[d], {"shard": spot.away(d)})
            for d in range(1, spot.chips)
        ]
        mate = {"shard": spot.mate}
        self.near = [remote(own, full.at[spot_shard], self.on_send.at[0], self.on_recv.at[0], mate)]
        for d in range(1, spot.chips):
            at = full.at[lax.rem(spot.shard - 2 * d + spot.shards, spot.shards)]
            self.near.append(remote(at, at, self.on_send.at[d], self.on_recv.at[d], mate))

    def start_far(self):
        for copy in self.far:
            copy.start()

    def start_near(self):
        self.keep.start()
        self.near[0].start()

    def pass_on(self):
        for d, copy in enumerate(self.far, 1):
            copy.wait_recv()
            self.near[d].start()

    def wait_own(self):
        self.keep.wait()
        self.near[0].wait_recv()

    def wait_near(self):
        for copy in self.near[1:]:
            copy.wait_recv()

    def wait_sent(self):
        for copy in self.far + self.near:
            copy.wait_send()


def forward_kernel(
    dims, tokens, gains, table, wq, wk, wv, wo, wi0, wi1, wff,
    normed, hidden, normed_two, attended, lse, pieces_out, full_q, full_k, full_v, full_o, full_0, full_1, full_2,
    weights, acc, bias, staged, pieces, mixed, heads_in, branch, branch_in,
    local_sem, far_send, far_recv, near_send, near_recv, head_send, head_recv, back_send, back_recv,
    swap_send, swap_recv, out_sem,
):
    spot = Spot(*dims.mesh)
    n, seqs, part, cols, head_dim = dims.n, dims.seqs, dims.part, dims.cols, dims.head_dim
    me, shards = spot.me, spot.shards
    shard_rows = weights.shape[2]
    rows = seqs * part
    lanes = 2 * head_dim
    per = 2
    spot.barrier()

    def gather(i, own, full):
        sems = [local_sem.at[i], far_send.at[i], far_recv.at[i], near_send.at[i], near_recv.at[i]]
        return Gather(spot, own, full, sems)

    loads = [gather(i, w, weights.at[i]) for i, w in enumerate((wq, wk, wv, wo))]
    loads += [gather(4 + i, w, f) for i, (w, f) in enumerate(((wi0, full_0), (wi1, full_1), (wff, full_2)))]
    for load in loads[:3]:
        load.start_far()
    for load in loads[:3]:
        load.start_near()

    @pl.loop(0, rows // 64)
    def _(i):
        at = pl.ds(pl.multiple_of(i * 64, 64), 64)
        values = tokens[at, :].astype(F32)
        normed[at, :] = (values * rms_scale(values) * gains[0:1, :]).astype(BF16)

    for head in range(dims.own_heads):
        bias_rows(table[head : head + 1, :], bias.at[head])

    def term(i, shard):
        at = pl.ds(pl.multiple_of(shard * shard_rows, 128), shard_rows)
        return dot(normed[:, at], weights[i, shard])

    moves = []
    for i, load in enumerate(loads[:3]):
        load.wait_own()
        acc[...] = term(i, spot.shard)
        acc[...] += term(i, spot.mate)
        load.pass_on()
        if i == 2:
            for later in loads[3:]:
                later.start_far()
            for later in loads[3:]:
                later.start_near()
        for d in range(1, spot.chips):
            acc[...] += term(i, lax.rem(spot.shard - 2 * d + shards, shards))
        load.wait_near()
        for d in range(1, spot.chips):
            acc[...] += term(i, lax.rem(spot.mate - 2 * d + shards, shards))
        for k in range(n):
            for s in range(seqs):
                staged[i, k, s] = acc[s * part : (s + 1) * part, k * cols : (k + 1) * cols].astype(BF16)
        for d in range(1, n):
            peer = lax.rem(me + d, n)
            move = remote(
                staged.at[i, peer], pieces.at[i, me], head_send.at[i, d], head_recv.at[i, d], {"ctx": peer}
            )
            move.start()
            moves.append(move)
        pieces[i, me] = staged[i, me]
    outs = [
        pltpu.make_async_copy(weights.at[i], full, out_sem.at[i])
        for i, full in enumerate((full_q, full_k, full_v, full_o))
    ]
    for copy in outs[:3]:
        copy.start()
    for move in moves:
        move.wait_recv()
    loads[3].wait_own()
    loads[3].pass_on()
    outs.append(pltpu.make_async_copy(pieces, pieces_out, out_sem.at[4]))
    outs[4].start()

    def back(s, at, to):
        return remote(mixed.at[s, at], heads_in.at[me, s], back_send.at[s, at], back_recv.at[s, me], {"ctx": to})

    @pl.loop(0, seqs * n)
    def _(step):
        s, a = step // n, lax.rem(step, n)
        lane = lax.broadcasted_iota(jnp.int32, (part, lanes), 1)
        log_total = jnp.zeros((part, lanes), F32)
        for group in range(cols // lanes):
            span = slice(group * lanes, (group + 1) * lanes)
            result = jnp.zeros((part, lanes), F32)
            for j in range(per):
                head = group * per + j
                mask = (lane >= j * head_dim) & (lane < (j + 1) * head_dim)
                query = jnp.where(mask, pieces[0, a, s, :, span], 0)
                scores = jnp.concatenate(
                    [
                        contract_cols(query, pieces[1, b, s, :, span])
                        + bias[head, :, pl.ds(pl.multiple_of((n + b - a) * part, part), part)]
                        for b in range(n)
                    ],
                    axis=1,
                )
                peak = jnp.max(scores, axis=1, keepdims=True)
                expo = jnp.exp(scores - peak)
                total = jnp.sum(expo, axis=1, keepdims=True)
                probs = (expo * (1.0 / total)).astype(BF16)
                summed = sum(
                    dot(probs[:, b * part : (b + 1) * part], pieces[2, b, s, :, span]) for b in range(n)
                )
                result = jnp.where(mask, summed, result)
                log_total = jnp.where(lane == head, peak + jnp.log(total), log_total)
            mixed[s, a, :, span] = result.astype(BF16)
        lse[s, a] = log_total

        @pl.when(a != me)
        def _():
            back(s, a, a).start()

        @pl.when(a == me)
        def _():
            heads_in[a, s] = mixed[s, a]

    loads[3].wait_near()
    outs[3].start()
    swaps = []
    for s in range(seqs):
        at = slice(s * part, (s + 1) * part)
        for d in range(1, n):
            peer = lax.rem(me + d, n)
            remote(
                mixed.at[s, 0], heads_in.at[peer, s], back_send.at[s, peer], back_recv.at[s, peer], {"ctx": peer}
            ).wait_recv()
        for k in range(n):
            attended[at, k * cols : (k + 1) * cols] = heads_in[k, s]
        for j in range(shards):
            branch[s, :, j * shard_rows : (j + 1) * shard_rows] = contract_cols(
                attended[at, :], weights[3, j]
            ).astype(BF16)
        swap = remote(branch.at[s], branch_in.at[s], swap_send.at[s], swap_recv.at[s], {"tp": 1 - spot.half})
        swap.start()
        swaps.append(swap)
    loads[4].wait_own()
    loads[4].pass_on()
    for s in range(seqs):
        swaps[s].wait_recv()

        @pl.loop(0, part // 64)
        def _(i):
            here = pl.ds(pl.multiple_of(i * 64, 64), 64)
            at = pl.ds(pl.multiple_of(s * part + i * 64, 64), 64)
            values = tokens[at, :].astype(F32) + (
                branch[s, here, :].astype(F32) + branch_in[s, here, :].astype(F32)
            )
            hidden[at, :] = values
            normed_two[at, :] = (values * rms_scale(values) * gains[1:2, :]).astype(BF16)

    for load in loads[5:]:
        load.wait_own()
        load.pass_on()
    for load in loads[4:]:
        load.wait_near()
    for load in loads:
        load.wait_sent()
    for move in moves + swaps:
        move.wait_send()
    for s in range(seqs):
        for d in range(1, n):
            peer = lax.rem(me + d, n)
            back(s, peer, peer).wait_send()
    for copy in outs:
        copy.wait()


class Dims:
    def __init__(self, links, seqs, part, width, inner_width, units, heads):
        self.mesh = (links.shard, links.ctx, links.tp)
        self.n, self.seqs, self.part, self.width = links.ctx, seqs, part, width
        self.inner_width, self.units = inner_width, units
        self.head_dim = inner_width // heads
        self.cols, self.own_heads = inner_width // links.ctx, heads // links.ctx
        self.shards, self.shard_rows = links.shard, width // links.shard


def forward_call(dims):
    rows, width, n, part, seqs = dims.seqs * dims.part, dims.width, dims.n, dims.part, dims.seqs
    shards, shard_rows, inner, units = dims.shards, dims.shard_rows, dims.inner_width, dims.units
    lanes, span = 2 * dims.head_dim, 2 * n * part
    vmem, anywhere = pl.BlockSpec(memory_space=pltpu.VMEM), pl.BlockSpec(memory_space=pl.ANY)
    shape = jax.ShapeDtypeStruct
    dma = pltpu.SemaphoreType.DMA
    chips = shards // 2
    block = (seqs, part, dims.cols)
    return pl.pallas_call(
        functools.partial(forward_kernel, dims),
        in_specs=[vmem] * 3 + [anywhere] * 7,
        out_specs=[vmem] * 5 + [anywhere] * 8,
        out_shape=[
            shape((rows, width), BF16),
            shape((rows, width), F32),
            shape((rows, width), BF16),
            shape((rows, inner), BF16),
            shape((seqs, n, part, lanes), F32),
            shape((3, n) + block, BF16),
        ]
        + [shape((shards, shard_rows, inner), BF16)] * 4
        + [shape((shards, shard_rows, units), BF16)] * 3,
        scratch_shapes=[
            pltpu.VMEM((4, shards, shard_rows, inner), BF16),
            pltpu.VMEM((rows, inner), F32),
            pltpu.VMEM((dims.own_heads, part, span), F32),
            pltpu.VMEM((3, n) + block, BF16),
            pltpu.VMEM((3, n) + block, BF16),
            pltpu.VMEM((seqs, n, part, dims.cols), BF16),
            pltpu.VMEM((n,) + block, BF16),
            pltpu.VMEM((seqs, part, width), BF16),
            pltpu.VMEM((seqs, part, width), BF16),
            dma((7,)),
            dma((7, chips)),
            dma((7, chips)),
            dma((7, chips)),
            dma((7, chips)),
            dma((3, n)),
            dma((3, n)),
            dma((seqs, n)),
            dma((seqs, n)),
            dma((seqs,)),
            dma((seqs,)),
            dma((5,)),
        ],
        compiler_params=pltpu.CompilerParams(
            vmem_limit_bytes=60 * 2**20, collective_id=0, has_side_effects=True
        ),
        name="forward",
    )


CHUNK = 512
SLOTS = 4


class Pump:
    def __init__(self, dims, spot, left, right, sources, from_heads, outs, buffers, sems, credits):
        self.dims, self.spot, self.left, self.right = dims, spot, left, right
        self.sources, self.from_heads, self.outs = sources, from_heads, outs
        self.core_out, self.core_in, self.far_out, self.far_in, self.line, self.line_in, self.across_in, self.done = buffers
        (
            self.right_sem, self.core_send, self.core_recv, self.far_send, self.far_recv, self.in_send, self.in_recv,
            self.across_send, self.across_recv, self.out_send, self.out_recv, self.fin_sem,
        ) = sems
        self.core_credit, self.far_credit, self.in_credit, self.across_credit, self.out_credit = credits
        units, heads = dims.units // CHUNK, dims.inner_width // CHUNK
        self.units, self.heads = units, heads
        self.early = 3 * units + heads
        self.total = 3 * units + 4 * heads
        self.bases = [(i * units, units) for i in range(3)]
        self.bases += [(3 * units + i * heads, heads) for i in range(4)]
        me, n = spot.me, dims.n
        middle = n // 2
        self.is_middle = (me == middle - 1) | (me == middle)
        self.is_end = (me == 0) | (me == n - 1)
        self.has_outer, self.has_inner = jnp.logical_not(self.is_end), jnp.logical_not(self.is_middle)
        low_side = me < middle
        self.facing = jnp.where(low_side, middle, middle - 1)
        toward, away = jnp.where(low_side, me + 1, me - 1), jnp.where(low_side, me - 1, me + 1)
        self.inner = jnp.where(self.is_middle, self.facing, toward)
        self.outer = jnp.where(self.is_end, self.inner, away)
        self.last = self.total + 10

    def core(self, c, k):
        return remote(
            self.core_out.at[lax.rem(c, 2)], self.core_in.at[k], self.core_send.at[lax.rem(c, 2)],
            self.core_recv.at[k], {"shard": self.spot.mate},
        )

    def far(self, k, d):
        return remote(
            self.far_out.at[k, d - 1], self.far_in.at[k, d - 1], self.far_send.at[k, d - 1],
            self.far_recv.at[k, d - 1], {"shard": self.spot.away(d)},
        )

    def inward(self, k):
        return remote(
            self.line.at[k], self.line_in.at[k], self.in_send.at[k], self.in_recv.at[k], {"ctx": self.inner}
        )

    def across(self, k):
        return remote(
            self.line.at[k], self.across_in.at[k], self.across_send.at[k], self.across_recv.at[k],
            {"ctx": self.facing},
        )

    def outward(self, k):
        return remote(
            self.done.at[k], self.done.at[k], self.out_send.at[k], self.out_recv.at[k], {"ctx": self.outer}
        )

    def spend(self, c, credit):
        @pl.when(c >= SLOTS)
        def _():
            pl.semaphore_wait(credit, 1)

    def give(self, c, credit, peer):
        @pl.when(c + SLOTS < self.total)
        def _():
            pl.semaphore_signal(credit, inc=1, device_id=peer, device_id_type=MESH)

    def term(self, c, shard, k):
        one = lambda b: jnp.where(c >= b, 1, 0)
        which = one(self.units) + one(3 * self.units) + one(self.early)
        rows = self.dims.shard_rows
        return dot(self.left[which, pl.ds(pl.multiple_of(shard * rows, rows), rows), :], self.right[k])

    def fetch(self, c):
        k = lax.rem(c, SLOTS)
        for (base, count), source in zip(self.bases, self.sources):
            @pl.when((c >= base) & (c < base + count))
            def _():
                at = pl.ds(pl.multiple_of((c - base) * CHUNK, CHUNK), CHUNK)
                pltpu.make_async_copy(source.at[:, at], self.right.at[k], self.right_sem.at[k]).start()

        @pl.when((c >= self.early) & (c < self.total))
        def _():
            dims = self.dims
            which, piece = (c - self.early) // self.heads, lax.rem(c - self.early, self.heads)
            per = CHUNK // dims.cols
            for i in range(per):
                for s in range(dims.seqs):
                    self.right[k, s * dims.part : (s + 1) * dims.part, i * dims.cols : (i + 1) * dims.cols] = (
                        self.from_heads[which, piece * per + i, s]
                    )

    def save(self, c, k):
        for (base, count), out in zip(self.bases, self.outs):
            @pl.when((c >= base) & (c < base + count))
            def _():
                at = pl.ds(pl.multiple_of((c - base) * CHUNK, CHUNK), CHUNK)
                pltpu.make_async_copy(self.done.at[k], out.at[:, at], self.fin_sem.at[k]).start()

    def settle(self, c, k):
        pltpu.make_async_copy(self.done.at[k], self.outs[0].at[:, pl.ds(0, CHUNK)], self.fin_sem.at[k]).wait()

        @pl.when(self.has_outer)
        def _():
            self.outward(k).wait_send()

        @pl.when(self.has_inner)
        def _():
            self.give(c, self.out_credit, {"ctx": self.inner})

    def deliver(self, c, k):
        @pl.when(self.has_inner)
        def _():
            self.outward(k).wait_recv()
            self.save(c, k)

            @pl.when(self.has_outer)
            def _():
                self.spend(c, self.out_credit)
                self.outward(k).start()

    def finish(self, c, k):
        @pl.when(self.is_middle)
        def _():
            self.across(k).wait_recv()
            self.across(k).wait_send()
            self.done[k] = (self.line[k].astype(F32) + self.across_in[k].astype(F32)).astype(BF16)
            self.give(c, self.across_credit, {"ctx": self.facing})
            self.save(c, k)

            @pl.when(self.has_outer)
            def _():
                self.spend(c, self.out_credit)
                self.outward(k).start()

        @pl.when(self.has_inner)
        def _():
            self.inward(k).wait_send()

    def collect(self, c, k):
        @pl.when(self.has_outer)
        def _():
            self.inward(k).wait_recv()
            self.line[k] = (self.line[k].astype(F32) + self.line_in[k].astype(F32)).astype(BF16)
            self.give(c, self.in_credit, {"ctx": self.outer})

        @pl.when(self.is_middle)
        def _():
            self.spend(c, self.across_credit)
            self.across(k).start()

        @pl.when(self.has_outer & self.has_inner)
        def _():
            self.spend(c, self.in_credit)
            self.inward(k).start()

    def own(self, c, k):
        total = self.term(c, self.spot.shard, k) + self.core_in[k, self.spot.chips - 1].astype(F32)
        for d in range(1, self.spot.chips):
            self.far(k, d).wait_send()
            self.far(k, d).wait_recv()
            total = total + self.far_in[k, d - 1].astype(F32)
        self.line[k] = total.astype(BF16)
        self.give(c, self.core_credit, {"shard": self.spot.mate})
        for d in range(1, self.spot.chips):
            sender = lax.rem(self.spot.shard - 2 * d + self.spot.shards, self.spot.shards)
            self.give(c, self.far_credit.at[d - 1], {"shard": sender})

        @pl.when(self.is_end & self.has_inner)
        def _():
            self.spend(c, self.in_credit)
            self.inward(k).start()

    def to_chips(self, c, k):
        self.core(c, k).wait_recv()
        self.core(c, k).wait_send()
        for d in range(1, self.spot.chips):
            pair = self.term(c, self.spot.away(d), k) + self.core_in[k, d - 1].astype(F32)
            self.far_out[k, d - 1] = pair.astype(BF16)
            self.spend(c, self.far_credit.at[d - 1])
            self.far(k, d).start()

    def to_core(self, c, k):
        @pl.when(c < self.early)
        def _():
            pltpu.make_async_copy(
                self.sources[0].at[:, pl.ds(0, CHUNK)], self.right.at[k], self.right_sem.at[k]
            ).wait()

        chips, half = self.spot.chips, lax.rem(c, 2)
        for d in range(1, chips + 1):
            shard = 2 * lax.rem(self.spot.chip + d, chips) + 1 - self.spot.core
            self.core_out[half, d - 1] = self.term(c, shard, k).astype(BF16)
        self.spend(c, self.core_credit)
        self.core(c, k).start()

    def step(self, t):
        def at(lag, stage):
            c = t - lag

            @pl.when((c >= 0) & (c < self.total))
            def _():
                stage(c, lax.rem(c, SLOTS))

        at(10, self.settle)
        at(9, self.deliver)
        at(7, self.finish)
        at(5, self.collect)
        at(3, self.own)

        @pl.when(t + 1 < self.total)
        def _():
            self.fetch(t + 1)

        at(1, self.to_chips)
        at(0, self.to_core)

    def steps(self, first, last):
        @pl.loop(first, last)
        def _(t):
            self.step(t)


def backward_kernel(
    dims, gain_two, table, lse, pieces,
    term, ffn_term, left_g, left_two, left_one, inner, grad_gate, grad_up, attended, hidden, cotangent,
    wo, wq, wk, wv,
    down_out, gate_out, up_out, o_out, q_out, k_out, v_out,
    grad_hidden, ffn_other, term_one, other_one, ffn_gain, table_out,
    left, right, core_out, core_in, far_out, far_in, line, line_in, across_in, done,
    swap_in, staged, grads, grads_out, grads_in,
    right_sem, core_send, core_recv, far_send, far_recv, in_send, in_recv, across_send, across_recv,
    out_send, out_recv, fin_sem, swap_send, swap_recv, head_send, head_recv, back_send, back_recv,
    one_send, one_recv, ffn_sem, local_sem,
    core_credit, far_credit, in_credit, across_credit, out_credit,
):
    spot = Spot(*dims.mesh)
    n, seqs, part, cols, head_dim, width = dims.n, dims.seqs, dims.part, dims.cols, dims.head_dim, dims.width
    me, shards, shard_rows = spot.me, spot.shards, dims.shard_rows
    lanes, per = 2 * head_dim, 2
    groups = cols // lanes
    span = table.shape[1]
    other_half = {"tp": 1 - spot.half}
    pump = Pump(
        dims, spot, left, right, (inner, grad_gate, grad_up, attended), grads_in,
        (down_out, gate_out, up_out, o_out, q_out, k_out, v_out),
        (core_out, core_in, far_out, far_in, line, line_in, across_in, done),
        (
            right_sem, core_send, core_recv, far_send, far_recv, in_send, in_recv, across_send, across_recv,
            out_send, out_recv, fin_sem,
        ),
        (core_credit, far_credit, in_credit, across_credit, out_credit),
    )
    loads = [
        pltpu.make_async_copy(source, left.at[i], local_sem.at[i])
        for i, source in ((0, left_g), (1, left_two), (3, left_one))
    ]
    for load in loads:
        load.start()
    pump.fetch(0)
    spot.barrier()
    swaps = [
        remote(term.at[s], swap_in.at[s], swap_send.at[s], swap_recv.at[s], other_half) for s in range(seqs)
    ]
    for swap in swaps:
        swap.start()
    for load in loads:
        load.wait()
    ffn_gain[...] = jnp.zeros_like(ffn_gain)
    table_out[...] = jnp.zeros_like(table_out)
    pump.steps(0, 4)

    def head_move(s, peer):
        return remote(
            staged.at[peer, s], grads.at[me, s], head_send.at[s, peer], head_recv.at[s, me], {"ctx": peer}
        )

    def head_wait(s, peer):
        remote(
            staged.at[peer, s], grads.at[peer, s], head_send.at[s, peer], head_recv.at[s, peer], {"ctx": peer}
        ).wait_recv()

    def second_norm(s, weights, values, given, own, result, sem):
        at = pl.ds(s * part, part)
        copies = [
            pltpu.make_async_copy(hidden.at[at, :], values, sem.at[0]),
            pltpu.make_async_copy(cotangent.at[at, :], given, sem.at[1]),
            pltpu.make_async_copy(term.at[s], own, sem.at[2]),
        ]
        for copy in copies:
            copy.start()
        for copy in copies:
            copy.wait()
        swaps[s].wait_recv()

        @pl.loop(0, part // 64)
        def _(i):
            here = pl.ds(pl.multiple_of(i * 64, 64), 64)
            h = values[here, :]
            grad = own[here, :].astype(F32) + swap_in[s, here, :].astype(F32)
            scale = rms_scale(h)
            ffn_gain[...] += jnp.sum(grad * h * scale, axis=0, keepdims=True)
            total = given[here, :].astype(F32) + rms_back(h, scale, gain_two[...], grad)
            result[here, :] = total
            own[here, :] = total.astype(BF16)

        saved = pltpu.make_async_copy(result, grad_hidden.at[at, :], sem.at[0])
        saved.start()
        total = dot(own[:, :shard_rows], weights[0])
        for j in range(1, shards):
            total += dot(own[:, j * shard_rows : (j + 1) * shard_rows], weights[j])
        for k in range(n):
            staged[k, s] = total[:, k * cols : (k + 1) * cols].astype(BF16)
        for d in range(1, n):
            head_move(s, lax.rem(me + d, n)).start()
        grads[me, s] = staged[me, s]
        left[2, :, s * part : (s + 1) * part] = own[...].T
        saved.wait()

    def second_norms(weights, values, given, own, result, sem):
        load = pltpu.make_async_copy(wo, weights, sem.at[3])
        load.start()
        load.wait()
        for s in range(seqs):
            second_norm(s, weights, values, given, own, result, sem)
            if s == 0:
                pump.steps(4, 5)

    pl.run_scoped(
        second_norms,
        pltpu.VMEM((shards, shard_rows, dims.inner_width), BF16),
        pltpu.VMEM((part, width), F32),
        pltpu.VMEM((part, width), BF16),
        pltpu.VMEM((part, width), BF16),
        pltpu.VMEM((part, width), F32),
        pltpu.SemaphoreType.DMA((4,)),
    )
    ffn_swap = remote(ffn_term, ffn_other, ffn_sem.at[0], ffn_sem.at[1], other_half)
    ffn_swap.start()
    pump.steps(5, 7)

    def back_move(j, s, peer):
        return remote(
            grads_out.at[j, peer, s], grads_in.at[j, me, s], back_send.at[j, s, peer], back_recv.at[j, s, me],
            {"ctx": peer},
        )

    def back_wait(j, s, peer):
        remote(
            grads_out.at[j, peer, s], grads_in.at[j, peer, s], back_send.at[j, s, peer], back_recv.at[j, s, peer],
            {"ctx": peer},
        ).wait_recv()

    def attention(bias, sums, grad_k, grad_v):
        @pl.loop(0, seqs * groups * n)
        def _(i):
            a, group, s = lax.rem(i, n), lax.rem(i // n, groups), i // (n * groups)
            at = pl.ds(pl.multiple_of(group * lanes, lanes), lanes)

            @pl.when((a == 0) & (group == 0))
            def _():
                for d in range(1, n):
                    head_wait(s, lax.rem(me + d, n))

            @pl.when(a == 0)
            def _():
                for j in range(per):
                    bias_rows(table[pl.ds(group * per + j, 1), :], bias.at[j])
                sums[...] = jnp.zeros_like(sums)
                grad_k[...] = jnp.zeros_like(grad_k)
                grad_v[...] = jnp.zeros_like(grad_v)

            lane = lax.broadcasted_iota(jnp.int32, (part, lanes), 1)
            result = jnp.zeros((part, lanes), F32)
            for j in range(per):
                mask = (lane >= j * head_dim) & (lane < (j + 1) * head_dim)
                query = jnp.where(mask, pieces[0, a, s, :, at], 0)
                upstream = jnp.where(mask, grads[a, s, :, at], 0)
                log_total = jnp.sum(jnp.where(lane == group * per + j, lse[s, a], 0.0), axis=1, keepdims=True)
                windows = [pl.ds(pl.multiple_of((n + b - a) * part, part), part) for b in range(n)]
                probs, grad_probs = [], []
                for b in range(n):
                    scores = contract_cols(query, pieces[1, b, s, :, at]) + bias[j, :, windows[b]]
                    probs.append(jnp.exp(scores - log_total))
                    grad_probs.append(contract_cols(upstream, pieces[2, b, s, :, at]))
                delta = sum(jnp.sum(g * p, axis=1, keepdims=True) for g, p in zip(grad_probs, probs))
                summed = None
                for b in range(n):
                    grad_scores = (probs[b] * (grad_probs[b] - delta)).astype(BF16)
                    sums[j, :, windows[b]] += grad_scores.astype(F32)
                    product = dot(grad_scores, pieces[1, b, s, :, at])
                    summed = product if summed is None else summed + product
                    grad_k[b] += contract_rows(grad_scores, query)
                    grad_v[b] += contract_rows(probs[b].astype(BF16), upstream)
                result = jnp.where(mask, summed, result)
            grads_out[0, a, s, :, at] = result.astype(BF16)

            @pl.when(a == n - 1)
            def _():
                for b in range(n):
                    grads_out[1, b, s, :, at] = grad_k[b].astype(BF16)
                    grads_out[2, b, s, :, at] = grad_v[b].astype(BF16)
                for j in range(per):
                    table_out[pl.ds(group * per + j, 1), :] += diagonal_sums(sums.at[j])

            @pl.when((a == n - 1) & (group == groups - 1))
            def _():
                for j in range(3):
                    for d in range(1, n):
                        back_move(j, s, lax.rem(me + d, n)).start()
                    grads_in[j, me, s] = grads_out[j, me, s]

            @pl.when(a == n - 1)
            def _():
                pump.step(7 + i // n)

    pl.run_scoped(
        attention,
        pltpu.VMEM((per, part, span), F32),
        pltpu.VMEM((per, part, span), F32),
        pltpu.VMEM((n, part, lanes), F32),
        pltpu.VMEM((n, part, lanes), F32),
    )
    after = 7 + seqs * groups
    pump.steps(after, after + 1)
    for s in range(seqs):
        for j in range(3):
            for d in range(1, n):
                back_wait(j, s, lax.rem(me + d, n))

    def first_norm_terms(weights, values, sem):
        def load(shard):
            return [
                pltpu.make_async_copy(w.at[shard], weights.at[shard % 2, j], sem.at[shard % 2, j])
                for j, w in enumerate((wq, wk, wv))
            ]

        for copy in load(0):
            copy.start()
        for j in range(3):
            for s in range(seqs):
                for k in range(n):
                    values[j, s * part : (s + 1) * part, k * cols : (k + 1) * cols] = grads_in[j, k, s]
        for shard in range(shards):
            if shard + 1 < shards:
                for copy in load(shard + 1):
                    copy.start()
            for copy in load(shard):
                copy.wait()
            total = contract_cols(values[0], weights[shard % 2, 0])
            total += contract_cols(values[1], weights[shard % 2, 1])
            total += contract_cols(values[2], weights[shard % 2, 2])
            for s in range(seqs):
                term_one[s, :, shard * shard_rows : (shard + 1) * shard_rows] = (
                    total[s * part : (s + 1) * part].astype(BF16)
                )

    pl.run_scoped(
        first_norm_terms,
        pltpu.VMEM((2, 3, shard_rows, dims.inner_width), BF16),
        pltpu.VMEM((3, seqs * part, dims.inner_width), BF16),
        pltpu.SemaphoreType.DMA((2, 3)),
    )
    ones = [
        remote(term_one.at[s], other_one.at[s], one_send.at[s], one_recv.at[s], other_half) for s in range(seqs)
    ]
    for swap in ones:
        swap.start()
    pump.steps(after + 1, pump.last)
    for swap in swaps:
        swap.wait_send()
    for copy in ones + [ffn_swap]:
        copy.wait_recv()
        copy.wait_send()
    for s in range(seqs):
        for d in range(1, n):
            peer = lax.rem(me + d, n)
            head_move(s, peer).wait_send()
            for j in range(3):
                back_move(j, s, peer).wait_send()


def backward_call(dims):
    rows, width, n, part, seqs = dims.seqs * dims.part, dims.width, dims.n, dims.part, dims.seqs
    shards, shard_rows, inner, units, cols = dims.shards, dims.shard_rows, dims.inner_width, dims.units, dims.cols
    span, chips = 2 * n * part, dims.shards // 2
    vmem, anywhere = pl.BlockSpec(memory_space=pltpu.VMEM), pl.BlockSpec(memory_space=pl.ANY)
    shape, dma, regular = jax.ShapeDtypeStruct, pltpu.SemaphoreType.DMA, pltpu.SemaphoreType.REGULAR
    far = max(chips - 1, 1)
    block = (shard_rows, CHUNK)
    return pl.pallas_call(
        functools.partial(backward_kernel, dims),
        in_specs=[vmem] * 4 + [anywhere] * 15,
        out_specs=[anywhere] * 9 + [vmem, anywhere, vmem, vmem],
        out_shape=[shape((shard_rows, units), BF16)] * 3
        + [shape((shard_rows, inner), BF16)] * 4
        + [
            shape((rows, width), F32),
            shape((rows, width), BF16),
            shape((seqs, part, width), BF16),
            shape((seqs, part, width), BF16),
            shape((1, width), F32),
            shape((dims.own_heads, span), F32),
        ],
        scratch_shapes=[
            pltpu.VMEM((4, width, rows), BF16),
            pltpu.VMEM((SLOTS, rows, CHUNK), BF16),
            pltpu.VMEM((2, chips) + block, BF16),
            pltpu.VMEM((SLOTS, chips) + block, BF16),
            pltpu.VMEM((SLOTS, far) + block, BF16),
            pltpu.VMEM((SLOTS, far) + block, BF16),
            pltpu.VMEM((SLOTS,) + block, BF16),
            pltpu.VMEM((SLOTS,) + block, BF16),
            pltpu.VMEM((SLOTS,) + block, BF16),
            pltpu.VMEM((SLOTS,) + block, BF16),
            pltpu.VMEM((seqs, part, width), BF16),
            pltpu.VMEM((n, seqs, part, cols), BF16),
            pltpu.VMEM((n, seqs, part, cols), BF16),
            pltpu.VMEM((3, n, seqs, part, cols), BF16),
            pltpu.VMEM((3, n, seqs, part, cols), BF16),
            dma((SLOTS,)),
            dma((2,)),
            dma((SLOTS,)),
            dma((SLOTS, far)),
            dma((SLOTS, far)),
        ]
        + [dma((SLOTS,))] * 7
        + [dma((seqs,))] * 2
        + [dma((seqs, n))] * 2
        + [dma((3, seqs, n))] * 2
        + [dma((seqs,))] * 2
        + [dma((2,)), dma((4,))]
        + [regular, regular((far,)), regular, regular, regular],
        compiler_params=pltpu.CompilerParams(
            vmem_limit_bytes=62 * 2**20, collective_id=1, has_side_effects=True
        ),
        name="backward",
    )


def ring(n, d):
    return [(i, (i + d) % n) for i in range(n)]


class Links:
    def __init__(self, mesh):
        self.shard, self.ctx, self.tp = mesh.shape["shard"], mesh.shape["ctx"], mesh.shape["tp"]
        self.chips = self.shard // 2

    def to_core(self, value):
        return lax.ppermute(value, "shard", [(i, i ^ 1) for i in range(self.shard)])

    def to_chip(self, value, d):
        n = self.shard
        return lax.ppermute(value, "shard", [(i, (i + 2 * d) % n) for i in range(n)])

    def tp_sum(self, value):
        if self.tp != 2:
            return lax.psum(value, "tp").astype(F32)
        other = lax.ppermute(value, "tp", ring(2, 1))
        return value.astype(F32) + other.astype(F32)

    def ctx_sum(self, value):
        low = value.astype(BF16)
        if self.ctx != 4:
            return lax.psum(low, "ctx").astype(F32)
        inward = lax.ppermute(low, "ctx", [(0, 1), (3, 2)])
        half = (low.astype(F32) + inward.astype(F32)).astype(BF16)
        across = lax.ppermute(half, "ctx", [(1, 2), (2, 1)])
        whole = (half.astype(F32) + across.astype(F32)).astype(BF16)
        outward = lax.ppermute(whole, "ctx", [(1, 0), (2, 3)])
        me = lax.axis_index("ctx")
        middle = (me == 1) | (me == 2)
        return jnp.where(middle, whole, outward).astype(F32)

    def shard_sums(self, left, right):
        n, chips = self.shard, self.chips
        rows = left.shape[1] // n
        me = lax.axis_index("shard")
        chip, core = me // 2, me % 2

        def term(chip_at, core_at):
            at = (2 * chip_at + core_at) * rows
            return contract_rows(lax.dynamic_slice_in_dim(left, at, rows, 1), right)

        def chip_of(d):
            return lax.rem(chip + d, chips)

        order = list(range(1, chips)) + [0]
        got = {d: self.to_core(term(chip_of(d), 1 - core).astype(BF16)) for d in order}
        total = None
        arrived = []
        for d in order:
            pair = term(chip_of(d), core) + got[d].astype(F32)
            if d:
                arrived.append(self.to_chip(pair.astype(BF16), d))
            else:
                total = pair
        for value in arrived:
            total = total + value.astype(F32)
        return total

    def small_sum(self, value):
        for axis, n in (("shard", self.shard), ("ctx", self.ctx)):
            step = 1
            while step < n:
                value = value + lax.ppermute(value, axis, [(i, i ^ step) for i in range(n)])
                step *= 2
        return value


def per_device(
    links,
    tokens,
    cotangent,
    buckets,
    query_weight,
    key_weight,
    value_weight,
    output_weight,
    gate_weight,
    up_weight,
    down_weight,
    norm_gain,
    ffn_gain,
    bucket_bias_table,
):
    seqs, part, width = tokens.shape
    rows = seqs * part
    slots, heads = bucket_bias_table.shape
    inner_width = query_weight.shape[1]
    head_dim = inner_width // heads
    n = links.ctx
    cols = inner_width // n
    own_heads = heads // n
    me = lax.axis_index("ctx")
    gain_one = norm_gain.astype(F32)
    gain_two = ffn_gain.astype(F32)

    def gathered(weight):
        return lax.all_gather(weight, "shard", axis=0, tiled=True)

    def at_ctx(d):
        return lax.rem(me + d + n, n)

    corner = lax.dynamic_slice(buckets, (0, me * part), (part, part))
    later, earlier = corner[0, :], corner[:, 0]
    reach = n * part
    by_offset = jnp.concatenate(
        [
            jnp.broadcast_to(earlier[part - 1 :], (reach - part + 1,)),
            earlier[:0:-1],
            later,
            jnp.broadcast_to(later[part - 1 :], (reach - part,)),
        ]
    )
    indicator = by_offset[None, :] == jnp.arange(slots, dtype=jnp.int32)[:, None]
    own_table = lax.dynamic_slice(bucket_bias_table, (0, me * own_heads), (slots, own_heads))
    offset_bias = lax.dot_general(
        own_table, indicator.astype(BF16), (((0,), (0,)), ((), ())), preferred_element_type=F32
    )
    groups = cols // (2 * head_dim)
    offset_bias = offset_bias.reshape(groups, 2, 2 * reach)

    dims = Dims(links, seqs, part, width, inner_width, gate_weight.shape[1], heads)
    normed, hidden, normed_two, attended, lse, pieces, *full = forward_call(dims)(
        tokens.reshape(rows, width),
        jnp.stack([gain_one, gain_two]),
        offset_bias.reshape(own_heads, 2 * reach),
        query_weight, key_weight, value_weight, output_weight, gate_weight, up_weight, down_weight,
    )
    wi0, wi1, wff = (w.reshape(width, w.shape[2]) for w in full[4:])
    inputs = tokens.reshape(rows, width).astype(F32)
    scale_one = rms_scale(inputs)

    gate = dot(normed_two, wi0)
    up = dot(normed_two, wi1)
    inner = geglu(gate, up).astype(BF16)
    ffn_term = contract_cols(inner, wff).astype(BF16)
    upstream_low = cotangent.reshape(rows, width)
    grad_inner = dot(upstream_low, wff)
    unused, geglu_backward_pull = jax.vjp(geglu, gate, up)
    grad_gate, grad_up = geglu_backward_pull(grad_inner)
    grad_gate = grad_gate.astype(BF16)
    grad_up = grad_up.astype(BF16)
    term_two = (contract_cols(grad_gate, wi0) + contract_cols(grad_up, wi1)).astype(BF16)
    *weight_grads, grad_hidden, ffn_other, term_one, other_one, grad_ffn_gain, offset_grad = backward_call(dims)(
        gain_two.reshape(1, width), offset_bias.reshape(own_heads, 2 * reach), lse, pieces,
        term_two.reshape(seqs, part, width), ffn_term, upstream_low.T, normed_two.T, normed.T,
        inner, grad_gate, grad_up, attended, hidden, upstream_low,
        full[3], full[0], full[1], full[2],
    )
    grad_down_w, grad_gate_w, grad_up_w, grad_output_w, grad_query_w, grad_key_w, grad_value_w = (
        g.astype(F32) for g in weight_grads
    )
    result = (hidden + (ffn_term.astype(F32) + ffn_other.astype(F32))).astype(BF16).reshape(seqs, part, width)
    grad_ffn_gain = grad_ffn_gain[0]
    table_part = jnp.sum(jnp.where(indicator[:, None, :], offset_grad[None], 0.0), axis=-1)
    grad_table = lax.dynamic_update_slice(
        jnp.zeros((slots, heads), F32), table_part, (0, me * own_heads)
    )
    grad_normed = (term_one.astype(F32) + other_one.astype(F32)).reshape(rows, width)
    grad_norm_gain = jnp.sum(grad_normed * inputs * scale_one, axis=0)
    grad_inputs = grad_hidden + rms_back(inputs, scale_one, gain_one, grad_normed)
    small = links.small_sum(jnp.concatenate([grad_norm_gain, grad_ffn_gain, grad_table.reshape(-1)]))
    return (
        result,
        grad_inputs.reshape(seqs, part, width),
        grad_query_w,
        grad_key_w,
        grad_value_w,
        grad_output_w,
        grad_gate_w,
        grad_up_w,
        grad_down_w,
        small[:width],
        small[width : 2 * width],
        small[2 * width :].reshape(slots, heads),
    )


def solution(mesh):
    rows, weights = P("shard", "ctx", None), P("shard", "tp")
    return jax.shard_map(
        functools.partial(per_device, Links(mesh)),
        mesh=mesh,
        in_specs=(rows, rows, P("ctx", None)) + (weights,) * 7 + (P(), P(), P(None, "tp")),
        out_specs=(rows, rows) + (weights,) * 7 + (P(), P(), P(None, "tp")),
        check_vma=False,
    )
```

```python
import functools

import jax
import jax.numpy as jnp
from jax import lax
from jax.experimental import pallas as pl
from jax.experimental.pallas import tpu as pltpu
from jax.sharding import PartitionSpec as P

F32 = jnp.float32
BF16 = jnp.bfloat16
VMEM_LIMIT = 48 * 2**20


def contract_rows(left, right):
    return lax.dot_general(left, right, (((0,), (0,)), ((), ())), preferred_element_type=F32)


def contract_cols(left, right):
    return lax.dot_general(left, right, (((1,), (1,)), ((), ())), preferred_element_type=F32)


def dot(left, right):
    return jnp.dot(left, right, preferred_element_type=F32)


def rms_scale(values):
    return lax.rsqrt(jnp.mean(values * values, axis=-1, keepdims=True) + 1e-06)


def rms_back(values, scale, gain, upstream):
    weighted = upstream * gain
    inner_average = jnp.mean(values * weighted, axis=-1, keepdims=True)
    return scale * weighted - values * scale * scale * scale * inner_average


def geglu(gate, up):
    return jax.nn.gelu(gate, approximate=True) * up


def bias_rows(table_row, out):
    span = out.shape[1]
    out[0:1, :] = table_row
    done = 1
    while done < out.shape[0]:
        out[done : 2 * done, :] = pltpu.roll(out[0:done, :], done, 1)
        done *= 2
    del span


def diagonal_sums(acc):
    rows, span = acc.shape
    total = acc[...]
    while rows > 1:
        rows //= 2
        total = total[:rows] + pltpu.roll(total[rows:], span - rows, 1)
    return total


MESH = pl.DeviceIdType.MESH


class Spot:
    def __init__(self, shards, ctx, tp):
        self.shards, self.chips, self.n, self.tps = shards, shards // 2, ctx, tp
        self.shard, self.me, self.half = (lax.axis_index(a) for a in ("shard", "ctx", "tp"))
        self.chip, self.core = self.shard // 2, lax.rem(self.shard, 2)
        self.mate = 2 * self.chip + 1 - self.core

    def away(self, d):
        return lax.rem(self.shard + 2 * d, self.shards)

    def barrier(self):
        peers = [{"shard": self.mate}] + [{"shard": self.away(d)} for d in range(1, self.chips)]
        peers += [{"ctx": lax.rem(self.me + d, self.n)} for d in range(1, self.n)]
        peers += [{"tp": 1 - self.half}]
        semaphore = pltpu.get_barrier_semaphore()
        for peer in peers:
            pl.semaphore_signal(semaphore, inc=1, device_id=peer, device_id_type=MESH)
        pl.semaphore_wait(semaphore, len(peers))


def remote(src, dst, send, recv, peer):
    return pltpu.make_async_remote_copy(
        src_ref=src, dst_ref=dst, send_sem=send, recv_sem=recv, device_id=peer, device_id_type=MESH
    )


class Keep:
    def __init__(self, jobs, room, sem):
        self.halves = []
        for i, (own, full) in enumerate(jobs):
            self.halves.append(pltpu.make_async_copy(own, room, sem.at[0]))
            self.halves.append(pltpu.make_async_copy(room, full, sem.at[1]))
        self.at = 0
        self.halves[0].start()

    def step(self):
        if self.at < len(self.halves):
            self.halves[self.at].wait()
            self.at += 1
            if self.at < len(self.halves):
                self.halves[self.at].start()

    def start(self):
        pass

    def wait(self):
        while self.at < len(self.halves):
            self.step()


class Gather:
    def __init__(self, spot, own, full, sems, keep=None):
        self.spot, self.own, self.full = spot, own, full
        self.local, self.send, self.recv, self.on_send, self.on_recv = sems
        spot_shard = spot.shard
        self.keep = keep or pltpu.make_async_copy(own, full.at[spot_shard], self.local)
        self.far = [
            remote(own, full.at[spot_shard], self.send.at[d], self.recv.at[d], {"shard": spot.away(d)})
            for d in range(1, spot.chips)
        ]
        mate = {"shard": spot.mate}
        self.near = [remote(own, full.at[spot_shard], self.on_send.at[0], self.on_recv.at[0], mate)]
        for d in range(1, spot.chips):
            at = full.at[lax.rem(spot.shard - 2 * d + spot.shards, spot.shards)]
            self.near.append(remote(at, at, self.on_send.at[d], self.on_recv.at[d], mate))

    def start_far(self):
        for copy in self.far:
            copy.start()

    def start_near(self):
        self.keep.start()
        self.near[0].start()

    def pass_on(self):
        for d, copy in enumerate(self.far, 1):
            copy.wait_recv()
            self.near[d].start()

    def wait_own(self):
        self.keep.wait()
        self.near[0].wait_recv()

    def wait_near(self):
        for copy in self.near[1:]:
            copy.wait_recv()

    def wait_sent(self):
        for copy in self.far + self.near:
            copy.wait_send()


class Spread:
    def __init__(self, spot, own, full, keep, sems):
        self.spot, self.own, self.full, self.keep = spot, own, full, keep
        (
            self.far_send, self.far_recv, self.right_send, self.right_recv, self.left_send, self.left_recv,
            self.mate_send, self.mate_recv,
        ) = sems
        self.part = full.shape[1] // spot.n
        n, me = spot.n, spot.me
        self.near = remote(
            own, full.at[spot.shard], self.mate_send.at[0, 0], self.mate_recv.at[0, 0], {"shard": spot.mate}
        )
        mine = pl.ds(pl.multiple_of(me * self.part, self.part), self.part)
        self.far = [
            remote(
                own.at[mine], full.at[spot.shard, mine], self.far_send.at[d], self.far_recv.at[d],
                {"shard": spot.away(d)},
            )
            for d in range(1, spot.chips)
        ]
        self.can_right, self.can_left = me + 1 < n, me > 0

    def piece(self, d, z):
        source = lax.rem(self.spot.shard - 2 * d + self.spot.shards, self.spot.shards)
        return self.full.at[source, pl.ds(pl.multiple_of(z * self.part, self.part), self.part)]

    def tell(self, d, z):
        at = self.piece(d, z)
        return remote(at, at, self.mate_send.at[d, z], self.mate_recv.at[d, z], {"shard": self.spot.mate})

    def right(self, d, h, z):
        at, to = self.piece(d, z), {"ctx": lax.rem(self.spot.me + 1, self.spot.n)}
        return remote(at, at, self.right_send.at[d, h], self.right_recv.at[d, h], to)

    def left(self, d, h, z):
        at, to = self.piece(d, z), {"ctx": lax.rem(self.spot.me - 1 + self.spot.n, self.spot.n)}
        return remote(at, at, self.left_send.at[d, h], self.left_recv.at[d, h], to)

    def pairs(self):
        return range(1, self.spot.chips)

    def start(self):
        for copy in self.far:
            copy.start()

    def start_near(self):
        self.keep.start()
        self.near.start()

    def send_on(self, d, h, z, right, left):
        self.tell(d, z).start()
        if right:
            @pl.when(self.can_right)
            def _():
                self.right(d, h, z).start()

        if left:
            @pl.when(self.can_left)
            def _():
                self.left(d, h, z).start()

    def arrived(self):
        for d in self.pairs():
            self.far[d - 1].wait_recv()
            self.send_on(d, 1, self.spot.me, True, True)

    def hop(self, h):
        me, n = self.spot.me, self.spot.n
        for d in self.pairs():
            @pl.when(me - h >= 0)
            def _():
                self.right(d, h, me - h).wait_recv()
                self.send_on(d, h + 1, me - h, h + 1 < n, False)

            @pl.when(me + h < n)
            def _():
                self.left(d, h, me + h).wait_recv()
                self.send_on(d, h + 1, me + h, False, h + 1 < n)

    def wait(self):
        me, n = self.spot.me, self.spot.n
        self.keep.wait()
        self.near.wait_recv()
        self.near.wait_send()
        for d in self.pairs():
            self.far[d - 1].wait_send()
            for z in range(n):
                self.tell(d, z).wait_recv()
                self.tell(d, z).wait_send()
            for h in range(1, n):
                @pl.when((me - h + 1 >= 0) & self.can_right)
                def _():
                    self.right(d, h, me - h + 1).wait_send()

                @pl.when((me + h - 1 < n) & self.can_left)
                def _():
                    self.left(d, h, me + h - 1).wait_send()


def forward_kernel(
    dims, tokens, cotangent, gains, table, wq, wk, wv, wo, wi0, wi1, wff,
    hidden, normed_two, attended, lse, pieces_out, left_g, left_one, left_two,
    full_q, full_k, full_v, full_o, full_0, full_1, full_2,
    normed, flipped, weights, acc, bias, staged, pieces, mixed, heads_in, rolled, branch_in,
    local_sem, far_send, far_recv, near_send, near_recv, head_send, head_recv, back_send, back_recv,
    room, keep_sem,
    swap_send, swap_recv, out_sem, *spread_sems,
):
    spot = Spot(*dims.mesh)
    n, seqs, part, cols, head_dim = dims.n, dims.seqs, dims.part, dims.cols, dims.head_dim
    me, shards = spot.me, spot.shards
    shard_rows = weights.shape[2]
    rows = seqs * part
    lanes = 2 * head_dim
    per = 2
    spot.barrier()

    def gather(i, own, full, keep=None):
        sems = [local_sem.at[i], far_send.at[i], far_recv.at[i], near_send.at[i], near_recv.at[i]]
        return Gather(spot, own, full, sems, keep)

    loads = [gather(i, w, weights.at[i]) for i, w in enumerate((wq, wk, wv, wo))]
    keep = Keep(
        [(w, full.at[spot.shard]) for w, full in ((wi0, full_0), (wi1, full_1), (wff, full_2))], room, keep_sem
    )
    loads.append(gather(4, wi0, full_0, keep))
    spreads = [
        Spread(spot, own, full, keep, [sem.at[i] for sem in spread_sems])
        for i, (own, full) in enumerate(((wi1, full_1), (wff, full_2)))
    ]
    flips = []

    def flip(value, out):
        if flips:
            flips[-1].wait()
        flipped[...] = value.T
        flips.append(pltpu.make_async_copy(flipped, out, out_sem.at[5]))
        flips[-1].start()

    loads[0].start_far()
    for load in loads[:3]:
        load.start_near()

    @pl.loop(0, rows // 64)
    def _(i):
        at = pl.ds(pl.multiple_of(i * 64, 64), 64)
        values = tokens[at, :].astype(F32)
        normed[at, :] = (values * rms_scale(values) * gains[0:1, :]).astype(BF16)

    for head in range(dims.own_heads):
        bias_rows(table[head : head + 1, :], rolled)
        bias[head] = rolled[...].astype(BF16)

    def term(i, shard):
        at = pl.ds(pl.multiple_of(shard * shard_rows, 128), shard_rows)
        return dot(normed[:, at], weights[i, shard])

    moves = []
    for i, load in enumerate(loads[:3]):
        load.wait_own()
        acc[...] = term(i, spot.shard)
        acc[...] += term(i, spot.mate)
        keep.step()
        load.pass_on()
        if i < 2:
            loads[i + 1].start_far()
        else:
            for spread in spreads:
                spread.start()
            for later in loads[3:] + spreads:
                later.start_near()
        keep.step()
        for d in range(1, spot.chips):
            acc[...] += term(i, lax.rem(spot.shard - 2 * d + shards, shards))
        load.wait_near()
        for d in range(1, spot.chips):
            acc[...] += term(i, lax.rem(spot.mate - 2 * d + shards, shards))
        for k in range(n):
            for s in range(seqs):
                staged[i, k, s] = acc[s * part : (s + 1) * part, k * cols : (k + 1) * cols].astype(BF16)
        for d in range(1, n):
            peer = lax.rem(me + d, n)
            move = remote(
                staged.at[i, peer], pieces.at[i, me], head_send.at[i, d], head_recv.at[i, d], {"ctx": peer}
            )
            move.start()
            moves.append(move)
        pieces[i, me] = staged[i, me]
    outs = [
        pltpu.make_async_copy(weights.at[i], full, out_sem.at[i])
        for i, full in enumerate((full_q, full_k, full_v, full_o))
    ]
    for copy in outs[:3]:
        copy.start()
    flip(normed[...], left_one)
    spreads[0].arrived()
    spreads[1].arrived()
    loads[3].start_far()
    flip(cotangent[...], left_g)
    for move in moves:
        move.wait_recv()
    loads[3].wait_own()
    outs.append(pltpu.make_async_copy(pieces, pieces_out, out_sem.at[4]))
    outs[4].start()

    def back(s, at, to):
        return remote(mixed.at[s, at], heads_in.at[me, s], back_send.at[s, at], back_recv.at[s, me], {"ctx": to})

    @pl.loop(0, seqs * n)
    def _(step):
        s, a = step // n, lax.rem(step, n)
        lane = lax.broadcasted_iota(jnp.int32, (part, lanes), 1)
        log_total = jnp.zeros((part, lanes), F32)
        for group in range(cols // lanes):
            span = slice(group * lanes, (group + 1) * lanes)
            result = jnp.zeros((part, lanes), F32)
            for j in range(per):
                head = group * per + j
                mask = (lane >= j * head_dim) & (lane < (j + 1) * head_dim)
                query = jnp.where(mask, pieces[0, a, s, :, span], 0)
                scores = jnp.concatenate(
                    [
                        contract_cols(query, pieces[1, b, s, :, span])
                        + bias[head, :, pl.ds(pl.multiple_of((n + b - a) * part, part), part)].astype(F32)
                        for b in range(n)
                    ],
                    axis=1,
                )
                peak = jnp.max(scores, axis=1, keepdims=True)
                expo = jnp.exp(scores - peak)
                total = jnp.sum(expo, axis=1, keepdims=True)
                probs = (expo * (1.0 / total)).astype(BF16)
                summed = sum(
                    dot(probs[:, b * part : (b + 1) * part], pieces[2, b, s, :, span]) for b in range(n)
                )
                result = jnp.where(mask, summed, result)
                log_total = jnp.where(lane == head, peak + jnp.log(total), log_total)
            mixed[s, a, :, span] = result.astype(BF16)
        lse[s, a] = log_total

        @pl.when(a != me)
        def _():
            back(s, a, a).start()

        @pl.when(a == me)
        def _():
            heads_in[a, s] = mixed[s, a]

        @pl.when(step == 2)
        def _():
            spreads[0].hop(1)

        @pl.when(step == 4)
        def _():
            loads[3].pass_on()
            loads[4].start_far()

        @pl.when(step == 5)
        def _():
            spreads[1].hop(1)

    if n > 2:
        spreads[0].hop(2)
    loads[3].wait_near()
    outs[3].start()
    swaps = []
    for s in range(seqs):
        at = pl.ds(s * part, part)
        for d in range(1, n):
            peer = lax.rem(me + d, n)
            remote(
                mixed.at[s, 0], heads_in.at[peer, s], back_send.at[s, peer], back_recv.at[s, peer], {"ctx": peer}
            ).wait_recv()
        for k in range(n):
            attended[at, k * cols : (k + 1) * cols] = heads_in[k, s]
        for j in range(shards):
            normed[at, j * shard_rows : (j + 1) * shard_rows] = contract_cols(
                attended[at, :], weights[3, j]
            ).astype(BF16)
        swap = remote(normed.at[at], branch_in.at[s], swap_send.at[s], swap_recv.at[s], {"tp": 1 - spot.half})
        swap.start()
        swaps.append(swap)
    if n > 2:
        spreads[1].hop(2)
    for h in range(3, n):
        for spread in spreads:
            spread.hop(h)
    loads[4].wait_own()
    loads[4].pass_on()
    for s in range(seqs):
        swaps[s].wait_recv()

        @pl.loop(0, part // 64)
        def _(i):
            here = pl.ds(pl.multiple_of(i * 64, 64), 64)
            at = pl.ds(pl.multiple_of(s * part + i * 64, 64), 64)
            values = tokens[at, :].astype(F32) + (
                normed[at, :].astype(F32) + branch_in[s, here, :].astype(F32)
            )
            hidden[at, :] = values
            normed_two[at, :] = (values * rms_scale(values) * gains[1:2, :]).astype(BF16)

    flip(normed_two[...], left_two)
    loads[4].wait_near()
    for spread in spreads:
        spread.wait()
    for load in loads:
        load.wait_sent()
    for move in moves + swaps:
        move.wait_send()
    for s in range(seqs):
        for d in range(1, n):
            peer = lax.rem(me + d, n)
            back(s, peer, peer).wait_send()
    for copy in outs + flips[-1:]:
        copy.wait()


class Dims:
    def __init__(self, links, seqs, part, width, inner_width, units, heads):
        self.mesh = (links.shard, links.ctx, links.tp)
        self.n, self.seqs, self.part, self.width = links.ctx, seqs, part, width
        self.inner_width, self.units = inner_width, units
        self.head_dim = inner_width // heads
        self.cols, self.own_heads = inner_width // links.ctx, heads // links.ctx
        self.shards, self.shard_rows = links.shard, width // links.shard


def forward_call(dims):
    rows, width, n, part, seqs = dims.seqs * dims.part, dims.width, dims.n, dims.part, dims.seqs
    shards, shard_rows, inner, units = dims.shards, dims.shard_rows, dims.inner_width, dims.units
    lanes, span = 2 * dims.head_dim, 2 * n * part
    vmem, anywhere = pl.BlockSpec(memory_space=pltpu.VMEM), pl.BlockSpec(memory_space=pl.ANY)
    shape = jax.ShapeDtypeStruct
    dma = pltpu.SemaphoreType.DMA
    chips = shards // 2
    block = (seqs, part, dims.cols)
    return pl.pallas_call(
        functools.partial(forward_kernel, dims),
        in_specs=[vmem] * 4 + [anywhere] * 7,
        out_specs=[vmem] * 4 + [anywhere] * 11,
        out_shape=[
            shape((rows, width), F32),
            shape((rows, width), BF16),
            shape((rows, inner), BF16),
            shape((seqs, n, part, lanes), F32),
            shape((3, n) + block, BF16),
        ]
        + [shape((width, rows), BF16)] * 3
        + [shape((shards, shard_rows, inner), BF16)] * 4
        + [shape((shards, shard_rows, units), BF16)] * 3,
        scratch_shapes=[
            pltpu.VMEM((rows, width), BF16),
            pltpu.VMEM((width, rows), BF16),
            pltpu.VMEM((4, shards, shard_rows, inner), BF16),
            pltpu.VMEM((rows, inner), F32),
            pltpu.VMEM((dims.own_heads, part, span), BF16),
            pltpu.VMEM((3, n) + block, BF16),
            pltpu.VMEM((3, n) + block, BF16),
            pltpu.VMEM((seqs, n, part, dims.cols), BF16),
            pltpu.VMEM((n,) + block, BF16),
            pltpu.VMEM((part, span), F32),
            pltpu.VMEM((seqs, part, width), BF16),
            dma((7,)),
            dma((7, chips)),
            dma((7, chips)),
            dma((7, chips)),
            dma((7, chips)),
            dma((3, n)),
            dma((3, n)),
            dma((seqs, n)),
            dma((seqs, n)),
            pltpu.VMEM((shard_rows, units), BF16),
            dma((2,)),
            dma((seqs,)),
            dma((seqs,)),
            dma((6,)),
        ]
        + [dma((2, chips))] * 2
        + [dma((2, chips, n))] * 6,
        compiler_params=pltpu.CompilerParams(
            vmem_limit_bytes=60 * 2**20, collective_id=0, has_side_effects=True
        ),
        name="forward",
    )


CHUNK = 512
SLOTS = 4


class Pump:
    def __init__(self, dims, spot, left, right, sources, from_heads, outs, buffers, sems, credits):
        self.dims, self.spot, self.left, self.right = dims, spot, left, right
        self.fed, self.attended = sources
        self.from_heads, self.outs = from_heads, outs
        self.core_out, self.core_in, self.far_out, self.far_in, self.line, self.line_in, self.across_in, self.done = buffers
        (
            self.right_sem, self.core_send, self.core_recv, self.far_send, self.far_recv, self.in_send, self.in_recv,
            self.across_send, self.across_recv, self.out_send, self.out_recv, self.fin_sem,
        ) = sems
        self.core_credit, self.far_credit, self.in_credit, self.across_credit, self.out_credit = credits
        units, heads = dims.units // CHUNK, dims.inner_width // CHUNK
        self.units, self.heads = units, heads
        self.early = 3 * units + heads
        self.total = 3 * units + 4 * heads
        self.bases = [(i * units, units) for i in range(3)]
        self.bases += [(3 * units + i * heads, heads) for i in range(4)]
        me, n = spot.me, dims.n
        middle = n // 2
        self.is_middle = (me == middle - 1) | (me == middle)
        self.is_end = (me == 0) | (me == n - 1)
        self.has_outer, self.has_inner = jnp.logical_not(self.is_end), jnp.logical_not(self.is_middle)
        low_side = me < middle
        self.facing = jnp.where(low_side, middle, middle - 1)
        toward, away = jnp.where(low_side, me + 1, me - 1), jnp.where(low_side, me - 1, me + 1)
        self.inner = jnp.where(self.is_middle, self.facing, toward)
        self.outer = jnp.where(self.is_end, self.inner, away)
        self.last = self.total + 10

    def core(self, c, k):
        return remote(
            self.core_out.at[lax.rem(c, 2)], self.core_in.at[k], self.core_send.at[lax.rem(c, 2)],
            self.core_recv.at[k], {"shard": self.spot.mate},
        )

    def far(self, k, d):
        return remote(
            self.far_out.at[lax.rem(k, 2), d - 1], self.far_in.at[k, d - 1], self.far_send.at[k, d - 1],
            self.far_recv.at[k, d - 1], {"shard": self.spot.away(d)},
        )

    def inward(self, k):
        half = k
        return remote(
            self.line.at[k], self.line_in.at[half], self.in_send.at[k], self.in_recv.at[half], {"ctx": self.inner}
        )

    def across(self, k):
        return remote(
            self.line.at[k], self.across_in.at[k], self.across_send.at[k],
            self.across_recv.at[k], {"ctx": self.facing},
        )

    def outward(self, k):
        return remote(
            self.done.at[k], self.done.at[k], self.out_send.at[k], self.out_recv.at[k], {"ctx": self.outer}
        )

    def spend(self, c, credit, slots=SLOTS):
        @pl.when(c >= slots)
        def _():
            pl.semaphore_wait(credit, 1)

    def give(self, c, credit, peer, slots=SLOTS):
        @pl.when(c + slots < self.total)
        def _():
            pl.semaphore_signal(credit, inc=1, device_id=peer, device_id_type=MESH)

    def term(self, c, shard, k):
        one = lambda b: jnp.where(c >= b, 1, 0)
        which = one(self.units) + one(3 * self.units) - 2 * one(self.early)
        rows = self.dims.shard_rows
        return dot(self.left[which, pl.ds(pl.multiple_of(shard * rows, rows), rows), :], self.right[k])

    def fetch(self, c):
        k, fed = lax.rem(c, SLOTS), 3 * self.units

        @pl.when(c < fed)
        def _():
            source = self.fed.at[c // self.units, lax.rem(c, self.units)]
            pltpu.make_async_copy(source, self.right.at[k], self.right_sem.at[k]).start()

        @pl.when((c >= fed) & (c < self.early))
        def _():
            at = pl.ds(pl.multiple_of((c - fed) * CHUNK, CHUNK), CHUNK)
            pltpu.make_async_copy(self.attended.at[:, at], self.right.at[k], self.right_sem.at[k]).start()

        @pl.when((c >= self.early) & (c < self.total))
        def _():
            dims = self.dims
            which, piece = (c - self.early) // self.heads, lax.rem(c - self.early, self.heads)
            per = CHUNK // dims.cols
            for i in range(per):
                for s in range(dims.seqs):
                    self.right[k, s * dims.part : (s + 1) * dims.part, i * dims.cols : (i + 1) * dims.cols] = (
                        self.from_heads[which, piece * per + i, s]
                    )

    def save(self, c, k):
        for (base, count), out in zip(self.bases, self.outs):
            @pl.when((c >= base) & (c < base + count))
            def _():
                at = pl.ds(pl.multiple_of((c - base) * CHUNK, CHUNK), CHUNK)
                pltpu.make_async_copy(self.done.at[k], out.at[:, at], self.fin_sem.at[k]).start()

    def settle(self, c, k):
        pltpu.make_async_copy(self.done.at[k], self.outs[0].at[:, pl.ds(0, CHUNK)], self.fin_sem.at[k]).wait()

        @pl.when(self.has_outer)
        def _():
            self.outward(k).wait_send()

        @pl.when(self.has_inner)
        def _():
            self.give(c, self.out_credit, {"ctx": self.inner})

    def deliver(self, c, k):
        @pl.when(self.has_inner)
        def _():
            self.outward(k).wait_recv()
            self.save(c, k)

            @pl.when(self.has_outer)
            def _():
                self.spend(c, self.out_credit)
                self.outward(k).start()

    def finish(self, c, k):
        @pl.when(self.is_middle)
        def _():
            self.across(k).wait_recv()
            self.across(k).wait_send()
            self.done[k] = (self.line[k].astype(F32) + self.across_in[k].astype(F32)).astype(BF16)
            self.give(c, self.across_credit, {"ctx": self.facing})
            self.save(c, k)

            @pl.when(self.has_outer)
            def _():
                self.spend(c, self.out_credit)
                self.outward(k).start()

        @pl.when(self.has_inner)
        def _():
            self.inward(k).wait_send()

    def collect(self, c, k):
        @pl.when(self.has_outer)
        def _():
            self.inward(k).wait_recv()
            self.line[k] = (self.line[k].astype(F32) + self.line_in[k].astype(F32)).astype(BF16)
            self.give(c, self.in_credit, {"ctx": self.outer})

        @pl.when(self.is_middle)
        def _():
            self.spend(c, self.across_credit)
            self.across(k).start()

        @pl.when(self.has_outer & self.has_inner)
        def _():
            self.spend(c, self.in_credit)
            self.inward(k).start()

    def own(self, c, k):
        total = self.term(c, self.spot.shard, k) + self.core_in[k, self.spot.chips - 1].astype(F32)
        for d in range(1, self.spot.chips):
            self.far(k, d).wait_send()
            self.far(k, d).wait_recv()
            total = total + self.far_in[k, d - 1].astype(F32)
        self.line[k] = total.astype(BF16)
        self.give(c, self.core_credit, {"shard": self.spot.mate})
        for d in range(1, self.spot.chips):
            sender = lax.rem(self.spot.shard - 2 * d + self.spot.shards, self.spot.shards)
            self.give(c, self.far_credit.at[d - 1], {"shard": sender})

        @pl.when(self.is_end & self.has_inner)
        def _():
            self.spend(c, self.in_credit)
            self.inward(k).start()

    def to_chips(self, c, k):
        self.core(c, k).wait_recv()
        self.core(c, k).wait_send()
        for d in range(1, self.spot.chips):
            pair = self.term(c, self.spot.away(d), k) + self.core_in[k, d - 1].astype(F32)
            self.far_out[lax.rem(k, 2), d - 1] = pair.astype(BF16)
            self.spend(c, self.far_credit.at[d - 1])
            self.far(k, d).start()

    def to_core(self, c, k):
        @pl.when(c < self.early)
        def _():
            pltpu.make_async_copy(self.fed.at[0, 0], self.right.at[k], self.right_sem.at[k]).wait()

        chips, half = self.spot.chips, lax.rem(c, 2)
        for d in range(1, chips + 1):
            shard = 2 * lax.rem(self.spot.chip + d, chips) + 1 - self.spot.core
            self.core_out[half, d - 1] = self.term(c, shard, k).astype(BF16)
        self.spend(c, self.core_credit)
        self.core(c, k).start()

    def step(self, t):
        def at(lag, stage):
            c = t - lag

            @pl.when((c >= 0) & (c < self.total))
            def _():
                stage(c, lax.rem(c, SLOTS))

        @pl.when(t < self.total)
        def _():
            self.fetch(t)

        at(10, self.settle)
        at(9, self.deliver)
        at(7, self.finish)
        at(5, self.collect)
        at(3, self.own)

        at(1, self.to_chips)
        at(0, self.to_core)

    def steps(self, first, last):
        @pl.loop(first, last)
        def _(t):
            self.step(t)


UNITS = 256


def geglu_both(gate, up, upstream):
    root, cube = 0.7978845608028654, 0.044715
    square = gate * gate
    bent = jnp.tanh(root * gate * (1.0 + cube * square))
    half = 0.5 * (1.0 + bent)
    gelu = gate * half
    slope = half + 0.5 * gate * (1.0 - bent * bent) * (root * (1.0 + 3.0 * cube * square))
    return gelu * up, upstream * up * slope, upstream * gelu


def backward_kernel(
    dims, gain_two, table,
    lse_from, pieces_from, left_g, left_two, left_one, normed_two, attended, hidden, cotangent,
    wo, wq, wk, wv, wi0, wi1, wff,
    down_out, gate_out, up_out, o_out, q_out, k_out, v_out,
    grad_hidden, ffn_term, ffn_other, term_one, other_one, ffn_gain, table_out,
    left, right, core_out, core_in, far_out, far_in, line, line_in, across_in, done,
    fed, term, swap_in, grads, grads_out, grads_in,
    right_sem, core_send, core_recv, far_send, far_recv, in_send, in_recv, across_send, across_recv,
    out_send, out_recv, fin_sem, swap_send, swap_recv, head_send, head_recv, back_send, back_recv,
    one_send, one_recv, ffn_sem, local_sem,
    core_credit, far_credit, in_credit, across_credit, out_credit,
):
    spot = Spot(*dims.mesh)
    n, seqs, part, cols, head_dim, width = dims.n, dims.seqs, dims.part, dims.cols, dims.head_dim, dims.width
    me, shards, shard_rows, units = spot.me, spot.shards, dims.shard_rows, dims.units
    rows = seqs * part
    lanes, per = 2 * head_dim, 2
    groups = cols // lanes
    span = table.shape[1]
    other_half = {"tp": 1 - spot.half}
    pump = Pump(
        dims, spot, left, right, (fed, attended), grads_in,
        (down_out, gate_out, up_out, o_out, q_out, k_out, v_out),
        (core_out, core_in, far_out, far_in, line, line_in, across_in, done),
        (
            right_sem, core_send, core_recv, far_send, far_recv, in_send, in_recv, across_send, across_recv,
            out_send, out_recv, fin_sem,
        ),
        (core_credit, far_credit, in_credit, across_credit, out_credit),
    )
    lefts = [
        pltpu.make_async_copy(source, left.at[i], local_sem.at[i])
        for i, source in ((0, left_g), (1, left_two), (0, left_one))
    ]
    spot.barrier()
    ffn_gain[...] = jnp.zeros_like(ffn_gain)
    table_out[...] = jnp.zeros_like(table_out)

    def feed(weights, values, given, sem, value_sem):
        inputs = [
            pltpu.make_async_copy(normed_two, values, value_sem.at[0]),
            pltpu.make_async_copy(cotangent, given, value_sem.at[1]),
        ]

        def load(u):
            slot = lax.rem(u, 2)
            at = pl.ds(pl.multiple_of(u * UNITS, UNITS), UNITS)
            return [
                pltpu.make_async_copy(w.at[:, :, at], weights.at[slot, j], sem.at[slot, j])
                for j, w in enumerate((wi0, wi1, wff))
            ]

        for copy in load(0) + inputs + lefts[:2]:
            copy.start()
        for copy in inputs:
            copy.wait()
        each = CHUNK // UNITS

        @pl.loop(0, units // CHUNK)
        def _(c):
            for i in range(each):
                u = c * each + i

                @pl.when(u + 1 < units // UNITS)
                def _():
                    for copy in load(u + 1):
                        copy.start()

                for copy in load(u):
                    copy.wait()
                slot = lax.rem(u, 2)
                gate = dot(values[...], weights[slot, 0].reshape(width, UNITS))
                up = dot(values[...], weights[slot, 1].reshape(width, UNITS))
                upstream = dot(given[...], weights[slot, 2].reshape(width, UNITS))
                for j, made in enumerate(geglu_both(gate, up, upstream)):
                    fed[j, c, :, i * UNITS : (i + 1) * UNITS] = made.astype(BF16)

            @pl.when(c == 0)
            def _():
                for copy in lefts[:2]:
                    copy.wait()

            pump.step(c)

    pl.run_scoped(
        feed,
        pltpu.VMEM((2, 3, shards, shard_rows, UNITS), BF16),
        pltpu.VMEM((rows, width), BF16),
        pltpu.VMEM((rows, width), BF16),
        pltpu.SemaphoreType.DMA((2, 3)),
        pltpu.SemaphoreType.DMA((2,)),
    )
    fed_steps = units // CHUNK

    def feed_terms(weights, block, sem, block_sem):
        def load(j, w, slot):
            return pltpu.make_async_copy(w.at[j], weights.at[slot], sem.at[slot])

        def product(slot, which):
            total = None
            for c in range(units // CHUNK):
                at = slice(c * CHUNK, (c + 1) * CHUNK)
                made = contract_cols(fed[which, c], weights[slot, :, at])
                total = made if total is None else total + made
            return total

        def columns(j):
            return pl.ds(pl.multiple_of(j * shard_rows, shard_rows), shard_rows)

        load(0, wi0, 0).start()
        load(0, wi1, 1).start()

        @pl.loop(0, shards)
        def _(j):
            total = None
            for slot, w in enumerate((wi0, wi1)):
                load(j, w, slot).wait()
                made = product(slot, 1 + slot)
                total = made if total is None else total + made

                @pl.when(j + 1 < shards)
                def _():
                    load(j + 1, w, slot).start()

            for s in range(seqs):
                term[s, :, columns(j)] = total[s * part : (s + 1) * part].astype(BF16)

        for swap in swaps:
            swap.start()
        load(0, wff, 0).start()
        pump.steps(fed_steps, fed_steps + 1)

        @pl.loop(0, shards)
        def _(j):
            slot = lax.rem(j, 2)

            @pl.when(j + 1 < shards)
            def _():
                load(j + 1, wff, 1 - slot).start()

            load(j, wff, slot).wait()
            block[...] = product(slot, 0).astype(BF16)
            copy = pltpu.make_async_copy(block, ffn_term.at[:, columns(j)], block_sem.at[0])
            copy.start()
            copy.wait()

        pump.steps(fed_steps + 1, fed_steps + 2)

    swaps = [
        remote(term.at[s], swap_in.at[s], swap_send.at[s], swap_recv.at[s], other_half) for s in range(seqs)
    ]
    pl.run_scoped(
        feed_terms,
        pltpu.VMEM((2, shard_rows, units), BF16),
        pltpu.VMEM((rows, shard_rows), BF16),
        pltpu.SemaphoreType.DMA((2,)),
        pltpu.SemaphoreType.DMA((1,)),
    )
    so_far = fed_steps + 2

    def head_move(s, peer):
        return remote(
            grads_out.at[0, peer, s], grads.at[me, s], head_send.at[s, peer], head_recv.at[s, me], {"ctx": peer}
        )

    def head_wait(s, peer):
        remote(
            grads_out.at[0, peer, s], grads.at[peer, s], head_send.at[s, peer], head_recv.at[s, peer], {"ctx": peer}
        ).wait_recv()

    def second_norm(s, weights, values, given, own, sem):
        at = pl.ds(s * part, part)
        copies = [
            pltpu.make_async_copy(hidden.at[at, :], values, sem.at[0]),
            pltpu.make_async_copy(cotangent.at[at, :], given, sem.at[1]),
        ]
        for copy in copies:
            copy.start()
        for copy in copies:
            copy.wait()
        swaps[s].wait_recv()

        @pl.loop(0, part // 64)
        def _(i):
            here = pl.ds(pl.multiple_of(i * 64, 64), 64)
            h = values[here, :]
            grad = term[s, here, :].astype(F32) + swap_in[s, here, :].astype(F32)
            scale = rms_scale(h)
            ffn_gain[...] += jnp.sum(grad * h * scale, axis=0, keepdims=True)
            total = given[here, :].astype(F32) + rms_back(h, scale, gain_two[...], grad)
            values[here, :] = total
            own[here, :] = total.astype(BF16)

        saved = pltpu.make_async_copy(values, grad_hidden.at[at, :], sem.at[0])
        saved.start()
        total = dot(own[:, :shard_rows], weights[0])
        for j in range(1, shards):
            total += dot(own[:, j * shard_rows : (j + 1) * shard_rows], weights[j])
        for k in range(n):
            grads_out[0, k, s] = total[:, k * cols : (k + 1) * cols].astype(BF16)
        for d in range(1, n):
            head_move(s, lax.rem(me + d, n)).start()
        grads[me, s] = grads_out[0, me, s]
        left[2, :, s * part : (s + 1) * part] = own[...].T
        saved.wait()

    def second_norms(weights, values, given, own, sem):
        load = pltpu.make_async_copy(wo, weights, sem.at[3])
        load.start()
        load.wait()
        for s in range(seqs):
            second_norm(s, weights, values, given, own, sem)
            if s == 0:
                pump.steps(so_far, so_far + 1)

    pl.run_scoped(
        second_norms,
        pltpu.VMEM((shards, shard_rows, dims.inner_width), BF16),
        pltpu.VMEM((part, width), F32),
        pltpu.VMEM((part, width), BF16),
        pltpu.VMEM((part, width), BF16),
        pltpu.SemaphoreType.DMA((4,)),
    )
    ffn_swap = remote(ffn_term, ffn_other, ffn_sem.at[0], ffn_sem.at[1], other_half)
    ffn_swap.start()
    pump.steps(so_far + 1, so_far + 2)
    so_far += 2

    def back_move(j, s, peer):
        return remote(
            grads_out.at[j, peer, s], grads_in.at[j, me, s], back_send.at[j, s, peer], back_recv.at[j, s, me],
            {"ctx": peer},
        )

    def back_wait(j, s, peer):
        remote(
            grads_out.at[j, peer, s], grads_in.at[j, peer, s], back_send.at[j, s, peer], back_recv.at[j, s, peer],
            {"ctx": peer},
        ).wait_recv()

    def attention(pieces, lse, bias, sums, grad_k, grad_v, sem):
        @pl.loop(0, seqs * groups * n)
        def _(i):
            a, group, s = lax.rem(i, n), lax.rem(i // n, groups), i // (n * groups)
            at = pl.ds(pl.multiple_of(group * lanes, lanes), lanes)

            @pl.when((a == 0) & (group == 0))
            def _():
                here = [
                    pltpu.make_async_copy(pieces_from.at[:, :, s], pieces, sem.at[0]),
                    pltpu.make_async_copy(lse_from.at[s], lse, sem.at[1]),
                ]
                for copy in here:
                    copy.start()
                for copy in here:
                    copy.wait()
                for d in range(1, n):
                    head_wait(s, lax.rem(me + d, n))
                    head_move(s, lax.rem(me + d, n)).wait_send()

            @pl.when(a == 0)
            def _():
                for j in range(per):
                    bias_rows(table[pl.ds(group * per + j, 1), :], sums.at[j])
                bias[...] = sums[...].astype(BF16)
                sums[...] = jnp.zeros_like(sums)
                grad_k[...] = jnp.zeros_like(grad_k)
                grad_v[...] = jnp.zeros_like(grad_v)

            lane = lax.broadcasted_iota(jnp.int32, (part, lanes), 1)
            result = jnp.zeros((part, lanes), F32)
            for j in range(per):
                mask = (lane >= j * head_dim) & (lane < (j + 1) * head_dim)
                query = jnp.where(mask, pieces[0, a, :, at], 0)
                upstream = jnp.where(mask, grads[a, s, :, at], 0)
                log_total = jnp.sum(jnp.where(lane == group * per + j, lse[a], 0.0), axis=1, keepdims=True)
                windows = [pl.ds(pl.multiple_of((n + b - a) * part, part), part) for b in range(n)]
                probs, grad_probs = [], []
                for b in range(n):
                    scores = contract_cols(query, pieces[1, b, :, at]) + bias[j, :, windows[b]].astype(F32)
                    probs.append(jnp.exp(scores - log_total))
                    grad_probs.append(contract_cols(upstream, pieces[2, b, :, at]))
                delta = sum(jnp.sum(g * p, axis=1, keepdims=True) for g, p in zip(grad_probs, probs))
                summed = None
                for b in range(n):
                    grad_scores = (probs[b] * (grad_probs[b] - delta)).astype(BF16)
                    sums[j, :, windows[b]] += grad_scores.astype(F32)
                    product = dot(grad_scores, pieces[1, b, :, at])
                    summed = product if summed is None else summed + product
                    grad_k[b] += contract_rows(grad_scores, query)
                    grad_v[b] += contract_rows(probs[b].astype(BF16), upstream)
                result = jnp.where(mask, summed, result)
            grads_out[0, a, s, :, at] = result.astype(BF16)

            @pl.when(a == n - 1)
            def _():
                for b in range(n):
                    grads_out[1, b, s, :, at] = grad_k[b].astype(BF16)
                    grads_out[2, b, s, :, at] = grad_v[b].astype(BF16)
                for j in range(per):
                    table_out[pl.ds(group * per + j, 1), :] += diagonal_sums(sums.at[j])

            @pl.when((a == n - 1) & (group == groups - 1))
            def _():
                for j in range(3):
                    for d in range(1, n):
                        back_move(j, s, lax.rem(me + d, n)).start()
                    grads_in[j, me, s] = grads_out[j, me, s]

            @pl.when(a == n - 1)
            def _():
                pump.step(so_far + i // n)

    pl.run_scoped(
        attention,
        pltpu.VMEM((3, n, part, cols), BF16),
        pltpu.VMEM((n, part, lanes), F32),
        pltpu.VMEM((per, part, span), BF16),
        pltpu.VMEM((per, part, span), F32),
        pltpu.VMEM((n, part, lanes), F32),
        pltpu.VMEM((n, part, lanes), F32),
        pltpu.SemaphoreType.DMA((2,)),
    )
    so_far += seqs * groups
    lefts[2].start()
    lefts[2].wait()
    pump.steps(so_far, so_far + 3)
    so_far += 3
    for s in range(seqs):
        for j in range(3):
            for d in range(1, n):
                back_wait(j, s, lax.rem(me + d, n))

    def first_norm_terms(weights, values, sem):
        def load(shard):
            return [
                pltpu.make_async_copy(w.at[shard], weights.at[shard % 2, j], sem.at[shard % 2, j])
                for j, w in enumerate((wq, wk, wv))
            ]

        for copy in load(0):
            copy.start()
        for j in range(3):
            for s in range(seqs):
                for k in range(n):
                    values[j, s * part : (s + 1) * part, k * cols : (k + 1) * cols] = grads_in[j, k, s]
        for shard in range(shards):
            if shard + 1 < shards:
                for copy in load(shard + 1):
                    copy.start()
            for copy in load(shard):
                copy.wait()
            total = contract_cols(values[0], weights[shard % 2, 0])
            total += contract_cols(values[1], weights[shard % 2, 1])
            total += contract_cols(values[2], weights[shard % 2, 2])
            for s in range(seqs):
                term_one[s, :, shard * shard_rows : (shard + 1) * shard_rows] = (
                    total[s * part : (s + 1) * part].astype(BF16)
                )

    pl.run_scoped(
        first_norm_terms,
        pltpu.VMEM((2, 3, shard_rows, dims.inner_width), BF16),
        pltpu.VMEM((3, seqs * part, dims.inner_width), BF16),
        pltpu.SemaphoreType.DMA((2, 3)),
    )
    ones = [
        remote(term_one.at[s], other_one.at[s], one_send.at[s], one_recv.at[s], other_half) for s in range(seqs)
    ]
    for swap in ones:
        swap.start()
    pump.steps(so_far, pump.last)
    for swap in swaps:
        swap.wait_send()
    for copy in ones + [ffn_swap]:
        copy.wait_recv()
        copy.wait_send()
    for s in range(seqs):
        for d in range(1, n):
            peer = lax.rem(me + d, n)
            for j in range(3):
                back_move(j, s, peer).wait_send()


def backward_call(dims):
    rows, width, n, part, seqs = dims.seqs * dims.part, dims.width, dims.n, dims.part, dims.seqs
    shards, shard_rows, inner, units, cols = dims.shards, dims.shard_rows, dims.inner_width, dims.units, dims.cols
    span, chips = 2 * n * part, dims.shards // 2
    vmem, anywhere = pl.BlockSpec(memory_space=pltpu.VMEM), pl.BlockSpec(memory_space=pl.ANY)
    shape, dma, regular = jax.ShapeDtypeStruct, pltpu.SemaphoreType.DMA, pltpu.SemaphoreType.REGULAR
    far = max(chips - 1, 1)
    block = (shard_rows, CHUNK)
    return pl.pallas_call(
        functools.partial(backward_kernel, dims),
        in_specs=[vmem] * 2 + [anywhere] * 16,
        out_specs=[anywhere] * 10 + [vmem, anywhere, vmem, vmem],
        out_shape=[shape((shard_rows, units), BF16)] * 3
        + [shape((shard_rows, inner), BF16)] * 4
        + [
            shape((rows, width), F32),
            shape((rows, width), BF16),
            shape((rows, width), BF16),
            shape((seqs, part, width), BF16),
            shape((seqs, part, width), BF16),
            shape((1, width), F32),
            shape((dims.own_heads, span), F32),
        ],
        scratch_shapes=[
            pltpu.VMEM((3, width, rows), BF16),
            pltpu.VMEM((SLOTS, rows, CHUNK), BF16),
            pltpu.VMEM((2, chips) + block, BF16),
            pltpu.VMEM((SLOTS, chips) + block, BF16),
            pltpu.VMEM((2, far) + block, BF16),
            pltpu.VMEM((SLOTS, far) + block, BF16),
            pltpu.VMEM((SLOTS,) + block, BF16),
            pltpu.VMEM((SLOTS,) + block, BF16),
            pltpu.VMEM((SLOTS,) + block, BF16),
            pltpu.VMEM((SLOTS,) + block, BF16),
            pltpu.VMEM((3, units // CHUNK, rows, CHUNK), BF16),
            pltpu.VMEM((seqs, part, width), BF16),
            pltpu.VMEM((seqs, part, width), BF16),
            pltpu.VMEM((n, seqs, part, cols), BF16),
            pltpu.VMEM((3, n, seqs, part, cols), BF16),
            pltpu.VMEM((3, n, seqs, part, cols), BF16),
            dma((SLOTS,)),
            dma((2,)),
            dma((SLOTS,)),
            dma((SLOTS, far)),
            dma((SLOTS, far)),
        ]
        + [dma((SLOTS,))] * 7
        + [dma((seqs,))] * 2
        + [dma((seqs, n))] * 2
        + [dma((3, seqs, n))] * 2
        + [dma((seqs,))] * 2
        + [dma((2,)), dma((4,))]
        + [regular, regular((far,)), regular, regular, regular],
        compiler_params=pltpu.CompilerParams(
            vmem_limit_bytes=62 * 2**20, collective_id=1, has_side_effects=True
        ),
        name="backward",
    )


def ring(n, d):
    return [(i, (i + d) % n) for i in range(n)]


class Links:
    def __init__(self, mesh):
        self.shard, self.ctx, self.tp = mesh.shape["shard"], mesh.shape["ctx"], mesh.shape["tp"]
        self.chips = self.shard // 2

    def to_core(self, value):
        return lax.ppermute(value, "shard", [(i, i ^ 1) for i in range(self.shard)])

    def to_chip(self, value, d):
        n = self.shard
        return lax.ppermute(value, "shard", [(i, (i + 2 * d) % n) for i in range(n)])

    def tp_sum(self, value):
        if self.tp != 2:
            return lax.psum(value, "tp").astype(F32)
        other = lax.ppermute(value, "tp", ring(2, 1))
        return value.astype(F32) + other.astype(F32)

    def ctx_sum(self, value):
        low = value.astype(BF16)
        if self.ctx != 4:
            return lax.psum(low, "ctx").astype(F32)
        inward = lax.ppermute(low, "ctx", [(0, 1), (3, 2)])
        half = (low.astype(F32) + inward.astype(F32)).astype(BF16)
        across = lax.ppermute(half, "ctx", [(1, 2), (2, 1)])
        whole = (half.astype(F32) + across.astype(F32)).astype(BF16)
        outward = lax.ppermute(whole, "ctx", [(1, 0), (2, 3)])
        me = lax.axis_index("ctx")
        middle = (me == 1) | (me == 2)
        return jnp.where(middle, whole, outward).astype(F32)

    def shard_sums(self, left, right):
        n, chips = self.shard, self.chips
        rows = left.shape[1] // n
        me = lax.axis_index("shard")
        chip, core = me // 2, me % 2

        def term(chip_at, core_at):
            at = (2 * chip_at + core_at) * rows
            return contract_rows(lax.dynamic_slice_in_dim(left, at, rows, 1), right)

        def chip_of(d):
            return lax.rem(chip + d, chips)

        order = list(range(1, chips)) + [0]
        got = {d: self.to_core(term(chip_of(d), 1 - core).astype(BF16)) for d in order}
        total = None
        arrived = []
        for d in order:
            pair = term(chip_of(d), core) + got[d].astype(F32)
            if d:
                arrived.append(self.to_chip(pair.astype(BF16), d))
            else:
                total = pair
        for value in arrived:
            total = total + value.astype(F32)
        return total

    def small_sum(self, value):
        for axis, n in (("shard", self.shard), ("ctx", self.ctx)):
            step = 1
            while step < n:
                value = value + lax.ppermute(value, axis, [(i, i ^ step) for i in range(n)])
                step *= 2
        return value


def per_device(
    links,
    tokens,
    cotangent,
    buckets,
    query_weight,
    key_weight,
    value_weight,
    output_weight,
    gate_weight,
    up_weight,
    down_weight,
    norm_gain,
    ffn_gain,
    bucket_bias_table,
):
    seqs, part, width = tokens.shape
    rows = seqs * part
    slots, heads = bucket_bias_table.shape
    inner_width = query_weight.shape[1]
    head_dim = inner_width // heads
    n = links.ctx
    cols = inner_width // n
    own_heads = heads // n
    me = lax.axis_index("ctx")
    gain_one = norm_gain.astype(F32)
    gain_two = ffn_gain.astype(F32)

    def gathered(weight):
        return lax.all_gather(weight, "shard", axis=0, tiled=True)

    def at_ctx(d):
        return lax.rem(me + d + n, n)

    corner = lax.dynamic_slice(buckets, (0, me * part), (part, part))
    later, earlier = corner[0, :], corner[:, 0]
    reach = n * part
    by_offset = jnp.concatenate(
        [
            jnp.broadcast_to(earlier[part - 1 :], (reach - part + 1,)),
            earlier[:0:-1],
            later,
            jnp.broadcast_to(later[part - 1 :], (reach - part,)),
        ]
    )
    indicator = by_offset[None, :] == jnp.arange(slots, dtype=jnp.int32)[:, None]
    own_table = lax.dynamic_slice(bucket_bias_table, (0, me * own_heads), (slots, own_heads))
    offset_bias = lax.dot_general(
        own_table, indicator.astype(BF16), (((0,), (0,)), ((), ())), preferred_element_type=F32
    )
    groups = cols // (2 * head_dim)
    offset_bias = offset_bias.reshape(groups, 2, 2 * reach)

    dims = Dims(links, seqs, part, width, inner_width, gate_weight.shape[1], heads)
    token_rows, upstream = tokens.reshape(rows, width), cotangent.reshape(rows, width)
    bias_table = offset_bias.reshape(own_heads, 2 * reach)
    hidden, normed_two, attended, lse, pieces, *lefts_and_weights = forward_call(dims)(
        token_rows, upstream, jnp.stack([gain_one, gain_two]), bias_table,
        query_weight, key_weight, value_weight, output_weight, gate_weight, up_weight, down_weight,
    )
    left_g, left_one, left_two, wq, wk, wv, wo, wi0, wi1, wff = lefts_and_weights
    *weight_grads, grad_hidden, ffn_term, ffn_other, term_one, other_one, grad_ffn_gain, offset_grad = backward_call(dims)(
        gain_two.reshape(1, width), bias_table,
        lse, pieces, left_g, left_two, left_one, normed_two, attended, hidden, upstream,
        wo, wq, wk, wv, wi0, wi1, wff,
    )
    inputs = token_rows.astype(F32)
    scale_one = rms_scale(inputs)
    grad_down_w, grad_gate_w, grad_up_w, grad_output_w, grad_query_w, grad_key_w, grad_value_w = (
        g.astype(F32) for g in weight_grads
    )
    result = (hidden + (ffn_term.astype(F32) + ffn_other.astype(F32))).astype(BF16).reshape(seqs, part, width)
    grad_ffn_gain = grad_ffn_gain[0]
    table_part = jnp.sum(jnp.where(indicator[:, None, :], offset_grad[None], 0.0), axis=-1)
    grad_table = lax.dynamic_update_slice(
        jnp.zeros((slots, heads), F32), table_part, (0, me * own_heads)
    )
    grad_normed = (term_one.astype(F32) + other_one.astype(F32)).reshape(rows, width)
    grad_norm_gain = jnp.sum(grad_normed * inputs * scale_one, axis=0)
    grad_inputs = grad_hidden + rms_back(inputs, scale_one, gain_one, grad_normed)
    small = links.small_sum(jnp.concatenate([grad_norm_gain, grad_ffn_gain, grad_table.reshape(-1)]))
    return (
        result,
        grad_inputs.reshape(seqs, part, width),
        grad_query_w,
        grad_key_w,
        grad_value_w,
        grad_output_w,
        grad_gate_w,
        grad_up_w,
        grad_down_w,
        small[:width],
        small[width : 2 * width],
        small[2 * width :].reshape(slots, heads),
    )


def solution(mesh):
    rows, weights = P("shard", "ctx", None), P("shard", "tp")
    return jax.shard_map(
        functools.partial(per_device, Links(mesh)),
        mesh=mesh,
        in_specs=(rows, rows, P("ctx", None)) + (weights,) * 7 + (P(), P(), P(None, "tp")),
        out_specs=(rows, rows) + (weights,) * 7 + (P(), P(), P(None, "tp")),
        check_vma=False,
    )
```

```python
import functools

import jax
import jax.numpy as jnp
from jax import lax
from jax.experimental import pallas as pl
from jax.experimental.pallas import tpu as pltpu
from jax.sharding import PartitionSpec as P

F32 = jnp.float32
BF16 = jnp.bfloat16
VMEM_LIMIT = 48 * 2**20


def contract_rows(left, right):
    return lax.dot_general(left, right, (((0,), (0,)), ((), ())), preferred_element_type=F32)


def contract_cols(left, right):
    return lax.dot_general(left, right, (((1,), (1,)), ((), ())), preferred_element_type=F32)


def dot(left, right):
    return jnp.dot(left, right, preferred_element_type=F32)


def rms_scale(values):
    return lax.rsqrt(jnp.mean(values * values, axis=-1, keepdims=True) + 1e-06)


def rms_back(values, scale, gain, upstream):
    weighted = upstream * gain
    inner_average = jnp.mean(values * weighted, axis=-1, keepdims=True)
    return scale * weighted - values * scale * scale * scale * inner_average


def geglu(gate, up):
    return jax.nn.gelu(gate, approximate=True) * up


def bias_rows(table_row, out):
    span = out.shape[1]
    out[0:1, :] = table_row
    done = 1
    while done < out.shape[0]:
        out[done : 2 * done, :] = pltpu.roll(out[0:done, :], done, 1)
        done *= 2
    del span


def diagonal_sums(acc):
    rows, span = acc.shape
    total = acc[...]
    while rows > 1:
        rows //= 2
        total = total[:rows] + pltpu.roll(total[rows:], span - rows, 1)
    return total


MESH = pl.DeviceIdType.MESH


class Spot:
    def __init__(self, shards, ctx, tp):
        self.shards, self.chips, self.n, self.tps = shards, shards // 2, ctx, tp
        self.shard, self.me, self.half = (lax.axis_index(a) for a in ("shard", "ctx", "tp"))
        self.chip, self.core = self.shard // 2, lax.rem(self.shard, 2)
        self.mate = 2 * self.chip + 1 - self.core

    def away(self, d):
        return lax.rem(self.shard + 2 * d, self.shards)

    def barrier(self):
        peers = [{"shard": self.mate}] + [{"shard": self.away(d)} for d in range(1, self.chips)]
        peers += [{"ctx": lax.rem(self.me + d, self.n)} for d in range(1, self.n)]
        peers += [{"tp": 1 - self.half}]
        semaphore = pltpu.get_barrier_semaphore()
        for peer in peers:
            pl.semaphore_signal(semaphore, inc=1, device_id=peer, device_id_type=MESH)
        pl.semaphore_wait(semaphore, len(peers))


def remote(src, dst, send, recv, peer):
    return pltpu.make_async_remote_copy(
        src_ref=src, dst_ref=dst, send_sem=send, recv_sem=recv, device_id=peer, device_id_type=MESH
    )


class Keep:
    def __init__(self, jobs, room, sem):
        self.halves = []
        for i, (own, full) in enumerate(jobs):
            self.halves.append(pltpu.make_async_copy(own, room, sem.at[0]))
            self.halves.append(pltpu.make_async_copy(room, full, sem.at[1]))
        self.at = 0
        self.halves[0].start()

    def step(self):
        if self.at < len(self.halves):
            self.halves[self.at].wait()
            self.at += 1
            if self.at < len(self.halves):
                self.halves[self.at].start()

    def start(self):
        pass

    def wait(self):
        while self.at < len(self.halves):
            self.step()


class Gather:
    def __init__(self, spot, own, full, sems, keep=None):
        self.spot, self.own, self.full = spot, own, full
        self.local, self.send, self.recv, self.on_send, self.on_recv = sems
        spot_shard = spot.shard
        self.keep = keep or pltpu.make_async_copy(own, full.at[spot_shard], self.local)
        self.far = [
            remote(own, full.at[spot_shard], self.send.at[d], self.recv.at[d], {"shard": spot.away(d)})
            for d in range(1, spot.chips)
        ]
        mate = {"shard": spot.mate}
        self.near = [remote(own, full.at[spot_shard], self.on_send.at[0], self.on_recv.at[0], mate)]
        for d in range(1, spot.chips):
            at = full.at[lax.rem(spot.shard - 2 * d + spot.shards, spot.shards)]
            self.near.append(remote(at, at, self.on_send.at[d], self.on_recv.at[d], mate))

    def start_far(self):
        for copy in self.far:
            copy.start()

    def start_near(self):
        self.keep.start()
        self.near[0].start()

    def pass_on(self):
        for d, copy in enumerate(self.far, 1):
            copy.wait_recv()
            self.near[d].start()

    def wait_own(self):
        self.keep.wait()
        self.near[0].wait_recv()

    def wait_near(self):
        for copy in self.near[1:]:
            copy.wait_recv()

    def wait_sent(self):
        for copy in self.far + self.near:
            copy.wait_send()


class Spread:
    def __init__(self, spot, own, full, keep, sems, direct=0):
        self.spot, self.own, self.full, self.keep, self.direct = spot, own, full, keep, direct
        (
            self.far_send, self.far_recv, self.right_send, self.right_recv, self.left_send, self.left_recv,
            self.mate_send, self.mate_recv,
        ) = sems
        self.part = (full.shape[1] - direct) // spot.n
        n, me = spot.n, spot.me
        self.near = remote(
            own, full.at[spot.shard], self.mate_send.at[0, 0], self.mate_recv.at[0, 0], {"shard": spot.mate}
        )
        mine = self.at(me)
        self.far = [
            remote(
                own.at[mine], full.at[spot.shard, mine], self.far_send.at[d, 0], self.far_recv.at[d, 0],
                {"shard": spot.away(d)},
            )
            for d in range(1, spot.chips)
        ]
        whole = pl.ds(0, direct)
        self.far_direct = [
            remote(
                own.at[whole], full.at[spot.shard, whole], self.far_send.at[d, 1], self.far_recv.at[d, 1],
                {"shard": spot.away(d)},
            )
            for d in range(1, spot.chips)
            if direct
        ]
        self.can_right, self.can_left = me + 1 < n, me > 0

    def at(self, z):
        return pl.ds(pl.multiple_of(self.direct + z * self.part, 16), self.part)

    def source(self, d):
        return lax.rem(self.spot.shard - 2 * d + self.spot.shards, self.spot.shards)

    def piece(self, d, z):
        return self.full.at[self.source(d), self.at(z)]

    def tell_direct(self, d):
        at = self.full.at[self.source(d), pl.ds(0, self.direct)]
        n = self.spot.n
        return remote(at, at, self.mate_send.at[d, n], self.mate_recv.at[d, n], {"shard": self.spot.mate})

    def start_direct(self):
        for copy in self.far_direct:
            copy.start()

    def pass_on(self):
        for d, copy in enumerate(self.far_direct, 1):
            copy.wait_recv()
            self.tell_direct(d).start()

    def tell(self, d, z):
        at = self.piece(d, z)
        return remote(at, at, self.mate_send.at[d, z], self.mate_recv.at[d, z], {"shard": self.spot.mate})

    def right(self, d, h, z):
        at, to = self.piece(d, z), {"ctx": lax.rem(self.spot.me + 1, self.spot.n)}
        return remote(at, at, self.right_send.at[d, h], self.right_recv.at[d, h], to)

    def left(self, d, h, z):
        at, to = self.piece(d, z), {"ctx": lax.rem(self.spot.me - 1 + self.spot.n, self.spot.n)}
        return remote(at, at, self.left_send.at[d, h], self.left_recv.at[d, h], to)

    def pairs(self):
        return range(1, self.spot.chips)

    def start(self):
        for copy in self.far:
            copy.start()

    def start_near(self):
        self.near.start()

    def send_on(self, d, h, z, right, left):
        self.tell(d, z).start()
        if right:
            @pl.when(self.can_right)
            def _():
                self.right(d, h, z).start()

        if left:
            @pl.when(self.can_left)
            def _():
                self.left(d, h, z).start()

    def arrived(self):
        for d in self.pairs():
            self.far[d - 1].wait_recv()
            self.send_on(d, 1, self.spot.me, True, True)

    def hop(self, h):
        me, n = self.spot.me, self.spot.n
        for d in self.pairs():
            @pl.when(me - h >= 0)
            def _():
                self.right(d, h, me - h).wait_recv()
                self.send_on(d, h + 1, me - h, h + 1 < n, False)

            @pl.when(me + h < n)
            def _():
                self.left(d, h, me + h).wait_recv()
                self.send_on(d, h + 1, me + h, False, h + 1 < n)

    def wait(self):
        me, n = self.spot.me, self.spot.n
        self.keep.wait()
        self.near.wait_recv()
        self.near.wait_send()
        for d, copy in enumerate(self.far_direct, 1):
            copy.wait_send()
            self.tell_direct(d).wait_recv()
            self.tell_direct(d).wait_send()
        for d in self.pairs():
            self.far[d - 1].wait_send()
            for z in range(n):
                self.tell(d, z).wait_recv()
                self.tell(d, z).wait_send()
            for h in range(1, n):
                @pl.when((me - h + 1 >= 0) & self.can_right)
                def _():
                    self.right(d, h, me - h + 1).wait_send()

                @pl.when((me + h - 1 < n) & self.can_left)
                def _():
                    self.left(d, h, me + h - 1).wait_send()


def forward_kernel(
    dims, tokens, cotangent, gains, table, wq, wk, wv, wo, wi0, wi1, wff,
    hidden, normed_two, attended, lse, pieces_out, left_g, left_one, left_two,
    full_q, full_k, full_v, full_o, full_0, full_1, full_2,
    normed, flipped, weights, acc, bias, staged, pieces, mixed, heads_in, rolled, branch_in,
    local_sem, far_send, far_recv, near_send, near_recv, head_send, head_recv, back_send, back_recv,
    room, keep_sem,
    swap_send, swap_recv, out_sem, *spread_sems,
):
    spot = Spot(*dims.mesh)
    n, seqs, part, cols, head_dim = dims.n, dims.seqs, dims.part, dims.cols, dims.head_dim
    me, shards = spot.me, spot.shards
    shard_rows = weights.shape[2]
    rows = seqs * part
    lanes = 2 * head_dim
    per = 2
    spot.barrier()

    def gather(i, own, full, keep=None):
        sems = [local_sem.at[i], far_send.at[i], far_recv.at[i], near_send.at[i], near_recv.at[i]]
        return Gather(spot, own, full, sems, keep)

    loads = [None] + [gather(i, w, weights.at[i]) for i, w in ((1, wk), (2, wv), (3, wo))]
    keep = Keep(
        [(w, full.at[spot.shard]) for w, full in ((wi0, full_0), (wi1, full_1), (wff, full_2))], room, keep_sem
    )
    loads.append(gather(4, wi0, full_0, keep))
    spreads = [
        Spread(spot, own, full, keep, [sem.at[i] for sem in spread_sems], direct)
        for i, (own, full, direct) in enumerate(((wi1, full_1, shard_rows // 2), (wff, full_2, 0)))
    ]
    keep_first = pltpu.make_async_copy(wq, weights.at[0, spot.shard], local_sem.at[0])
    spreads.append(Spread(spot, wq, weights.at[0], keep_first, [sem.at[2] for sem in spread_sems]))
    flips = []

    def flip(value, out):
        if flips:
            flips[-1].wait()
        flipped[...] = value.T
        flips.append(pltpu.make_async_copy(flipped, out, out_sem.at[5]))
        flips[-1].start()

    first = spreads[2]
    first.start()
    for load in loads[1:3]:
        load.start_far()
    first.keep.start()
    first.start_near()
    for load in loads[1:3]:
        load.start_near()

    @pl.loop(0, rows // 64)
    def _(i):
        at = pl.ds(pl.multiple_of(i * 64, 64), 64)
        values = tokens[at, :].astype(F32)
        normed[at, :] = (values * rms_scale(values) * gains[0:1, :]).astype(BF16)

    for head in range(dims.own_heads):
        bias_rows(table[head : head + 1, :], rolled)
        bias[head] = rolled[...].astype(BF16)

    def term(i, shard):
        at = pl.ds(pl.multiple_of(shard * shard_rows, 128), shard_rows)
        return dot(normed[:, at], weights[i, shard])

    moves = []
    first.arrived()
    for h in range(1, n):
        first.hop(h)
    for i, load in enumerate(loads[:3]):
        if i == 0:
            first.wait()
        else:
            load.wait_own()
        acc[...] = term(i, spot.shard)
        acc[...] += term(i, spot.mate)
        keep.step()
        if i:
            load.pass_on()
        if i == 2:
            for spread in spreads[:2]:
                spread.start()
            for later in loads[3:] + spreads[:2]:
                later.start_near()
        keep.step()
        for d in range(1, spot.chips):
            acc[...] += term(i, lax.rem(spot.shard - 2 * d + shards, shards))
        if i:
            load.wait_near()
        for d in range(1, spot.chips):
            acc[...] += term(i, lax.rem(spot.mate - 2 * d + shards, shards))
        for k in range(n):
            for s in range(seqs):
                staged[i, k, s] = acc[s * part : (s + 1) * part, k * cols : (k + 1) * cols].astype(BF16)
        for d in range(1, n):
            peer = lax.rem(me + d, n)
            move = remote(
                staged.at[i, peer], pieces.at[i, me], head_send.at[i, d], head_recv.at[i, d], {"ctx": peer}
            )
            move.start()
            moves.append(move)
        pieces[i, me] = staged[i, me]
    outs = [
        pltpu.make_async_copy(weights.at[i], full, out_sem.at[i])
        for i, full in enumerate((full_q, full_k, full_v, full_o))
    ]
    for copy in outs[:3]:
        copy.start()
    flip(normed[...], left_one)
    spreads[0].arrived()
    spreads[1].arrived()
    loads[3].start_far()
    flip(cotangent[...], left_g)
    for move in moves:
        move.wait_recv()
    loads[3].wait_own()
    outs.append(pltpu.make_async_copy(pieces, pieces_out, out_sem.at[4]))
    outs[4].start()

    def back(s, at, to):
        return remote(mixed.at[s, at], heads_in.at[me, s], back_send.at[s, at], back_recv.at[s, me], {"ctx": to})

    def attend(s, a):
        step = s * n + a
        lane = lax.broadcasted_iota(jnp.int32, (part, lanes), 1)
        log_total = jnp.zeros((part, lanes), F32)
        for group in range(cols // lanes):
            span = slice(group * lanes, (group + 1) * lanes)
            result = jnp.zeros((part, lanes), F32)
            for j in range(per):
                head = group * per + j
                mask = (lane >= j * head_dim) & (lane < (j + 1) * head_dim)
                query = jnp.where(mask, pieces[0, a, s, :, span], 0)
                scores = jnp.concatenate(
                    [
                        contract_cols(query, pieces[1, b, s, :, span])
                        + bias[head, :, pl.ds(pl.multiple_of((n + b - a) * part, part), part)].astype(F32)
                        for b in range(n)
                    ],
                    axis=1,
                )
                peak = jnp.max(scores, axis=1, keepdims=True)
                expo = jnp.exp(scores - peak)
                total = jnp.sum(expo, axis=1, keepdims=True)
                probs = (expo * (1.0 / total)).astype(BF16)
                summed = sum(
                    dot(probs[:, b * part : (b + 1) * part], pieces[2, b, s, :, span]) for b in range(n)
                )
                result = jnp.where(mask, summed, result)
                log_total = jnp.where(lane == head, peak + jnp.log(total), log_total)
            mixed[s, a, :, span] = result.astype(BF16)
        lse[s, a] = log_total

        @pl.when(a != me)
        def _():
            back(s, a, a).start()

        @pl.when(a == me)
        def _():
            heads_in[a, s] = mixed[s, a]

        @pl.when(step == 1)
        def _():
            spreads[0].hop(1)

        @pl.when(step == 3)
        def _():
            loads[3].pass_on()
            loads[4].start_far()
            spreads[0].start_direct()

        @pl.when(step == 4)
        def _():
            spreads[1].hop(1)

    swaps = []

    def project(s):
        at = pl.ds(s * part, part)
        for d in range(1, n):
            peer = lax.rem(me + d, n)
            remote(
                mixed.at[s, 0], heads_in.at[peer, s], back_send.at[s, peer], back_recv.at[s, peer], {"ctx": peer}
            ).wait_recv()
        for k in range(n):
            attended[at, k * cols : (k + 1) * cols] = heads_in[k, s]
        for j in range(shards):
            normed[at, j * shard_rows : (j + 1) * shard_rows] = contract_cols(
                attended[at, :], weights[3, j]
            ).astype(BF16)
        swap = remote(normed.at[at], branch_in.at[s], swap_send.at[s], swap_recv.at[s], {"tp": 1 - spot.half})
        swap.start()
        swaps.append(swap)

    for s in range(seqs):
        pl.loop(0, n)(functools.partial(attend, s))
        if s == 0:
            loads[3].wait_near()
            outs[3].start()
            if n > 2:
                spreads[0].hop(2)
        project(s)
    if n > 2:
        spreads[1].hop(2)
    for h in range(3, n):
        for spread in spreads[:2]:
            spread.hop(h)
    loads[4].wait_own()
    loads[4].pass_on()
    spreads[0].pass_on()
    for s in range(seqs):
        swaps[s].wait_recv()

        @pl.loop(0, part // 64)
        def _(i):
            here = pl.ds(pl.multiple_of(i * 64, 64), 64)
            at = pl.ds(pl.multiple_of(s * part + i * 64, 64), 64)
            values = tokens[at, :].astype(F32) + (
                normed[at, :].astype(F32) + branch_in[s, here, :].astype(F32)
            )
            hidden[at, :] = values
            normed_two[at, :] = (values * rms_scale(values) * gains[1:2, :]).astype(BF16)

    flip(normed_two[...], left_two)
    loads[4].wait_near()
    for spread in spreads[:2]:
        spread.wait()
    for load in loads[1:]:
        load.wait_sent()
    for move in moves + swaps:
        move.wait_send()
    for s in range(seqs):
        for d in range(1, n):
            peer = lax.rem(me + d, n)
            back(s, peer, peer).wait_send()
    for copy in outs + flips[-1:]:
        copy.wait()


class Dims:
    def __init__(self, links, seqs, part, width, inner_width, units, heads):
        self.mesh = (links.shard, links.ctx, links.tp)
        self.n, self.seqs, self.part, self.width = links.ctx, seqs, part, width
        self.inner_width, self.units = inner_width, units
        self.head_dim = inner_width // heads
        self.cols, self.own_heads = inner_width // links.ctx, heads // links.ctx
        self.shards, self.shard_rows = links.shard, width // links.shard


def forward_call(dims):
    rows, width, n, part, seqs = dims.seqs * dims.part, dims.width, dims.n, dims.part, dims.seqs
    shards, shard_rows, inner, units = dims.shards, dims.shard_rows, dims.inner_width, dims.units
    lanes, span = 2 * dims.head_dim, 2 * n * part
    vmem, anywhere = pl.BlockSpec(memory_space=pltpu.VMEM), pl.BlockSpec(memory_space=pl.ANY)
    shape = jax.ShapeDtypeStruct
    dma = pltpu.SemaphoreType.DMA
    chips = shards // 2
    block = (seqs, part, dims.cols)
    return pl.pallas_call(
        functools.partial(forward_kernel, dims),
        in_specs=[vmem] * 4 + [anywhere] * 7,
        out_specs=[vmem] * 4 + [anywhere] * 11,
        out_shape=[
            shape((rows, width), F32),
            shape((rows, width), BF16),
            shape((rows, inner), BF16),
            shape((seqs, n, part, lanes), F32),
            shape((3, n) + block, BF16),
        ]
        + [shape((width, rows), BF16)] * 3
        + [shape((shards, shard_rows, inner), BF16)] * 4
        + [shape((shards, shard_rows, units), BF16)] * 3,
        scratch_shapes=[
            pltpu.VMEM((rows, width), BF16),
            pltpu.VMEM((width, rows), BF16),
            pltpu.VMEM((4, shards, shard_rows, inner), BF16),
            pltpu.VMEM((rows, inner), F32),
            pltpu.VMEM((dims.own_heads, part, span), BF16),
            pltpu.VMEM((3, n) + block, BF16),
            pltpu.VMEM((3, n) + block, BF16),
            pltpu.VMEM((seqs, n, part, dims.cols), BF16),
            pltpu.VMEM((n,) + block, BF16),
            pltpu.VMEM((part, span), F32),
            pltpu.VMEM((seqs, part, width), BF16),
            dma((7,)),
            dma((7, chips)),
            dma((7, chips)),
            dma((7, chips)),
            dma((7, chips)),
            dma((3, n)),
            dma((3, n)),
            dma((seqs, n)),
            dma((seqs, n)),
            pltpu.VMEM((shard_rows, units), BF16),
            dma((2,)),
            dma((seqs,)),
            dma((seqs,)),
            dma((6,)),
        ]
        + [dma((3, chips, 2))] * 2
        + [dma((3, chips, n))] * 4
        + [dma((3, chips, n + 1))] * 2,
        compiler_params=pltpu.CompilerParams(
            vmem_limit_bytes=60 * 2**20, collective_id=0, has_side_effects=True
        ),
        name="forward",
    )


CHUNK = 512
SLOTS = 4


class Pump:
    def __init__(self, dims, spot, left, right, sources, from_heads, outs, buffers, sems, credits):
        self.dims, self.spot, self.left, self.right = dims, spot, left, right
        self.fed, self.attended = sources
        self.from_heads, self.outs = from_heads, outs
        self.core_out, self.core_in, self.far_out, self.far_in, self.line, self.line_in, self.across_in, self.done = buffers
        (
            self.right_sem, self.core_send, self.core_recv, self.far_send, self.far_recv, self.in_send, self.in_recv,
            self.across_send, self.across_recv, self.out_send, self.out_recv, self.fin_sem,
        ) = sems
        self.core_credit, self.far_credit, self.in_credit, self.across_credit, self.out_credit = credits
        units, heads = dims.units // CHUNK, dims.inner_width // CHUNK
        self.units, self.heads = units, heads
        self.early = 3 * units + heads
        self.total = 3 * units + 4 * heads
        self.bases = [(i * units, units) for i in range(3)]
        self.bases += [(3 * units + i * heads, heads) for i in range(4)]
        me, n = spot.me, dims.n
        middle = n // 2
        self.is_middle = (me == middle - 1) | (me == middle)
        self.is_end = (me == 0) | (me == n - 1)
        self.has_outer, self.has_inner = jnp.logical_not(self.is_end), jnp.logical_not(self.is_middle)
        low_side = me < middle
        self.facing = jnp.where(low_side, middle, middle - 1)
        toward, away = jnp.where(low_side, me + 1, me - 1), jnp.where(low_side, me - 1, me + 1)
        self.inner = jnp.where(self.is_middle, self.facing, toward)
        self.outer = jnp.where(self.is_end, self.inner, away)
        self.last = self.total + 10

    def core(self, c, k):
        return remote(
            self.core_out.at[lax.rem(c, 2)], self.core_in.at[k], self.core_send.at[lax.rem(c, 2)],
            self.core_recv.at[k], {"shard": self.spot.mate},
        )

    def far(self, k, d):
        return remote(
            self.far_out.at[lax.rem(k, 2), d - 1], self.far_in.at[k, d - 1], self.far_send.at[k, d - 1],
            self.far_recv.at[k, d - 1], {"shard": self.spot.away(d)},
        )

    def inward(self, k):
        half = k
        return remote(
            self.line.at[k], self.line_in.at[half], self.in_send.at[k], self.in_recv.at[half], {"ctx": self.inner}
        )

    def across(self, k):
        return remote(
            self.line.at[k], self.across_in.at[k], self.across_send.at[k],
            self.across_recv.at[k], {"ctx": self.facing},
        )

    def outward(self, k):
        return remote(
            self.done.at[k], self.done.at[k], self.out_send.at[k], self.out_recv.at[k], {"ctx": self.outer}
        )

    def spend(self, c, credit, slots=SLOTS):
        @pl.when(c >= slots)
        def _():
            pl.semaphore_wait(credit, 1)

    def give(self, c, credit, peer, slots=SLOTS):
        @pl.when(c + slots < self.total)
        def _():
            pl.semaphore_signal(credit, inc=1, device_id=peer, device_id_type=MESH)

    def term(self, c, shard, k):
        one = lambda b: jnp.where(c >= b, 1, 0)
        which = one(self.units) + one(3 * self.units) - 2 * one(self.early)
        rows = self.dims.shard_rows
        return dot(self.left[which, pl.ds(pl.multiple_of(shard * rows, rows), rows), :], self.right[k])

    def fetch(self, c):
        k, fed = lax.rem(c, SLOTS), 3 * self.units

        @pl.when(c < fed)
        def _():
            source = self.fed.at[c // self.units, lax.rem(c, self.units)]
            pltpu.make_async_copy(source, self.right.at[k], self.right_sem.at[k]).start()

        @pl.when((c >= fed) & (c < self.early))
        def _():
            at = pl.ds(pl.multiple_of((c - fed) * CHUNK, CHUNK), CHUNK)
            pltpu.make_async_copy(self.attended.at[:, at], self.right.at[k], self.right_sem.at[k]).start()

        @pl.when((c >= self.early) & (c < self.total))
        def _():
            dims = self.dims
            which, piece = (c - self.early) // self.heads, lax.rem(c - self.early, self.heads)
            per = CHUNK // dims.cols
            for i in range(per):
                for s in range(dims.seqs):
                    self.right[k, s * dims.part : (s + 1) * dims.part, i * dims.cols : (i + 1) * dims.cols] = (
                        self.from_heads[which, piece * per + i, s]
                    )

    def save(self, c, k):
        for (base, count), out in zip(self.bases, self.outs):
            @pl.when((c >= base) & (c < base + count))
            def _():
                at = pl.ds(pl.multiple_of((c - base) * CHUNK, CHUNK), CHUNK)
                pltpu.make_async_copy(self.done.at[k], out.at[:, at], self.fin_sem.at[k]).start()

    def settle(self, c, k):
        pltpu.make_async_copy(self.done.at[k], self.outs[0].at[:, pl.ds(0, CHUNK)], self.fin_sem.at[k]).wait()

        @pl.when(self.has_outer)
        def _():
            self.outward(k).wait_send()

        @pl.when(self.has_inner)
        def _():
            self.give(c, self.out_credit, {"ctx": self.inner})

    def deliver(self, c, k):
        @pl.when(self.has_inner)
        def _():
            self.outward(k).wait_recv()
            self.save(c, k)

            @pl.when(self.has_outer)
            def _():
                self.spend(c, self.out_credit)
                self.outward(k).start()

    def finish(self, c, k):
        @pl.when(self.is_middle)
        def _():
            self.across(k).wait_recv()
            self.across(k).wait_send()
            self.done[k] = (self.line[k].astype(F32) + self.across_in[k].astype(F32)).astype(BF16)
            self.give(c, self.across_credit, {"ctx": self.facing})
            self.save(c, k)

            @pl.when(self.has_outer)
            def _():
                self.spend(c, self.out_credit)
                self.outward(k).start()

        @pl.when(self.has_inner)
        def _():
            self.inward(k).wait_send()

    def collect(self, c, k):
        @pl.when(self.has_outer)
        def _():
            self.inward(k).wait_recv()
            self.line[k] = (self.line[k].astype(F32) + self.line_in[k].astype(F32)).astype(BF16)
            self.give(c, self.in_credit, {"ctx": self.outer})

        @pl.when(self.is_middle)
        def _():
            self.spend(c, self.across_credit)
            self.across(k).start()

        @pl.when(self.has_outer & self.has_inner)
        def _():
            self.spend(c, self.in_credit)
            self.inward(k).start()

    def own(self, c, k):
        total = self.term(c, self.spot.shard, k) + self.core_in[k, self.spot.chips - 1].astype(F32)
        for d in range(1, self.spot.chips):
            self.far(k, d).wait_send()
            self.far(k, d).wait_recv()
            total = total + self.far_in[k, d - 1].astype(F32)
        self.line[k] = total.astype(BF16)
        self.give(c, self.core_credit, {"shard": self.spot.mate})
        for d in range(1, self.spot.chips):
            sender = lax.rem(self.spot.shard - 2 * d + self.spot.shards, self.spot.shards)
            self.give(c, self.far_credit.at[d - 1], {"shard": sender})

        @pl.when(self.is_end & self.has_inner)
        def _():
            self.spend(c, self.in_credit)
            self.inward(k).start()

    def to_chips(self, c, k):
        self.core(c, k).wait_recv()
        self.core(c, k).wait_send()
        for d in range(1, self.spot.chips):
            pair = self.term(c, self.spot.away(d), k) + self.core_in[k, d - 1].astype(F32)
            self.far_out[lax.rem(k, 2), d - 1] = pair.astype(BF16)
            self.spend(c, self.far_credit.at[d - 1])
            self.far(k, d).start()

    def to_core(self, c, k):
        @pl.when(c < self.early)
        def _():
            pltpu.make_async_copy(self.fed.at[0, 0], self.right.at[k], self.right_sem.at[k]).wait()

        chips, half = self.spot.chips, lax.rem(c, 2)
        for d in range(1, chips + 1):
            shard = 2 * lax.rem(self.spot.chip + d, chips) + 1 - self.spot.core
            self.core_out[half, d - 1] = self.term(c, shard, k).astype(BF16)
        self.spend(c, self.core_credit)
        self.core(c, k).start()

    def step(self, t):
        def at(lag, stage):
            c = t - lag

            @pl.when((c >= 0) & (c < self.total))
            def _():
                stage(c, lax.rem(c, SLOTS))

        @pl.when(t < self.total)
        def _():
            self.fetch(t)

        at(10, self.settle)
        at(9, self.deliver)
        at(7, self.finish)
        at(5, self.collect)
        at(3, self.own)

        at(1, self.to_chips)
        at(0, self.to_core)

    def steps(self, first, last):
        @pl.loop(first, last)
        def _(t):
            self.step(t)


UNITS = 256


def geglu_both(gate, up, upstream):
    root, cube = 0.7978845608028654, 0.044715
    square = gate * gate
    bent = jnp.tanh(root * gate * (1.0 + cube * square))
    half = 0.5 * (1.0 + bent)
    gelu = gate * half
    slope = half + 0.5 * gate * (1.0 - bent * bent) * (root * (1.0 + 3.0 * cube * square))
    return gelu * up, upstream * up * slope, upstream * gelu


def backward_kernel(
    dims, gain_two, table,
    lse_from, pieces_from, left_g, left_two, left_one, normed_two, attended, hidden, cotangent,
    wo, wq, wk, wv, wi0, wi1, wff,
    down_out, gate_out, up_out, o_out, q_out, k_out, v_out,
    grad_hidden, ffn_term, ffn_other, term_one, other_one, ffn_gain, table_out,
    left, right, core_out, core_in, far_out, far_in, line, line_in, across_in, done,
    fed, term, swap_in, grads, grads_out, grads_in,
    right_sem, core_send, core_recv, far_send, far_recv, in_send, in_recv, across_send, across_recv,
    out_send, out_recv, fin_sem, swap_send, swap_recv, head_send, head_recv, back_send, back_recv,
    one_send, one_recv, ffn_sem, local_sem,
    core_credit, far_credit, in_credit, across_credit, out_credit,
):
    spot = Spot(*dims.mesh)
    n, seqs, part, cols, head_dim, width = dims.n, dims.seqs, dims.part, dims.cols, dims.head_dim, dims.width
    me, shards, shard_rows, units = spot.me, spot.shards, dims.shard_rows, dims.units
    rows = seqs * part
    lanes, per = 2 * head_dim, 2
    groups = cols // lanes
    span = table.shape[1]
    other_half = {"tp": 1 - spot.half}
    pump = Pump(
        dims, spot, left, right, (fed, attended), grads_in,
        (down_out, gate_out, up_out, o_out, q_out, k_out, v_out),
        (core_out, core_in, far_out, far_in, line, line_in, across_in, done),
        (
            right_sem, core_send, core_recv, far_send, far_recv, in_send, in_recv, across_send, across_recv,
            out_send, out_recv, fin_sem,
        ),
        (core_credit, far_credit, in_credit, across_credit, out_credit),
    )
    lefts = [
        pltpu.make_async_copy(source, left.at[i], local_sem.at[i])
        for i, source in ((0, left_g), (1, left_two), (0, left_one))
    ]
    spot.barrier()
    ffn_gain[...] = jnp.zeros_like(ffn_gain)
    table_out[...] = jnp.zeros_like(table_out)

    def feed(weights, values, given, sem, value_sem):
        inputs = [
            pltpu.make_async_copy(normed_two, values, value_sem.at[0]),
            pltpu.make_async_copy(cotangent, given, value_sem.at[1]),
        ]

        def load(u):
            slot = lax.rem(u, 2)
            at = pl.ds(pl.multiple_of(u * UNITS, UNITS), UNITS)
            return [
                pltpu.make_async_copy(w.at[:, :, at], weights.at[slot, j], sem.at[slot, j])
                for j, w in enumerate((wi0, wi1, wff))
            ]

        for copy in load(0) + inputs + lefts[:2]:
            copy.start()
        for copy in inputs:
            copy.wait()
        each = CHUNK // UNITS

        @pl.loop(0, units // CHUNK)
        def _(c):
            for i in range(each):
                u = c * each + i

                @pl.when(u + 1 < units // UNITS)
                def _():
                    for copy in load(u + 1):
                        copy.start()

                for copy in load(u):
                    copy.wait()
                slot = lax.rem(u, 2)
                gate = dot(values[...], weights[slot, 0].reshape(width, UNITS))
                up = dot(values[...], weights[slot, 1].reshape(width, UNITS))
                upstream = dot(given[...], weights[slot, 2].reshape(width, UNITS))
                for j, made in enumerate(geglu_both(gate, up, upstream)):
                    fed[j, c, :, i * UNITS : (i + 1) * UNITS] = made.astype(BF16)

            @pl.when(c == 0)
            def _():
                for copy in lefts[:2]:
                    copy.wait()

            pump.step(c)

    pl.run_scoped(
        feed,
        pltpu.VMEM((2, 3, shards, shard_rows, UNITS), BF16),
        pltpu.VMEM((rows, width), BF16),
        pltpu.VMEM((rows, width), BF16),
        pltpu.SemaphoreType.DMA((2, 3)),
        pltpu.SemaphoreType.DMA((2,)),
    )
    fed_steps = units // CHUNK

    def feed_terms(weights, block, sem, block_sem):
        def load(j, w, slot):
            return pltpu.make_async_copy(w.at[j], weights.at[slot], sem.at[slot])

        def product(slot, which):
            total = None
            for c in range(units // CHUNK):
                at = slice(c * CHUNK, (c + 1) * CHUNK)
                made = contract_cols(fed[which, c], weights[slot, :, at])
                total = made if total is None else total + made
            return total

        def columns(j):
            return pl.ds(pl.multiple_of(j * shard_rows, shard_rows), shard_rows)

        load(0, wi0, 0).start()
        load(0, wi1, 1).start()

        @pl.loop(0, shards)
        def _(j):
            total = None
            for slot, w in enumerate((wi0, wi1)):
                load(j, w, slot).wait()
                made = product(slot, 1 + slot)
                total = made if total is None else total + made

                @pl.when(j + 1 < shards)
                def _():
                    load(j + 1, w, slot).start()

            for s in range(seqs):
                term[s, :, columns(j)] = total[s * part : (s + 1) * part].astype(BF16)

            @pl.when(j == 1)
            def _():
                pump.step(fed_steps)

        for swap in swaps:
            swap.start()
        load(0, wff, 0).start()
        pump.steps(fed_steps + 1, fed_steps + 2)

        @pl.loop(0, shards)
        def _(j):
            slot = lax.rem(j, 2)

            @pl.when(j + 1 < shards)
            def _():
                load(j + 1, wff, 1 - slot).start()

            load(j, wff, slot).wait()
            block[...] = product(slot, 0).astype(BF16)
            copy = pltpu.make_async_copy(block, ffn_term.at[:, columns(j)], block_sem.at[0])
            copy.start()
            copy.wait()

            @pl.when(j == 1)
            def _():
                pump.step(fed_steps + 2)

        pump.steps(fed_steps + 3, fed_steps + 4)

    swaps = [
        remote(term.at[s], swap_in.at[s], swap_send.at[s], swap_recv.at[s], other_half) for s in range(seqs)
    ]
    pl.run_scoped(
        feed_terms,
        pltpu.VMEM((2, shard_rows, units), BF16),
        pltpu.VMEM((rows, shard_rows), BF16),
        pltpu.SemaphoreType.DMA((2,)),
        pltpu.SemaphoreType.DMA((1,)),
    )
    so_far = fed_steps + 4

    def head_move(s, peer):
        return remote(
            grads_out.at[0, peer, s], grads.at[me, s], head_send.at[s, peer], head_recv.at[s, me], {"ctx": peer}
        )

    def head_wait(s, peer):
        remote(
            grads_out.at[0, peer, s], grads.at[peer, s], head_send.at[s, peer], head_recv.at[s, peer], {"ctx": peer}
        ).wait_recv()

    def second_norm(s, weights, values, given, own, sem):
        at = pl.ds(s * part, part)
        copies = [
            pltpu.make_async_copy(hidden.at[at, :], values, sem.at[0]),
            pltpu.make_async_copy(cotangent.at[at, :], given, sem.at[1]),
        ]
        for copy in copies:
            copy.start()
        for copy in copies:
            copy.wait()
        swaps[s].wait_recv()

        @pl.loop(0, part // 64)
        def _(i):
            here = pl.ds(pl.multiple_of(i * 64, 64), 64)
            h = values[here, :]
            grad = term[s, here, :].astype(F32) + swap_in[s, here, :].astype(F32)
            scale = rms_scale(h)
            ffn_gain[...] += jnp.sum(grad * h * scale, axis=0, keepdims=True)
            total = given[here, :].astype(F32) + rms_back(h, scale, gain_two[...], grad)
            values[here, :] = total
            own[here, :] = total.astype(BF16)

        saved = pltpu.make_async_copy(values, grad_hidden.at[at, :], sem.at[0])
        saved.start()
        total = dot(own[:, :shard_rows], weights[0])
        for j in range(1, shards):
            total += dot(own[:, j * shard_rows : (j + 1) * shard_rows], weights[j])
        for k in range(n):
            grads_out[0, k, s] = total[:, k * cols : (k + 1) * cols].astype(BF16)
        for d in range(1, n):
            head_move(s, lax.rem(me + d, n)).start()
        grads[me, s] = grads_out[0, me, s]
        left[2, :, s * part : (s + 1) * part] = own[...].T
        saved.wait()

    def second_norms(weights, values, given, own, sem):
        load = pltpu.make_async_copy(wo, weights, sem.at[3])
        load.start()
        load.wait()
        for s in range(seqs):
            second_norm(s, weights, values, given, own, sem)
            if s == 0:
                pump.steps(so_far, so_far + 1)

    pl.run_scoped(
        second_norms,
        pltpu.VMEM((shards, shard_rows, dims.inner_width), BF16),
        pltpu.VMEM((part, width), F32),
        pltpu.VMEM((part, width), BF16),
        pltpu.VMEM((part, width), BF16),
        pltpu.SemaphoreType.DMA((4,)),
    )
    ffn_swap = remote(ffn_term, ffn_other, ffn_sem.at[0], ffn_sem.at[1], other_half)
    ffn_swap.start()
    pump.steps(so_far + 1, so_far + 2)
    so_far += 2

    def back_move(j, s, peer):
        return remote(
            grads_out.at[j, peer, s], grads_in.at[j, me, s], back_send.at[j, s, peer], back_recv.at[j, s, me],
            {"ctx": peer},
        )

    def back_wait(j, s, peer):
        remote(
            grads_out.at[j, peer, s], grads_in.at[j, peer, s], back_send.at[j, s, peer], back_recv.at[j, s, peer],
            {"ctx": peer},
        ).wait_recv()

    def attention(pieces, lse, bias, sums, grad_k, grad_v, sem):
        @pl.loop(0, seqs * groups * n)
        def _(i):
            a, group, s = lax.rem(i, n), lax.rem(i // n, groups), i // (n * groups)
            at = pl.ds(pl.multiple_of(group * lanes, lanes), lanes)

            @pl.when((a == 0) & (group == 0))
            def _():
                here = [
                    pltpu.make_async_copy(pieces_from.at[:, :, s], pieces, sem.at[0]),
                    pltpu.make_async_copy(lse_from.at[s], lse, sem.at[1]),
                ]
                for copy in here:
                    copy.start()
                for copy in here:
                    copy.wait()
                for d in range(1, n):
                    head_wait(s, lax.rem(me + d, n))
                    head_move(s, lax.rem(me + d, n)).wait_send()

            @pl.when(a == 0)
            def _():
                for j in range(per):
                    bias_rows(table[pl.ds(group * per + j, 1), :], sums.at[j])
                bias[...] = sums[...].astype(BF16)
                sums[...] = jnp.zeros_like(sums)
                grad_k[...] = jnp.zeros_like(grad_k)
                grad_v[...] = jnp.zeros_like(grad_v)

            lane = lax.broadcasted_iota(jnp.int32, (part, lanes), 1)
            result = jnp.zeros((part, lanes), F32)
            for j in range(per):
                mask = (lane >= j * head_dim) & (lane < (j + 1) * head_dim)
                query = jnp.where(mask, pieces[0, a, :, at], 0)
                upstream = jnp.where(mask, grads[a, s, :, at], 0)
                log_total = jnp.sum(jnp.where(lane == group * per + j, lse[a], 0.0), axis=1, keepdims=True)
                windows = [pl.ds(pl.multiple_of((n + b - a) * part, part), part) for b in range(n)]
                probs, grad_probs = [], []
                for b in range(n):
                    scores = contract_cols(query, pieces[1, b, :, at]) + bias[j, :, windows[b]].astype(F32)
                    probs.append(jnp.exp(scores - log_total))
                    grad_probs.append(contract_cols(upstream, pieces[2, b, :, at]))
                delta = sum(jnp.sum(g * p, axis=1, keepdims=True) for g, p in zip(grad_probs, probs))
                summed = None
                for b in range(n):
                    grad_scores = (probs[b] * (grad_probs[b] - delta)).astype(BF16)
                    sums[j, :, windows[b]] += grad_scores.astype(F32)
                    product = dot(grad_scores, pieces[1, b, :, at])
                    summed = product if summed is None else summed + product
                    grad_k[b] += contract_rows(grad_scores, query)
                    grad_v[b] += contract_rows(probs[b].astype(BF16), upstream)
                result = jnp.where(mask, summed, result)
            grads_out[0, a, s, :, at] = result.astype(BF16)

            @pl.when(a == n - 1)
            def _():
                for b in range(n):
                    grads_out[1, b, s, :, at] = grad_k[b].astype(BF16)
                    grads_out[2, b, s, :, at] = grad_v[b].astype(BF16)
                for j in range(per):
                    table_out[pl.ds(group * per + j, 1), :] += diagonal_sums(sums.at[j])

            @pl.when((a == n - 1) & (group == groups - 1))
            def _():
                for j in range(3):
                    for d in range(1, n):
                        back_move(j, s, lax.rem(me + d, n)).start()
                    grads_in[j, me, s] = grads_out[j, me, s]

            @pl.when(a == n - 1)
            def _():
                pump.step(so_far + i // n)

    pl.run_scoped(
        attention,
        pltpu.VMEM((3, n, part, cols), BF16),
        pltpu.VMEM((n, part, lanes), F32),
        pltpu.VMEM((per, part, span), BF16),
        pltpu.VMEM((per, part, span), F32),
        pltpu.VMEM((n, part, lanes), F32),
        pltpu.VMEM((n, part, lanes), F32),
        pltpu.SemaphoreType.DMA((2,)),
    )
    so_far += seqs * groups
    lefts[2].start()
    lefts[2].wait()
    pump.steps(so_far, so_far + 1)
    so_far += 1
    assert so_far <= pump.early
    for s in range(seqs):
        for j in range(3):
            for d in range(1, n):
                back_wait(j, s, lax.rem(me + d, n))

    def first_norm_terms(weights, values, sem):
        def load(shard):
            return [
                pltpu.make_async_copy(w.at[shard], weights.at[shard % 2, j], sem.at[shard % 2, j])
                for j, w in enumerate((wq, wk, wv))
            ]

        for copy in load(0):
            copy.start()
        for j in range(3):
            for s in range(seqs):
                for k in range(n):
                    values[j, s * part : (s + 1) * part, k * cols : (k + 1) * cols] = grads_in[j, k, s]
        for shard in range(shards):
            if shard + 1 < shards:
                for copy in load(shard + 1):
                    copy.start()
            for copy in load(shard):
                copy.wait()
            total = contract_cols(values[0], weights[shard % 2, 0])
            total += contract_cols(values[1], weights[shard % 2, 1])
            total += contract_cols(values[2], weights[shard % 2, 2])
            for s in range(seqs):
                term_one[s, :, shard * shard_rows : (shard + 1) * shard_rows] = (
                    total[s * part : (s + 1) * part].astype(BF16)
                )

    pl.run_scoped(
        first_norm_terms,
        pltpu.VMEM((2, 3, shard_rows, dims.inner_width), BF16),
        pltpu.VMEM((3, seqs * part, dims.inner_width), BF16),
        pltpu.SemaphoreType.DMA((2, 3)),
    )
    ones = [
        remote(term_one.at[s], other_one.at[s], one_send.at[s], one_recv.at[s], other_half) for s in range(seqs)
    ]
    for swap in ones:
        swap.start()
    pump.steps(so_far, pump.last)
    for swap in swaps:
        swap.wait_send()
    for copy in ones + [ffn_swap]:
        copy.wait_recv()
        copy.wait_send()
    for s in range(seqs):
        for d in range(1, n):
            peer = lax.rem(me + d, n)
            for j in range(3):
                back_move(j, s, peer).wait_send()


def backward_call(dims):
    rows, width, n, part, seqs = dims.seqs * dims.part, dims.width, dims.n, dims.part, dims.seqs
    shards, shard_rows, inner, units, cols = dims.shards, dims.shard_rows, dims.inner_width, dims.units, dims.cols
    span, chips = 2 * n * part, dims.shards // 2
    vmem, anywhere = pl.BlockSpec(memory_space=pltpu.VMEM), pl.BlockSpec(memory_space=pl.ANY)
    shape, dma, regular = jax.ShapeDtypeStruct, pltpu.SemaphoreType.DMA, pltpu.SemaphoreType.REGULAR
    far = max(chips - 1, 1)
    block = (shard_rows, CHUNK)
    return pl.pallas_call(
        functools.partial(backward_kernel, dims),
        in_specs=[vmem] * 2 + [anywhere] * 16,
        out_specs=[anywhere] * 10 + [vmem, anywhere, vmem, vmem],
        out_shape=[shape((shard_rows, units), BF16)] * 3
        + [shape((shard_rows, inner), BF16)] * 4
        + [
            shape((rows, width), F32),
            shape((rows, width), BF16),
            shape((rows, width), BF16),
            shape((seqs, part, width), BF16),
            shape((seqs, part, width), BF16),
            shape((1, width), F32),
            shape((dims.own_heads, span), F32),
        ],
        scratch_shapes=[
            pltpu.VMEM((3, width, rows), BF16),
            pltpu.VMEM((SLOTS, rows, CHUNK), BF16),
            pltpu.VMEM((2, chips) + block, BF16),
            pltpu.VMEM((SLOTS, chips) + block, BF16),
            pltpu.VMEM((2, far) + block, BF16),
            pltpu.VMEM((SLOTS, far) + block, BF16),
            pltpu.VMEM((SLOTS,) + block, BF16),
            pltpu.VMEM((SLOTS,) + block, BF16),
            pltpu.VMEM((SLOTS,) + block, BF16),
            pltpu.VMEM((SLOTS,) + block, BF16),
            pltpu.VMEM((3, units // CHUNK, rows, CHUNK), BF16),
            pltpu.VMEM((seqs, part, width), BF16),
            pltpu.VMEM((seqs, part, width), BF16),
            pltpu.VMEM((n, seqs, part, cols), BF16),
            pltpu.VMEM((3, n, seqs, part, cols), BF16),
            pltpu.VMEM((3, n, seqs, part, cols), BF16),
            dma((SLOTS,)),
            dma((2,)),
            dma((SLOTS,)),
            dma((SLOTS, far)),
            dma((SLOTS, far)),
        ]
        + [dma((SLOTS,))] * 7
        + [dma((seqs,))] * 2
        + [dma((seqs, n))] * 2
        + [dma((3, seqs, n))] * 2
        + [dma((seqs,))] * 2
        + [dma((2,)), dma((4,))]
        + [regular, regular((far,)), regular, regular, regular],
        compiler_params=pltpu.CompilerParams(
            vmem_limit_bytes=62 * 2**20, collective_id=1, has_side_effects=True
        ),
        name="backward",
    )


def ring(n, d):
    return [(i, (i + d) % n) for i in range(n)]


class Links:
    def __init__(self, mesh):
        self.shard, self.ctx, self.tp = mesh.shape["shard"], mesh.shape["ctx"], mesh.shape["tp"]
        self.chips = self.shard // 2

    def to_core(self, value):
        return lax.ppermute(value, "shard", [(i, i ^ 1) for i in range(self.shard)])

    def to_chip(self, value, d):
        n = self.shard
        return lax.ppermute(value, "shard", [(i, (i + 2 * d) % n) for i in range(n)])

    def tp_sum(self, value):
        if self.tp != 2:
            return lax.psum(value, "tp").astype(F32)
        other = lax.ppermute(value, "tp", ring(2, 1))
        return value.astype(F32) + other.astype(F32)

    def ctx_sum(self, value):
        low = value.astype(BF16)
        if self.ctx != 4:
            return lax.psum(low, "ctx").astype(F32)
        inward = lax.ppermute(low, "ctx", [(0, 1), (3, 2)])
        half = (low.astype(F32) + inward.astype(F32)).astype(BF16)
        across = lax.ppermute(half, "ctx", [(1, 2), (2, 1)])
        whole = (half.astype(F32) + across.astype(F32)).astype(BF16)
        outward = lax.ppermute(whole, "ctx", [(1, 0), (2, 3)])
        me = lax.axis_index("ctx")
        middle = (me == 1) | (me == 2)
        return jnp.where(middle, whole, outward).astype(F32)

    def shard_sums(self, left, right):
        n, chips = self.shard, self.chips
        rows = left.shape[1] // n
        me = lax.axis_index("shard")
        chip, core = me // 2, me % 2

        def term(chip_at, core_at):
            at = (2 * chip_at + core_at) * rows
            return contract_rows(lax.dynamic_slice_in_dim(left, at, rows, 1), right)

        def chip_of(d):
            return lax.rem(chip + d, chips)

        order = list(range(1, chips)) + [0]
        got = {d: self.to_core(term(chip_of(d), 1 - core).astype(BF16)) for d in order}
        total = None
        arrived = []
        for d in order:
            pair = term(chip_of(d), core) + got[d].astype(F32)
            if d:
                arrived.append(self.to_chip(pair.astype(BF16), d))
            else:
                total = pair
        for value in arrived:
            total = total + value.astype(F32)
        return total

    def small_sum(self, value):
        for axis, n in (("shard", self.shard), ("ctx", self.ctx)):
            step = 1
            while step < n:
                value = value + lax.ppermute(value, axis, [(i, i ^ step) for i in range(n)])
                step *= 2
        return value


def per_device(
    links,
    tokens,
    cotangent,
    buckets,
    query_weight,
    key_weight,
    value_weight,
    output_weight,
    gate_weight,
    up_weight,
    down_weight,
    norm_gain,
    ffn_gain,
    bucket_bias_table,
):
    seqs, part, width = tokens.shape
    rows = seqs * part
    slots, heads = bucket_bias_table.shape
    inner_width = query_weight.shape[1]
    head_dim = inner_width // heads
    n = links.ctx
    cols = inner_width // n
    own_heads = heads // n
    me = lax.axis_index("ctx")
    gain_one = norm_gain.astype(F32)
    gain_two = ffn_gain.astype(F32)

    def gathered(weight):
        return lax.all_gather(weight, "shard", axis=0, tiled=True)

    def at_ctx(d):
        return lax.rem(me + d + n, n)

    corner = lax.dynamic_slice(buckets, (0, me * part), (part, part))
    later, earlier = corner[0, :], corner[:, 0]
    reach = n * part
    by_offset = jnp.concatenate(
        [
            jnp.broadcast_to(earlier[part - 1 :], (reach - part + 1,)),
            earlier[:0:-1],
            later,
            jnp.broadcast_to(later[part - 1 :], (reach - part,)),
        ]
    )
    indicator = by_offset[None, :] == jnp.arange(slots, dtype=jnp.int32)[:, None]
    own_table = lax.dynamic_slice(bucket_bias_table, (0, me * own_heads), (slots, own_heads))
    offset_bias = lax.dot_general(
        own_table, indicator.astype(BF16), (((0,), (0,)), ((), ())), preferred_element_type=F32
    )
    groups = cols // (2 * head_dim)
    offset_bias = offset_bias.reshape(groups, 2, 2 * reach)

    dims = Dims(links, seqs, part, width, inner_width, gate_weight.shape[1], heads)
    token_rows, upstream = tokens.reshape(rows, width), cotangent.reshape(rows, width)
    bias_table = offset_bias.reshape(own_heads, 2 * reach)
    hidden, normed_two, attended, lse, pieces, *lefts_and_weights = forward_call(dims)(
        token_rows, upstream, jnp.stack([gain_one, gain_two]), bias_table,
        query_weight, key_weight, value_weight, output_weight, gate_weight, up_weight, down_weight,
    )
    left_g, left_one, left_two, wq, wk, wv, wo, wi0, wi1, wff = lefts_and_weights
    *weight_grads, grad_hidden, ffn_term, ffn_other, term_one, other_one, grad_ffn_gain, offset_grad = backward_call(dims)(
        gain_two.reshape(1, width), bias_table,
        lse, pieces, left_g, left_two, left_one, normed_two, attended, hidden, upstream,
        wo, wq, wk, wv, wi0, wi1, wff,
    )
    inputs = token_rows.astype(F32)
    scale_one = rms_scale(inputs)
    grad_down_w, grad_gate_w, grad_up_w, grad_output_w, grad_query_w, grad_key_w, grad_value_w = (
        g.astype(F32) for g in weight_grads
    )
    result = (hidden + (ffn_term.astype(F32) + ffn_other.astype(F32))).astype(BF16).reshape(seqs, part, width)
    grad_ffn_gain = grad_ffn_gain[0]
    table_part = jnp.sum(jnp.where(indicator[:, None, :], offset_grad[None], 0.0), axis=-1)
    grad_table = lax.dynamic_update_slice(
        jnp.zeros((slots, heads), F32), table_part, (0, me * own_heads)
    )
    grad_normed = (term_one.astype(F32) + other_one.astype(F32)).reshape(rows, width)
    grad_norm_gain = jnp.sum(grad_normed * inputs * scale_one, axis=0)
    grad_inputs = grad_hidden + rms_back(inputs, scale_one, gain_one, grad_normed)
    small = links.small_sum(jnp.concatenate([grad_norm_gain, grad_ffn_gain, grad_table.reshape(-1)]))
    return (
        result,
        grad_inputs.reshape(seqs, part, width),
        grad_query_w,
        grad_key_w,
        grad_value_w,
        grad_output_w,
        grad_gate_w,
        grad_up_w,
        grad_down_w,
        small[:width],
        small[width : 2 * width],
        small[2 * width :].reshape(slots, heads),
    )


def solution(mesh):
    rows, weights = P("shard", "ctx", None), P("shard", "tp")
    return jax.shard_map(
        functools.partial(per_device, Links(mesh)),
        mesh=mesh,
        in_specs=(rows, rows, P("ctx", None)) + (weights,) * 7 + (P(), P(), P(None, "tp")),
        out_specs=(rows, rows) + (weights,) * 7 + (P(), P(), P(None, "tp")),
        check_vma=False,
    )
```

```python
import functools

import jax
import jax.numpy as jnp
from jax import lax
from jax.experimental import pallas as pl
from jax.experimental.pallas import tpu as pltpu
from jax.sharding import PartitionSpec as P

F32 = jnp.float32
BF16 = jnp.bfloat16
VMEM_LIMIT = 48 * 2**20


def contract_rows(left, right):
    return lax.dot_general(left, right, (((0,), (0,)), ((), ())), preferred_element_type=F32)


def contract_cols(left, right):
    return lax.dot_general(left, right, (((1,), (1,)), ((), ())), preferred_element_type=F32)


def dot(left, right):
    return jnp.dot(left, right, preferred_element_type=F32)


def rms_scale(values):
    return lax.rsqrt(jnp.mean(values * values, axis=-1, keepdims=True) + 1e-06)


def rms_back(values, scale, gain, upstream):
    weighted = upstream * gain
    inner_average = jnp.mean(values * weighted, axis=-1, keepdims=True)
    return scale * weighted - values * scale * scale * scale * inner_average


def bias_rows(table_row, out):
    span = out.shape[1]
    out[0:1, :] = table_row
    done = 1
    while done < out.shape[0]:
        out[done : 2 * done, :] = pltpu.roll(out[0:done, :], done, 1)
        done *= 2
    del span


def diagonal_sums(acc):
    rows, span = acc.shape
    total = acc[...]
    while rows > 1:
        rows //= 2
        total = total[:rows] + pltpu.roll(total[rows:], span - rows, 1)
    return total


MESH = pl.DeviceIdType.MESH


class Spot:
    def __init__(self, shards, ctx, tp):
        self.shards, self.chips, self.n, self.tps = shards, shards // 2, ctx, tp
        self.shard, self.me, self.half = (lax.axis_index(a) for a in ("shard", "ctx", "tp"))
        self.chip, self.core = self.shard // 2, lax.rem(self.shard, 2)
        self.mate = 2 * self.chip + 1 - self.core

    def away(self, d):
        return lax.rem(self.shard + 2 * d, self.shards)

    def barrier(self):
        peers = [{"shard": self.mate}] + [{"shard": self.away(d)} for d in range(1, self.chips)]
        peers += [{"ctx": lax.rem(self.me + d, self.n)} for d in range(1, self.n)]
        peers += [{"tp": 1 - self.half}]
        semaphore = pltpu.get_barrier_semaphore()
        for peer in peers:
            pl.semaphore_signal(semaphore, inc=1, device_id=peer, device_id_type=MESH)
        pl.semaphore_wait(semaphore, len(peers))


def remote(src, dst, send, recv, peer):
    return pltpu.make_async_remote_copy(
        src_ref=src, dst_ref=dst, send_sem=send, recv_sem=recv, device_id=peer, device_id_type=MESH
    )


class Keep:
    def __init__(self, jobs, room, sem):
        self.halves = []
        for i, (own, full) in enumerate(jobs):
            self.halves.append(pltpu.make_async_copy(own, room, sem.at[0]))
            self.halves.append(pltpu.make_async_copy(room, full, sem.at[1]))
        self.at = 0
        self.halves[0].start()

    def step(self):
        if self.at < len(self.halves):
            self.halves[self.at].wait()
            self.at += 1
            if self.at < len(self.halves):
                self.halves[self.at].start()

    def start(self):
        pass

    def wait(self):
        while self.at < len(self.halves):
            self.step()


class Gather:
    def __init__(self, spot, own, full, sems, keep=None):
        self.spot, self.own, self.full = spot, own, full
        self.local, self.send, self.recv, self.on_send, self.on_recv = sems
        spot_shard = spot.shard
        self.keep = keep or pltpu.make_async_copy(own, full.at[spot_shard], self.local)
        self.far = [
            remote(own, full.at[spot_shard], self.send.at[d], self.recv.at[d], {"shard": spot.away(d)})
            for d in range(1, spot.chips)
        ]
        mate = {"shard": spot.mate}
        self.near = [remote(own, full.at[spot_shard], self.on_send.at[0], self.on_recv.at[0], mate)]
        for d in range(1, spot.chips):
            at = full.at[lax.rem(spot.shard - 2 * d + spot.shards, spot.shards)]
            self.near.append(remote(at, at, self.on_send.at[d], self.on_recv.at[d], mate))

    def start_far(self):
        for copy in self.far:
            copy.start()

    def start_near(self):
        self.keep.start()
        self.near[0].start()

    def pass_on(self):
        for d, copy in enumerate(self.far, 1):
            copy.wait_recv()
            self.near[d].start()

    def wait_own(self):
        self.keep.wait()
        self.near[0].wait_recv()

    def wait_near(self):
        for copy in self.near[1:]:
            copy.wait_recv()

    def wait_sent(self):
        for copy in self.far + self.near:
            copy.wait_send()


class Spread:
    def __init__(self, spot, own, full, keep, sems, direct=0):
        self.spot, self.own, self.full, self.keep, self.direct = spot, own, full, keep, direct
        (
            self.far_send, self.far_recv, self.right_send, self.right_recv, self.left_send, self.left_recv,
            self.mate_send, self.mate_recv,
        ) = sems
        self.part = (full.shape[1] - direct) // spot.n
        n, me = spot.n, spot.me
        self.near = remote(
            own, full.at[spot.shard], self.mate_send.at[0, 0], self.mate_recv.at[0, 0], {"shard": spot.mate}
        )
        mine = self.at(me)
        self.far = [
            remote(
                own.at[mine], full.at[spot.shard, mine], self.far_send.at[d, 0], self.far_recv.at[d, 0],
                {"shard": spot.away(d)},
            )
            for d in range(1, spot.chips)
        ]
        whole = pl.ds(0, direct)
        self.far_direct = [
            remote(
                own.at[whole], full.at[spot.shard, whole], self.far_send.at[d, 1], self.far_recv.at[d, 1],
                {"shard": spot.away(d)},
            )
            for d in range(1, spot.chips)
            if direct
        ]
        self.can_right, self.can_left = me + 1 < n, me > 0

    def at(self, z):
        return pl.ds(pl.multiple_of(self.direct + z * self.part, 16), self.part)

    def source(self, d):
        return lax.rem(self.spot.shard - 2 * d + self.spot.shards, self.spot.shards)

    def piece(self, d, z):
        return self.full.at[self.source(d), self.at(z)]

    def tell_direct(self, d):
        at = self.full.at[self.source(d), pl.ds(0, self.direct)]
        n = self.spot.n
        return remote(at, at, self.mate_send.at[d, n], self.mate_recv.at[d, n], {"shard": self.spot.mate})

    def start_direct(self):
        for copy in self.far_direct:
            copy.start()

    def pass_on(self):
        for d, copy in enumerate(self.far_direct, 1):
            copy.wait_recv()
            self.tell_direct(d).start()

    def tell(self, d, z):
        at = self.piece(d, z)
        return remote(at, at, self.mate_send.at[d, z], self.mate_recv.at[d, z], {"shard": self.spot.mate})

    def right(self, d, h, z):
        at, to = self.piece(d, z), {"ctx": lax.rem(self.spot.me + 1, self.spot.n)}
        return remote(at, at, self.right_send.at[d, h], self.right_recv.at[d, h], to)

    def left(self, d, h, z):
        at, to = self.piece(d, z), {"ctx": lax.rem(self.spot.me - 1 + self.spot.n, self.spot.n)}
        return remote(at, at, self.left_send.at[d, h], self.left_recv.at[d, h], to)

    def pairs(self):
        return range(1, self.spot.chips)

    def start(self):
        for copy in self.far:
            copy.start()

    def start_near(self):
        self.near.start()

    def send_on(self, d, h, z, right, left):
        self.tell(d, z).start()
        if right:
            @pl.when(self.can_right)
            def _():
                self.right(d, h, z).start()

        if left:
            @pl.when(self.can_left)
            def _():
                self.left(d, h, z).start()

    def arrived(self):
        for d in self.pairs():
            self.far[d - 1].wait_recv()
            self.send_on(d, 1, self.spot.me, True, True)

    def hop(self, h):
        me, n = self.spot.me, self.spot.n
        for d in self.pairs():
            @pl.when(me - h >= 0)
            def _():
                self.right(d, h, me - h).wait_recv()
                self.send_on(d, h + 1, me - h, h + 1 < n, False)

            @pl.when(me + h < n)
            def _():
                self.left(d, h, me + h).wait_recv()
                self.send_on(d, h + 1, me + h, False, h + 1 < n)

    def wait(self):
        me, n = self.spot.me, self.spot.n
        self.keep.wait()
        self.near.wait_recv()
        self.near.wait_send()
        for d, copy in enumerate(self.far_direct, 1):
            copy.wait_send()
            self.tell_direct(d).wait_recv()
            self.tell_direct(d).wait_send()
        for d in self.pairs():
            self.far[d - 1].wait_send()
            for z in range(n):
                self.tell(d, z).wait_recv()
                self.tell(d, z).wait_send()
            for h in range(1, n):
                @pl.when((me - h + 1 >= 0) & self.can_right)
                def _():
                    self.right(d, h, me - h + 1).wait_send()

                @pl.when((me + h - 1 < n) & self.can_left)
                def _():
                    self.left(d, h, me + h - 1).wait_send()


def offset_buckets(dims, me, some_rows, out):
    part, reach = dims.part, dims.n * dims.part
    at = pl.ds(pl.multiple_of(me * part, part), part)
    later = some_rows[0, 0:1, at].astype(F32)
    earlier = some_rows[1, 7:8, at].astype(F32)
    lane = lax.broadcasted_iota(jnp.int32, (1, part), 1)
    out[:, : reach - part] = jnp.broadcast_to(earlier[:, :1], (1, reach - part))
    out[:, reach - part : reach] = jnp.where(lane == 0, earlier[:, :1], pltpu.roll(earlier, 1, 1))
    out[:, reach : reach + part] = later
    out[:, reach + part :] = jnp.broadcast_to(later[:, part - 1 :], (1, reach - part))


def forward_kernel(
    dims, tokens, cotangent, gain_one, gain_two, table, buckets, wq, wk, wv, wo, wi0, wi1, wff,
    hidden, normed_two, attended, lse, by_offset, bias_table, pieces_out, left_g, left_one, left_two,
    full_q, full_k, full_v, full_o, full_0, full_1, full_2,
    normed, flipped, weights, acc, bias, staged, pieces, mixed, heads_in, rolled, branch_in,
    local_sem, far_send, far_recv, near_send, near_recv, head_send, head_recv, back_send, back_recv,
    room, some_rows, keep_sem, row_sem,
    swap_send, swap_recv, out_sem, *spread_sems,
):
    spot = Spot(*dims.mesh)
    n, seqs, part, cols, head_dim = dims.n, dims.seqs, dims.part, dims.cols, dims.head_dim
    me, shards = spot.me, spot.shards
    shard_rows = weights.shape[2]
    rows = seqs * part
    lanes = 2 * head_dim
    per = 2
    spot.barrier()

    def gather(i, own, full, keep=None):
        sems = [local_sem.at[i], far_send.at[i], far_recv.at[i], near_send.at[i], near_recv.at[i]]
        return Gather(spot, own, full, sems, keep)

    loads = [None] + [gather(i, w, weights.at[i]) for i, w in ((1, wk), (2, wv), (3, wo))]
    keep = Keep(
        [(w, full.at[spot.shard]) for w, full in ((wi0, full_0), (wi1, full_1), (wff, full_2))], room, keep_sem
    )
    loads.append(gather(4, wi0, full_0, keep))
    spreads = [
        Spread(spot, own, full, keep, [sem.at[i] for sem in spread_sems], direct)
        for i, (own, full, direct) in enumerate(((wi1, full_1, shard_rows // 2), (wff, full_2, 0)))
    ]
    keep_first = pltpu.make_async_copy(wq, weights.at[0, spot.shard], local_sem.at[0])
    spreads.append(Spread(spot, wq, weights.at[0], keep_first, [sem.at[2] for sem in spread_sems]))
    flips = []

    def flip(value, out):
        if flips:
            flips[-1].wait()
        flipped[...] = value.T
        flips.append(pltpu.make_async_copy(flipped, out, out_sem.at[5]))
        flips[-1].start()

    first = spreads[2]
    first.start()
    for load in loads[1:3]:
        load.start_far()
    first.keep.start()
    first.start_near()
    for load in loads[1:3]:
        load.start_near()

    row_copies = [
        pltpu.make_async_copy(buckets.at[pl.ds(at, 8)], some_rows.at[i], row_sem.at[i])
        for i, at in enumerate((0, part - 8))
    ]
    for copy in row_copies:
        copy.start()

    @pl.loop(0, rows // 64)
    def _(i):
        at = pl.ds(pl.multiple_of(i * 64, 64), 64)
        values = tokens[at, :].astype(F32)
        normed[at, :] = (values * rms_scale(values) * gain_one[...].astype(F32)).astype(BF16)

    for copy in row_copies:
        copy.wait()
    offset_buckets(dims, me, some_rows, by_offset)
    slots = table.shape[0]
    hot = by_offset[...] == lax.broadcasted_iota(jnp.int32, (slots, by_offset.shape[1]), 0).astype(F32)
    lane = lax.broadcasted_iota(jnp.int32, table.shape, 1)
    for head in range(dims.own_heads):
        own = lane == me * dims.own_heads + head
        column = jnp.sum(jnp.where(own, table[...].astype(F32), 0.0), axis=1, keepdims=True)
        bias_table[head : head + 1, :] = jnp.sum(jnp.where(hot, column, 0.0), axis=0, keepdims=True)
        bias_rows(bias_table[head : head + 1, :], rolled)
        bias[head] = rolled[...].astype(BF16)

    def term(i, shard):
        at = pl.ds(pl.multiple_of(shard * shard_rows, 128), shard_rows)
        return dot(normed[:, at], weights[i, shard])

    moves = []
    first.arrived()
    for h in range(1, n):
        first.hop(h)
    for i, load in enumerate(loads[:3]):
        if i == 0:
            first.wait()
        else:
            load.wait_own()
        acc[...] = term(i, spot.shard)
        acc[...] += term(i, spot.mate)
        keep.step()
        if i:
            load.pass_on()
        if i == 2:
            for spread in spreads[:2]:
                spread.start()
            for later in loads[3:] + spreads[:2]:
                later.start_near()
        keep.step()
        for d in range(1, spot.chips):
            acc[...] += term(i, lax.rem(spot.shard - 2 * d + shards, shards))
        if i:
            load.wait_near()
        for d in range(1, spot.chips):
            acc[...] += term(i, lax.rem(spot.mate - 2 * d + shards, shards))
        for k in range(n):
            for s in range(seqs):
                staged[i, k, s] = acc[s * part : (s + 1) * part, k * cols : (k + 1) * cols].astype(BF16)
        for d in range(1, n):
            peer = lax.rem(me + d, n)
            move = remote(
                staged.at[i, peer], pieces.at[i, me], head_send.at[i, d], head_recv.at[i, d], {"ctx": peer}
            )
            move.start()
            moves.append(move)
        pieces[i, me] = staged[i, me]
    outs = [
        pltpu.make_async_copy(weights.at[i], full, out_sem.at[i])
        for i, full in enumerate((full_q, full_k, full_v, full_o))
    ]
    for copy in outs[:3]:
        copy.start()
    flip(normed[...], left_one)
    spreads[0].arrived()
    spreads[1].arrived()
    loads[3].start_far()
    flip(cotangent[...], left_g)
    for move in moves:
        move.wait_recv()
    loads[3].wait_own()
    outs.append(pltpu.make_async_copy(pieces, pieces_out, out_sem.at[4]))
    outs[4].start()

    def back(s, at, to):
        return remote(mixed.at[s, at], heads_in.at[me, s], back_send.at[s, at], back_recv.at[s, me], {"ctx": to})

    def attend(s, a):
        step = s * n + a
        lane = lax.broadcasted_iota(jnp.int32, (part, lanes), 1)
        log_total = jnp.zeros((part, lanes), F32)
        for group in range(cols // lanes):
            span = slice(group * lanes, (group + 1) * lanes)
            result = jnp.zeros((part, lanes), F32)
            for j in range(per):
                head = group * per + j
                mask = (lane >= j * head_dim) & (lane < (j + 1) * head_dim)
                query = jnp.where(mask, pieces[0, a, s, :, span], 0)
                scores = jnp.concatenate(
                    [
                        contract_cols(query, pieces[1, b, s, :, span])
                        + bias[head, :, pl.ds(pl.multiple_of((n + b - a) * part, part), part)].astype(F32)
                        for b in range(n)
                    ],
                    axis=1,
                )
                peak = jnp.max(scores, axis=1, keepdims=True)
                expo = jnp.exp(scores - peak)
                total = jnp.sum(expo, axis=1, keepdims=True)
                probs = (expo * (1.0 / total)).astype(BF16)
                summed = sum(
                    dot(probs[:, b * part : (b + 1) * part], pieces[2, b, s, :, span]) for b in range(n)
                )
                result = jnp.where(mask, summed, result)
                log_total = jnp.where(lane == head, peak + jnp.log(total), log_total)
            mixed[s, a, :, span] = result.astype(BF16)
        lse[s, a] = log_total

        @pl.when(a != me)
        def _():
            back(s, a, a).start()

        @pl.when(a == me)
        def _():
            heads_in[a, s] = mixed[s, a]

        @pl.when(step == 1)
        def _():
            spreads[0].hop(1)

        @pl.when(step == 3)
        def _():
            loads[3].pass_on()
            loads[4].start_far()
            spreads[0].start_direct()

        @pl.when(step == 4)
        def _():
            spreads[1].hop(1)

    swaps = []

    def project(s):
        at = pl.ds(s * part, part)
        for d in range(1, n):
            peer = lax.rem(me + d, n)
            remote(
                mixed.at[s, 0], heads_in.at[peer, s], back_send.at[s, peer], back_recv.at[s, peer], {"ctx": peer}
            ).wait_recv()
        for k in range(n):
            attended[at, k * cols : (k + 1) * cols] = heads_in[k, s]
        for j in range(shards):
            normed[at, j * shard_rows : (j + 1) * shard_rows] = contract_cols(
                attended[at, :], weights[3, j]
            ).astype(BF16)
        swap = remote(normed.at[at], branch_in.at[s], swap_send.at[s], swap_recv.at[s], {"tp": 1 - spot.half})
        swap.start()
        swaps.append(swap)

    for s in range(seqs):
        pl.loop(0, n)(functools.partial(attend, s))
        if s == 0:
            loads[3].wait_near()
            outs[3].start()
            if n > 2:
                spreads[0].hop(2)
        project(s)
    if n > 2:
        spreads[1].hop(2)
    for h in range(3, n):
        for spread in spreads[:2]:
            spread.hop(h)
    loads[4].wait_own()
    loads[4].pass_on()
    spreads[0].pass_on()
    for s in range(seqs):
        swaps[s].wait_recv()

        @pl.loop(0, part // 64)
        def _(i):
            here = pl.ds(pl.multiple_of(i * 64, 64), 64)
            at = pl.ds(pl.multiple_of(s * part + i * 64, 64), 64)
            values = tokens[at, :].astype(F32) + (
                normed[at, :].astype(F32) + branch_in[s, here, :].astype(F32)
            )
            hidden[at, :] = values
            normed_two[at, :] = (values * rms_scale(values) * gain_two[...].astype(F32)).astype(BF16)

    flip(normed_two[...], left_two)
    loads[4].wait_near()
    for spread in spreads[:2]:
        spread.wait()
    for load in loads[1:]:
        load.wait_sent()
    for move in moves + swaps:
        move.wait_send()
    for s in range(seqs):
        for d in range(1, n):
            peer = lax.rem(me + d, n)
            back(s, peer, peer).wait_send()
    for copy in outs + flips[-1:]:
        copy.wait()


class Dims:
    def __init__(self, mesh, seqs, part, width, inner_width, units, heads, slots):
        self.mesh = shards, ctx, tp = tuple(mesh.shape[a] for a in ("shard", "ctx", "tp"))
        self.slots = slots
        self.n, self.seqs, self.part, self.width = ctx, seqs, part, width
        self.inner_width, self.units = inner_width, units
        self.head_dim = inner_width // heads
        self.cols, self.own_heads = inner_width // ctx, heads // ctx
        self.shards, self.shard_rows = shards, width // shards


def forward_call(dims):
    rows, width, n, part, seqs = dims.seqs * dims.part, dims.width, dims.n, dims.part, dims.seqs
    shards, shard_rows, inner, units = dims.shards, dims.shard_rows, dims.inner_width, dims.units
    lanes, span = 2 * dims.head_dim, 2 * n * part
    vmem, anywhere = pl.BlockSpec(memory_space=pltpu.VMEM), pl.BlockSpec(memory_space=pl.ANY)
    shape = jax.ShapeDtypeStruct
    dma = pltpu.SemaphoreType.DMA
    chips = shards // 2
    block = (seqs, part, dims.cols)
    return pl.pallas_call(
        functools.partial(forward_kernel, dims),
        in_specs=[vmem] * 5 + [anywhere] * 8,
        out_specs=[vmem] * 6 + [anywhere] * 11,
        out_shape=[
            shape((rows, width), F32),
            shape((rows, width), BF16),
            shape((rows, inner), BF16),
            shape((seqs, n, part, lanes), F32),
            shape((1, span), F32),
            shape((dims.own_heads, span), F32),
            shape((3, n) + block, BF16),
        ]
        + [shape((width, rows), BF16)] * 3
        + [shape((shards, shard_rows, inner), BF16)] * 4
        + [shape((shards, shard_rows, units), BF16)] * 3,
        scratch_shapes=[
            pltpu.VMEM((rows, width), BF16),
            pltpu.VMEM((width, rows), BF16),
            pltpu.VMEM((4, shards, shard_rows, inner), BF16),
            pltpu.VMEM((rows, inner), F32),
            pltpu.VMEM((dims.own_heads, part, span), BF16),
            pltpu.VMEM((3, n) + block, BF16),
            pltpu.VMEM((3, n) + block, BF16),
            pltpu.VMEM((seqs, n, part, dims.cols), BF16),
            pltpu.VMEM((n,) + block, BF16),
            pltpu.VMEM((part, span), F32),
            pltpu.VMEM((seqs, part, width), BF16),
            dma((7,)),
            dma((7, chips)),
            dma((7, chips)),
            dma((7, chips)),
            dma((7, chips)),
            dma((3, n)),
            dma((3, n)),
            dma((seqs, n)),
            dma((seqs, n)),
            pltpu.VMEM((shard_rows, units), BF16),
            pltpu.VMEM((2, 8, n * part), jnp.int32),
            dma((2,)),
            dma((2,)),
            dma((seqs,)),
            dma((seqs,)),
            dma((6,)),
        ]
        + [dma((3, chips, 2))] * 2
        + [dma((3, chips, n))] * 4
        + [dma((3, chips, n + 1))] * 2,
        compiler_params=pltpu.CompilerParams(
            vmem_limit_bytes=60 * 2**20, collective_id=0, has_side_effects=True
        ),
        name="forward",
    )


CHUNK = 512
SLOTS = 4
LAYER_STEPS = 4
INPUT_STEPS = 3


class Pump:
    def __init__(self, dims, spot, left, right, sources, from_heads, outs, buffers, sems, credits):
        self.dims, self.spot, self.left, self.right = dims, spot, left, right
        self.fed, self.attended = sources
        self.from_heads, self.outs = from_heads, outs
        self.core_out, self.core_in, self.far_out, self.far_in, self.line, self.line_in, self.across_in, self.done = buffers
        (
            self.right_sem, self.core_send, self.core_recv, self.far_send, self.far_recv, self.in_send, self.in_recv,
            self.across_send, self.across_recv, self.out_send, self.out_recv, self.fin_sem,
        ) = sems
        self.core_credit, self.far_credit, self.in_credit, self.across_credit, self.out_credit = credits
        units, heads = dims.units // CHUNK, dims.inner_width // CHUNK
        self.units, self.heads = units, heads
        self.early = 3 * units + heads
        self.total = 3 * units + 4 * heads
        self.bases = [(i * units, units) for i in range(3)]
        self.bases += [(3 * units + i * heads, heads) for i in range(4)]
        me, n = spot.me, dims.n
        middle = n // 2
        self.is_middle = (me == middle - 1) | (me == middle)
        self.is_end = (me == 0) | (me == n - 1)
        self.has_outer, self.has_inner = jnp.logical_not(self.is_end), jnp.logical_not(self.is_middle)
        low_side = me < middle
        self.facing = jnp.where(low_side, middle, middle - 1)
        toward, away = jnp.where(low_side, me + 1, me - 1), jnp.where(low_side, me - 1, me + 1)
        self.inner = jnp.where(self.is_middle, self.facing, toward)
        self.outer = jnp.where(self.is_end, self.inner, away)
        self.last = self.total + 10

    def core(self, c, k):
        return remote(
            self.core_out.at[lax.rem(c, 2)], self.core_in.at[k], self.core_send.at[lax.rem(c, 2)],
            self.core_recv.at[k], {"shard": self.spot.mate},
        )

    def far(self, k, d):
        return remote(
            self.far_out.at[lax.rem(k, 2), d - 1], self.far_in.at[k, d - 1], self.far_send.at[k, d - 1],
            self.far_recv.at[k, d - 1], {"shard": self.spot.away(d)},
        )

    def inward(self, k):
        half = k
        return remote(
            self.line.at[k], self.line_in.at[half], self.in_send.at[k], self.in_recv.at[half], {"ctx": self.inner}
        )

    def across(self, k):
        return remote(
            self.line.at[k], self.across_in.at[k], self.across_send.at[k],
            self.across_recv.at[k], {"ctx": self.facing},
        )

    def outward(self, k):
        return remote(
            self.done.at[k], self.done.at[k], self.out_send.at[k], self.out_recv.at[k], {"ctx": self.outer}
        )

    def spend(self, c, credit, slots=SLOTS):
        @pl.when(c >= slots)
        def _():
            pl.semaphore_wait(credit, 1)

    def give(self, c, credit, peer, slots=SLOTS):
        @pl.when(c + slots < self.total)
        def _():
            pl.semaphore_signal(credit, inc=1, device_id=peer, device_id_type=MESH)

    def term(self, c, shard, k):
        one = lambda b: jnp.where(c >= b, 1, 0)
        which = one(self.units) + one(3 * self.units) - 2 * one(self.early)
        rows = self.dims.shard_rows
        return dot(self.left[which, pl.ds(pl.multiple_of(shard * rows, rows), rows), :], self.right[k])

    def fetch(self, c):
        k, fed = lax.rem(c, SLOTS), 3 * self.units

        @pl.when(c < fed)
        def _():
            source = self.fed.at[c // self.units, lax.rem(c, self.units)]
            pltpu.make_async_copy(source, self.right.at[k], self.right_sem.at[k]).start()

        @pl.when((c >= fed) & (c < self.early))
        def _():
            at = pl.ds(pl.multiple_of((c - fed) * CHUNK, CHUNK), CHUNK)
            pltpu.make_async_copy(self.attended.at[:, at], self.right.at[k], self.right_sem.at[k]).start()

        @pl.when((c >= self.early) & (c < self.total))
        def _():
            dims = self.dims
            which, piece = (c - self.early) // self.heads, lax.rem(c - self.early, self.heads)
            per = CHUNK // dims.cols
            for i in range(per):
                for s in range(dims.seqs):
                    self.right[k, s * dims.part : (s + 1) * dims.part, i * dims.cols : (i + 1) * dims.cols] = (
                        self.from_heads[which, piece * per + i, s]
                    )

    def save(self, c, k):
        for (base, count), out in zip(self.bases, self.outs):
            @pl.when((c >= base) & (c < base + count))
            def _():
                at = pl.ds(pl.multiple_of((c - base) * CHUNK, CHUNK), CHUNK)
                pltpu.make_async_copy(self.done.at[k], out.at[:, at], self.fin_sem.at[k]).start()

    def settle(self, c, k):
        pltpu.make_async_copy(self.done.at[k], self.outs[0].at[:, pl.ds(0, CHUNK)], self.fin_sem.at[k]).wait()

        @pl.when(self.has_outer)
        def _():
            self.outward(k).wait_send()

        @pl.when(self.has_inner)
        def _():
            self.give(c, self.out_credit, {"ctx": self.inner})

    def deliver(self, c, k):
        @pl.when(self.has_inner)
        def _():
            self.outward(k).wait_recv()
            self.save(c, k)

            @pl.when(self.has_outer)
            def _():
                self.spend(c, self.out_credit)
                self.outward(k).start()

    def finish(self, c, k):
        @pl.when(self.is_middle)
        def _():
            self.across(k).wait_recv()
            self.across(k).wait_send()
            self.done[k] = (self.line[k].astype(F32) + self.across_in[k].astype(F32)).astype(BF16)
            self.give(c, self.across_credit, {"ctx": self.facing})
            self.save(c, k)

            @pl.when(self.has_outer)
            def _():
                self.spend(c, self.out_credit)
                self.outward(k).start()

        @pl.when(self.has_inner)
        def _():
            self.inward(k).wait_send()

    def collect(self, c, k):
        @pl.when(self.has_outer)
        def _():
            self.inward(k).wait_recv()
            self.line[k] = (self.line[k].astype(F32) + self.line_in[k].astype(F32)).astype(BF16)
            self.give(c, self.in_credit, {"ctx": self.outer})

        @pl.when(self.is_middle)
        def _():
            self.spend(c, self.across_credit)
            self.across(k).start()

        @pl.when(self.has_outer & self.has_inner)
        def _():
            self.spend(c, self.in_credit)
            self.inward(k).start()

    def own(self, c, k):
        total = self.term(c, self.spot.shard, k) + self.core_in[k, self.spot.chips - 1].astype(F32)
        for d in range(1, self.spot.chips):
            self.far(k, d).wait_send()
            self.far(k, d).wait_recv()
            total = total + self.far_in[k, d - 1].astype(F32)
        self.line[k] = total.astype(BF16)
        self.give(c, self.core_credit, {"shard": self.spot.mate})
        for d in range(1, self.spot.chips):
            sender = lax.rem(self.spot.shard - 2 * d + self.spot.shards, self.spot.shards)
            self.give(c, self.far_credit.at[d - 1], {"shard": sender})

        @pl.when(self.is_end & self.has_inner)
        def _():
            self.spend(c, self.in_credit)
            self.inward(k).start()

    def to_chips(self, c, k):
        self.core(c, k).wait_recv()
        self.core(c, k).wait_send()
        for d in range(1, self.spot.chips):
            pair = self.term(c, self.spot.away(d), k) + self.core_in[k, d - 1].astype(F32)
            self.far_out[lax.rem(k, 2), d - 1] = pair.astype(BF16)
            self.spend(c, self.far_credit.at[d - 1])
            self.far(k, d).start()

    def to_core(self, c, k):
        @pl.when(c < self.early)
        def _():
            pltpu.make_async_copy(self.fed.at[0, 0], self.right.at[k], self.right_sem.at[k]).wait()

        chips, half = self.spot.chips, lax.rem(c, 2)
        for d in range(1, chips + 1):
            shard = 2 * lax.rem(self.spot.chip + d, chips) + 1 - self.spot.core
            self.core_out[half, d - 1] = self.term(c, shard, k).astype(BF16)
        self.spend(c, self.core_credit)
        self.core(c, k).start()

    def step(self, t):
        def at(lag, stage):
            c = t - lag

            @pl.when((c >= 0) & (c < self.total))
            def _():
                stage(c, lax.rem(c, SLOTS))

        @pl.when(t < self.total)
        def _():
            self.fetch(t)

        at(10, self.settle)
        at(9, self.deliver)
        at(7, self.finish)
        at(5, self.collect)
        at(3, self.own)

        at(1, self.to_chips)
        at(0, self.to_core)

    def steps(self, first, last):
        @pl.loop(first, last)
        def _(t):
            self.step(t)


UNITS = 256


def geglu_both(gate, up, upstream):
    root, cube = 0.7978845608028654, 0.044715
    square = gate * gate
    bent = jnp.tanh(root * gate * (1.0 + cube * square))
    half = 0.5 * (1.0 + bent)
    gelu = gate * half
    slope = half + 0.5 * gate * (1.0 - bent * bent) * (root * (1.0 + 3.0 * cube * square))
    return gelu * up, upstream * up * slope, upstream * gelu


def backward_kernel(
    dims, gain_one, gain_two, table, by_offset,
    tokens, lse_from, pieces_from, left_g, left_two, left_one, normed_two, attended, hidden, cotangent,
    wo, wq, wk, wv, wi0, wi1, wff,
    down_out, gate_out, up_out, o_out, q_out, k_out, v_out,
    layer_out, input_grad, grad_hidden, ffn_term, ffn_other, small_out,
    other_one, norm_gain, ffn_gain, table_out, small, small_in,
    left, right, core_out, core_in, far_out, far_in, line, line_in, across_in, done,
    fed, term, swap_in, grads, grads_out, grads_in,
    right_sem, core_send, core_recv, far_send, far_recv, in_send, in_recv, across_send, across_recv,
    out_send, out_recv, fin_sem, swap_send, swap_recv, head_send, head_recv, back_send, back_recv,
    one_send, one_recv, ffn_sem, local_sem, small_send, small_recv,
    core_credit, far_credit, in_credit, across_credit, out_credit,
):
    spot = Spot(*dims.mesh)
    n, seqs, part, cols, head_dim, width = dims.n, dims.seqs, dims.part, dims.cols, dims.head_dim, dims.width
    me, shards, shard_rows, units = spot.me, spot.shards, dims.shard_rows, dims.units
    rows = seqs * part
    lanes, per = 2 * head_dim, 2
    groups = cols // lanes
    span = table.shape[1]
    other_half = {"tp": 1 - spot.half}
    pump = Pump(
        dims, spot, left, right, (fed, attended), grads_in,
        (down_out, gate_out, up_out, o_out, q_out, k_out, v_out),
        (core_out, core_in, far_out, far_in, line, line_in, across_in, done),
        (
            right_sem, core_send, core_recv, far_send, far_recv, in_send, in_recv, across_send, across_recv,
            out_send, out_recv, fin_sem,
        ),
        (core_credit, far_credit, in_credit, across_credit, out_credit),
    )
    lefts = [
        pltpu.make_async_copy(source, left.at[i], local_sem.at[i])
        for i, source in ((0, left_g), (1, left_two), (0, left_one))
    ]
    spot.barrier()
    ffn_gain[...] = jnp.zeros_like(ffn_gain)
    norm_gain[...] = jnp.zeros_like(norm_gain)
    table_out[...] = jnp.zeros_like(table_out)

    def feed(weights, values, given, sem, value_sem):
        inputs = [
            pltpu.make_async_copy(normed_two, values, value_sem.at[0]),
            pltpu.make_async_copy(cotangent, given, value_sem.at[1]),
        ]

        def load(u):
            slot = lax.rem(u, 2)
            at = pl.ds(pl.multiple_of(u * UNITS, UNITS), UNITS)
            return [
                pltpu.make_async_copy(w.at[:, :, at], weights.at[slot, j], sem.at[slot, j])
                for j, w in enumerate((wi0, wi1, wff))
            ]

        for copy in load(0) + inputs + lefts[:2]:
            copy.start()
        for copy in inputs:
            copy.wait()
        each = CHUNK // UNITS

        @pl.loop(0, units // CHUNK)
        def _(c):
            for i in range(each):
                u = c * each + i

                @pl.when(u + 1 < units // UNITS)
                def _():
                    for copy in load(u + 1):
                        copy.start()

                for copy in load(u):
                    copy.wait()
                slot = lax.rem(u, 2)
                gate = dot(values[...], weights[slot, 0].reshape(width, UNITS))
                up = dot(values[...], weights[slot, 1].reshape(width, UNITS))
                upstream = dot(given[...], weights[slot, 2].reshape(width, UNITS))
                for j, made in enumerate(geglu_both(gate, up, upstream)):
                    fed[j, c, :, i * UNITS : (i + 1) * UNITS] = made.astype(BF16)

            @pl.when(c == 0)
            def _():
                for copy in lefts[:2]:
                    copy.wait()

            pump.step(c)

    pl.run_scoped(
        feed,
        pltpu.VMEM((2, 3, shards, shard_rows, UNITS), BF16),
        pltpu.VMEM((rows, width), BF16),
        pltpu.VMEM((rows, width), BF16),
        pltpu.SemaphoreType.DMA((2, 3)),
        pltpu.SemaphoreType.DMA((2,)),
    )
    fed_steps = units // CHUNK

    def feed_terms(weights, block, sem, block_sem):
        def load(j, w, slot):
            return pltpu.make_async_copy(w.at[j], weights.at[slot], sem.at[slot])

        def product(slot, which):
            total = None
            for c in range(units // CHUNK):
                at = slice(c * CHUNK, (c + 1) * CHUNK)
                made = contract_cols(fed[which, c], weights[slot, :, at])
                total = made if total is None else total + made
            return total

        def columns(j):
            return pl.ds(pl.multiple_of(j * shard_rows, shard_rows), shard_rows)

        load(0, wi0, 0).start()
        load(0, wi1, 1).start()

        @pl.loop(0, shards)
        def _(j):
            total = None
            for slot, w in enumerate((wi0, wi1)):
                load(j, w, slot).wait()
                made = product(slot, 1 + slot)
                total = made if total is None else total + made

                @pl.when(j + 1 < shards)
                def _():
                    load(j + 1, w, slot).start()

            for s in range(seqs):
                term[s, :, columns(j)] = total[s * part : (s + 1) * part].astype(BF16)

            @pl.when(j == 1)
            def _():
                pump.step(fed_steps)

        for swap in swaps:
            swap.start()
        load(0, wff, 0).start()
        pump.steps(fed_steps + 1, fed_steps + 2)

        @pl.loop(0, shards)
        def _(j):
            slot = lax.rem(j, 2)

            @pl.when(j + 1 < shards)
            def _():
                load(j + 1, wff, 1 - slot).start()

            load(j, wff, slot).wait()
            block[...] = product(slot, 0).astype(BF16)
            copy = pltpu.make_async_copy(block, ffn_term.at[:, columns(j)], block_sem.at[0])
            copy.start()
            copy.wait()

            @pl.when(j == 1)
            def _():
                pump.step(fed_steps + 2)

        pump.steps(fed_steps + 3, fed_steps + 4)

    swaps = [
        remote(term.at[s], swap_in.at[s], swap_send.at[s], swap_recv.at[s], other_half) for s in range(seqs)
    ]
    pl.run_scoped(
        feed_terms,
        pltpu.VMEM((2, shard_rows, units), BF16),
        pltpu.VMEM((rows, shard_rows), BF16),
        pltpu.SemaphoreType.DMA((2,)),
        pltpu.SemaphoreType.DMA((1,)),
    )
    so_far = fed_steps + 4

    def head_move(s, peer):
        return remote(
            grads_out.at[0, peer, s], grads.at[me, s], head_send.at[s, peer], head_recv.at[s, me], {"ctx": peer}
        )

    def head_wait(s, peer):
        remote(
            grads_out.at[0, peer, s], grads.at[peer, s], head_send.at[s, peer], head_recv.at[s, peer], {"ctx": peer}
        ).wait_recv()

    def second_norm(s, weights, values, given, own, sem):
        at = pl.ds(s * part, part)
        copies = [
            pltpu.make_async_copy(hidden.at[at, :], values, sem.at[0]),
            pltpu.make_async_copy(cotangent.at[at, :], given, sem.at[1]),
        ]
        for copy in copies:
            copy.start()
        for copy in copies:
            copy.wait()
        swaps[s].wait_recv()

        @pl.loop(0, part // 64)
        def _(i):
            here = pl.ds(pl.multiple_of(i * 64, 64), 64)
            h = values[here, :]
            grad = term[s, here, :].astype(F32) + swap_in[s, here, :].astype(F32)
            scale = rms_scale(h)
            ffn_gain[...] += jnp.sum(grad * h * scale, axis=0, keepdims=True)
            total = given[here, :].astype(F32) + rms_back(h, scale, gain_two[...].astype(F32), grad)
            values[here, :] = total
            own[here, :] = total.astype(BF16)

        saved = pltpu.make_async_copy(values, grad_hidden.at[at, :], sem.at[0])
        saved.start()
        total = dot(own[:, :shard_rows], weights[0])
        for j in range(1, shards):
            total += dot(own[:, j * shard_rows : (j + 1) * shard_rows], weights[j])
        for k in range(n):
            grads_out[0, k, s] = total[:, k * cols : (k + 1) * cols].astype(BF16)
        for d in range(1, n):
            head_move(s, lax.rem(me + d, n)).start()
        grads[me, s] = grads_out[0, me, s]
        left[2, :, s * part : (s + 1) * part] = own[...].T
        saved.wait()

    def second_norms(weights, values, given, own, sem):
        load = pltpu.make_async_copy(wo, weights, sem.at[3])
        load.start()
        load.wait()
        for s in range(seqs):
            second_norm(s, weights, values, given, own, sem)
            if s == 0:
                pump.steps(so_far, so_far + 1)

    pl.run_scoped(
        second_norms,
        pltpu.VMEM((shards, shard_rows, dims.inner_width), BF16),
        pltpu.VMEM((part, width), F32),
        pltpu.VMEM((part, width), BF16),
        pltpu.VMEM((part, width), BF16),
        pltpu.SemaphoreType.DMA((4,)),
    )
    ffn_swap = remote(ffn_term, ffn_other, ffn_sem.at[0], ffn_sem.at[1], other_half)
    ffn_swap.start()
    pump.steps(so_far + 1, so_far + 2)
    so_far += 2

    def back_move(j, s, peer):
        return remote(
            grads_out.at[j, peer, s], grads_in.at[j, me, s], back_send.at[j, s, peer], back_recv.at[j, s, me],
            {"ctx": peer},
        )

    def back_wait(j, s, peer):
        remote(
            grads_out.at[j, peer, s], grads_in.at[j, peer, s], back_send.at[j, s, peer], back_recv.at[j, s, peer],
            {"ctx": peer},
        ).wait_recv()

    def attention(pieces, lse, bias, sums, grad_k, grad_v, sem):
        @pl.loop(0, seqs * groups * n)
        def _(i):
            a, group, s = lax.rem(i, n), lax.rem(i // n, groups), i // (n * groups)
            at = pl.ds(pl.multiple_of(group * lanes, lanes), lanes)

            @pl.when((a == 0) & (group == 0))
            def _():
                here = [
                    pltpu.make_async_copy(pieces_from.at[:, :, s], pieces, sem.at[0]),
                    pltpu.make_async_copy(lse_from.at[s], lse, sem.at[1]),
                ]
                for copy in here:
                    copy.start()
                for copy in here:
                    copy.wait()
                for d in range(1, n):
                    head_wait(s, lax.rem(me + d, n))
                    head_move(s, lax.rem(me + d, n)).wait_send()

            @pl.when(a == 0)
            def _():
                for j in range(per):
                    bias_rows(table[pl.ds(group * per + j, 1), :], sums.at[j])
                bias[...] = sums[...].astype(BF16)
                sums[...] = jnp.zeros_like(sums)
                grad_k[...] = jnp.zeros_like(grad_k)
                grad_v[...] = jnp.zeros_like(grad_v)

            lane = lax.broadcasted_iota(jnp.int32, (part, lanes), 1)
            result = jnp.zeros((part, lanes), F32)
            for j in range(per):
                mask = (lane >= j * head_dim) & (lane < (j + 1) * head_dim)
                query = jnp.where(mask, pieces[0, a, :, at], 0)
                upstream = jnp.where(mask, grads[a, s, :, at], 0)
                log_total = jnp.sum(jnp.where(lane == group * per + j, lse[a], 0.0), axis=1, keepdims=True)
                windows = [pl.ds(pl.multiple_of((n + b - a) * part, part), part) for b in range(n)]
                probs, grad_probs = [], []
                for b in range(n):
                    scores = contract_cols(query, pieces[1, b, :, at]) + bias[j, :, windows[b]].astype(F32)
                    probs.append(jnp.exp(scores - log_total))
                    grad_probs.append(contract_cols(upstream, pieces[2, b, :, at]))
                delta = sum(jnp.sum(g * p, axis=1, keepdims=True) for g, p in zip(grad_probs, probs))
                summed = None
                for b in range(n):
                    grad_scores = (probs[b] * (grad_probs[b] - delta)).astype(BF16)
                    sums[j, :, windows[b]] += grad_scores.astype(F32)
                    product = dot(grad_scores, pieces[1, b, :, at])
                    summed = product if summed is None else summed + product
                    grad_k[b] += contract_rows(grad_scores, query)
                    grad_v[b] += contract_rows(probs[b].astype(BF16), upstream)
                result = jnp.where(mask, summed, result)
            grads_out[0, a, s, :, at] = result.astype(BF16)

            @pl.when(a == n - 1)
            def _():
                for b in range(n):
                    grads_out[1, b, s, :, at] = grad_k[b].astype(BF16)
                    grads_out[2, b, s, :, at] = grad_v[b].astype(BF16)
                for j in range(per):
                    table_out[pl.ds(group * per + j, 1), :] += diagonal_sums(sums.at[j])

            @pl.when((a == n - 1) & (group == groups - 1))
            def _():
                for j in range(3):
                    for d in range(1, n):
                        back_move(j, s, lax.rem(me + d, n)).start()
                    grads_in[j, me, s] = grads_out[j, me, s]

            @pl.when(a == n - 1)
            def _():
                pump.step(so_far + i // n)

    pl.run_scoped(
        attention,
        pltpu.VMEM((3, n, part, cols), BF16),
        pltpu.VMEM((n, part, lanes), F32),
        pltpu.VMEM((per, part, span), BF16),
        pltpu.VMEM((per, part, span), F32),
        pltpu.VMEM((n, part, lanes), F32),
        pltpu.VMEM((n, part, lanes), F32),
        pltpu.SemaphoreType.DMA((2,)),
    )
    so_far += seqs * groups
    lefts[2].start()
    lefts[2].wait()
    pump.steps(so_far, so_far + 1)
    so_far += 1
    assert so_far <= pump.early
    for s in range(seqs):
        for j in range(3):
            for d in range(1, n):
                back_wait(j, s, lax.rem(me + d, n))

    for copy in swaps:
        copy.wait_send()

    def first_norm_terms(weights, values, sem):
        def load(shard):
            return [
                pltpu.make_async_copy(w.at[shard], weights.at[shard % 2, j], sem.at[shard % 2, j])
                for j, w in enumerate((wq, wk, wv))
            ]

        for copy in load(0):
            copy.start()
        for j in range(3):
            for s in range(seqs):
                for k in range(n):
                    values[j, s * part : (s + 1) * part, k * cols : (k + 1) * cols] = grads_in[j, k, s]
        for shard in range(shards):
            if shard + 1 < shards:
                for copy in load(shard + 1):
                    copy.start()
            for copy in load(shard):
                copy.wait()
            total = contract_cols(values[0], weights[shard % 2, 0])
            total += contract_cols(values[1], weights[shard % 2, 1])
            total += contract_cols(values[2], weights[shard % 2, 2])
            for s in range(seqs):
                term[s, :, shard * shard_rows : (shard + 1) * shard_rows] = (
                    total[s * part : (s + 1) * part].astype(BF16)
                )

    pl.run_scoped(
        first_norm_terms,
        pltpu.VMEM((2, 3, shard_rows, dims.inner_width), BF16),
        pltpu.VMEM((3, seqs * part, dims.inner_width), BF16),
        pltpu.SemaphoreType.DMA((2, 3)),
    )
    ones = [
        remote(term.at[s], other_one.at[s], one_send.at[s], one_recv.at[s], other_half) for s in range(seqs)
    ]
    for swap in ones:
        swap.start()
    pump.steps(so_far, so_far + LAYER_STEPS)
    so_far += LAYER_STEPS
    ffn_swap.wait_recv()

    def layer_output(values, own, other, sem):
        for s in range(seqs):
            at = pl.ds(s * part, part)
            copies = [
                pltpu.make_async_copy(source.at[at, :], to, sem.at[i])
                for i, (source, to) in enumerate(((hidden, values), (ffn_term, own), (ffn_other, other)))
            ]
            for copy in copies:
                copy.start()
            for copy in copies:
                copy.wait()

            @pl.loop(0, part // 64)
            def _(i):
                here = pl.ds(pl.multiple_of(i * 64, 64), 64)
                total = own[here, :].astype(F32) + other[here, :].astype(F32)
                own[here, :] = (values[here, :] + total).astype(BF16)

            saved = pltpu.make_async_copy(own, layer_out.at[at, :], sem.at[0])
            saved.start()
            saved.wait()

    pl.run_scoped(
        layer_output,
        pltpu.VMEM((part, width), F32),
        pltpu.VMEM((part, width), BF16),
        pltpu.VMEM((part, width), BF16),
        pltpu.SemaphoreType.DMA((3,)),
    )
    pump.steps(so_far, so_far + INPUT_STEPS)
    so_far += INPUT_STEPS

    def first_norm_back(values, given, sem):
        for s in range(seqs):
            at = pl.ds(s * part, part)
            copies = [
                pltpu.make_async_copy(source.at[at, :], to, sem.at[i])
                for i, (source, to) in enumerate(((grad_hidden, values), (tokens, given)))
            ]
            for copy in copies:
                copy.start()
            for copy in copies:
                copy.wait()
            ones[s].wait_recv()

            @pl.loop(0, part // 64)
            def _(i):
                here = pl.ds(pl.multiple_of(i * 64, 64), 64)
                x = given[here, :].astype(F32)
                grad = term[s, here, :].astype(F32) + other_one[s, here, :].astype(F32)
                scale = rms_scale(x)
                norm_gain[...] += jnp.sum(grad * x * scale, axis=0, keepdims=True)
                values[here, :] += rms_back(x, scale, gain_one[...].astype(F32), grad)

            saved = pltpu.make_async_copy(values, input_grad.at[at, :], sem.at[0])
            saved.start()
            saved.wait()

    pl.run_scoped(
        first_norm_back,
        pltpu.VMEM((part, width), F32),
        pltpu.VMEM((part, width), BF16),
        pltpu.SemaphoreType.DMA((2,)),
    )

    lines, slots = width // 128, small.shape[1] - 2 * (width // 128)
    for i in range(lines):
        small[0, i : i + 1, :] = norm_gain[:, i * 128 : (i + 1) * 128]
        small[0, lines + i : lines + i + 1, :] = ffn_gain[:, i * 128 : (i + 1) * 128]
    hot = by_offset[...] == lax.broadcasted_iota(jnp.int32, (slots, span), 0).astype(F32)
    lane = lax.broadcasted_iota(jnp.int32, (slots, 128), 1)
    table_part = jnp.zeros((slots, 128), F32)
    for head in range(dims.own_heads):
        column = jnp.sum(jnp.where(hot, table_out[head : head + 1, :], 0.0), axis=1, keepdims=True)
        table_part = jnp.where(lane == me * dims.own_heads + head, column, table_part)
    small[0, 2 * lines :, :] = table_part
    partners = []
    for axis, at, count in (("shard", spot.shard, shards), ("ctx", me, n)):
        step = 1
        while step < count:
            partners.append({axis: at + step * (1 - 2 * lax.rem(at // step, 2))})
            step *= 2
    for i, partner in enumerate(partners):
        copy = remote(small.at[i], small_in.at[i], small_send.at[i], small_recv.at[i], partner)
        copy.start()
        pump.steps(so_far, so_far + 1)
        so_far += 1
        copy.wait_recv()
        copy.wait_send()
        small[i + 1] = small[i] + small_in[i]
    small_out[...] = small[len(partners)]
    pump.steps(so_far, pump.last)
    for copy in ones + [ffn_swap]:
        copy.wait_send()
    for s in range(seqs):
        for d in range(1, n):
            peer = lax.rem(me + d, n)
            for j in range(3):
                back_move(j, s, peer).wait_send()


def backward_call(dims):
    rows, width, n, part, seqs = dims.seqs * dims.part, dims.width, dims.n, dims.part, dims.seqs
    shards, shard_rows, inner, units, cols = dims.shards, dims.shard_rows, dims.inner_width, dims.units, dims.cols
    span, chips = 2 * n * part, dims.shards // 2
    vmem, anywhere = pl.BlockSpec(memory_space=pltpu.VMEM), pl.BlockSpec(memory_space=pl.ANY)
    shape, dma, regular = jax.ShapeDtypeStruct, pltpu.SemaphoreType.DMA, pltpu.SemaphoreType.REGULAR
    far = max(chips - 1, 1)
    stages = (shards * n).bit_length() - 1
    lines = 2 * (width // 128) + dims.slots
    block = (shard_rows, CHUNK)
    return pl.pallas_call(
        functools.partial(backward_kernel, dims),
        in_specs=[vmem] * 4 + [anywhere] * 17,
        out_specs=[anywhere] * 12 + [vmem],
        out_shape=[shape((shard_rows, units), BF16)] * 3
        + [shape((shard_rows, inner), BF16)] * 4
        + [
            shape((rows, width), BF16),
            shape((rows, width), F32),
            shape((rows, width), F32),
            shape((rows, width), BF16),
            shape((rows, width), BF16),
            shape((lines, 128), F32),
        ],
        scratch_shapes=[
            pltpu.VMEM((seqs, part, width), BF16),
            pltpu.VMEM((1, width), F32),
            pltpu.VMEM((1, width), F32),
            pltpu.VMEM((dims.own_heads, span), F32),
            pltpu.VMEM((stages + 1, lines, 128), F32),
            pltpu.VMEM((stages, lines, 128), F32),
            pltpu.VMEM((3, width, rows), BF16),
            pltpu.VMEM((SLOTS, rows, CHUNK), BF16),
            pltpu.VMEM((2, chips) + block, BF16),
            pltpu.VMEM((SLOTS, chips) + block, BF16),
            pltpu.VMEM((2, far) + block, BF16),
            pltpu.VMEM((SLOTS, far) + block, BF16),
            pltpu.VMEM((SLOTS,) + block, BF16),
            pltpu.VMEM((SLOTS,) + block, BF16),
            pltpu.VMEM((SLOTS,) + block, BF16),
            pltpu.VMEM((SLOTS,) + block, BF16),
            pltpu.VMEM((3, units // CHUNK, rows, CHUNK), BF16),
            pltpu.VMEM((seqs, part, width), BF16),
            pltpu.VMEM((seqs, part, width), BF16),
            pltpu.VMEM((n, seqs, part, cols), BF16),
            pltpu.VMEM((3, n, seqs, part, cols), BF16),
            pltpu.VMEM((3, n, seqs, part, cols), BF16),
            dma((SLOTS,)),
            dma((2,)),
            dma((SLOTS,)),
            dma((SLOTS, far)),
            dma((SLOTS, far)),
        ]
        + [dma((SLOTS,))] * 7
        + [dma((seqs,))] * 2
        + [dma((seqs, n))] * 2
        + [dma((3, seqs, n))] * 2
        + [dma((seqs,))] * 2
        + [dma((2,)), dma((4,)), dma((stages,)), dma((stages,))]
        + [regular, regular((far,)), regular, regular, regular],
        compiler_params=pltpu.CompilerParams(
            vmem_limit_bytes=62 * 2**20, collective_id=1, has_side_effects=True
        ),
        name="backward",
    )


def per_device(
    mesh,
    tokens,
    cotangent,
    buckets,
    query_weight,
    key_weight,
    value_weight,
    output_weight,
    gate_weight,
    up_weight,
    down_weight,
    norm_gain,
    ffn_gain,
    bucket_bias_table,
):
    seqs, part, width = tokens.shape
    rows, inner_width = seqs * part, query_weight.shape[1]
    slots, heads = bucket_bias_table.shape
    dims = Dims(mesh, seqs, part, width, inner_width, gate_weight.shape[1], heads, slots)
    token_rows, upstream = tokens.reshape(rows, width), cotangent.reshape(rows, width)
    gain_one, gain_two = norm_gain.reshape(1, width), ffn_gain.reshape(1, width)
    hidden, normed_two, attended, lse, by_offset, bias_table, pieces, *lefts_and_weights = forward_call(dims)(
        token_rows, upstream, gain_one, gain_two, bucket_bias_table, buckets,
        query_weight, key_weight, value_weight, output_weight, gate_weight, up_weight, down_weight,
    )
    left_g, left_one, left_two, wq, wk, wv, wo, wi0, wi1, wff = lefts_and_weights
    *weight_grads, result, grad_inputs, unused, unused_own, unused_other, small = backward_call(dims)(
        gain_one, gain_two, bias_table, by_offset,
        token_rows, lse, pieces, left_g, left_two, left_one, normed_two, attended, hidden, upstream,
        wo, wq, wk, wv, wi0, wi1, wff,
    )
    grad_down_w, grad_gate_w, grad_up_w, grad_output_w, grad_query_w, grad_key_w, grad_value_w = (
        g.astype(F32) for g in weight_grads
    )
    lines = width // 128
    return (
        result.reshape(seqs, part, width),
        grad_inputs.reshape(seqs, part, width),
        grad_query_w,
        grad_key_w,
        grad_value_w,
        grad_output_w,
        grad_gate_w,
        grad_up_w,
        grad_down_w,
        small[:lines].reshape(width),
        small[lines : 2 * lines].reshape(width),
        small[2 * lines :, :heads],
    )


def solution(mesh):
    rows, weights = P("shard", "ctx", None), P("shard", "tp")
    return jax.shard_map(
        functools.partial(per_device, mesh),
        mesh=mesh,
        in_specs=(rows, rows, P("ctx", None)) + (weights,) * 7 + (P(), P(), P(None, "tp")),
        out_specs=(rows, rows) + (weights,) * 7 + (P(), P(), P(None, "tp")),
        check_vma=False,
    )
```

```python
import functools

import jax
import jax.numpy as jnp
from jax import lax
from jax.experimental import pallas as pl
from jax.experimental.pallas import tpu as pltpu
from jax.sharding import PartitionSpec as P

F32 = jnp.float32
BF16 = jnp.bfloat16
VMEM_LIMIT = 48 * 2**20


def contract_rows(left, right):
    return lax.dot_general(left, right, (((0,), (0,)), ((), ())), preferred_element_type=F32)


def contract_cols(left, right):
    return lax.dot_general(left, right, (((1,), (1,)), ((), ())), preferred_element_type=F32)


def dot(left, right):
    return jnp.dot(left, right, preferred_element_type=F32)


def rms_scale(values):
    return lax.rsqrt(jnp.mean(values * values, axis=-1, keepdims=True) + 1e-06)


def rms_back(values, scale, gain, upstream):
    weighted = upstream * gain
    inner_average = jnp.mean(values * weighted, axis=-1, keepdims=True)
    return scale * weighted - values * scale * scale * scale * inner_average


def bias_rows(table_row, out):
    span = out.shape[1]
    out[0:1, :] = table_row
    done = 1
    while done < out.shape[0]:
        out[done : 2 * done, :] = pltpu.roll(out[0:done, :], done, 1)
        done *= 2
    del span


def diagonal_sums(acc):
    rows, span = acc.shape
    total = acc[...]
    while rows > 1:
        rows //= 2
        total = total[:rows] + pltpu.roll(total[rows:], span - rows, 1)
    return total


MESH = pl.DeviceIdType.MESH


class Spot:
    def __init__(self, shards, ctx, tp):
        self.shards, self.chips, self.n, self.tps = shards, shards // 2, ctx, tp
        self.shard, self.me, self.half = (lax.axis_index(a) for a in ("shard", "ctx", "tp"))
        self.chip, self.core = self.shard // 2, lax.rem(self.shard, 2)
        self.mate = 2 * self.chip + 1 - self.core

    def away(self, d):
        return lax.rem(self.shard + 2 * d, self.shards)

    def barrier(self):
        peers = [{"shard": self.mate}] + [{"shard": self.away(d)} for d in range(1, self.chips)]
        peers += [{"ctx": lax.rem(self.me + d, self.n)} for d in range(1, self.n)]
        peers += [{"tp": 1 - self.half}]
        semaphore = pltpu.get_barrier_semaphore()
        for peer in peers:
            pl.semaphore_signal(semaphore, inc=1, device_id=peer, device_id_type=MESH)
        return lambda: pl.semaphore_wait(semaphore, len(peers))


def remote(src, dst, send, recv, peer):
    return pltpu.make_async_remote_copy(
        src_ref=src, dst_ref=dst, send_sem=send, recv_sem=recv, device_id=peer, device_id_type=MESH
    )


class Keep:
    def __init__(self, jobs, room, sem):
        self.halves = []
        for i, (own, full) in enumerate(jobs):
            self.halves.append(pltpu.make_async_copy(own, room, sem.at[0]))
            self.halves.append(pltpu.make_async_copy(room, full, sem.at[1]))
        self.at = 0
        self.halves[0].start()

    def step(self):
        if self.at < len(self.halves):
            self.halves[self.at].wait()
            self.at += 1
            if self.at < len(self.halves):
                self.halves[self.at].start()

    def start(self):
        pass

    def wait(self):
        while self.at < len(self.halves):
            self.step()


class Gather:
    def __init__(self, spot, own, full, sems, keep=None):
        self.spot, self.own, self.full = spot, own, full
        self.local, self.send, self.recv, self.on_send, self.on_recv = sems
        spot_shard = spot.shard
        self.keep = keep or pltpu.make_async_copy(own, full.at[spot_shard], self.local)
        self.far = [
            remote(own, full.at[spot_shard], self.send.at[d], self.recv.at[d], {"shard": spot.away(d)})
            for d in range(1, spot.chips)
        ]
        mate = {"shard": spot.mate}
        self.near = [remote(own, full.at[spot_shard], self.on_send.at[0], self.on_recv.at[0], mate)]
        for d in range(1, spot.chips):
            at = full.at[lax.rem(spot.shard - 2 * d + spot.shards, spot.shards)]
            self.near.append(remote(at, at, self.on_send.at[d], self.on_recv.at[d], mate))

    def start_far(self):
        for copy in self.far:
            copy.start()

    def start_near(self):
        self.keep.start()
        self.near[0].start()

    def pass_on(self):
        for d, copy in enumerate(self.far, 1):
            copy.wait_recv()
            self.near[d].start()

    def wait_own(self):
        self.keep.wait()
        self.near[0].wait_recv()

    def wait_near(self):
        for copy in self.near[1:]:
            copy.wait_recv()

    def wait_sent(self):
        for copy in self.far + self.near:
            copy.wait_send()


class Spread:
    def __init__(self, spot, own, full, keep, sems, direct=0):
        self.spot, self.own, self.full, self.keep, self.direct = spot, own, full, keep, direct
        (
            self.far_send, self.far_recv, self.right_send, self.right_recv, self.left_send, self.left_recv,
            self.mate_send, self.mate_recv,
        ) = sems
        self.part = (full.shape[1] - direct) // spot.n
        n, me = spot.n, spot.me
        self.near = remote(
            own, full.at[spot.shard], self.mate_send.at[0, 0], self.mate_recv.at[0, 0], {"shard": spot.mate}
        )
        mine = self.at(me)
        self.far = [
            remote(
                own.at[mine], full.at[spot.shard, mine], self.far_send.at[d, 0], self.far_recv.at[d, 0],
                {"shard": spot.away(d)},
            )
            for d in range(1, spot.chips)
        ]
        whole = pl.ds(0, direct)
        self.far_direct = [
            remote(
                own.at[whole], full.at[spot.shard, whole], self.far_send.at[d, 1], self.far_recv.at[d, 1],
                {"shard": spot.away(d)},
            )
            for d in range(1, spot.chips)
            if direct
        ]
        self.can_right, self.can_left = me + 1 < n, me > 0

    def at(self, z):
        return pl.ds(pl.multiple_of(self.direct + z * self.part, 16), self.part)

    def source(self, d):
        return lax.rem(self.spot.shard - 2 * d + self.spot.shards, self.spot.shards)

    def piece(self, d, z):
        return self.full.at[self.source(d), self.at(z)]

    def tell_direct(self, d):
        at = self.full.at[self.source(d), pl.ds(0, self.direct)]
        n = self.spot.n
        return remote(at, at, self.mate_send.at[d, n], self.mate_recv.at[d, n], {"shard": self.spot.mate})

    def start_direct(self):
        for copy in self.far_direct:
            copy.start()

    def pass_on(self):
        for d, copy in enumerate(self.far_direct, 1):
            copy.wait_recv()
            self.tell_direct(d).start()

    def tell(self, d, z):
        at = self.piece(d, z)
        return remote(at, at, self.mate_send.at[d, z], self.mate_recv.at[d, z], {"shard": self.spot.mate})

    def right(self, d, h, z):
        at, to = self.piece(d, z), {"ctx": lax.rem(self.spot.me + 1, self.spot.n)}
        return remote(at, at, self.right_send.at[d, h], self.right_recv.at[d, h], to)

    def left(self, d, h, z):
        at, to = self.piece(d, z), {"ctx": lax.rem(self.spot.me - 1 + self.spot.n, self.spot.n)}
        return remote(at, at, self.left_send.at[d, h], self.left_recv.at[d, h], to)

    def pairs(self):
        return range(1, self.spot.chips)

    def start(self):
        for copy in self.far:
            copy.start()

    def start_near(self):
        self.near.start()

    def send_on(self, d, h, z, right, left):
        self.tell(d, z).start()
        if right:
            @pl.when(self.can_right)
            def _():
                self.right(d, h, z).start()

        if left:
            @pl.when(self.can_left)
            def _():
                self.left(d, h, z).start()

    def arrived(self):
        for d in self.pairs():
            self.far[d - 1].wait_recv()
            self.send_on(d, 1, self.spot.me, True, True)

    def hop(self, h):
        me, n = self.spot.me, self.spot.n
        for d in self.pairs():
            @pl.when(me - h >= 0)
            def _():
                self.right(d, h, me - h).wait_recv()
                self.send_on(d, h + 1, me - h, h + 1 < n, False)

            @pl.when(me + h < n)
            def _():
                self.left(d, h, me + h).wait_recv()
                self.send_on(d, h + 1, me + h, False, h + 1 < n)

    def wait(self):
        me, n = self.spot.me, self.spot.n
        self.keep.wait()
        self.near.wait_recv()
        self.near.wait_send()
        for d, copy in enumerate(self.far_direct, 1):
            copy.wait_send()
            self.tell_direct(d).wait_recv()
            self.tell_direct(d).wait_send()
        for d in self.pairs():
            self.far[d - 1].wait_send()
            for z in range(n):
                self.tell(d, z).wait_recv()
                self.tell(d, z).wait_send()
            for h in range(1, n):
                @pl.when((me - h + 1 >= 0) & self.can_right)
                def _():
                    self.right(d, h, me - h + 1).wait_send()

                @pl.when((me + h - 1 < n) & self.can_left)
                def _():
                    self.left(d, h, me + h - 1).wait_send()


def offset_buckets(dims, me, some_rows, out):
    part, reach = dims.part, dims.n * dims.part
    at = pl.ds(pl.multiple_of(me * part, part), part)
    later = some_rows[0, 0:1, at].astype(F32)
    earlier = some_rows[1, 7:8, at].astype(F32)
    lane = lax.broadcasted_iota(jnp.int32, (1, part), 1)
    out[:, : reach - part] = jnp.broadcast_to(earlier[:, :1], (1, reach - part))
    out[:, reach - part : reach] = jnp.where(lane == 0, earlier[:, :1], pltpu.roll(earlier, 1, 1))
    out[:, reach : reach + part] = later
    out[:, reach + part :] = jnp.broadcast_to(later[:, part - 1 :], (1, reach - part))


def forward_kernel(
    dims, tokens, cotangent, gain_one, gain_two, table, buckets, wq, wk, wv, wo, wi0, wi1, wff,
    hidden, normed_two, attended, lse, by_offset, bias_table, pieces_out, left_g, left_one, left_two,
    full_q, full_k, full_v, full_o, full_0, full_1, full_2,
    normed, flipped, weights, acc, bias, staged, pieces, mixed, heads_in, rolled, branch_in,
    local_sem, far_send, far_recv, near_send, near_recv, head_send, head_recv, back_send, back_recv,
    room, some_rows, keep_sem, row_sem,
    swap_send, swap_recv, out_sem, *spread_sems,
):
    spot = Spot(*dims.mesh)
    n, seqs, part, cols, head_dim = dims.n, dims.seqs, dims.part, dims.cols, dims.head_dim
    me, shards = spot.me, spot.shards
    shard_rows = weights.shape[2]
    rows = seqs * part
    lanes = 2 * head_dim
    per = 2
    spot.barrier()()

    def gather(i, own, full, keep=None):
        sems = [local_sem.at[i], far_send.at[i], far_recv.at[i], near_send.at[i], near_recv.at[i]]
        return Gather(spot, own, full, sems, keep)

    loads = [None] + [gather(i, w, weights.at[i]) for i, w in ((1, wk), (2, wv), (3, wo))]
    keep = Keep(
        [(w, full.at[spot.shard]) for w, full in ((wi0, full_0), (wi1, full_1), (wff, full_2))], room, keep_sem
    )
    loads.append(gather(4, wi0, full_0, keep))
    spreads = [
        Spread(spot, own, full, keep, [sem.at[i] for sem in spread_sems], direct)
        for i, (own, full, direct) in enumerate(((wi1, full_1, shard_rows // 2), (wff, full_2, 0)))
    ]
    keep_first = pltpu.make_async_copy(wq, weights.at[0, spot.shard], local_sem.at[0])
    spreads.append(Spread(spot, wq, weights.at[0], keep_first, [sem.at[2] for sem in spread_sems]))
    flips = []

    def flip(value, out):
        if flips:
            flips[-1].wait()
        flipped[...] = value.T
        flips.append(pltpu.make_async_copy(flipped, out, out_sem.at[5]))
        flips[-1].start()

    first = spreads[2]
    first.start()
    for load in loads[1:3]:
        load.start_far()
    first.keep.start()
    first.start_near()
    for load in loads[1:3]:
        load.start_near()

    row_copies = [
        pltpu.make_async_copy(buckets.at[pl.ds(at, 8)], some_rows.at[i], row_sem.at[i])
        for i, at in enumerate((0, part - 8))
    ]
    for copy in row_copies:
        copy.start()

    @pl.loop(0, rows // 64)
    def _(i):
        at = pl.ds(pl.multiple_of(i * 64, 64), 64)
        values = tokens[at, :].astype(F32)
        normed[at, :] = (values * rms_scale(values) * gain_one[...].astype(F32)).astype(BF16)

    for copy in row_copies:
        copy.wait()
    offset_buckets(dims, me, some_rows, by_offset)
    slots = table.shape[0]
    hot = by_offset[...] == lax.broadcasted_iota(jnp.int32, (slots, by_offset.shape[1]), 0).astype(F32)
    lane = lax.broadcasted_iota(jnp.int32, table.shape, 1)
    for head in range(dims.own_heads):
        own = lane == me * dims.own_heads + head
        column = jnp.sum(jnp.where(own, table[...].astype(F32), 0.0), axis=1, keepdims=True)
        bias_table[head : head + 1, :] = jnp.sum(jnp.where(hot, column, 0.0), axis=0, keepdims=True)
        bias_rows(bias_table[head : head + 1, :], rolled)
        bias[head] = rolled[...].astype(BF16)

    def term(i, shard):
        at = pl.ds(pl.multiple_of(shard * shard_rows, 128), shard_rows)
        return dot(normed[:, at], weights[i, shard])

    moves = []
    first.arrived()
    for h in range(1, n):
        first.hop(h)
    for i, load in enumerate(loads[:3]):
        if i == 0:
            first.wait()
        else:
            load.wait_own()
        acc[...] = term(i, spot.shard)
        acc[...] += term(i, spot.mate)
        keep.step()
        if i:
            load.pass_on()
        if i == 2:
            for spread in spreads[:2]:
                spread.start()
            loads[3].start_far()
            loads[4].start_far()
            spreads[0].start_direct()
            for later in loads[3:] + spreads[:2]:
                later.start_near()
        keep.step()
        for d in range(1, spot.chips):
            acc[...] += term(i, lax.rem(spot.shard - 2 * d + shards, shards))
        if i:
            load.wait_near()
        for d in range(1, spot.chips):
            acc[...] += term(i, lax.rem(spot.mate - 2 * d + shards, shards))
        for k in range(n):
            for s in range(seqs):
                staged[i, k, s] = acc[s * part : (s + 1) * part, k * cols : (k + 1) * cols].astype(BF16)
        for d in range(1, n):
            peer = lax.rem(me + d, n)
            move = remote(
                staged.at[i, peer], pieces.at[i, me], head_send.at[i, d], head_recv.at[i, d], {"ctx": peer}
            )
            move.start()
            moves.append(move)
        pieces[i, me] = staged[i, me]
    outs = [
        pltpu.make_async_copy(weights.at[i], full, out_sem.at[i])
        for i, full in enumerate((full_q, full_k, full_v, full_o))
    ]
    for copy in outs[:3]:
        copy.start()
    flip(normed[...], left_one)
    spreads[0].arrived()
    spreads[1].arrived()
    flip(cotangent[...], left_g)
    for move in moves:
        move.wait_recv()
    loads[3].wait_own()
    outs.append(pltpu.make_async_copy(pieces, pieces_out, out_sem.at[4]))
    outs[4].start()

    def back(s, at, to):
        return remote(mixed.at[s, at], heads_in.at[me, s], back_send.at[s, at], back_recv.at[s, me], {"ctx": to})

    def attend(s, a):
        step = s * n + a
        lane = lax.broadcasted_iota(jnp.int32, (part, lanes), 1)
        log_total = jnp.zeros((part, lanes), F32)
        for group in range(cols // lanes):
            span = slice(group * lanes, (group + 1) * lanes)
            result = jnp.zeros((part, lanes), F32)
            for j in range(per):
                head = group * per + j
                mask = (lane >= j * head_dim) & (lane < (j + 1) * head_dim)
                query = jnp.where(mask, pieces[0, a, s, :, span], 0)
                scores = jnp.concatenate(
                    [
                        contract_cols(query, pieces[1, b, s, :, span])
                        + bias[head, :, pl.ds(pl.multiple_of((n + b - a) * part, part), part)].astype(F32)
                        for b in range(n)
                    ],
                    axis=1,
                )
                peak = jnp.max(scores, axis=1, keepdims=True)
                expo = jnp.exp(scores - peak)
                total = jnp.sum(expo, axis=1, keepdims=True)
                probs = (expo * (1.0 / total)).astype(BF16)
                summed = sum(
                    dot(probs[:, b * part : (b + 1) * part], pieces[2, b, s, :, span]) for b in range(n)
                )
                result = jnp.where(mask, summed, result)
                log_total = jnp.where(lane == head, peak + jnp.log(total), log_total)
            mixed[s, a, :, span] = result.astype(BF16)
        lse[s, a] = log_total

        @pl.when(a != me)
        def _():
            back(s, a, a).start()

        @pl.when(a == me)
        def _():
            heads_in[a, s] = mixed[s, a]

        @pl.when(step == 1)
        def _():
            spreads[0].hop(1)

        @pl.when(step == 3)
        def _():
            loads[3].pass_on()

        @pl.when(step == 4)
        def _():
            spreads[1].hop(1)

    swaps = []

    def project(s):
        at = pl.ds(s * part, part)
        for d in range(1, n):
            peer = lax.rem(me + d, n)
            remote(
                mixed.at[s, 0], heads_in.at[peer, s], back_send.at[s, peer], back_recv.at[s, peer], {"ctx": peer}
            ).wait_recv()
        for k in range(n):
            attended[at, k * cols : (k + 1) * cols] = heads_in[k, s]
        for j in range(shards):
            normed[at, j * shard_rows : (j + 1) * shard_rows] = contract_cols(
                attended[at, :], weights[3, j]
            ).astype(BF16)
        swap = remote(normed.at[at], branch_in.at[s], swap_send.at[s], swap_recv.at[s], {"tp": 1 - spot.half})
        swap.start()
        swaps.append(swap)

    for s in range(seqs):
        pl.loop(0, n)(functools.partial(attend, s))
        if s == 0:
            loads[3].wait_near()
            outs[3].start()
            if n > 2:
                spreads[0].hop(2)
        project(s)
    if n > 2:
        spreads[1].hop(2)
    for h in range(3, n):
        for spread in spreads[:2]:
            spread.hop(h)
    loads[4].wait_own()
    loads[4].pass_on()
    spreads[0].pass_on()
    for s in range(seqs):
        swaps[s].wait_recv()

        @pl.loop(0, part // 64)
        def _(i):
            here = pl.ds(pl.multiple_of(i * 64, 64), 64)
            at = pl.ds(pl.multiple_of(s * part + i * 64, 64), 64)
            values = tokens[at, :].astype(F32) + (
                normed[at, :].astype(F32) + branch_in[s, here, :].astype(F32)
            )
            hidden[at, :] = values
            normed_two[at, :] = (values * rms_scale(values) * gain_two[...].astype(F32)).astype(BF16)

    flip(normed_two[...], left_two)
    loads[4].wait_near()
    for spread in spreads[:2]:
        spread.wait()
    for load in loads[1:]:
        load.wait_sent()
    for move in moves + swaps:
        move.wait_send()
    for s in range(seqs):
        for d in range(1, n):
            peer = lax.rem(me + d, n)
            back(s, peer, peer).wait_send()
    for copy in outs + flips[-1:]:
        copy.wait()


class Dims:
    def __init__(self, mesh, seqs, part, width, inner_width, units, heads, slots):
        self.mesh = shards, ctx, tp = tuple(mesh.shape[a] for a in ("shard", "ctx", "tp"))
        self.slots = slots
        self.n, self.seqs, self.part, self.width = ctx, seqs, part, width
        self.inner_width, self.units = inner_width, units
        self.head_dim = inner_width // heads
        self.cols, self.own_heads = inner_width // ctx, heads // ctx
        self.shards, self.shard_rows = shards, width // shards


def forward_call(dims):
    rows, width, n, part, seqs = dims.seqs * dims.part, dims.width, dims.n, dims.part, dims.seqs
    shards, shard_rows, inner, units = dims.shards, dims.shard_rows, dims.inner_width, dims.units
    lanes, span = 2 * dims.head_dim, 2 * n * part
    vmem, anywhere = pl.BlockSpec(memory_space=pltpu.VMEM), pl.BlockSpec(memory_space=pl.ANY)
    shape = jax.ShapeDtypeStruct
    dma = pltpu.SemaphoreType.DMA
    chips = shards // 2
    block = (seqs, part, dims.cols)
    return pl.pallas_call(
        functools.partial(forward_kernel, dims),
        in_specs=[vmem] * 5 + [anywhere] * 8,
        out_specs=[vmem] * 6 + [anywhere] * 11,
        out_shape=[
            shape((rows, width), F32),
            shape((rows, width), BF16),
            shape((rows, inner), BF16),
            shape((seqs, n, part, lanes), F32),
            shape((1, span), F32),
            shape((dims.own_heads, span), F32),
            shape((3, n) + block, BF16),
        ]
        + [shape((width, rows), BF16)] * 3
        + [shape((shards, shard_rows, inner), BF16)] * 4
        + [shape((shards, shard_rows, units), BF16)] * 3,
        scratch_shapes=[
            pltpu.VMEM((rows, width), BF16),
            pltpu.VMEM((width, rows), BF16),
            pltpu.VMEM((4, shards, shard_rows, inner), BF16),
            pltpu.VMEM((rows, inner), F32),
            pltpu.VMEM((dims.own_heads, part, span), BF16),
            pltpu.VMEM((3, n) + block, BF16),
            pltpu.VMEM((3, n) + block, BF16),
            pltpu.VMEM((seqs, n, part, dims.cols), BF16),
            pltpu.VMEM((n,) + block, BF16),
            pltpu.VMEM((part, span), F32),
            pltpu.VMEM((seqs, part, width), BF16),
            dma((7,)),
            dma((7, chips)),
            dma((7, chips)),
            dma((7, chips)),
            dma((7, chips)),
            dma((3, n)),
            dma((3, n)),
            dma((seqs, n)),
            dma((seqs, n)),
            pltpu.VMEM((shard_rows, units), BF16),
            pltpu.VMEM((2, 8, n * part), jnp.int32),
            dma((2,)),
            dma((2,)),
            dma((seqs,)),
            dma((seqs,)),
            dma((6,)),
        ]
        + [dma((3, chips, 2))] * 2
        + [dma((3, chips, n))] * 4
        + [dma((3, chips, n + 1))] * 2,
        compiler_params=pltpu.CompilerParams(
            vmem_limit_bytes=60 * 2**20, collective_id=0, has_side_effects=True
        ),
        name="forward",
    )


CHUNK = 512
SLOTS = 4
LAYER_STEPS = 4
INPUT_STEPS = 3


class Pump:
    def __init__(self, dims, spot, left, right, sources, from_heads, outs, buffers, sems, credits):
        self.dims, self.spot, self.left, self.right = dims, spot, left, right
        self.fed, self.attended = sources
        self.from_heads, self.outs = from_heads, outs
        self.core_out, self.core_in, self.far_out, self.far_in, self.line, self.line_in, self.across_in, self.done = buffers
        (
            self.right_sem, self.core_send, self.core_recv, self.far_send, self.far_recv, self.in_send, self.in_recv,
            self.across_send, self.across_recv, self.out_send, self.out_recv, self.fin_sem,
        ) = sems
        self.core_credit, self.far_credit, self.in_credit, self.across_credit, self.out_credit = credits
        units, heads = dims.units // CHUNK, dims.inner_width // CHUNK
        self.units, self.heads = units, heads
        self.early = 3 * units + heads
        self.total = 3 * units + 4 * heads
        self.bases = [(i * units, units) for i in range(3)]
        self.bases += [(3 * units + i * heads, heads) for i in range(4)]
        me, n = spot.me, dims.n
        middle = n // 2
        self.is_middle = (me == middle - 1) | (me == middle)
        self.is_end = (me == 0) | (me == n - 1)
        self.has_outer, self.has_inner = jnp.logical_not(self.is_end), jnp.logical_not(self.is_middle)
        low_side = me < middle
        self.facing = jnp.where(low_side, middle, middle - 1)
        toward, away = jnp.where(low_side, me + 1, me - 1), jnp.where(low_side, me - 1, me + 1)
        self.inner = jnp.where(self.is_middle, self.facing, toward)
        self.outer = jnp.where(self.is_end, self.inner, away)
        self.last = self.total + 10

    def core(self, c, k):
        return remote(
            self.core_out.at[lax.rem(c, 2)], self.core_in.at[k], self.core_send.at[lax.rem(c, 2)],
            self.core_recv.at[k], {"shard": self.spot.mate},
        )

    def far(self, k, d):
        return remote(
            self.far_out.at[lax.rem(k, 2), d - 1], self.far_in.at[k, d - 1], self.far_send.at[k, d - 1],
            self.far_recv.at[k, d - 1], {"shard": self.spot.away(d)},
        )

    def inward(self, k):
        half = k
        return remote(
            self.line.at[k], self.line_in.at[half], self.in_send.at[k], self.in_recv.at[half], {"ctx": self.inner}
        )

    def across(self, k):
        return remote(
            self.line.at[k], self.across_in.at[k], self.across_send.at[k],
            self.across_recv.at[k], {"ctx": self.facing},
        )

    def outward(self, k):
        return remote(
            self.done.at[k], self.done.at[k], self.out_send.at[k], self.out_recv.at[k], {"ctx": self.outer}
        )

    def spend(self, c, credit, slots=SLOTS):
        @pl.when(c >= slots)
        def _():
            pl.semaphore_wait(credit, 1)

    def give(self, c, credit, peer, slots=SLOTS):
        @pl.when(c + slots < self.total)
        def _():
            pl.semaphore_signal(credit, inc=1, device_id=peer, device_id_type=MESH)

    def term(self, c, shard, k):
        one = lambda b: jnp.where(c >= b, 1, 0)
        which = one(self.units) + one(3 * self.units) - 2 * one(self.early)
        rows = self.dims.shard_rows
        return dot(self.left[which, pl.ds(pl.multiple_of(shard * rows, rows), rows), :], self.right[k])

    def fetch(self, c):
        k, fed = lax.rem(c, SLOTS), 3 * self.units

        @pl.when(c < fed)
        def _():
            source = self.fed.at[c // self.units, lax.rem(c, self.units)]
            pltpu.make_async_copy(source, self.right.at[k], self.right_sem.at[k]).start()

        @pl.when((c >= fed) & (c < self.early))
        def _():
            at = pl.ds(pl.multiple_of((c - fed) * CHUNK, CHUNK), CHUNK)
            pltpu.make_async_copy(self.attended.at[:, at], self.right.at[k], self.right_sem.at[k]).start()

        @pl.when((c >= self.early) & (c < self.total))
        def _():
            dims = self.dims
            which, piece = (c - self.early) // self.heads, lax.rem(c - self.early, self.heads)
            per = CHUNK // dims.cols
            for i in range(per):
                for s in range(dims.seqs):
                    self.right[k, s * dims.part : (s + 1) * dims.part, i * dims.cols : (i + 1) * dims.cols] = (
                        self.from_heads[which, piece * per + i, s]
                    )

    def save(self, c, k):
        for (base, count), out in zip(self.bases, self.outs):
            @pl.when((c >= base) & (c < base + count))
            def _():
                at = pl.ds(pl.multiple_of((c - base) * CHUNK, CHUNK), CHUNK)
                pltpu.make_async_copy(self.done.at[k], out.at[:, at], self.fin_sem.at[k]).start()

    def settle(self, c, k):
        pltpu.make_async_copy(self.done.at[k], self.outs[0].at[:, pl.ds(0, CHUNK)], self.fin_sem.at[k]).wait()

        @pl.when(self.has_outer)
        def _():
            self.outward(k).wait_send()

        @pl.when(self.has_inner)
        def _():
            self.give(c, self.out_credit, {"ctx": self.inner})

    def deliver(self, c, k):
        @pl.when(self.has_inner)
        def _():
            self.outward(k).wait_recv()
            self.save(c, k)

            @pl.when(self.has_outer)
            def _():
                self.spend(c, self.out_credit)
                self.outward(k).start()

    def finish(self, c, k):
        @pl.when(self.is_middle)
        def _():
            self.across(k).wait_recv()
            self.across(k).wait_send()
            self.done[k] = (self.line[k].astype(F32) + self.across_in[k].astype(F32)).astype(BF16)
            self.give(c, self.across_credit, {"ctx": self.facing})
            self.save(c, k)

            @pl.when(self.has_outer)
            def _():
                self.spend(c, self.out_credit)
                self.outward(k).start()

        @pl.when(self.has_inner)
        def _():
            self.inward(k).wait_send()

    def collect(self, c, k):
        @pl.when(self.has_outer)
        def _():
            self.inward(k).wait_recv()
            self.line[k] = (self.line[k].astype(F32) + self.line_in[k].astype(F32)).astype(BF16)
            self.give(c, self.in_credit, {"ctx": self.outer})

        @pl.when(self.is_middle)
        def _():
            self.spend(c, self.across_credit)
            self.across(k).start()

        @pl.when(self.has_outer & self.has_inner)
        def _():
            self.spend(c, self.in_credit)
            self.inward(k).start()

    def own(self, c, k):
        total = self.term(c, self.spot.shard, k) + self.core_in[k, self.spot.chips - 1].astype(F32)
        for d in range(1, self.spot.chips):
            self.far(k, d).wait_send()
            self.far(k, d).wait_recv()
            total = total + self.far_in[k, d - 1].astype(F32)
        self.line[k] = total.astype(BF16)
        self.give(c, self.core_credit, {"shard": self.spot.mate})
        for d in range(1, self.spot.chips):
            sender = lax.rem(self.spot.shard - 2 * d + self.spot.shards, self.spot.shards)
            self.give(c, self.far_credit.at[d - 1], {"shard": sender})

        @pl.when(self.is_end & self.has_inner)
        def _():
            self.spend(c, self.in_credit)
            self.inward(k).start()

    def to_chips(self, c, k):
        self.core(c, k).wait_recv()
        self.core(c, k).wait_send()
        for d in range(1, self.spot.chips):
            pair = self.term(c, self.spot.away(d), k) + self.core_in[k, d - 1].astype(F32)
            self.far_out[lax.rem(k, 2), d - 1] = pair.astype(BF16)
            self.spend(c, self.far_credit.at[d - 1])
            self.far(k, d).start()

    def to_core(self, c, k):
        @pl.when(c < self.early)
        def _():
            pltpu.make_async_copy(self.fed.at[0, 0], self.right.at[k], self.right_sem.at[k]).wait()

        chips, half = self.spot.chips, lax.rem(c, 2)
        for d in range(1, chips + 1):
            shard = 2 * lax.rem(self.spot.chip + d, chips) + 1 - self.spot.core
            self.core_out[half, d - 1] = self.term(c, shard, k).astype(BF16)
        self.spend(c, self.core_credit)
        self.core(c, k).start()

    def step(self, t):
        def at(lag, stage):
            c = t - lag

            @pl.when((c >= 0) & (c < self.total))
            def _():
                stage(c, lax.rem(c, SLOTS))

        @pl.when(t < self.total)
        def _():
            self.fetch(t)

        at(10, self.settle)
        at(9, self.deliver)
        at(7, self.finish)
        at(5, self.collect)
        at(3, self.own)

        at(1, self.to_chips)
        at(0, self.to_core)

    def steps(self, first, last):
        @pl.loop(first, last)
        def _(t):
            self.step(t)


UNITS = 256


def geglu_both(gate, up, upstream):
    root, cube = 0.7978845608028654, 0.044715
    square = gate * gate
    bent = jnp.tanh(root * gate * (1.0 + cube * square))
    half = 0.5 * (1.0 + bent)
    gelu = gate * half
    slope = half + 0.5 * gate * (1.0 - bent * bent) * (root * (1.0 + 3.0 * cube * square))
    return gelu * up, upstream * up * slope, upstream * gelu


def backward_kernel(
    dims, gain_one, gain_two, table, by_offset,
    tokens, lse_from, pieces_from, left_g, left_two, left_one, normed_two, attended, hidden, cotangent,
    wo, wq, wk, wv, wi0, wi1, wff,
    down_out, gate_out, up_out, o_out, q_out, k_out, v_out,
    layer_out, input_grad, grad_hidden, ffn_term, ffn_other, small_out,
    other_one, norm_gain, ffn_gain, table_out, small, small_in,
    left, right, core_out, core_in, far_out, far_in, line, line_in, across_in, done,
    fed, term, swap_in, grads, grads_out, grads_in,
    right_sem, core_send, core_recv, far_send, far_recv, in_send, in_recv, across_send, across_recv,
    out_send, out_recv, fin_sem, swap_send, swap_recv, head_send, head_recv, back_send, back_recv,
    one_send, one_recv, ffn_sem, local_sem, small_send, small_recv,
    core_credit, far_credit, in_credit, across_credit, out_credit,
):
    spot = Spot(*dims.mesh)
    n, seqs, part, cols, head_dim, width = dims.n, dims.seqs, dims.part, dims.cols, dims.head_dim, dims.width
    me, shards, shard_rows, units = spot.me, spot.shards, dims.shard_rows, dims.units
    rows = seqs * part
    lanes, per = 2 * head_dim, 2
    groups = cols // lanes
    span = table.shape[1]
    other_half = {"tp": 1 - spot.half}
    pump = Pump(
        dims, spot, left, right, (fed, attended), grads_in,
        (down_out, gate_out, up_out, o_out, q_out, k_out, v_out),
        (core_out, core_in, far_out, far_in, line, line_in, across_in, done),
        (
            right_sem, core_send, core_recv, far_send, far_recv, in_send, in_recv, across_send, across_recv,
            out_send, out_recv, fin_sem,
        ),
        (core_credit, far_credit, in_credit, across_credit, out_credit),
    )
    lefts = [
        pltpu.make_async_copy(source, left.at[i], local_sem.at[i])
        for i, source in ((0, left_g), (1, left_two), (0, left_one))
    ]
    all_here = spot.barrier()
    ffn_gain[...] = jnp.zeros_like(ffn_gain)
    norm_gain[...] = jnp.zeros_like(norm_gain)
    table_out[...] = jnp.zeros_like(table_out)

    def feed(weights, values, given, sem, value_sem):
        inputs = [
            pltpu.make_async_copy(normed_two, values, value_sem.at[0]),
            pltpu.make_async_copy(cotangent, given, value_sem.at[1]),
        ]

        def load(u):
            slot = lax.rem(u, 2)
            at = pl.ds(pl.multiple_of(u * UNITS, UNITS), UNITS)
            return [
                pltpu.make_async_copy(w.at[:, :, at], weights.at[slot, j], sem.at[slot, j])
                for j, w in enumerate((wi0, wi1, wff))
            ]

        for copy in load(0) + inputs + lefts[:2]:
            copy.start()
        for copy in inputs:
            copy.wait()
        each = CHUNK // UNITS

        @pl.loop(0, units // CHUNK)
        def _(c):
            for i in range(each):
                u = c * each + i

                @pl.when(u + 1 < units // UNITS)
                def _():
                    for copy in load(u + 1):
                        copy.start()

                for copy in load(u):
                    copy.wait()
                slot = lax.rem(u, 2)
                gate = dot(values[...], weights[slot, 0].reshape(width, UNITS))
                up = dot(values[...], weights[slot, 1].reshape(width, UNITS))
                upstream = dot(given[...], weights[slot, 2].reshape(width, UNITS))
                for j, made in enumerate(geglu_both(gate, up, upstream)):
                    fed[j, c, :, i * UNITS : (i + 1) * UNITS] = made.astype(BF16)

            @pl.when(c == 0)
            def _():
                for copy in lefts[:2]:
                    copy.wait()
                all_here()

            pump.step(c)

    pl.run_scoped(
        feed,
        pltpu.VMEM((2, 3, shards, shard_rows, UNITS), BF16),
        pltpu.VMEM((rows, width), BF16),
        pltpu.VMEM((rows, width), BF16),
        pltpu.SemaphoreType.DMA((2, 3)),
        pltpu.SemaphoreType.DMA((2,)),
    )
    fed_steps = units // CHUNK

    def feed_terms(weights, block, sem, block_sem):
        def load(j, w, slot):
            return pltpu.make_async_copy(w.at[j], weights.at[slot], sem.at[slot])

        def product(slot, which):
            total = None
            for c in range(units // CHUNK):
                at = slice(c * CHUNK, (c + 1) * CHUNK)
                made = contract_cols(fed[which, c], weights[slot, :, at])
                total = made if total is None else total + made
            return total

        def columns(j):
            return pl.ds(pl.multiple_of(j * shard_rows, shard_rows), shard_rows)

        load(0, wi0, 0).start()
        load(0, wi1, 1).start()

        @pl.loop(0, shards)
        def _(j):
            total = None
            for slot, w in enumerate((wi0, wi1)):
                load(j, w, slot).wait()
                made = product(slot, 1 + slot)
                total = made if total is None else total + made

                @pl.when(j + 1 < shards)
                def _():
                    load(j + 1, w, slot).start()

            for s in range(seqs):
                term[s, :, columns(j)] = total[s * part : (s + 1) * part].astype(BF16)

            @pl.when(j == 1)
            def _():
                pump.step(fed_steps)

        for swap in swaps:
            swap.start()
        load(0, wff, 0).start()
        pump.steps(fed_steps + 1, fed_steps + 2)

        @pl.loop(0, shards)
        def _(j):
            slot = lax.rem(j, 2)

            @pl.when(j + 1 < shards)
            def _():
                load(j + 1, wff, 1 - slot).start()

            load(j, wff, slot).wait()
            block[...] = product(slot, 0).astype(BF16)
            copy = pltpu.make_async_copy(block, ffn_term.at[:, columns(j)], block_sem.at[0])
            copy.start()
            copy.wait()

            @pl.when(j == 1)
            def _():
                pump.step(fed_steps + 2)

        pump.steps(fed_steps + 3, fed_steps + 4)

    swaps = [
        remote(term.at[s], swap_in.at[s], swap_send.at[s], swap_recv.at[s], other_half) for s in range(seqs)
    ]
    pl.run_scoped(
        feed_terms,
        pltpu.VMEM((2, shard_rows, units), BF16),
        pltpu.VMEM((rows, shard_rows), BF16),
        pltpu.SemaphoreType.DMA((2,)),
        pltpu.SemaphoreType.DMA((1,)),
    )
    so_far = fed_steps + 4

    def head_move(s, peer):
        return remote(
            grads_out.at[0, peer, s], grads.at[me, s], head_send.at[s, peer], head_recv.at[s, me], {"ctx": peer}
        )

    def head_wait(s, peer):
        remote(
            grads_out.at[0, peer, s], grads.at[peer, s], head_send.at[s, peer], head_recv.at[s, peer], {"ctx": peer}
        ).wait_recv()

    def second_norm(s, weights, values, given, own, sem):
        at = pl.ds(s * part, part)
        copies = [
            pltpu.make_async_copy(hidden.at[at, :], values, sem.at[0]),
            pltpu.make_async_copy(cotangent.at[at, :], given, sem.at[1]),
        ]
        for copy in copies:
            copy.start()
        for copy in copies:
            copy.wait()
        swaps[s].wait_recv()

        @pl.loop(0, part // 64)
        def _(i):
            here = pl.ds(pl.multiple_of(i * 64, 64), 64)
            h = values[here, :]
            grad = term[s, here, :].astype(F32) + swap_in[s, here, :].astype(F32)
            scale = rms_scale(h)
            ffn_gain[...] += jnp.sum(grad * h * scale, axis=0, keepdims=True)
            total = given[here, :].astype(F32) + rms_back(h, scale, gain_two[...].astype(F32), grad)
            values[here, :] = total
            own[here, :] = total.astype(BF16)

        saved = pltpu.make_async_copy(values, grad_hidden.at[at, :], sem.at[0])
        saved.start()
        total = dot(own[:, :shard_rows], weights[0])
        for j in range(1, shards):
            total += dot(own[:, j * shard_rows : (j + 1) * shard_rows], weights[j])
        for k in range(n):
            grads_out[0, k, s] = total[:, k * cols : (k + 1) * cols].astype(BF16)
        for d in range(1, n):
            head_move(s, lax.rem(me + d, n)).start()
        grads[me, s] = grads_out[0, me, s]
        left[2, :, s * part : (s + 1) * part] = own[...].T
        saved.wait()

    def second_norms(weights, values, given, own, sem):
        load = pltpu.make_async_copy(wo, weights, sem.at[3])
        load.start()
        load.wait()
        for s in range(seqs):
            second_norm(s, weights, values, given, own, sem)
            if s == 0:
                pump.steps(so_far, so_far + 1)

    pl.run_scoped(
        second_norms,
        pltpu.VMEM((shards, shard_rows, dims.inner_width), BF16),
        pltpu.VMEM((part, width), F32),
        pltpu.VMEM((part, width), BF16),
        pltpu.VMEM((part, width), BF16),
        pltpu.SemaphoreType.DMA((4,)),
    )
    ffn_swap = remote(ffn_term, ffn_other, ffn_sem.at[0], ffn_sem.at[1], other_half)
    ffn_swap.start()
    pump.steps(so_far + 1, so_far + 2)
    so_far += 2

    def back_move(j, s, peer):
        return remote(
            grads_out.at[j, peer, s], grads_in.at[j, me, s], back_send.at[j, s, peer], back_recv.at[j, s, me],
            {"ctx": peer},
        )

    def back_wait(j, s, peer):
        remote(
            grads_out.at[j, peer, s], grads_in.at[j, peer, s], back_send.at[j, s, peer], back_recv.at[j, s, peer],
            {"ctx": peer},
        ).wait_recv()

    def attention(pieces, lse, bias, sums, grad_k, grad_v, sem):
        @pl.loop(0, seqs * groups * n)
        def _(i):
            a, group, s = lax.rem(i, n), lax.rem(i // n, groups), i // (n * groups)
            at = pl.ds(pl.multiple_of(group * lanes, lanes), lanes)

            @pl.when((a == 0) & (group == 0))
            def _():
                here = [
                    pltpu.make_async_copy(pieces_from.at[:, :, s], pieces, sem.at[0]),
                    pltpu.make_async_copy(lse_from.at[s], lse, sem.at[1]),
                ]
                for copy in here:
                    copy.start()
                for copy in here:
                    copy.wait()
                for d in range(1, n):
                    head_wait(s, lax.rem(me + d, n))
                    head_move(s, lax.rem(me + d, n)).wait_send()

            @pl.when(a == 0)
            def _():
                for j in range(per):
                    bias_rows(table[pl.ds(group * per + j, 1), :], sums.at[j])
                bias[...] = sums[...].astype(BF16)
                sums[...] = jnp.zeros_like(sums)
                grad_k[...] = jnp.zeros_like(grad_k)
                grad_v[...] = jnp.zeros_like(grad_v)

            lane = lax.broadcasted_iota(jnp.int32, (part, lanes), 1)
            result = jnp.zeros((part, lanes), F32)
            for j in range(per):
                mask = (lane >= j * head_dim) & (lane < (j + 1) * head_dim)
                query = jnp.where(mask, pieces[0, a, :, at], 0)
                upstream = jnp.where(mask, grads[a, s, :, at], 0)
                log_total = jnp.sum(jnp.where(lane == group * per + j, lse[a], 0.0), axis=1, keepdims=True)
                windows = [pl.ds(pl.multiple_of((n + b - a) * part, part), part) for b in range(n)]
                probs, grad_probs = [], []
                for b in range(n):
                    scores = contract_cols(query, pieces[1, b, :, at]) + bias[j, :, windows[b]].astype(F32)
                    probs.append(jnp.exp(scores - log_total))
                    grad_probs.append(contract_cols(upstream, pieces[2, b, :, at]))
                delta = sum(jnp.sum(g * p, axis=1, keepdims=True) for g, p in zip(grad_probs, probs))
                summed = None
                for b in range(n):
                    grad_scores = (probs[b] * (grad_probs[b] - delta)).astype(BF16)
                    sums[j, :, windows[b]] += grad_scores.astype(F32)
                    product = dot(grad_scores, pieces[1, b, :, at])
                    summed = product if summed is None else summed + product
                    grad_k[b] += contract_rows(grad_scores, query)
                    grad_v[b] += contract_rows(probs[b].astype(BF16), upstream)
                result = jnp.where(mask, summed, result)
            grads_out[0, a, s, :, at] = result.astype(BF16)

            @pl.when(a == n - 1)
            def _():
                for b in range(n):
                    grads_out[1, b, s, :, at] = grad_k[b].astype(BF16)
                    grads_out[2, b, s, :, at] = grad_v[b].astype(BF16)
                for j in range(per):
                    table_out[pl.ds(group * per + j, 1), :] += diagonal_sums(sums.at[j])

            @pl.when((a == n - 1) & (group == groups - 1))
            def _():
                for j in range(3):
                    for d in range(1, n):
                        back_move(j, s, lax.rem(me + d, n)).start()
                    grads_in[j, me, s] = grads_out[j, me, s]

            @pl.when(a == n - 1)
            def _():
                pump.step(so_far + i // n)

    pl.run_scoped(
        attention,
        pltpu.VMEM((3, n, part, cols), BF16),
        pltpu.VMEM((n, part, lanes), F32),
        pltpu.VMEM((per, part, span), BF16),
        pltpu.VMEM((per, part, span), F32),
        pltpu.VMEM((n, part, lanes), F32),
        pltpu.VMEM((n, part, lanes), F32),
        pltpu.SemaphoreType.DMA((2,)),
    )
    so_far += seqs * groups
    lefts[2].start()
    lefts[2].wait()
    pump.steps(so_far, so_far + 1)
    so_far += 1
    assert so_far <= pump.early
    for s in range(seqs):
        for j in range(3):
            for d in range(1, n):
                back_wait(j, s, lax.rem(me + d, n))

    for copy in swaps:
        copy.wait_send()

    def first_norm_terms(weights, values, sem):
        def load(shard):
            return [
                pltpu.make_async_copy(w.at[shard], weights.at[shard % 2, j], sem.at[shard % 2, j])
                for j, w in enumerate((wq, wk, wv))
            ]

        for copy in load(0):
            copy.start()
        for j in range(3):
            for s in range(seqs):
                for k in range(n):
                    values[j, s * part : (s + 1) * part, k * cols : (k + 1) * cols] = grads_in[j, k, s]
        for shard in range(shards):
            if shard + 1 < shards:
                for copy in load(shard + 1):
                    copy.start()
            for copy in load(shard):
                copy.wait()
            total = contract_cols(values[0], weights[shard % 2, 0])
            total += contract_cols(values[1], weights[shard % 2, 1])
            total += contract_cols(values[2], weights[shard % 2, 2])
            for s in range(seqs):
                term[s, :, shard * shard_rows : (shard + 1) * shard_rows] = (
                    total[s * part : (s + 1) * part].astype(BF16)
                )

    pl.run_scoped(
        first_norm_terms,
        pltpu.VMEM((2, 3, shard_rows, dims.inner_width), BF16),
        pltpu.VMEM((3, seqs * part, dims.inner_width), BF16),
        pltpu.SemaphoreType.DMA((2, 3)),
    )
    ones = [
        remote(term.at[s], other_one.at[s], one_send.at[s], one_recv.at[s], other_half) for s in range(seqs)
    ]
    for swap in ones:
        swap.start()
    pump.steps(so_far, so_far + LAYER_STEPS)
    so_far += LAYER_STEPS
    ffn_swap.wait_recv()

    def layer_output(values, own, other, sem):
        for s in range(seqs):
            at = pl.ds(s * part, part)
            copies = [
                pltpu.make_async_copy(source.at[at, :], to, sem.at[i])
                for i, (source, to) in enumerate(((hidden, values), (ffn_term, own), (ffn_other, other)))
            ]
            for copy in copies:
                copy.start()
            for copy in copies:
                copy.wait()

            @pl.loop(0, part // 64)
            def _(i):
                here = pl.ds(pl.multiple_of(i * 64, 64), 64)
                total = own[here, :].astype(F32) + other[here, :].astype(F32)
                own[here, :] = (values[here, :] + total).astype(BF16)

            saved = pltpu.make_async_copy(own, layer_out.at[at, :], sem.at[0])
            saved.start()
            saved.wait()

    pl.run_scoped(
        layer_output,
        pltpu.VMEM((part, width), F32),
        pltpu.VMEM((part, width), BF16),
        pltpu.VMEM((part, width), BF16),
        pltpu.SemaphoreType.DMA((3,)),
    )
    pump.steps(so_far, so_far + INPUT_STEPS)
    so_far += INPUT_STEPS

    def first_norm_back(values, given, sem):
        for s in range(seqs):
            at = pl.ds(s * part, part)
            copies = [
                pltpu.make_async_copy(source.at[at, :], to, sem.at[i])
                for i, (source, to) in enumerate(((grad_hidden, values), (tokens, given)))
            ]
            for copy in copies:
                copy.start()
            for copy in copies:
                copy.wait()
            ones[s].wait_recv()

            @pl.loop(0, part // 64)
            def _(i):
                here = pl.ds(pl.multiple_of(i * 64, 64), 64)
                x = given[here, :].astype(F32)
                grad = term[s, here, :].astype(F32) + other_one[s, here, :].astype(F32)
                scale = rms_scale(x)
                norm_gain[...] += jnp.sum(grad * x * scale, axis=0, keepdims=True)
                values[here, :] += rms_back(x, scale, gain_one[...].astype(F32), grad)

            saved = pltpu.make_async_copy(values, input_grad.at[at, :], sem.at[0])
            saved.start()
            saved.wait()

    pl.run_scoped(
        first_norm_back,
        pltpu.VMEM((part, width), F32),
        pltpu.VMEM((part, width), BF16),
        pltpu.SemaphoreType.DMA((2,)),
    )

    lines, slots = width // 128, small.shape[1] - 2 * (width // 128)
    for i in range(lines):
        small[0, i : i + 1, :] = norm_gain[:, i * 128 : (i + 1) * 128]
        small[0, lines + i : lines + i + 1, :] = ffn_gain[:, i * 128 : (i + 1) * 128]
    hot = by_offset[...] == lax.broadcasted_iota(jnp.int32, (slots, span), 0).astype(F32)
    lane = lax.broadcasted_iota(jnp.int32, (slots, 128), 1)
    table_part = jnp.zeros((slots, 128), F32)
    for head in range(dims.own_heads):
        column = jnp.sum(jnp.where(hot, table_out[head : head + 1, :], 0.0), axis=1, keepdims=True)
        table_part = jnp.where(lane == me * dims.own_heads + head, column, table_part)
    small[0, 2 * lines :, :] = table_part
    partners = []
    for axis, at, count in (("shard", spot.shard, shards), ("ctx", me, n)):
        step = 1
        while step < count:
            partners.append({axis: at + step * (1 - 2 * lax.rem(at // step, 2))})
            step *= 2
    for i, partner in enumerate(partners):
        copy = remote(small.at[i], small_in.at[i], small_send.at[i], small_recv.at[i], partner)
        copy.start()
        pump.steps(so_far, so_far + 1)
        so_far += 1
        copy.wait_recv()
        copy.wait_send()
        small[i + 1] = small[i] + small_in[i]
    small_out[...] = small[len(partners)]
    pump.steps(so_far, pump.last)
    for copy in ones + [ffn_swap]:
        copy.wait_send()
    for s in range(seqs):
        for d in range(1, n):
            peer = lax.rem(me + d, n)
            for j in range(3):
                back_move(j, s, peer).wait_send()


def backward_call(dims):
    rows, width, n, part, seqs = dims.seqs * dims.part, dims.width, dims.n, dims.part, dims.seqs
    shards, shard_rows, inner, units, cols = dims.shards, dims.shard_rows, dims.inner_width, dims.units, dims.cols
    span, chips = 2 * n * part, dims.shards // 2
    vmem, anywhere = pl.BlockSpec(memory_space=pltpu.VMEM), pl.BlockSpec(memory_space=pl.ANY)
    shape, dma, regular = jax.ShapeDtypeStruct, pltpu.SemaphoreType.DMA, pltpu.SemaphoreType.REGULAR
    far = max(chips - 1, 1)
    stages = (shards * n).bit_length() - 1
    lines = 2 * (width // 128) + dims.slots
    block = (shard_rows, CHUNK)
    return pl.pallas_call(
        functools.partial(backward_kernel, dims),
        in_specs=[vmem] * 4 + [anywhere] * 17,
        out_specs=[anywhere] * 12 + [vmem],
        out_shape=[shape((shard_rows, units), BF16)] * 3
        + [shape((shard_rows, inner), BF16)] * 4
        + [
            shape((rows, width), BF16),
            shape((rows, width), F32),
            shape((rows, width), F32),
            shape((rows, width), BF16),
            shape((rows, width), BF16),
            shape((lines, 128), F32),
        ],
        scratch_shapes=[
            pltpu.VMEM((seqs, part, width), BF16),
            pltpu.VMEM((1, width), F32),
            pltpu.VMEM((1, width), F32),
            pltpu.VMEM((dims.own_heads, span), F32),
            pltpu.VMEM((stages + 1, lines, 128), F32),
            pltpu.VMEM((stages, lines, 128), F32),
            pltpu.VMEM((3, width, rows), BF16),
            pltpu.VMEM((SLOTS, rows, CHUNK), BF16),
            pltpu.VMEM((2, chips) + block, BF16),
            pltpu.VMEM((SLOTS, chips) + block, BF16),
            pltpu.VMEM((2, far) + block, BF16),
            pltpu.VMEM((SLOTS, far) + block, BF16),
            pltpu.VMEM((SLOTS,) + block, BF16),
            pltpu.VMEM((SLOTS,) + block, BF16),
            pltpu.VMEM((SLOTS,) + block, BF16),
            pltpu.VMEM((SLOTS,) + block, BF16),
            pltpu.VMEM((3, units // CHUNK, rows, CHUNK), BF16),
            pltpu.VMEM((seqs, part, width), BF16),
            pltpu.VMEM((seqs, part, width), BF16),
            pltpu.VMEM((n, seqs, part, cols), BF16),
            pltpu.VMEM((3, n, seqs, part, cols), BF16),
            pltpu.VMEM((3, n, seqs, part, cols), BF16),
            dma((SLOTS,)),
            dma((2,)),
            dma((SLOTS,)),
            dma((SLOTS, far)),
            dma((SLOTS, far)),
        ]
        + [dma((SLOTS,))] * 7
        + [dma((seqs,))] * 2
        + [dma((seqs, n))] * 2
        + [dma((3, seqs, n))] * 2
        + [dma((seqs,))] * 2
        + [dma((2,)), dma((4,)), dma((stages,)), dma((stages,))]
        + [regular, regular((far,)), regular, regular, regular],
        compiler_params=pltpu.CompilerParams(
            vmem_limit_bytes=62 * 2**20, collective_id=1, has_side_effects=True
        ),
        name="backward",
    )


TILE = 64


def finish_kernel(count, *refs):
    sources, outs = refs[:count], refs[count : 2 * count]
    taken, made = refs[2 * count : 3 * count], refs[3 * count : 4 * count]
    take_sem, save_sem = refs[4 * count :]
    tiles = [source.shape[0] // TILE for source in sources]

    def at(i):
        return pl.ds(pl.multiple_of(i * TILE, TILE), TILE)

    def take(j, i):
        return pltpu.make_async_copy(sources[j].at[at(i)], taken[j].at[at(i)], take_sem.at[j, i])

    def save(j, i):
        return pltpu.make_async_copy(made[j].at[at(i)], outs[j].at[at(i)], save_sem.at[j, i])

    for j in range(count):
        @pl.loop(0, tiles[j])
        def _(i):
            take(j, i).start()

    for j in range(count):
        @pl.loop(0, tiles[j])
        def _(i):
            take(j, i).wait()
            if made[j].dtype != taken[j].dtype:
                made[j][at(i), :] = taken[j][at(i), :].astype(made[j].dtype)
            save(j, i).start()

    for j in range(count):
        @pl.loop(0, tiles[j])
        def _(i):
            save(j, i).wait()


def finish(sources, types):
    count = len(sources)
    taken = [pltpu.VMEM(s.shape, s.dtype) for s in sources]
    made = [pltpu.VMEM(s.shape, t) for s, t in zip(sources, types)]
    same = [s.dtype == t for s, t in zip(sources, types)]
    tiles = max(s.shape[0] for s in sources) // TILE

    def kernel(*refs):
        refs = list(refs)
        made_at = iter(refs[3 * count : -2])
        full = [refs[2 * count + j] if same[j] else next(made_at) for j in range(count)]
        finish_kernel(count, *refs[: 3 * count], *full, *refs[-2:])

    return pl.pallas_call(
        kernel,
        in_specs=[pl.BlockSpec(memory_space=pl.ANY)] * count,
        out_specs=[pl.BlockSpec(memory_space=pl.ANY)] * count,
        out_shape=[jax.ShapeDtypeStruct(s.shape, t) for s, t in zip(sources, types)],
        scratch_shapes=taken
        + [m for m, keep in zip(made, same) if not keep]
        + [pltpu.SemaphoreType.DMA((count, tiles))] * 2,
        compiler_params=pltpu.CompilerParams(vmem_limit_bytes=56 * 2**20),
        name="finish",
    )(*sources)


def per_device(
    mesh,
    tokens,
    cotangent,
    buckets,
    query_weight,
    key_weight,
    value_weight,
    output_weight,
    gate_weight,
    up_weight,
    down_weight,
    norm_gain,
    ffn_gain,
    bucket_bias_table,
):
    seqs, part, width = tokens.shape
    rows, inner_width = seqs * part, query_weight.shape[1]
    slots, heads = bucket_bias_table.shape
    dims = Dims(mesh, seqs, part, width, inner_width, gate_weight.shape[1], heads, slots)
    token_rows, upstream = tokens.reshape(rows, width), cotangent.reshape(rows, width)
    gain_one, gain_two = norm_gain.reshape(1, width), ffn_gain.reshape(1, width)
    hidden, normed_two, attended, lse, by_offset, bias_table, pieces, *lefts_and_weights = forward_call(dims)(
        token_rows, upstream, gain_one, gain_two, bucket_bias_table, buckets,
        query_weight, key_weight, value_weight, output_weight, gate_weight, up_weight, down_weight,
    )
    left_g, left_one, left_two, wq, wk, wv, wo, wi0, wi1, wff = lefts_and_weights
    *weight_grads, result, grad_inputs, unused, unused_own, unused_other, small = backward_call(dims)(
        gain_one, gain_two, bias_table, by_offset,
        token_rows, lse, pieces, left_g, left_two, left_one, normed_two, attended, hidden, upstream,
        wo, wq, wk, wv, wi0, wi1, wff,
    )
    *weight_grads, grad_inputs, result = finish(weight_grads + [grad_inputs, result], [F32] * 8 + [BF16])
    grad_down_w, grad_gate_w, grad_up_w, grad_output_w, grad_query_w, grad_key_w, grad_value_w = weight_grads
    lines = width // 128
    return (
        result.reshape(seqs, part, width),
        grad_inputs.reshape(seqs, part, width),
        grad_query_w,
        grad_key_w,
        grad_value_w,
        grad_output_w,
        grad_gate_w,
        grad_up_w,
        grad_down_w,
        small[:lines].reshape(width),
        small[lines : 2 * lines].reshape(width),
        small[2 * lines :, :heads],
    )


def solution(mesh):
    rows, weights = P("shard", "ctx", None), P("shard", "tp")
    return jax.shard_map(
        functools.partial(per_device, mesh),
        mesh=mesh,
        in_specs=(rows, rows, P("ctx", None)) + (weights,) * 7 + (P(), P(), P(None, "tp")),
        out_specs=(rows, rows) + (weights,) * 7 + (P(), P(), P(None, "tp")),
        check_vma=False,
    )
```

```python
import functools

import jax
import jax.numpy as jnp
from jax import lax
from jax.experimental import pallas as pl
from jax.experimental.pallas import tpu as pltpu
from jax.sharding import PartitionSpec as P

F32 = jnp.float32
BF16 = jnp.bfloat16
VMEM_LIMIT = 48 * 2**20


def contract_rows(left, right):
    return lax.dot_general(left, right, (((0,), (0,)), ((), ())), preferred_element_type=F32)


def contract_cols(left, right):
    return lax.dot_general(left, right, (((1,), (1,)), ((), ())), preferred_element_type=F32)


def dot(left, right):
    return jnp.dot(left, right, preferred_element_type=F32)


def rms_scale(values):
    return lax.rsqrt(jnp.mean(values * values, axis=-1, keepdims=True) + 1e-06)


def rms_back(values, scale, gain, upstream):
    weighted = upstream * gain
    inner_average = jnp.mean(values * weighted, axis=-1, keepdims=True)
    return scale * weighted - values * scale * scale * scale * inner_average


def bias_rows(table_row, out):
    span = out.shape[1]
    out[0:1, :] = table_row
    done = 1
    while done < out.shape[0]:
        out[done : 2 * done, :] = pltpu.roll(out[0:done, :], done, 1)
        done *= 2
    del span


def diagonal_sums(acc):
    rows, span = acc.shape
    total = acc[...]
    while rows > 1:
        rows //= 2
        total = total[:rows] + pltpu.roll(total[rows:], span - rows, 1)
    return total


MESH = pl.DeviceIdType.MESH


class Spot:
    def __init__(self, shards, ctx, tp):
        self.shards, self.chips, self.n, self.tps = shards, shards // 2, ctx, tp
        self.shard, self.me, self.half = (lax.axis_index(a) for a in ("shard", "ctx", "tp"))
        self.chip, self.core = self.shard // 2, lax.rem(self.shard, 2)
        self.mate = 2 * self.chip + 1 - self.core

    def away(self, d):
        return lax.rem(self.shard + 2 * d, self.shards)

    def barrier(self):
        peers = [{"shard": self.mate}] + [{"shard": self.away(d)} for d in range(1, self.chips)]
        peers += [{"ctx": lax.rem(self.me + d, self.n)} for d in range(1, self.n)]
        peers += [{"tp": 1 - self.half}]
        semaphore = pltpu.get_barrier_semaphore()
        for peer in peers:
            pl.semaphore_signal(semaphore, inc=1, device_id=peer, device_id_type=MESH)
        return lambda: pl.semaphore_wait(semaphore, len(peers))


def remote(src, dst, send, recv, peer):
    return pltpu.make_async_remote_copy(
        src_ref=src, dst_ref=dst, send_sem=send, recv_sem=recv, device_id=peer, device_id_type=MESH
    )


class Keep:
    def __init__(self, jobs, room, sem):
        self.halves = []
        for i, (own, full) in enumerate(jobs):
            self.halves.append(pltpu.make_async_copy(own, room, sem.at[0]))
            self.halves.append(pltpu.make_async_copy(room, full, sem.at[1]))
        self.at = 0
        self.halves[0].start()

    def step(self):
        if self.at < len(self.halves):
            self.halves[self.at].wait()
            self.at += 1
            if self.at < len(self.halves):
                self.halves[self.at].start()

    def start(self):
        pass

    def wait(self):
        while self.at < len(self.halves):
            self.step()


class Gather:
    def __init__(self, spot, own, full, sems, keep=None):
        self.spot, self.own, self.full = spot, own, full
        self.local, self.send, self.recv, self.on_send, self.on_recv = sems
        spot_shard = spot.shard
        self.keep = keep or pltpu.make_async_copy(own, full.at[spot_shard], self.local)
        self.far = [
            remote(own, full.at[spot_shard], self.send.at[d], self.recv.at[d], {"shard": spot.away(d)})
            for d in range(1, spot.chips)
        ]
        mate = {"shard": spot.mate}
        self.near = [remote(own, full.at[spot_shard], self.on_send.at[0], self.on_recv.at[0], mate)]
        for d in range(1, spot.chips):
            at = full.at[lax.rem(spot.shard - 2 * d + spot.shards, spot.shards)]
            self.near.append(remote(at, at, self.on_send.at[d], self.on_recv.at[d], mate))

    def start_far(self):
        for copy in self.far:
            copy.start()

    def start_near(self):
        self.keep.start()
        self.near[0].start()

    def pass_on(self):
        for d, copy in enumerate(self.far, 1):
            copy.wait_recv()
            self.near[d].start()

    def wait_own(self):
        self.keep.wait()
        self.near[0].wait_recv()

    def wait_near(self):
        for copy in self.near[1:]:
            copy.wait_recv()

    def wait_sent(self):
        for copy in self.far + self.near:
            copy.wait_send()


class Spread:
    def __init__(self, spot, own, full, keep, sems, direct=0):
        self.spot, self.own, self.full, self.keep, self.direct = spot, own, full, keep, direct
        (
            self.far_send, self.far_recv, self.right_send, self.right_recv, self.left_send, self.left_recv,
            self.mate_send, self.mate_recv,
        ) = sems
        self.part = (full.shape[1] - direct) // spot.n
        n, me = spot.n, spot.me
        self.near = remote(
            own, full.at[spot.shard], self.mate_send.at[0, 0], self.mate_recv.at[0, 0], {"shard": spot.mate}
        )
        mine = self.at(me)
        self.far = [
            remote(
                own.at[mine], full.at[spot.shard, mine], self.far_send.at[d, 0], self.far_recv.at[d, 0],
                {"shard": spot.away(d)},
            )
            for d in range(1, spot.chips)
        ]
        whole = pl.ds(0, direct)
        self.far_direct = [
            remote(
                own.at[whole], full.at[spot.shard, whole], self.far_send.at[d, 1], self.far_recv.at[d, 1],
                {"shard": spot.away(d)},
            )
            for d in range(1, spot.chips)
            if direct
        ]
        self.can_right, self.can_left = me + 1 < n, me > 0

    def at(self, z):
        return pl.ds(pl.multiple_of(self.direct + z * self.part, 16), self.part)

    def source(self, d):
        return lax.rem(self.spot.shard - 2 * d + self.spot.shards, self.spot.shards)

    def piece(self, d, z):
        return self.full.at[self.source(d), self.at(z)]

    def tell_direct(self, d):
        at = self.full.at[self.source(d), pl.ds(0, self.direct)]
        n = self.spot.n
        return remote(at, at, self.mate_send.at[d, n], self.mate_recv.at[d, n], {"shard": self.spot.mate})

    def start_direct(self):
        for copy in self.far_direct:
            copy.start()

    def pass_on(self):
        for d, copy in enumerate(self.far_direct, 1):
            copy.wait_recv()
            self.tell_direct(d).start()

    def tell(self, d, z):
        at = self.piece(d, z)
        return remote(at, at, self.mate_send.at[d, z], self.mate_recv.at[d, z], {"shard": self.spot.mate})

    def right(self, d, h, z):
        at, to = self.piece(d, z), {"ctx": lax.rem(self.spot.me + 1, self.spot.n)}
        return remote(at, at, self.right_send.at[d, h], self.right_recv.at[d, h], to)

    def left(self, d, h, z):
        at, to = self.piece(d, z), {"ctx": lax.rem(self.spot.me - 1 + self.spot.n, self.spot.n)}
        return remote(at, at, self.left_send.at[d, h], self.left_recv.at[d, h], to)

    def pairs(self):
        return range(1, self.spot.chips)

    def start(self):
        for copy in self.far:
            copy.start()

    def start_near(self):
        self.near.start()

    def send_on(self, d, h, z, right, left):
        self.tell(d, z).start()
        if right:
            @pl.when(self.can_right)
            def _():
                self.right(d, h, z).start()

        if left:
            @pl.when(self.can_left)
            def _():
                self.left(d, h, z).start()

    def arrived(self):
        for d in self.pairs():
            self.far[d - 1].wait_recv()
            self.send_on(d, 1, self.spot.me, True, True)

    def hop(self, h):
        me, n = self.spot.me, self.spot.n
        for d in self.pairs():
            @pl.when(me - h >= 0)
            def _():
                self.right(d, h, me - h).wait_recv()
                self.send_on(d, h + 1, me - h, h + 1 < n, False)

            @pl.when(me + h < n)
            def _():
                self.left(d, h, me + h).wait_recv()
                self.send_on(d, h + 1, me + h, False, h + 1 < n)

    def wait(self):
        me, n = self.spot.me, self.spot.n
        self.keep.wait()
        self.near.wait_recv()
        self.near.wait_send()
        for d, copy in enumerate(self.far_direct, 1):
            copy.wait_send()
            self.tell_direct(d).wait_recv()
            self.tell_direct(d).wait_send()
        for d in self.pairs():
            self.far[d - 1].wait_send()
            for z in range(n):
                self.tell(d, z).wait_recv()
                self.tell(d, z).wait_send()
            for h in range(1, n):
                @pl.when((me - h + 1 >= 0) & self.can_right)
                def _():
                    self.right(d, h, me - h + 1).wait_send()

                @pl.when((me + h - 1 < n) & self.can_left)
                def _():
                    self.left(d, h, me + h - 1).wait_send()


def offset_buckets(dims, me, some_rows, out):
    part, reach = dims.part, dims.n * dims.part
    at = pl.ds(pl.multiple_of(me * part, part), part)
    later = some_rows[0, 0:1, at].astype(F32)
    earlier = some_rows[1, 7:8, at].astype(F32)
    lane = lax.broadcasted_iota(jnp.int32, (1, part), 1)
    out[:, : reach - part] = jnp.broadcast_to(earlier[:, :1], (1, reach - part))
    out[:, reach - part : reach] = jnp.where(lane == 0, earlier[:, :1], pltpu.roll(earlier, 1, 1))
    out[:, reach : reach + part] = later
    out[:, reach + part :] = jnp.broadcast_to(later[:, part - 1 :], (1, reach - part))


def forward_kernel(
    dims, tokens, cotangent, gains, table, buckets, wq, wk, wv, wo, wi0, wi1, wff,
    hidden, normed_two, attended, lse, by_offset, bias_table, pieces_out, left_g, left_one, left_two,
    full_q, full_k, full_v, full_o, full_0, full_1, full_2,
    normed, flipped, weights, acc, bias, staged, pieces, mixed, heads_in, rolled, branch_in,
    local_sem, far_send, far_recv, near_send, near_recv, head_send, head_recv, back_send, back_recv,
    room, some_rows, keep_sem, row_sem,
    swap_send, swap_recv, out_sem, *spread_sems,
):
    spot = Spot(*dims.mesh)
    n, seqs, part, cols, head_dim = dims.n, dims.seqs, dims.part, dims.cols, dims.head_dim
    me, shards = spot.me, spot.shards
    shard_rows = weights.shape[2]
    rows = seqs * part
    lanes = 2 * head_dim
    per = 2
    spot.barrier()()

    def gather(i, own, full, keep=None):
        sems = [local_sem.at[i], far_send.at[i], far_recv.at[i], near_send.at[i], near_recv.at[i]]
        return Gather(spot, own, full, sems, keep)

    loads = [None] + [gather(i, w, weights.at[i]) for i, w in ((1, wk), (2, wv), (3, wo))]
    keep = Keep(
        [(w, full.at[spot.shard]) for w, full in ((wi0, full_0), (wi1, full_1), (wff, full_2))], room, keep_sem
    )
    loads.append(gather(4, wi0, full_0, keep))
    spreads = [
        Spread(spot, own, full, keep, [sem.at[i] for sem in spread_sems], direct)
        for i, (own, full, direct) in enumerate(((wi1, full_1, shard_rows // 2), (wff, full_2, 0)))
    ]
    keep_first = pltpu.make_async_copy(wq, weights.at[0, spot.shard], local_sem.at[0])
    spreads.append(Spread(spot, wq, weights.at[0], keep_first, [sem.at[2] for sem in spread_sems]))
    flips = []

    def flip(value, out):
        if flips:
            flips[-1].wait()
        flipped[...] = value.T
        flips.append(pltpu.make_async_copy(flipped, out, out_sem.at[5]))
        flips[-1].start()

    first = spreads[2]
    first.start()
    for load in loads[1:3]:
        load.start_far()
    first.keep.start()
    first.start_near()
    for load in loads[1:3]:
        load.start_near()

    row_copies = [
        pltpu.make_async_copy(buckets.at[pl.ds(at, 8)], some_rows.at[i], row_sem.at[i])
        for i, at in enumerate((0, part - 8))
    ]
    for copy in row_copies:
        copy.start()

    @pl.loop(0, rows // 64)
    def _(i):
        at = pl.ds(pl.multiple_of(i * 64, 64), 64)
        values = tokens[at, :].astype(F32)
        normed[at, :] = (values * rms_scale(values) * gains[0:1, :]).astype(BF16)

    for copy in row_copies:
        copy.wait()
    offset_buckets(dims, me, some_rows, by_offset)
    slots = table.shape[0]
    hot = by_offset[...] == lax.broadcasted_iota(jnp.int32, (slots, by_offset.shape[1]), 0).astype(F32)
    lane = lax.broadcasted_iota(jnp.int32, table.shape, 1)
    for head in range(dims.own_heads):
        own = lane == me * dims.own_heads + head
        column = jnp.sum(jnp.where(own, table[...], 0.0), axis=1, keepdims=True)
        bias_table[head : head + 1, :] = jnp.sum(jnp.where(hot, column, 0.0), axis=0, keepdims=True)
        bias_rows(bias_table[head : head + 1, :], rolled)
        bias[head] = rolled[...].astype(BF16)

    def term(i, shard):
        at = pl.ds(pl.multiple_of(shard * shard_rows, 128), shard_rows)
        return dot(normed[:, at], weights[i, shard])

    moves = []
    first.arrived()
    for h in range(1, n):
        first.hop(h)
    for i, load in enumerate(loads[:3]):
        if i == 0:
            first.wait()
        else:
            load.wait_own()
        acc[...] = term(i, spot.shard)
        acc[...] += term(i, spot.mate)
        keep.step()
        if i:
            load.pass_on()
        if i == 2:
            for spread in spreads[:2]:
                spread.start()
            loads[3].start_far()
            loads[4].start_far()
            spreads[0].start_direct()
            for later in loads[3:] + spreads[:2]:
                later.start_near()
        keep.step()
        for d in range(1, spot.chips):
            acc[...] += term(i, lax.rem(spot.shard - 2 * d + shards, shards))
        if i:
            load.wait_near()
        for d in range(1, spot.chips):
            acc[...] += term(i, lax.rem(spot.mate - 2 * d + shards, shards))
        for k in range(n):
            for s in range(seqs):
                staged[i, k, s] = acc[s * part : (s + 1) * part, k * cols : (k + 1) * cols].astype(BF16)
        for d in range(1, n):
            peer = lax.rem(me + d, n)
            move = remote(
                staged.at[i, peer], pieces.at[i, me], head_send.at[i, d], head_recv.at[i, d], {"ctx": peer}
            )
            move.start()
            moves.append(move)
        pieces[i, me] = staged[i, me]
    outs = [
        pltpu.make_async_copy(weights.at[i], full, out_sem.at[i])
        for i, full in enumerate((full_q, full_k, full_v, full_o))
    ]
    for copy in outs[:3]:
        copy.start()
    flip(normed[...], left_one)
    spreads[0].arrived()
    spreads[1].arrived()
    flip(cotangent[...], left_g)
    for move in moves:
        move.wait_recv()
    loads[3].wait_own()
    outs.append(pltpu.make_async_copy(pieces, pieces_out, out_sem.at[4]))
    outs[4].start()

    def back(s, at, to):
        return remote(mixed.at[s, at], heads_in.at[me, s], back_send.at[s, at], back_recv.at[s, me], {"ctx": to})

    def attend(s, a):
        step = s * n + a
        lane = lax.broadcasted_iota(jnp.int32, (part, lanes), 1)
        log_total = jnp.zeros((part, lanes), F32)
        for group in range(cols // lanes):
            span = slice(group * lanes, (group + 1) * lanes)
            result = jnp.zeros((part, lanes), F32)
            for j in range(per):
                head = group * per + j
                mask = (lane >= j * head_dim) & (lane < (j + 1) * head_dim)
                query = jnp.where(mask, pieces[0, a, s, :, span], 0)
                scores = jnp.concatenate(
                    [
                        contract_cols(query, pieces[1, b, s, :, span])
                        + bias[head, :, pl.ds(pl.multiple_of((n + b - a) * part, part), part)].astype(F32)
                        for b in range(n)
                    ],
                    axis=1,
                )
                peak = jnp.max(scores, axis=1, keepdims=True)
                expo = jnp.exp(scores - peak)
                total = jnp.sum(expo, axis=1, keepdims=True)
                probs = (expo * (1.0 / total)).astype(BF16)
                summed = sum(
                    dot(probs[:, b * part : (b + 1) * part], pieces[2, b, s, :, span]) for b in range(n)
                )
                result = jnp.where(mask, summed, result)
                log_total = jnp.where(lane == head, peak + jnp.log(total), log_total)
            mixed[s, a, :, span] = result.astype(BF16)
        lse[s, a] = log_total

        @pl.when(a != me)
        def _():
            back(s, a, a).start()

        @pl.when(a == me)
        def _():
            heads_in[a, s] = mixed[s, a]

        @pl.when(step == 1)
        def _():
            spreads[0].hop(1)

        @pl.when(step == 3)
        def _():
            loads[3].pass_on()

        @pl.when(step == 4)
        def _():
            spreads[1].hop(1)

    swaps = []

    def project(s):
        at = pl.ds(s * part, part)
        for d in range(1, n):
            peer = lax.rem(me + d, n)
            remote(
                mixed.at[s, 0], heads_in.at[peer, s], back_send.at[s, peer], back_recv.at[s, peer], {"ctx": peer}
            ).wait_recv()
        for k in range(n):
            attended[at, k * cols : (k + 1) * cols] = heads_in[k, s]
        for j in range(shards):
            normed[at, j * shard_rows : (j + 1) * shard_rows] = contract_cols(
                attended[at, :], weights[3, j]
            ).astype(BF16)
        swap = remote(normed.at[at], branch_in.at[s], swap_send.at[s], swap_recv.at[s], {"tp": 1 - spot.half})
        swap.start()
        swaps.append(swap)

    for s in range(seqs):
        pl.loop(0, n)(functools.partial(attend, s))
        if s == 0:
            loads[3].wait_near()
            outs[3].start()
            if n > 2:
                spreads[0].hop(2)
        project(s)
    if n > 2:
        spreads[1].hop(2)
    for h in range(3, n):
        for spread in spreads[:2]:
            spread.hop(h)
    loads[4].wait_own()
    loads[4].pass_on()
    spreads[0].pass_on()
    for s in range(seqs):
        swaps[s].wait_recv()

        @pl.loop(0, part // 64)
        def _(i):
            here = pl.ds(pl.multiple_of(i * 64, 64), 64)
            at = pl.ds(pl.multiple_of(s * part + i * 64, 64), 64)
            values = tokens[at, :].astype(F32) + (
                normed[at, :].astype(F32) + branch_in[s, here, :].astype(F32)
            )
            hidden[at, :] = values
            normed_two[at, :] = (values * rms_scale(values) * gains[1:2, :]).astype(BF16)

    flip(normed_two[...], left_two)
    loads[4].wait_near()
    for spread in spreads[:2]:
        spread.wait()
    for load in loads[1:]:
        load.wait_sent()
    for move in moves + swaps:
        move.wait_send()
    for s in range(seqs):
        for d in range(1, n):
            peer = lax.rem(me + d, n)
            back(s, peer, peer).wait_send()
    for copy in outs + flips[-1:]:
        copy.wait()


class Dims:
    def __init__(self, mesh, seqs, part, width, inner_width, units, heads, slots):
        self.mesh = shards, ctx, tp = tuple(mesh.shape[a] for a in ("shard", "ctx", "tp"))
        self.slots = slots
        self.n, self.seqs, self.part, self.width = ctx, seqs, part, width
        self.inner_width, self.units = inner_width, units
        self.head_dim = inner_width // heads
        self.cols, self.own_heads = inner_width // ctx, heads // ctx
        self.shards, self.shard_rows = shards, width // shards


def forward_call(dims):
    rows, width, n, part, seqs = dims.seqs * dims.part, dims.width, dims.n, dims.part, dims.seqs
    shards, shard_rows, inner, units = dims.shards, dims.shard_rows, dims.inner_width, dims.units
    lanes, span = 2 * dims.head_dim, 2 * n * part
    vmem, anywhere = pl.BlockSpec(memory_space=pltpu.VMEM), pl.BlockSpec(memory_space=pl.ANY)
    shape = jax.ShapeDtypeStruct
    dma = pltpu.SemaphoreType.DMA
    chips = shards // 2
    block = (seqs, part, dims.cols)
    return pl.pallas_call(
        functools.partial(forward_kernel, dims),
        in_specs=[vmem] * 4 + [anywhere] * 8,
        out_specs=[vmem] * 6 + [anywhere] * 11,
        out_shape=[
            shape((rows, width), F32),
            shape((rows, width), BF16),
            shape((rows, inner), BF16),
            shape((seqs, n, part, lanes), F32),
            shape((1, span), F32),
            shape((dims.own_heads, span), F32),
            shape((3, n) + block, BF16),
        ]
        + [shape((width, rows), BF16)] * 3
        + [shape((shards, shard_rows, inner), BF16)] * 4
        + [shape((shards, shard_rows, units), BF16)] * 3,
        scratch_shapes=[
            pltpu.VMEM((rows, width), BF16),
            pltpu.VMEM((width, rows), BF16),
            pltpu.VMEM((4, shards, shard_rows, inner), BF16),
            pltpu.VMEM((rows, inner), F32),
            pltpu.VMEM((dims.own_heads, part, span), BF16),
            pltpu.VMEM((3, n) + block, BF16),
            pltpu.VMEM((3, n) + block, BF16),
            pltpu.VMEM((seqs, n, part, dims.cols), BF16),
            pltpu.VMEM((n,) + block, BF16),
            pltpu.VMEM((part, span), F32),
            pltpu.VMEM((seqs, part, width), BF16),
            dma((7,)),
            dma((7, chips)),
            dma((7, chips)),
            dma((7, chips)),
            dma((7, chips)),
            dma((3, n)),
            dma((3, n)),
            dma((seqs, n)),
            dma((seqs, n)),
            pltpu.VMEM((shard_rows, units), BF16),
            pltpu.VMEM((2, 8, n * part), jnp.int32),
            dma((2,)),
            dma((2,)),
            dma((seqs,)),
            dma((seqs,)),
            dma((6,)),
        ]
        + [dma((3, chips, 2))] * 2
        + [dma((3, chips, n))] * 4
        + [dma((3, chips, n + 1))] * 2,
        compiler_params=pltpu.CompilerParams(
            vmem_limit_bytes=60 * 2**20, collective_id=0, has_side_effects=True
        ),
        name="forward",
    )


CHUNK = 512
SLOTS = 4
LAYER_STEPS = 4
INPUT_STEPS = 3


class Pump:
    def __init__(self, dims, spot, left, right, sources, from_heads, outs, buffers, sems, credits):
        self.dims, self.spot, self.left, self.right = dims, spot, left, right
        self.fed, self.attended = sources
        self.from_heads, self.outs = from_heads, outs
        self.core_out, self.core_in, self.far_out, self.far_in, self.line, self.line_in, self.across_in, self.done = buffers
        (
            self.right_sem, self.core_send, self.core_recv, self.far_send, self.far_recv, self.in_send, self.in_recv,
            self.across_send, self.across_recv, self.out_send, self.out_recv, self.fin_sem,
        ) = sems
        self.core_credit, self.far_credit, self.in_credit, self.across_credit, self.out_credit = credits
        units, heads = dims.units // CHUNK, dims.inner_width // CHUNK
        self.units, self.heads = units, heads
        self.early = 3 * units + heads
        self.total = 3 * units + 4 * heads
        self.bases = [(i * units, units) for i in range(3)]
        self.bases += [(3 * units + i * heads, heads) for i in range(4)]
        me, n = spot.me, dims.n
        middle = n // 2
        self.is_middle = (me == middle - 1) | (me == middle)
        self.is_end = (me == 0) | (me == n - 1)
        self.has_outer, self.has_inner = jnp.logical_not(self.is_end), jnp.logical_not(self.is_middle)
        low_side = me < middle
        self.facing = jnp.where(low_side, middle, middle - 1)
        toward, away = jnp.where(low_side, me + 1, me - 1), jnp.where(low_side, me - 1, me + 1)
        self.inner = jnp.where(self.is_middle, self.facing, toward)
        self.outer = jnp.where(self.is_end, self.inner, away)
        self.last = self.total + 10

    def core(self, c, k):
        return remote(
            self.core_out.at[lax.rem(c, 2)], self.core_in.at[k], self.core_send.at[lax.rem(c, 2)],
            self.core_recv.at[k], {"shard": self.spot.mate},
        )

    def far(self, k, d):
        return remote(
            self.far_out.at[lax.rem(k, 2), d - 1], self.far_in.at[k, d - 1], self.far_send.at[k, d - 1],
            self.far_recv.at[k, d - 1], {"shard": self.spot.away(d)},
        )

    def inward(self, k):
        half = k
        return remote(
            self.line.at[k], self.line_in.at[half], self.in_send.at[k], self.in_recv.at[half], {"ctx": self.inner}
        )

    def across(self, k):
        return remote(
            self.line.at[k], self.across_in.at[k], self.across_send.at[k],
            self.across_recv.at[k], {"ctx": self.facing},
        )

    def outward(self, k):
        return remote(
            self.done.at[k], self.done.at[k], self.out_send.at[k], self.out_recv.at[k], {"ctx": self.outer}
        )

    def spend(self, c, credit, slots=SLOTS):
        @pl.when(c >= slots)
        def _():
            pl.semaphore_wait(credit, 1)

    def give(self, c, credit, peer, slots=SLOTS):
        @pl.when(c + slots < self.total)
        def _():
            pl.semaphore_signal(credit, inc=1, device_id=peer, device_id_type=MESH)

    def term(self, c, shard, k):
        one = lambda b: jnp.where(c >= b, 1, 0)
        which = one(self.units) + one(3 * self.units) - 2 * one(self.early)
        rows = self.dims.shard_rows
        return dot(self.left[which, pl.ds(pl.multiple_of(shard * rows, rows), rows), :], self.right[k])

    def fetch(self, c):
        k, fed = lax.rem(c, SLOTS), 3 * self.units

        @pl.when(c < fed)
        def _():
            source = self.fed.at[c // self.units, lax.rem(c, self.units)]
            pltpu.make_async_copy(source, self.right.at[k], self.right_sem.at[k]).start()

        @pl.when((c >= fed) & (c < self.early))
        def _():
            at = pl.ds(pl.multiple_of((c - fed) * CHUNK, CHUNK), CHUNK)
            pltpu.make_async_copy(self.attended.at[:, at], self.right.at[k], self.right_sem.at[k]).start()

        @pl.when((c >= self.early) & (c < self.total))
        def _():
            dims = self.dims
            which, piece = (c - self.early) // self.heads, lax.rem(c - self.early, self.heads)
            per = CHUNK // dims.cols
            for i in range(per):
                for s in range(dims.seqs):
                    self.right[k, s * dims.part : (s + 1) * dims.part, i * dims.cols : (i + 1) * dims.cols] = (
                        self.from_heads[which, piece * per + i, s]
                    )

    def save(self, c, k):
        for (base, count), out in zip(self.bases, self.outs):
            @pl.when((c >= base) & (c < base + count))
            def _():
                at = pl.ds(pl.multiple_of((c - base) * CHUNK, CHUNK), CHUNK)
                pltpu.make_async_copy(self.done.at[k], out.at[:, at], self.fin_sem.at[k]).start()

    def settle(self, c, k):
        pltpu.make_async_copy(self.done.at[k], self.outs[0].at[:, pl.ds(0, CHUNK)], self.fin_sem.at[k]).wait()

        @pl.when(self.has_outer)
        def _():
            self.outward(k).wait_send()

        @pl.when(self.has_inner)
        def _():
            self.give(c, self.out_credit, {"ctx": self.inner})

    def deliver(self, c, k):
        @pl.when(self.has_inner)
        def _():
            self.outward(k).wait_recv()
            self.save(c, k)

            @pl.when(self.has_outer)
            def _():
                self.spend(c, self.out_credit)
                self.outward(k).start()

    def finish(self, c, k):
        @pl.when(self.is_middle)
        def _():
            self.across(k).wait_recv()
            self.across(k).wait_send()
            self.done[k] = (self.line[k].astype(F32) + self.across_in[k].astype(F32)).astype(BF16)
            self.give(c, self.across_credit, {"ctx": self.facing})
            self.save(c, k)

            @pl.when(self.has_outer)
            def _():
                self.spend(c, self.out_credit)
                self.outward(k).start()

        @pl.when(self.has_inner)
        def _():
            self.inward(k).wait_send()

    def collect(self, c, k):
        @pl.when(self.has_outer)
        def _():
            self.inward(k).wait_recv()
            self.line[k] = (self.line[k].astype(F32) + self.line_in[k].astype(F32)).astype(BF16)
            self.give(c, self.in_credit, {"ctx": self.outer})

        @pl.when(self.is_middle)
        def _():
            self.spend(c, self.across_credit)
            self.across(k).start()

        @pl.when(self.has_outer & self.has_inner)
        def _():
            self.spend(c, self.in_credit)
            self.inward(k).start()

    def own(self, c, k):
        total = self.term(c, self.spot.shard, k) + self.core_in[k, self.spot.chips - 1].astype(F32)
        for d in range(1, self.spot.chips):
            self.far(k, d).wait_send()
            self.far(k, d).wait_recv()
            total = total + self.far_in[k, d - 1].astype(F32)
        self.line[k] = total.astype(BF16)
        self.give(c, self.core_credit, {"shard": self.spot.mate})
        for d in range(1, self.spot.chips):
            sender = lax.rem(self.spot.shard - 2 * d + self.spot.shards, self.spot.shards)
            self.give(c, self.far_credit.at[d - 1], {"shard": sender})

        @pl.when(self.is_end & self.has_inner)
        def _():
            self.spend(c, self.in_credit)
            self.inward(k).start()

    def to_chips(self, c, k):
        self.core(c, k).wait_recv()
        self.core(c, k).wait_send()
        for d in range(1, self.spot.chips):
            pair = self.term(c, self.spot.away(d), k) + self.core_in[k, d - 1].astype(F32)
            self.far_out[lax.rem(k, 2), d - 1] = pair.astype(BF16)
            self.spend(c, self.far_credit.at[d - 1])
            self.far(k, d).start()

    def to_core(self, c, k):
        @pl.when(c < self.early)
        def _():
            pltpu.make_async_copy(self.fed.at[0, 0], self.right.at[k], self.right_sem.at[k]).wait()

        chips, half = self.spot.chips, lax.rem(c, 2)
        for d in range(1, chips + 1):
            shard = 2 * lax.rem(self.spot.chip + d, chips) + 1 - self.spot.core
            self.core_out[half, d - 1] = self.term(c, shard, k).astype(BF16)
        self.spend(c, self.core_credit)
        self.core(c, k).start()

    def step(self, t):
        def at(lag, stage):
            c = t - lag

            @pl.when((c >= 0) & (c < self.total))
            def _():
                stage(c, lax.rem(c, SLOTS))

        @pl.when(t < self.total)
        def _():
            self.fetch(t)

        at(10, self.settle)
        at(9, self.deliver)
        at(7, self.finish)
        at(5, self.collect)
        at(3, self.own)

        at(1, self.to_chips)
        at(0, self.to_core)

    def steps(self, first, last):
        @pl.loop(first, last)
        def _(t):
            self.step(t)


UNITS = 256


def geglu_both(gate, up, upstream):
    root, cube = 0.7978845608028654, 0.044715
    square = gate * gate
    bent = jnp.tanh(root * gate * (1.0 + cube * square))
    half = 0.5 * (1.0 + bent)
    gelu = gate * half
    slope = half + 0.5 * gate * (1.0 - bent * bent) * (root * (1.0 + 3.0 * cube * square))
    return gelu * up, upstream * up * slope, upstream * gelu


def backward_kernel(
    dims, gains, table, by_offset,
    tokens, lse_from, pieces_from, left_g, left_two, left_one, normed_two, attended, hidden, cotangent,
    wo, wq, wk, wv, wi0, wi1, wff,
    down_out, gate_out, up_out, o_out, q_out, k_out, v_out,
    layer_out, input_grad, grad_hidden, ffn_term, ffn_other, small_out,
    other_one, norm_gain, ffn_gain, table_out, small, small_in,
    left, right, core_out, core_in, far_out, far_in, line, line_in, across_in, done,
    fed, term, swap_in, grads, grads_out, grads_in,
    right_sem, core_send, core_recv, far_send, far_recv, in_send, in_recv, across_send, across_recv,
    out_send, out_recv, fin_sem, swap_send, swap_recv, head_send, head_recv, back_send, back_recv,
    one_send, one_recv, ffn_sem, local_sem, small_send, small_recv,
    core_credit, far_credit, in_credit, across_credit, out_credit,
):
    spot = Spot(*dims.mesh)
    n, seqs, part, cols, head_dim, width = dims.n, dims.seqs, dims.part, dims.cols, dims.head_dim, dims.width
    me, shards, shard_rows, units = spot.me, spot.shards, dims.shard_rows, dims.units
    rows = seqs * part
    lanes, per = 2 * head_dim, 2
    groups = cols // lanes
    span = table.shape[1]
    other_half = {"tp": 1 - spot.half}
    pump = Pump(
        dims, spot, left, right, (fed, attended), grads_in,
        (down_out, gate_out, up_out, o_out, q_out, k_out, v_out),
        (core_out, core_in, far_out, far_in, line, line_in, across_in, done),
        (
            right_sem, core_send, core_recv, far_send, far_recv, in_send, in_recv, across_send, across_recv,
            out_send, out_recv, fin_sem,
        ),
        (core_credit, far_credit, in_credit, across_credit, out_credit),
    )
    lefts = [
        pltpu.make_async_copy(source, left.at[i], local_sem.at[i])
        for i, source in ((0, left_g), (1, left_two), (0, left_one))
    ]
    all_here = spot.barrier()
    ffn_gain[...] = jnp.zeros_like(ffn_gain)
    norm_gain[...] = jnp.zeros_like(norm_gain)
    table_out[...] = jnp.zeros_like(table_out)

    def feed(weights, values, given, sem, value_sem):
        inputs = [
            pltpu.make_async_copy(normed_two, values, value_sem.at[0]),
            pltpu.make_async_copy(cotangent, given, value_sem.at[1]),
        ]

        def load(u):
            slot = lax.rem(u, 2)
            at = pl.ds(pl.multiple_of(u * UNITS, UNITS), UNITS)
            return [
                pltpu.make_async_copy(w.at[:, :, at], weights.at[slot, j], sem.at[slot, j])
                for j, w in enumerate((wi0, wi1, wff))
            ]

        for copy in load(0) + inputs:
            copy.start()
        for copy in inputs:
            copy.wait()
        for copy in lefts[:2]:
            copy.start()
        each = CHUNK // UNITS

        @pl.loop(0, units // CHUNK)
        def _(c):
            for i in range(each):
                u = c * each + i

                @pl.when(u + 1 < units // UNITS)
                def _():
                    for copy in load(u + 1):
                        copy.start()

                for copy in load(u):
                    copy.wait()
                slot = lax.rem(u, 2)
                gate = dot(values[...], weights[slot, 0].reshape(width, UNITS))
                up = dot(values[...], weights[slot, 1].reshape(width, UNITS))
                upstream = dot(given[...], weights[slot, 2].reshape(width, UNITS))
                for j, made in enumerate(geglu_both(gate, up, upstream)):
                    fed[j, c, :, i * UNITS : (i + 1) * UNITS] = made.astype(BF16)

            @pl.when(c == 0)
            def _():
                for copy in lefts[:2]:
                    copy.wait()
                all_here()

            pump.step(c)

    pl.run_scoped(
        feed,
        pltpu.VMEM((2, 3, shards, shard_rows, UNITS), BF16),
        pltpu.VMEM((rows, width), BF16),
        pltpu.VMEM((rows, width), BF16),
        pltpu.SemaphoreType.DMA((2, 3)),
        pltpu.SemaphoreType.DMA((2,)),
    )
    fed_steps = units // CHUNK

    def feed_terms(weights, block, sem, block_sem):
        def load(j, w, slot):
            return pltpu.make_async_copy(w.at[j], weights.at[slot], sem.at[slot])

        def product(slot, which):
            total = None
            for c in range(units // CHUNK):
                at = slice(c * CHUNK, (c + 1) * CHUNK)
                made = contract_cols(fed[which, c], weights[slot, :, at])
                total = made if total is None else total + made
            return total

        def columns(j):
            return pl.ds(pl.multiple_of(j * shard_rows, shard_rows), shard_rows)

        load(0, wi0, 0).start()
        load(0, wi1, 1).start()

        @pl.loop(0, shards)
        def _(j):
            total = None
            for slot, w in enumerate((wi0, wi1)):
                load(j, w, slot).wait()
                made = product(slot, 1 + slot)
                total = made if total is None else total + made

                @pl.when(j + 1 < shards)
                def _():
                    load(j + 1, w, slot).start()

            for s in range(seqs):
                term[s, :, columns(j)] = total[s * part : (s + 1) * part].astype(BF16)

            @pl.when(j == 1)
            def _():
                pump.step(fed_steps)

        for swap in swaps:
            swap.start()
        load(0, wff, 0).start()
        pump.steps(fed_steps + 1, fed_steps + 2)

        @pl.loop(0, shards)
        def _(j):
            slot = lax.rem(j, 2)

            @pl.when(j + 1 < shards)
            def _():
                load(j + 1, wff, 1 - slot).start()

            load(j, wff, slot).wait()
            block[...] = product(slot, 0).astype(BF16)
            copy = pltpu.make_async_copy(block, ffn_term.at[:, columns(j)], block_sem.at[0])
            copy.start()
            copy.wait()

            @pl.when(j == 1)
            def _():
                pump.step(fed_steps + 2)

        pump.steps(fed_steps + 3, fed_steps + 4)

    swaps = [
        remote(term.at[s], swap_in.at[s], swap_send.at[s], swap_recv.at[s], other_half) for s in range(seqs)
    ]
    pl.run_scoped(
        feed_terms,
        pltpu.VMEM((2, shard_rows, units), BF16),
        pltpu.VMEM((rows, shard_rows), BF16),
        pltpu.SemaphoreType.DMA((2,)),
        pltpu.SemaphoreType.DMA((1,)),
    )
    so_far = fed_steps + 4

    def head_move(s, peer):
        return remote(
            grads_out.at[0, peer, s], grads.at[me, s], head_send.at[s, peer], head_recv.at[s, me], {"ctx": peer}
        )

    def head_wait(s, peer):
        remote(
            grads_out.at[0, peer, s], grads.at[peer, s], head_send.at[s, peer], head_recv.at[s, peer], {"ctx": peer}
        ).wait_recv()

    def second_norm(s, weights, values, given, own, sem):
        at = pl.ds(s * part, part)
        copies = [
            pltpu.make_async_copy(hidden.at[at, :], values, sem.at[0]),
            pltpu.make_async_copy(cotangent.at[at, :], given, sem.at[1]),
        ]
        for copy in copies:
            copy.start()
        for copy in copies:
            copy.wait()
        swaps[s].wait_recv()

        @pl.loop(0, part // 64)
        def _(i):
            here = pl.ds(pl.multiple_of(i * 64, 64), 64)
            h = values[here, :]
            grad = term[s, here, :].astype(F32) + swap_in[s, here, :].astype(F32)
            scale = rms_scale(h)
            ffn_gain[...] += jnp.sum(grad * h * scale, axis=0, keepdims=True)
            total = given[here, :].astype(F32) + rms_back(h, scale, gains[1:2, :], grad)
            values[here, :] = total
            own[here, :] = total.astype(BF16)

        saved = pltpu.make_async_copy(values, grad_hidden.at[at, :], sem.at[0])
        saved.start()
        total = dot(own[:, :shard_rows], weights[0])
        for j in range(1, shards):
            total += dot(own[:, j * shard_rows : (j + 1) * shard_rows], weights[j])
        for k in range(n):
            grads_out[0, k, s] = total[:, k * cols : (k + 1) * cols].astype(BF16)
        for d in range(1, n):
            head_move(s, lax.rem(me + d, n)).start()
        grads[me, s] = grads_out[0, me, s]
        left[2, :, s * part : (s + 1) * part] = own[...].T
        saved.wait()

    def second_norms(weights, values, given, own, sem):
        load = pltpu.make_async_copy(wo, weights, sem.at[3])
        load.start()
        load.wait()
        for s in range(seqs):
            second_norm(s, weights, values, given, own, sem)
            if s == 0:
                pump.steps(so_far, so_far + 1)

    pl.run_scoped(
        second_norms,
        pltpu.VMEM((shards, shard_rows, dims.inner_width), BF16),
        pltpu.VMEM((part, width), F32),
        pltpu.VMEM((part, width), BF16),
        pltpu.VMEM((part, width), BF16),
        pltpu.SemaphoreType.DMA((4,)),
    )
    ffn_swap = remote(ffn_term, ffn_other, ffn_sem.at[0], ffn_sem.at[1], other_half)
    ffn_swap.start()
    pump.steps(so_far + 1, so_far + 2)
    so_far += 2

    def back_move(j, s, peer):
        return remote(
            grads_out.at[j, peer, s], grads_in.at[j, me, s], back_send.at[j, s, peer], back_recv.at[j, s, me],
            {"ctx": peer},
        )

    def back_wait(j, s, peer):
        remote(
            grads_out.at[j, peer, s], grads_in.at[j, peer, s], back_send.at[j, s, peer], back_recv.at[j, s, peer],
            {"ctx": peer},
        ).wait_recv()

    def attention(pieces, lse, bias, sums, grad_k, grad_v, sem):
        @pl.loop(0, seqs * groups * n)
        def _(i):
            a, group, s = lax.rem(i, n), lax.rem(i // n, groups), i // (n * groups)
            at = pl.ds(pl.multiple_of(group * lanes, lanes), lanes)

            @pl.when((a == 0) & (group == 0))
            def _():
                here = [
                    pltpu.make_async_copy(pieces_from.at[:, :, s], pieces, sem.at[0]),
                    pltpu.make_async_copy(lse_from.at[s], lse, sem.at[1]),
                ]
                for copy in here:
                    copy.start()
                for copy in here:
                    copy.wait()
                for d in range(1, n):
                    head_wait(s, lax.rem(me + d, n))
                    head_move(s, lax.rem(me + d, n)).wait_send()

            @pl.when(a == 0)
            def _():
                for j in range(per):
                    bias_rows(table[pl.ds(group * per + j, 1), :], sums.at[j])
                bias[...] = sums[...].astype(BF16)
                sums[...] = jnp.zeros_like(sums)
                grad_k[...] = jnp.zeros_like(grad_k)
                grad_v[...] = jnp.zeros_like(grad_v)

            lane = lax.broadcasted_iota(jnp.int32, (part, lanes), 1)
            result = jnp.zeros((part, lanes), F32)
            for j in range(per):
                mask = (lane >= j * head_dim) & (lane < (j + 1) * head_dim)
                query = jnp.where(mask, pieces[0, a, :, at], 0)
                upstream = jnp.where(mask, grads[a, s, :, at], 0)
                log_total = jnp.sum(jnp.where(lane == group * per + j, lse[a], 0.0), axis=1, keepdims=True)
                windows = [pl.ds(pl.multiple_of((n + b - a) * part, part), part) for b in range(n)]
                probs, grad_probs = [], []
                for b in range(n):
                    scores = contract_cols(query, pieces[1, b, :, at]) + bias[j, :, windows[b]].astype(F32)
                    probs.append(jnp.exp(scores - log_total))
                    grad_probs.append(contract_cols(upstream, pieces[2, b, :, at]))
                delta = sum(jnp.sum(g * p, axis=1, keepdims=True) for g, p in zip(grad_probs, probs))
                summed = None
                for b in range(n):
                    grad_scores = (probs[b] * (grad_probs[b] - delta)).astype(BF16)
                    sums[j, :, windows[b]] += grad_scores.astype(F32)
                    product = dot(grad_scores, pieces[1, b, :, at])
                    summed = product if summed is None else summed + product
                    grad_k[b] += contract_rows(grad_scores, query)
                    grad_v[b] += contract_rows(probs[b].astype(BF16), upstream)
                result = jnp.where(mask, summed, result)
            grads_out[0, a, s, :, at] = result.astype(BF16)

            @pl.when(a == n - 1)
            def _():
                for b in range(n):
                    grads_out[1, b, s, :, at] = grad_k[b].astype(BF16)
                    grads_out[2, b, s, :, at] = grad_v[b].astype(BF16)
                for j in range(per):
                    table_out[pl.ds(group * per + j, 1), :] += diagonal_sums(sums.at[j])

            @pl.when((a == n - 1) & (group == groups - 1))
            def _():
                for j in range(3):
                    for d in range(1, n):
                        back_move(j, s, lax.rem(me + d, n)).start()
                    grads_in[j, me, s] = grads_out[j, me, s]

            @pl.when(a == n - 1)
            def _():
                pump.step(so_far + i // n)

    pl.run_scoped(
        attention,
        pltpu.VMEM((3, n, part, cols), BF16),
        pltpu.VMEM((n, part, lanes), F32),
        pltpu.VMEM((per, part, span), BF16),
        pltpu.VMEM((per, part, span), F32),
        pltpu.VMEM((n, part, lanes), F32),
        pltpu.VMEM((n, part, lanes), F32),
        pltpu.SemaphoreType.DMA((2,)),
    )
    so_far += seqs * groups
    lefts[2].start()
    lefts[2].wait()
    pump.steps(so_far, so_far + 1)
    so_far += 1
    assert so_far <= pump.early
    for s in range(seqs):
        for j in range(3):
            for d in range(1, n):
                back_wait(j, s, lax.rem(me + d, n))

    for copy in swaps:
        copy.wait_send()

    def first_norm_terms(weights, values, sem):
        def load(shard):
            return [
                pltpu.make_async_copy(w.at[shard], weights.at[shard % 2, j], sem.at[shard % 2, j])
                for j, w in enumerate((wq, wk, wv))
            ]

        for copy in load(0):
            copy.start()
        for j in range(3):
            for s in range(seqs):
                for k in range(n):
                    values[j, s * part : (s + 1) * part, k * cols : (k + 1) * cols] = grads_in[j, k, s]
        for shard in range(shards):
            if shard + 1 < shards:
                for copy in load(shard + 1):
                    copy.start()
            for copy in load(shard):
                copy.wait()
            total = contract_cols(values[0], weights[shard % 2, 0])
            total += contract_cols(values[1], weights[shard % 2, 1])
            total += contract_cols(values[2], weights[shard % 2, 2])
            for s in range(seqs):
                term[s, :, shard * shard_rows : (shard + 1) * shard_rows] = (
                    total[s * part : (s + 1) * part].astype(BF16)
                )

    pl.run_scoped(
        first_norm_terms,
        pltpu.VMEM((2, 3, shard_rows, dims.inner_width), BF16),
        pltpu.VMEM((3, seqs * part, dims.inner_width), BF16),
        pltpu.SemaphoreType.DMA((2, 3)),
    )
    ones = [
        remote(term.at[s], other_one.at[s], one_send.at[s], one_recv.at[s], other_half) for s in range(seqs)
    ]
    for swap in ones:
        swap.start()
    pump.steps(so_far, so_far + LAYER_STEPS)
    so_far += LAYER_STEPS
    ffn_swap.wait_recv()

    def layer_output(values, own, other, sem):
        for s in range(seqs):
            at = pl.ds(s * part, part)
            copies = [
                pltpu.make_async_copy(source.at[at, :], to, sem.at[i])
                for i, (source, to) in enumerate(((hidden, values), (ffn_term, own), (ffn_other, other)))
            ]
            for copy in copies:
                copy.start()
            for copy in copies:
                copy.wait()

            @pl.loop(0, part // 64)
            def _(i):
                here = pl.ds(pl.multiple_of(i * 64, 64), 64)
                total = own[here, :].astype(F32) + other[here, :].astype(F32)
                own[here, :] = (values[here, :] + total).astype(BF16)

            saved = pltpu.make_async_copy(own, layer_out.at[at, :], sem.at[0])
            saved.start()
            saved.wait()

    pl.run_scoped(
        layer_output,
        pltpu.VMEM((part, width), F32),
        pltpu.VMEM((part, width), BF16),
        pltpu.VMEM((part, width), BF16),
        pltpu.SemaphoreType.DMA((3,)),
    )
    pump.steps(so_far, so_far + INPUT_STEPS)
    so_far += INPUT_STEPS

    def first_norm_back(values, given, sem):
        for s in range(seqs):
            at = pl.ds(s * part, part)
            copies = [
                pltpu.make_async_copy(source.at[at, :], to, sem.at[i])
                for i, (source, to) in enumerate(((grad_hidden, values), (tokens, given)))
            ]
            for copy in copies:
                copy.start()
            for copy in copies:
                copy.wait()
            ones[s].wait_recv()

            @pl.loop(0, part // 64)
            def _(i):
                here = pl.ds(pl.multiple_of(i * 64, 64), 64)
                x = given[here, :].astype(F32)
                grad = term[s, here, :].astype(F32) + other_one[s, here, :].astype(F32)
                scale = rms_scale(x)
                norm_gain[...] += jnp.sum(grad * x * scale, axis=0, keepdims=True)
                values[here, :] += rms_back(x, scale, gains[0:1, :], grad)

            saved = pltpu.make_async_copy(values, input_grad.at[at, :], sem.at[0])
            saved.start()
            saved.wait()

    pl.run_scoped(
        first_norm_back,
        pltpu.VMEM((part, width), F32),
        pltpu.VMEM((part, width), BF16),
        pltpu.SemaphoreType.DMA((2,)),
    )

    lines, slots = width // 128, small.shape[1] - 2 * (width // 128)
    for i in range(lines):
        small[0, i : i + 1, :] = norm_gain[:, i * 128 : (i + 1) * 128]
        small[0, lines + i : lines + i + 1, :] = ffn_gain[:, i * 128 : (i + 1) * 128]
    hot = by_offset[...] == lax.broadcasted_iota(jnp.int32, (slots, span), 0).astype(F32)
    lane = lax.broadcasted_iota(jnp.int32, (slots, 128), 1)
    table_part = jnp.zeros((slots, 128), F32)
    for head in range(dims.own_heads):
        column = jnp.sum(jnp.where(hot, table_out[head : head + 1, :], 0.0), axis=1, keepdims=True)
        table_part = jnp.where(lane == me * dims.own_heads + head, column, table_part)
    small[0, 2 * lines :, :] = table_part
    partners = []
    for axis, at, count in (("shard", spot.shard, shards), ("ctx", me, n)):
        step = 1
        while step < count:
            partners.append({axis: at + step * (1 - 2 * lax.rem(at // step, 2))})
            step *= 2
    for i, partner in enumerate(partners):
        copy = remote(small.at[i], small_in.at[i], small_send.at[i], small_recv.at[i], partner)
        copy.start()
        pump.steps(so_far, so_far + 1)
        so_far += 1
        copy.wait_recv()
        copy.wait_send()
        small[i + 1] = small[i] + small_in[i]
    small_out[...] = small[len(partners)]
    pump.steps(so_far, pump.last)
    for copy in ones + [ffn_swap]:
        copy.wait_send()
    for s in range(seqs):
        for d in range(1, n):
            peer = lax.rem(me + d, n)
            for j in range(3):
                back_move(j, s, peer).wait_send()


def backward_call(dims):
    rows, width, n, part, seqs = dims.seqs * dims.part, dims.width, dims.n, dims.part, dims.seqs
    shards, shard_rows, inner, units, cols = dims.shards, dims.shard_rows, dims.inner_width, dims.units, dims.cols
    span, chips = 2 * n * part, dims.shards // 2
    vmem, anywhere = pl.BlockSpec(memory_space=pltpu.VMEM), pl.BlockSpec(memory_space=pl.ANY)
    shape, dma, regular = jax.ShapeDtypeStruct, pltpu.SemaphoreType.DMA, pltpu.SemaphoreType.REGULAR
    far = max(chips - 1, 1)
    stages = (shards * n).bit_length() - 1
    lines = 2 * (width // 128) + dims.slots
    block = (shard_rows, CHUNK)
    return pl.pallas_call(
        functools.partial(backward_kernel, dims),
        in_specs=[vmem] * 3 + [anywhere] * 17,
        out_specs=[anywhere] * 12 + [vmem],
        out_shape=[shape((shard_rows, units), BF16)] * 3
        + [shape((shard_rows, inner), BF16)] * 4
        + [
            shape((rows, width), BF16),
            shape((rows, width), F32),
            shape((rows, width), F32),
            shape((rows, width), BF16),
            shape((rows, width), BF16),
            shape((lines, 128), F32),
        ],
        scratch_shapes=[
            pltpu.VMEM((seqs, part, width), BF16),
            pltpu.VMEM((1, width), F32),
            pltpu.VMEM((1, width), F32),
            pltpu.VMEM((dims.own_heads, span), F32),
            pltpu.VMEM((stages + 1, lines, 128), F32),
            pltpu.VMEM((stages, lines, 128), F32),
            pltpu.VMEM((3, width, rows), BF16),
            pltpu.VMEM((SLOTS, rows, CHUNK), BF16),
            pltpu.VMEM((2, chips) + block, BF16),
            pltpu.VMEM((SLOTS, chips) + block, BF16),
            pltpu.VMEM((2, far) + block, BF16),
            pltpu.VMEM((SLOTS, far) + block, BF16),
            pltpu.VMEM((SLOTS,) + block, BF16),
            pltpu.VMEM((SLOTS,) + block, BF16),
            pltpu.VMEM((SLOTS,) + block, BF16),
            pltpu.VMEM((SLOTS,) + block, BF16),
            pltpu.VMEM((3, units // CHUNK, rows, CHUNK), BF16),
            pltpu.VMEM((seqs, part, width), BF16),
            pltpu.VMEM((seqs, part, width), BF16),
            pltpu.VMEM((n, seqs, part, cols), BF16),
            pltpu.VMEM((3, n, seqs, part, cols), BF16),
            pltpu.VMEM((3, n, seqs, part, cols), BF16),
            dma((SLOTS,)),
            dma((2,)),
            dma((SLOTS,)),
            dma((SLOTS, far)),
            dma((SLOTS, far)),
        ]
        + [dma((SLOTS,))] * 7
        + [dma((seqs,))] * 2
        + [dma((seqs, n))] * 2
        + [dma((3, seqs, n))] * 2
        + [dma((seqs,))] * 2
        + [dma((2,)), dma((4,)), dma((stages,)), dma((stages,))]
        + [regular, regular((far,)), regular, regular, regular],
        compiler_params=pltpu.CompilerParams(
            vmem_limit_bytes=62 * 2**20, collective_id=1, has_side_effects=True
        ),
        name="backward",
    )


TILE = 256


def finish_kernel(count, firsts, *refs):
    sources, outs = refs[:count], refs[count : 2 * count]
    taken, made = refs[2 * count : 3 * count], refs[3 * count : 4 * count]
    take_sem, save_sem = refs[4 * count :]
    sizes = [min(out.shape[0], TILE) for out in outs]
    tiles = [out.shape[0] // size for out, size in zip(outs, sizes)]

    def at(j, i, first=0):
        return pl.ds(pl.multiple_of(first + i * sizes[j], 16), sizes[j])

    def take(j, i):
        return pltpu.make_async_copy(sources[j].at[at(j, i, firsts[j])], taken[j].at[at(j, i)], take_sem.at[j, i])

    def save(j, i):
        return pltpu.make_async_copy(made[j].at[at(j, i)], outs[j].at[at(j, i)], save_sem.at[j, i])

    for j in range(count):
        @pl.loop(0, tiles[j])
        def _(i):
            take(j, i).start()

    for j in range(count):
        @pl.loop(0, tiles[j])
        def _(i):
            take(j, i).wait()
            if made[j].dtype != taken[j].dtype:
                made[j][at(j, i), :] = taken[j][at(j, i), :].astype(made[j].dtype)
            save(j, i).start()

    for j in range(count):
        @pl.loop(0, tiles[j])
        def _(i):
            save(j, i).wait()


def finish(jobs):
    count = len(jobs)
    sources, firsts, lengths, types = zip(*jobs)
    shapes = [(length, source.shape[1]) for source, length in zip(sources, lengths)]
    taken = [pltpu.VMEM(shape, source.dtype) for shape, source in zip(shapes, sources)]
    made = [pltpu.VMEM(shape, kind) for shape, kind in zip(shapes, types)]
    same = [source.dtype == kind for source, kind in zip(sources, types)]
    tiles = max(-(-length // TILE) for length in lengths)

    def kernel(*refs):
        refs = list(refs)
        made_at = iter(refs[3 * count : -2])
        full = [refs[2 * count + j] if same[j] else next(made_at) for j in range(count)]
        finish_kernel(count, firsts, *refs[: 3 * count], *full, *refs[-2:])

    return pl.pallas_call(
        kernel,
        in_specs=[pl.BlockSpec(memory_space=pl.ANY)] * count,
        out_specs=[pl.BlockSpec(memory_space=pl.ANY)] * count,
        out_shape=[jax.ShapeDtypeStruct(shape, kind) for shape, kind in zip(shapes, types)],
        scratch_shapes=taken
        + [m for m, keep in zip(made, same) if not keep]
        + [pltpu.SemaphoreType.DMA((count, tiles))] * 2,
        compiler_params=pltpu.CompilerParams(vmem_limit_bytes=56 * 2**20),
        name="finish",
    )(*sources)


def per_device(
    mesh,
    tokens,
    cotangent,
    buckets,
    query_weight,
    key_weight,
    value_weight,
    output_weight,
    gate_weight,
    up_weight,
    down_weight,
    norm_gain,
    ffn_gain,
    bucket_bias_table,
):
    seqs, part, width = tokens.shape
    rows, inner_width = seqs * part, query_weight.shape[1]
    slots, heads = bucket_bias_table.shape
    dims = Dims(mesh, seqs, part, width, inner_width, gate_weight.shape[1], heads, slots)
    token_rows, upstream = tokens.reshape(rows, width), cotangent.reshape(rows, width)
    gains = jnp.stack([norm_gain, ffn_gain]).astype(F32)
    hidden, normed_two, attended, lse, by_offset, bias_table, pieces, *lefts_and_weights = forward_call(dims)(
        token_rows, upstream, gains, bucket_bias_table.astype(F32), buckets,
        query_weight, key_weight, value_weight, output_weight, gate_weight, up_weight, down_weight,
    )
    left_g, left_one, left_two, wq, wk, wv, wo, wi0, wi1, wff = lefts_and_weights
    *weight_grads, result, grad_inputs, unused, unused_own, unused_other, small = backward_call(dims)(
        gains, bias_table, by_offset,
        token_rows, lse, pieces, left_g, left_two, left_one, normed_two, attended, hidden, upstream,
        wo, wq, wk, wv, wi0, wi1, wff,
    )
    lines = width // 128
    jobs = [(g, 0, g.shape[0], F32) for g in weight_grads]
    jobs += [(grad_inputs, 0, rows, F32), (result, 0, rows, BF16)]
    jobs += [(small, 0, lines, F32), (small, lines, lines, F32), (small, 2 * lines, slots, F32)]
    *weight_grads, grad_inputs, result, norm_gain_grad, ffn_gain_grad, table_grad = finish(jobs)
    grad_down_w, grad_gate_w, grad_up_w, grad_output_w, grad_query_w, grad_key_w, grad_value_w = weight_grads
    return (
        result.reshape(seqs, part, width),
        grad_inputs.reshape(seqs, part, width),
        grad_query_w,
        grad_key_w,
        grad_value_w,
        grad_output_w,
        grad_gate_w,
        grad_up_w,
        grad_down_w,
        norm_gain_grad.reshape(width),
        ffn_gain_grad.reshape(width),
        table_grad[:, :heads],
    )


def solution(mesh):
    rows, weights = P("shard", "ctx", None), P("shard", "tp")
    return jax.shard_map(
        functools.partial(per_device, mesh),
        mesh=mesh,
        in_specs=(rows, rows, P("ctx", None)) + (weights,) * 7 + (P(), P(), P(None, "tp")),
        out_specs=(rows, rows) + (weights,) * 7 + (P(), P(), P(None, "tp")),
        check_vma=False,
    )
```

```python
import functools

import jax
import jax.numpy as jnp
from jax import lax
from jax.experimental import pallas as pl
from jax.experimental.pallas import tpu as pltpu
from jax.sharding import PartitionSpec as P

F32 = jnp.float32
BF16 = jnp.bfloat16
VMEM_LIMIT = 48 * 2**20


def contract_rows(left, right):
    return lax.dot_general(left, right, (((0,), (0,)), ((), ())), preferred_element_type=F32)


def contract_cols(left, right):
    return lax.dot_general(left, right, (((1,), (1,)), ((), ())), preferred_element_type=F32)


def dot(left, right):
    return jnp.dot(left, right, preferred_element_type=F32)


def rms_scale(values):
    return lax.rsqrt(jnp.mean(values * values, axis=-1, keepdims=True) + 1e-06)


def rms_back(values, scale, gain, upstream):
    weighted = upstream * gain
    inner_average = jnp.mean(values * weighted, axis=-1, keepdims=True)
    return scale * weighted - values * scale * scale * scale * inner_average


def bias_rows(table_row, out):
    span = out.shape[1]
    out[0:1, :] = table_row
    done = 1
    while done < out.shape[0]:
        out[done : 2 * done, :] = pltpu.roll(out[0:done, :], done, 1)
        done *= 2
    del span


def diagonal_sums(acc):
    rows, span = acc.shape
    total = acc[...]
    while rows > 1:
        rows //= 2
        total = total[:rows] + pltpu.roll(total[rows:], span - rows, 1)
    return total


MESH = pl.DeviceIdType.MESH


class Spot:
    def __init__(self, shards, ctx, tp):
        self.shards, self.chips, self.n, self.tps = shards, shards // 2, ctx, tp
        self.shard, self.me, self.half = (lax.axis_index(a) for a in ("shard", "ctx", "tp"))
        self.chip, self.core = self.shard // 2, lax.rem(self.shard, 2)
        self.mate = 2 * self.chip + 1 - self.core

    def away(self, d):
        return lax.rem(self.shard + 2 * d, self.shards)

    def barrier(self):
        peers = [{"shard": self.mate}] + [{"shard": self.away(d)} for d in range(1, self.chips)]
        peers += [{"ctx": lax.rem(self.me + d, self.n)} for d in range(1, self.n)]
        peers += [{"tp": 1 - self.half}]
        semaphore = pltpu.get_barrier_semaphore()
        for peer in peers:
            pl.semaphore_signal(semaphore, inc=1, device_id=peer, device_id_type=MESH)
        return lambda: pl.semaphore_wait(semaphore, len(peers))


def remote(src, dst, send, recv, peer):
    return pltpu.make_async_remote_copy(
        src_ref=src, dst_ref=dst, send_sem=send, recv_sem=recv, device_id=peer, device_id_type=MESH
    )


class Keep:
    def __init__(self, jobs, room, sem):
        self.halves = []
        for i, (own, full) in enumerate(jobs):
            self.halves.append(pltpu.make_async_copy(own, room, sem.at[0]))
            self.halves.append(pltpu.make_async_copy(room, full, sem.at[1]))
        self.at = 0
        self.halves[0].start()

    def step(self):
        if self.at < len(self.halves):
            self.halves[self.at].wait()
            self.at += 1
            if self.at < len(self.halves):
                self.halves[self.at].start()

    def start(self):
        pass

    def wait(self):
        while self.at < len(self.halves):
            self.step()


class Gather:
    def __init__(self, spot, own, full, sems, keep=None):
        self.spot, self.own, self.full = spot, own, full
        self.local, self.send, self.recv, self.on_send, self.on_recv = sems
        spot_shard = spot.shard
        self.keep = keep or pltpu.make_async_copy(own, full.at[spot_shard], self.local)
        self.far = [
            remote(own, full.at[spot_shard], self.send.at[d], self.recv.at[d], {"shard": spot.away(d)})
            for d in range(1, spot.chips)
        ]
        mate = {"shard": spot.mate}
        self.near = [remote(own, full.at[spot_shard], self.on_send.at[0], self.on_recv.at[0], mate)]
        for d in range(1, spot.chips):
            at = full.at[lax.rem(spot.shard - 2 * d + spot.shards, spot.shards)]
            self.near.append(remote(at, at, self.on_send.at[d], self.on_recv.at[d], mate))

    def start_far(self):
        for copy in self.far:
            copy.start()

    def start_near(self):
        self.keep.start()
        self.near[0].start()

    def pass_on(self):
        for d, copy in enumerate(self.far, 1):
            copy.wait_recv()
            self.near[d].start()

    def wait_own(self):
        self.keep.wait()
        self.near[0].wait_recv()

    def wait_near(self):
        for copy in self.near[1:]:
            copy.wait_recv()

    def wait_sent(self):
        for copy in self.far + self.near:
            copy.wait_send()


class Spread:
    def __init__(self, spot, own, full, keep, sems, direct=0):
        self.spot, self.own, self.full, self.keep, self.direct = spot, own, full, keep, direct
        (
            self.far_send, self.far_recv, self.right_send, self.right_recv, self.left_send, self.left_recv,
            self.mate_send, self.mate_recv,
        ) = sems
        self.part = (full.shape[1] - direct) // spot.n
        n, me = spot.n, spot.me
        self.near = remote(
            own, full.at[spot.shard], self.mate_send.at[0, 0], self.mate_recv.at[0, 0], {"shard": spot.mate}
        )
        mine = self.at(me)
        self.far = [
            remote(
                own.at[mine], full.at[spot.shard, mine], self.far_send.at[d, 0], self.far_recv.at[d, 0],
                {"shard": spot.away(d)},
            )
            for d in range(1, spot.chips)
        ]
        whole = pl.ds(0, direct)
        self.far_direct = [
            remote(
                own.at[whole], full.at[spot.shard, whole], self.far_send.at[d, 1], self.far_recv.at[d, 1],
                {"shard": spot.away(d)},
            )
            for d in range(1, spot.chips)
            if direct
        ]
        self.can_right, self.can_left = me + 1 < n, me > 0

    def at(self, z):
        return pl.ds(pl.multiple_of(self.direct + z * self.part, 16), self.part)

    def source(self, d):
        return lax.rem(self.spot.shard - 2 * d + self.spot.shards, self.spot.shards)

    def piece(self, d, z):
        return self.full.at[self.source(d), self.at(z)]

    def tell_direct(self, d):
        at = self.full.at[self.source(d), pl.ds(0, self.direct)]
        n = self.spot.n
        return remote(at, at, self.mate_send.at[d, n], self.mate_recv.at[d, n], {"shard": self.spot.mate})

    def start_direct(self):
        for copy in self.far_direct:
            copy.start()

    def pass_on(self):
        for d, copy in enumerate(self.far_direct, 1):
            copy.wait_recv()
            self.tell_direct(d).start()

    def tell(self, d, z):
        at = self.piece(d, z)
        return remote(at, at, self.mate_send.at[d, z], self.mate_recv.at[d, z], {"shard": self.spot.mate})

    def right(self, d, h, z):
        at, to = self.piece(d, z), {"ctx": lax.rem(self.spot.me + 1, self.spot.n)}
        return remote(at, at, self.right_send.at[d, h], self.right_recv.at[d, h], to)

    def left(self, d, h, z):
        at, to = self.piece(d, z), {"ctx": lax.rem(self.spot.me - 1 + self.spot.n, self.spot.n)}
        return remote(at, at, self.left_send.at[d, h], self.left_recv.at[d, h], to)

    def pairs(self):
        return range(1, self.spot.chips)

    def start(self):
        for copy in self.far:
            copy.start()

    def start_near(self):
        self.near.start()

    def send_on(self, d, h, z, right, left):
        self.tell(d, z).start()
        if right:
            @pl.when(self.can_right)
            def _():
                self.right(d, h, z).start()

        if left:
            @pl.when(self.can_left)
            def _():
                self.left(d, h, z).start()

    def arrived(self):
        for d in self.pairs():
            self.far[d - 1].wait_recv()
            self.send_on(d, 1, self.spot.me, True, True)

    def hop(self, h):
        me, n = self.spot.me, self.spot.n
        for d in self.pairs():
            @pl.when(me - h >= 0)
            def _():
                self.right(d, h, me - h).wait_recv()
                self.send_on(d, h + 1, me - h, h + 1 < n, False)

            @pl.when(me + h < n)
            def _():
                self.left(d, h, me + h).wait_recv()
                self.send_on(d, h + 1, me + h, False, h + 1 < n)

    def wait(self):
        me, n = self.spot.me, self.spot.n
        self.keep.wait()
        self.near.wait_recv()
        self.near.wait_send()
        for d, copy in enumerate(self.far_direct, 1):
            copy.wait_send()
            self.tell_direct(d).wait_recv()
            self.tell_direct(d).wait_send()
        for d in self.pairs():
            self.far[d - 1].wait_send()
            for z in range(n):
                self.tell(d, z).wait_recv()
                self.tell(d, z).wait_send()
            for h in range(1, n):
                @pl.when((me - h + 1 >= 0) & self.can_right)
                def _():
                    self.right(d, h, me - h + 1).wait_send()

                @pl.when((me + h - 1 < n) & self.can_left)
                def _():
                    self.left(d, h, me + h - 1).wait_send()


def offset_buckets(dims, me, some_rows, out):
    part, reach = dims.part, dims.n * dims.part
    at = pl.ds(pl.multiple_of(me * part, part), part)
    later = some_rows[0, 0:1, at].astype(F32)
    earlier = some_rows[1, 7:8, at].astype(F32)
    lane = lax.broadcasted_iota(jnp.int32, (1, part), 1)
    out[:, : reach - part] = jnp.broadcast_to(earlier[:, :1], (1, reach - part))
    out[:, reach - part : reach] = jnp.where(lane == 0, earlier[:, :1], pltpu.roll(earlier, 1, 1))
    out[:, reach : reach + part] = later
    out[:, reach + part :] = jnp.broadcast_to(later[:, part - 1 :], (1, reach - part))


def forward_kernel(
    dims, tokens, cotangent, gains, table, buckets, wq, wk, wv, wo, wi0, wi1, wff,
    hidden, normed_two, attended, lse, by_offset, bias_table, pieces_out, left_g, left_one, left_two,
    full_q, full_k, full_v, full_o, full_0, full_1, full_2,
    normed, flipped, weights, acc, bias, staged, pieces, mixed, heads_in, rolled, branch_in,
    local_sem, far_send, far_recv, near_send, near_recv, head_send, head_recv, back_send, back_recv,
    room, some_rows, keep_sem, row_sem,
    swap_send, swap_recv, out_sem, *spread_sems,
):
    spot = Spot(*dims.mesh)
    n, seqs, part, cols, head_dim = dims.n, dims.seqs, dims.part, dims.cols, dims.head_dim
    me, shards = spot.me, spot.shards
    shard_rows = weights.shape[2]
    rows = seqs * part
    lanes = 2 * head_dim
    per = 2
    spot.barrier()()

    def gather(i, own, full, keep=None):
        sems = [local_sem.at[i], far_send.at[i], far_recv.at[i], near_send.at[i], near_recv.at[i]]
        return Gather(spot, own, full, sems, keep)

    loads = [None] + [gather(i, w, weights.at[i]) for i, w in ((1, wk), (2, wv), (3, wo))]
    keep = Keep(
        [(w, full.at[spot.shard]) for w, full in ((wi0, full_0), (wi1, full_1), (wff, full_2))], room, keep_sem
    )
    loads.append(gather(4, wi0, full_0, keep))
    spreads = [
        Spread(spot, own, full, keep, [sem.at[i] for sem in spread_sems], direct)
        for i, (own, full, direct) in enumerate(((wi1, full_1, shard_rows // 2), (wff, full_2, 0)))
    ]
    keep_first = pltpu.make_async_copy(wq, weights.at[0, spot.shard], local_sem.at[0])
    spreads.append(Spread(spot, wq, weights.at[0], keep_first, [sem.at[2] for sem in spread_sems]))
    flips = []

    def flip(value, out):
        if flips:
            flips[-1].wait()
        flipped[...] = value.T
        flips.append(pltpu.make_async_copy(flipped, out, out_sem.at[5]))
        flips[-1].start()

    first = spreads[2]
    first.start()
    for load in loads[1:3]:
        load.start_far()
    first.keep.start()
    first.start_near()
    for load in loads[1:3]:
        load.start_near()

    row_copies = [
        pltpu.make_async_copy(buckets.at[pl.ds(at, 8)], some_rows.at[i], row_sem.at[i])
        for i, at in enumerate((0, part - 8))
    ]
    for copy in row_copies:
        copy.start()

    @pl.loop(0, rows // 64)
    def _(i):
        at = pl.ds(pl.multiple_of(i * 64, 64), 64)
        values = tokens[at, :].astype(F32)
        normed[at, :] = (values * rms_scale(values) * gains[0:1, :]).astype(BF16)

    for copy in row_copies:
        copy.wait()
    offset_buckets(dims, me, some_rows, by_offset)
    slots = table.shape[0]
    hot = by_offset[...] == lax.broadcasted_iota(jnp.int32, (slots, by_offset.shape[1]), 0).astype(F32)
    lane = lax.broadcasted_iota(jnp.int32, table.shape, 1)
    for head in range(dims.own_heads):
        own = lane == me * dims.own_heads + head
        column = jnp.sum(jnp.where(own, table[...], 0.0), axis=1, keepdims=True)
        bias_table[head : head + 1, :] = jnp.sum(jnp.where(hot, column, 0.0), axis=0, keepdims=True)
        bias_rows(bias_table[head : head + 1, :], rolled)
        bias[head] = rolled[...].astype(BF16)

    def term(i, shard):
        at = pl.ds(pl.multiple_of(shard * shard_rows, 128), shard_rows)
        return dot(normed[:, at], weights[i, shard])

    moves = []
    first.arrived()
    for h in range(1, n):
        first.hop(h)
    for i, load in enumerate(loads[:3]):
        if i == 0:
            first.wait()
        else:
            load.wait_own()
        acc[...] = term(i, spot.shard)
        acc[...] += term(i, spot.mate)
        keep.step()
        if i:
            load.pass_on()
        if i == 2:
            for spread in spreads[:2]:
                spread.start()
            loads[3].start_far()
            loads[4].start_far()
            spreads[0].start_direct()
            for later in loads[3:] + spreads[:2]:
                later.start_near()
        keep.step()
        for d in range(1, spot.chips):
            acc[...] += term(i, lax.rem(spot.shard - 2 * d + shards, shards))
        if i:
            load.wait_near()
        for d in range(1, spot.chips):
            acc[...] += term(i, lax.rem(spot.mate - 2 * d + shards, shards))
        for k in range(n):
            for s in range(seqs):
                staged[i, k, s] = acc[s * part : (s + 1) * part, k * cols : (k + 1) * cols].astype(BF16)
        for d in range(1, n):
            peer = lax.rem(me + d, n)
            move = remote(
                staged.at[i, peer], pieces.at[i, me], head_send.at[i, d], head_recv.at[i, d], {"ctx": peer}
            )
            move.start()
            moves.append(move)
        pieces[i, me] = staged[i, me]
    outs = [
        pltpu.make_async_copy(weights.at[i], full, out_sem.at[i])
        for i, full in enumerate((full_q, full_k, full_v, full_o))
    ]
    for copy in outs[:3]:
        copy.start()
    flip(normed[...], left_one)
    spreads[0].arrived()
    spreads[1].arrived()
    flip(cotangent[...], left_g)
    for move in moves:
        move.wait_recv()
    loads[3].wait_own()
    outs.append(pltpu.make_async_copy(pieces, pieces_out, out_sem.at[4]))
    outs[4].start()

    def back(s, at, to):
        return remote(mixed.at[s, at], heads_in.at[me, s], back_send.at[s, at], back_recv.at[s, me], {"ctx": to})

    def attend(s, a):
        step = s * n + a
        lane = lax.broadcasted_iota(jnp.int32, (part, lanes), 1)
        log_total = jnp.zeros((part, lanes), F32)
        for group in range(cols // lanes):
            span = slice(group * lanes, (group + 1) * lanes)
            result = jnp.zeros((part, lanes), F32)
            for j in range(per):
                head = group * per + j
                mask = (lane >= j * head_dim) & (lane < (j + 1) * head_dim)
                query = jnp.where(mask, pieces[0, a, s, :, span], 0)
                scores = jnp.concatenate(
                    [
                        contract_cols(query, pieces[1, b, s, :, span])
                        + bias[head, :, pl.ds(pl.multiple_of((n + b - a) * part, part), part)].astype(F32)
                        for b in range(n)
                    ],
                    axis=1,
                )
                peak = jnp.max(scores, axis=1, keepdims=True)
                expo = jnp.exp(scores - peak)
                total = jnp.sum(expo, axis=1, keepdims=True)
                probs = (expo * (1.0 / total)).astype(BF16)
                summed = sum(
                    dot(probs[:, b * part : (b + 1) * part], pieces[2, b, s, :, span]) for b in range(n)
                )
                result = jnp.where(mask, summed, result)
                log_total = jnp.where(lane == head, peak + jnp.log(total), log_total)
            mixed[s, a, :, span] = result.astype(BF16)
        lse[s, a] = log_total

        @pl.when(a != me)
        def _():
            back(s, a, a).start()

        @pl.when(a == me)
        def _():
            heads_in[a, s] = mixed[s, a]

        @pl.when(step == 1)
        def _():
            spreads[0].hop(1)

        @pl.when(step == 3)
        def _():
            loads[3].pass_on()

        @pl.when(step == 4)
        def _():
            spreads[1].hop(1)

    swaps = []

    def project(s):
        at = pl.ds(s * part, part)
        for d in range(1, n):
            peer = lax.rem(me + d, n)
            remote(
                mixed.at[s, 0], heads_in.at[peer, s], back_send.at[s, peer], back_recv.at[s, peer], {"ctx": peer}
            ).wait_recv()
        for k in range(n):
            attended[at, k * cols : (k + 1) * cols] = heads_in[k, s]
        for j in range(shards):
            normed[at, j * shard_rows : (j + 1) * shard_rows] = contract_cols(
                attended[at, :], weights[3, j]
            ).astype(BF16)
        swap = remote(normed.at[at], branch_in.at[s], swap_send.at[s], swap_recv.at[s], {"tp": 1 - spot.half})
        swap.start()
        swaps.append(swap)

    for s in range(seqs):
        pl.loop(0, n)(functools.partial(attend, s))
        if s == 0:
            loads[3].wait_near()
            outs[3].start()
            if n > 2:
                spreads[0].hop(2)
        project(s)
    if n > 2:
        spreads[1].hop(2)
    for s in range(seqs):
        swaps[s].wait_recv()

        @pl.loop(0, part // 64)
        def _(i):
            here = pl.ds(pl.multiple_of(i * 64, 64), 64)
            at = pl.ds(pl.multiple_of(s * part + i * 64, 64), 64)
            values = tokens[at, :].astype(F32) + (
                normed[at, :].astype(F32) + branch_in[s, here, :].astype(F32)
            )
            hidden[at, :] = values
            normed_two[at, :] = (values * rms_scale(values) * gains[1:2, :]).astype(BF16)

    flip(normed_two[...], left_two)
    for h in range(3, n):
        for spread in spreads[:2]:
            spread.hop(h)
    loads[4].wait_own()
    loads[4].pass_on()
    spreads[0].pass_on()
    loads[4].wait_near()
    for spread in spreads[:2]:
        spread.wait()
    for load in loads[1:]:
        load.wait_sent()
    for move in moves + swaps:
        move.wait_send()
    for s in range(seqs):
        for d in range(1, n):
            peer = lax.rem(me + d, n)
            back(s, peer, peer).wait_send()
    for copy in outs + flips[-1:]:
        copy.wait()


class Dims:
    def __init__(self, mesh, seqs, part, width, inner_width, units, heads, slots):
        self.mesh = shards, ctx, tp = tuple(mesh.shape[a] for a in ("shard", "ctx", "tp"))
        self.slots = slots
        self.n, self.seqs, self.part, self.width = ctx, seqs, part, width
        self.inner_width, self.units = inner_width, units
        self.head_dim = inner_width // heads
        self.cols, self.own_heads = inner_width // ctx, heads // ctx
        self.shards, self.shard_rows = shards, width // shards


def forward_call(dims):
    rows, width, n, part, seqs = dims.seqs * dims.part, dims.width, dims.n, dims.part, dims.seqs
    shards, shard_rows, inner, units = dims.shards, dims.shard_rows, dims.inner_width, dims.units
    lanes, span = 2 * dims.head_dim, 2 * n * part
    vmem, anywhere = pl.BlockSpec(memory_space=pltpu.VMEM), pl.BlockSpec(memory_space=pl.ANY)
    shape = jax.ShapeDtypeStruct
    dma = pltpu.SemaphoreType.DMA
    chips = shards // 2
    block = (seqs, part, dims.cols)
    return pl.pallas_call(
        functools.partial(forward_kernel, dims),
        in_specs=[vmem] * 4 + [anywhere] * 8,
        out_specs=[vmem] * 6 + [anywhere] * 11,
        out_shape=[
            shape((rows, width), F32),
            shape((rows, width), BF16),
            shape((rows, inner), BF16),
            shape((seqs, n, part, lanes), F32),
            shape((1, span), F32),
            shape((dims.own_heads, span), F32),
            shape((3, n) + block, BF16),
        ]
        + [shape((width, rows), BF16)] * 3
        + [shape((shards, shard_rows, inner), BF16)] * 4
        + [shape((shards, shard_rows, units), BF16)] * 3,
        scratch_shapes=[
            pltpu.VMEM((rows, width), BF16),
            pltpu.VMEM((width, rows), BF16),
            pltpu.VMEM((4, shards, shard_rows, inner), BF16),
            pltpu.VMEM((rows, inner), F32),
            pltpu.VMEM((dims.own_heads, part, span), BF16),
            pltpu.VMEM((3, n) + block, BF16),
            pltpu.VMEM((3, n) + block, BF16),
            pltpu.VMEM((seqs, n, part, dims.cols), BF16),
            pltpu.VMEM((n,) + block, BF16),
            pltpu.VMEM((part, span), F32),
            pltpu.VMEM((seqs, part, width), BF16),
            dma((7,)),
            dma((7, chips)),
            dma((7, chips)),
            dma((7, chips)),
            dma((7, chips)),
            dma((3, n)),
            dma((3, n)),
            dma((seqs, n)),
            dma((seqs, n)),
            pltpu.VMEM((shard_rows, units), BF16),
            pltpu.VMEM((2, 8, n * part), jnp.int32),
            dma((2,)),
            dma((2,)),
            dma((seqs,)),
            dma((seqs,)),
            dma((6,)),
        ]
        + [dma((3, chips, 2))] * 2
        + [dma((3, chips, n))] * 4
        + [dma((3, chips, n + 1))] * 2,
        compiler_params=pltpu.CompilerParams(
            vmem_limit_bytes=60 * 2**20, collective_id=0, has_side_effects=True
        ),
        name="forward",
    )


CHUNK = 512
SLOTS = 4
LAYER_STEPS = 4
INPUT_STEPS = 3


class Pump:
    def __init__(self, dims, spot, left, right, sources, from_heads, outs, buffers, sems, credits):
        self.dims, self.spot, self.left, self.right = dims, spot, left, right
        self.fed, self.attended = sources
        self.from_heads, self.outs = from_heads, outs
        self.core_out, self.core_in, self.far_out, self.far_in, self.line, self.line_in, self.across_in, self.done = buffers
        (
            self.right_sem, self.core_send, self.core_recv, self.far_send, self.far_recv, self.in_send, self.in_recv,
            self.across_send, self.across_recv, self.out_send, self.out_recv, self.fin_sem,
        ) = sems
        self.core_credit, self.far_credit, self.in_credit, self.across_credit, self.out_credit = credits
        units, heads = dims.units // CHUNK, dims.inner_width // CHUNK
        self.units, self.heads = units, heads
        self.early = 3 * units + heads
        self.total = 3 * units + 4 * heads
        self.bases = [(i * units, units) for i in range(3)]
        self.bases += [(3 * units + i * heads, heads) for i in range(4)]
        me, n = spot.me, dims.n
        middle = n // 2
        self.is_middle = (me == middle - 1) | (me == middle)
        self.is_end = (me == 0) | (me == n - 1)
        self.has_outer, self.has_inner = jnp.logical_not(self.is_end), jnp.logical_not(self.is_middle)
        low_side = me < middle
        self.facing = jnp.where(low_side, middle, middle - 1)
        toward, away = jnp.where(low_side, me + 1, me - 1), jnp.where(low_side, me - 1, me + 1)
        self.inner = jnp.where(self.is_middle, self.facing, toward)
        self.outer = jnp.where(self.is_end, self.inner, away)
        self.last = self.total + 10

    def core(self, c, k):
        return remote(
            self.core_out.at[lax.rem(c, 2)], self.core_in.at[k], self.core_send.at[lax.rem(c, 2)],
            self.core_recv.at[k], {"shard": self.spot.mate},
        )

    def far(self, k, d):
        return remote(
            self.far_out.at[lax.rem(k, 2), d - 1], self.far_in.at[k, d - 1], self.far_send.at[k, d - 1],
            self.far_recv.at[k, d - 1], {"shard": self.spot.away(d)},
        )

    def inward(self, k):
        half = k
        return remote(
            self.line.at[k], self.line_in.at[half], self.in_send.at[k], self.in_recv.at[half], {"ctx": self.inner}
        )

    def across(self, k):
        return remote(
            self.line.at[k], self.across_in.at[k], self.across_send.at[k],
            self.across_recv.at[k], {"ctx": self.facing},
        )

    def outward(self, k):
        return remote(
            self.done.at[k], self.done.at[k], self.out_send.at[k], self.out_recv.at[k], {"ctx": self.outer}
        )

    def spend(self, c, credit, slots=SLOTS):
        @pl.when(c >= slots)
        def _():
            pl.semaphore_wait(credit, 1)

    def give(self, c, credit, peer, slots=SLOTS):
        @pl.when(c + slots < self.total)
        def _():
            pl.semaphore_signal(credit, inc=1, device_id=peer, device_id_type=MESH)

    def term(self, c, shard, k):
        one = lambda b: jnp.where(c >= b, 1, 0)
        which = one(self.units) + one(3 * self.units) - 2 * one(self.early)
        rows = self.dims.shard_rows
        return dot(self.left[which, pl.ds(pl.multiple_of(shard * rows, rows), rows), :], self.right[k])

    def fetch(self, c):
        k, fed = lax.rem(c, SLOTS), 3 * self.units

        @pl.when(c < fed)
        def _():
            source = self.fed.at[c // self.units, lax.rem(c, self.units)]
            pltpu.make_async_copy(source, self.right.at[k], self.right_sem.at[k]).start()

        @pl.when((c >= fed) & (c < self.early))
        def _():
            at = pl.ds(pl.multiple_of((c - fed) * CHUNK, CHUNK), CHUNK)
            pltpu.make_async_copy(self.attended.at[:, at], self.right.at[k], self.right_sem.at[k]).start()

        @pl.when((c >= self.early) & (c < self.total))
        def _():
            dims = self.dims
            which, piece = (c - self.early) // self.heads, lax.rem(c - self.early, self.heads)
            per = CHUNK // dims.cols
            for i in range(per):
                for s in range(dims.seqs):
                    self.right[k, s * dims.part : (s + 1) * dims.part, i * dims.cols : (i + 1) * dims.cols] = (
                        self.from_heads[which, piece * per + i, s]
                    )

    def save(self, c, k):
        for (base, count), out in zip(self.bases, self.outs):
            @pl.when((c >= base) & (c < base + count))
            def _():
                at = pl.ds(pl.multiple_of((c - base) * CHUNK, CHUNK), CHUNK)
                pltpu.make_async_copy(self.done.at[k], out.at[:, at], self.fin_sem.at[k]).start()

    def settle(self, c, k):
        pltpu.make_async_copy(self.done.at[k], self.outs[0].at[:, pl.ds(0, CHUNK)], self.fin_sem.at[k]).wait()

        @pl.when(self.has_outer)
        def _():
            self.outward(k).wait_send()

        @pl.when(self.has_inner)
        def _():
            self.give(c, self.out_credit, {"ctx": self.inner})

    def deliver(self, c, k):
        @pl.when(self.has_inner)
        def _():
            self.outward(k).wait_recv()
            self.save(c, k)

            @pl.when(self.has_outer)
            def _():
                self.spend(c, self.out_credit)
                self.outward(k).start()

    def finish(self, c, k):
        @pl.when(self.is_middle)
        def _():
            self.across(k).wait_recv()
            self.across(k).wait_send()
            self.done[k] = (self.line[k].astype(F32) + self.across_in[k].astype(F32)).astype(BF16)
            self.give(c, self.across_credit, {"ctx": self.facing})
            self.save(c, k)

            @pl.when(self.has_outer)
            def _():
                self.spend(c, self.out_credit)
                self.outward(k).start()

        @pl.when(self.has_inner)
        def _():
            self.inward(k).wait_send()

    def collect(self, c, k):
        @pl.when(self.has_outer)
        def _():
            self.inward(k).wait_recv()
            self.line[k] = (self.line[k].astype(F32) + self.line_in[k].astype(F32)).astype(BF16)
            self.give(c, self.in_credit, {"ctx": self.outer})

        @pl.when(self.is_middle)
        def _():
            self.spend(c, self.across_credit)
            self.across(k).start()

        @pl.when(self.has_outer & self.has_inner)
        def _():
            self.spend(c, self.in_credit)
            self.inward(k).start()

    def own(self, c, k):
        total = self.term(c, self.spot.shard, k) + self.core_in[k, self.spot.chips - 1].astype(F32)
        for d in range(1, self.spot.chips):
            self.far(k, d).wait_send()
            self.far(k, d).wait_recv()
            total = total + self.far_in[k, d - 1].astype(F32)
        self.line[k] = total.astype(BF16)
        self.give(c, self.core_credit, {"shard": self.spot.mate})
        for d in range(1, self.spot.chips):
            sender = lax.rem(self.spot.shard - 2 * d + self.spot.shards, self.spot.shards)
            self.give(c, self.far_credit.at[d - 1], {"shard": sender})

        @pl.when(self.is_end & self.has_inner)
        def _():
            self.spend(c, self.in_credit)
            self.inward(k).start()

    def to_chips(self, c, k):
        self.core(c, k).wait_recv()
        self.core(c, k).wait_send()
        for d in range(1, self.spot.chips):
            pair = self.term(c, self.spot.away(d), k) + self.core_in[k, d - 1].astype(F32)
            self.far_out[lax.rem(k, 2), d - 1] = pair.astype(BF16)
            self.spend(c, self.far_credit.at[d - 1])
            self.far(k, d).start()

    def to_core(self, c, k):
        @pl.when(c < self.early)
        def _():
            pltpu.make_async_copy(self.fed.at[0, 0], self.right.at[k], self.right_sem.at[k]).wait()

        chips, half = self.spot.chips, lax.rem(c, 2)
        for d in range(1, chips + 1):
            shard = 2 * lax.rem(self.spot.chip + d, chips) + 1 - self.spot.core
            self.core_out[half, d - 1] = self.term(c, shard, k).astype(BF16)
        self.spend(c, self.core_credit)
        self.core(c, k).start()

    def step(self, t):
        def at(lag, stage):
            c = t - lag

            @pl.when((c >= 0) & (c < self.total))
            def _():
                stage(c, lax.rem(c, SLOTS))

        @pl.when(t < self.total)
        def _():
            self.fetch(t)

        at(10, self.settle)
        at(9, self.deliver)
        at(7, self.finish)
        at(5, self.collect)
        at(3, self.own)

        at(1, self.to_chips)
        at(0, self.to_core)

    def steps(self, first, last):
        @pl.loop(first, last)
        def _(t):
            self.step(t)


UNITS = 256


def geglu_both(gate, up, upstream):
    root, cube = 0.7978845608028654, 0.044715
    square = gate * gate
    bent = jnp.tanh(root * gate * (1.0 + cube * square))
    half = 0.5 * (1.0 + bent)
    gelu = gate * half
    slope = half + 0.5 * gate * (1.0 - bent * bent) * (root * (1.0 + 3.0 * cube * square))
    return gelu * up, upstream * up * slope, upstream * gelu


def backward_kernel(
    dims, gains, table, by_offset,
    tokens, lse_from, pieces_from, left_g, left_two, left_one, normed_two, attended, hidden, cotangent,
    wo, wq, wk, wv, wi0, wi1, wff,
    down_out, gate_out, up_out, o_out, q_out, k_out, v_out,
    layer_out, input_grad, grad_hidden, ffn_term, ffn_other, small_out,
    other_one, norm_gain, ffn_gain, table_out, small, small_in,
    left, right, core_out, core_in, far_out, far_in, line, line_in, across_in, done,
    fed, term, swap_in, grads, grads_out, grads_in,
    right_sem, core_send, core_recv, far_send, far_recv, in_send, in_recv, across_send, across_recv,
    out_send, out_recv, fin_sem, swap_send, swap_recv, head_send, head_recv, back_send, back_recv,
    one_send, one_recv, ffn_sem, local_sem, small_send, small_recv,
    core_credit, far_credit, in_credit, across_credit, out_credit,
):
    spot = Spot(*dims.mesh)
    n, seqs, part, cols, head_dim, width = dims.n, dims.seqs, dims.part, dims.cols, dims.head_dim, dims.width
    me, shards, shard_rows, units = spot.me, spot.shards, dims.shard_rows, dims.units
    rows = seqs * part
    lanes, per = 2 * head_dim, 2
    groups = cols // lanes
    span = table.shape[1]
    other_half = {"tp": 1 - spot.half}
    pump = Pump(
        dims, spot, left, right, (fed, attended), grads_in,
        (down_out, gate_out, up_out, o_out, q_out, k_out, v_out),
        (core_out, core_in, far_out, far_in, line, line_in, across_in, done),
        (
            right_sem, core_send, core_recv, far_send, far_recv, in_send, in_recv, across_send, across_recv,
            out_send, out_recv, fin_sem,
        ),
        (core_credit, far_credit, in_credit, across_credit, out_credit),
    )
    lefts = [
        pltpu.make_async_copy(source, left.at[i], local_sem.at[i])
        for i, source in ((0, left_g), (1, left_two), (0, left_one))
    ]
    all_here = spot.barrier()
    ffn_gain[...] = jnp.zeros_like(ffn_gain)
    norm_gain[...] = jnp.zeros_like(norm_gain)
    table_out[...] = jnp.zeros_like(table_out)

    def feed(weights, values, given, sem, value_sem):
        inputs = [
            pltpu.make_async_copy(normed_two, values, value_sem.at[0]),
            pltpu.make_async_copy(cotangent, given, value_sem.at[1]),
        ]

        def load(u):
            slot = lax.rem(u, 2)
            at = pl.ds(pl.multiple_of(u * UNITS, UNITS), UNITS)
            return [
                pltpu.make_async_copy(w.at[:, :, at], weights.at[slot, j], sem.at[slot, j])
                for j, w in enumerate((wi0, wi1, wff))
            ]

        for copy in load(0) + inputs:
            copy.start()
        for copy in inputs:
            copy.wait()
        for copy in lefts[:2]:
            copy.start()
        each = CHUNK // UNITS

        @pl.loop(0, units // CHUNK)
        def _(c):
            for i in range(each):
                u = c * each + i

                @pl.when(u + 1 < units // UNITS)
                def _():
                    for copy in load(u + 1):
                        copy.start()

                for copy in load(u):
                    copy.wait()
                slot = lax.rem(u, 2)
                gate = dot(values[...], weights[slot, 0].reshape(width, UNITS))
                up = dot(values[...], weights[slot, 1].reshape(width, UNITS))
                upstream = dot(given[...], weights[slot, 2].reshape(width, UNITS))
                for j, made in enumerate(geglu_both(gate, up, upstream)):
                    fed[j, c, :, i * UNITS : (i + 1) * UNITS] = made.astype(BF16)

            @pl.when(c == 0)
            def _():
                for copy in lefts[:2]:
                    copy.wait()
                all_here()

            pump.step(c)

    pl.run_scoped(
        feed,
        pltpu.VMEM((2, 3, shards, shard_rows, UNITS), BF16),
        pltpu.VMEM((rows, width), BF16),
        pltpu.VMEM((rows, width), BF16),
        pltpu.SemaphoreType.DMA((2, 3)),
        pltpu.SemaphoreType.DMA((2,)),
    )
    fed_steps = units // CHUNK

    def feed_terms(weights, block, sem, block_sem):
        def load(j, w, slot):
            return pltpu.make_async_copy(w.at[j], weights.at[slot], sem.at[slot])

        def product(slot, which):
            total = None
            for c in range(units // CHUNK):
                at = slice(c * CHUNK, (c + 1) * CHUNK)
                made = contract_cols(fed[which, c], weights[slot, :, at])
                total = made if total is None else total + made
            return total

        def columns(j):
            return pl.ds(pl.multiple_of(j * shard_rows, shard_rows), shard_rows)

        load(0, wi0, 0).start()
        load(0, wi1, 1).start()

        @pl.loop(0, shards)
        def _(j):
            total = None
            for slot, w in enumerate((wi0, wi1)):
                load(j, w, slot).wait()
                made = product(slot, 1 + slot)
                total = made if total is None else total + made

                @pl.when(j + 1 < shards)
                def _():
                    load(j + 1, w, slot).start()

            for s in range(seqs):
                term[s, :, columns(j)] = total[s * part : (s + 1) * part].astype(BF16)

            @pl.when(j == 1)
            def _():
                pump.step(fed_steps)

        for swap in swaps:
            swap.start()
        load(0, wff, 0).start()
        pump.steps(fed_steps + 1, fed_steps + 2)

        @pl.loop(0, shards)
        def _(j):
            slot = lax.rem(j, 2)

            @pl.when(j + 1 < shards)
            def _():
                load(j + 1, wff, 1 - slot).start()

            load(j, wff, slot).wait()
            block[...] = product(slot, 0).astype(BF16)
            copy = pltpu.make_async_copy(block, ffn_term.at[:, columns(j)], block_sem.at[0])
            copy.start()
            copy.wait()

            @pl.when(j == 1)
            def _():
                pump.step(fed_steps + 2)

        pump.steps(fed_steps + 3, fed_steps + 4)

    swaps = [
        remote(term.at[s], swap_in.at[s], swap_send.at[s], swap_recv.at[s], other_half) for s in range(seqs)
    ]
    pl.run_scoped(
        feed_terms,
        pltpu.VMEM((2, shard_rows, units), BF16),
        pltpu.VMEM((rows, shard_rows), BF16),
        pltpu.SemaphoreType.DMA((2,)),
        pltpu.SemaphoreType.DMA((1,)),
    )
    so_far = fed_steps + 4

    def head_move(s, peer):
        return remote(
            grads_out.at[0, peer, s], grads.at[me, s], head_send.at[s, peer], head_recv.at[s, me], {"ctx": peer}
        )

    def head_wait(s, peer):
        remote(
            grads_out.at[0, peer, s], grads.at[peer, s], head_send.at[s, peer], head_recv.at[s, peer], {"ctx": peer}
        ).wait_recv()

    def second_norm(s, weights, values, given, own, sem):
        at = pl.ds(s * part, part)
        copies = [
            pltpu.make_async_copy(hidden.at[at, :], values, sem.at[0]),
            pltpu.make_async_copy(cotangent.at[at, :], given, sem.at[1]),
        ]
        for copy in copies:
            copy.start()
        for copy in copies:
            copy.wait()
        swaps[s].wait_recv()

        @pl.loop(0, part // 64)
        def _(i):
            here = pl.ds(pl.multiple_of(i * 64, 64), 64)
            h = values[here, :]
            grad = term[s, here, :].astype(F32) + swap_in[s, here, :].astype(F32)
            scale = rms_scale(h)
            ffn_gain[...] += jnp.sum(grad * h * scale, axis=0, keepdims=True)
            total = given[here, :].astype(F32) + rms_back(h, scale, gains[1:2, :], grad)
            values[here, :] = total
            own[here, :] = total.astype(BF16)

        saved = pltpu.make_async_copy(values, grad_hidden.at[at, :], sem.at[0])
        saved.start()
        total = dot(own[:, :shard_rows], weights[0])
        for j in range(1, shards):
            total += dot(own[:, j * shard_rows : (j + 1) * shard_rows], weights[j])
        for k in range(n):
            grads_out[0, k, s] = total[:, k * cols : (k + 1) * cols].astype(BF16)
        for d in range(1, n):
            head_move(s, lax.rem(me + d, n)).start()
        grads[me, s] = grads_out[0, me, s]
        left[2, :, s * part : (s + 1) * part] = own[...].T
        saved.wait()

    def second_norms(weights, values, given, own, sem):
        load = pltpu.make_async_copy(wo, weights, sem.at[3])
        load.start()
        load.wait()
        for s in range(seqs):
            second_norm(s, weights, values, given, own, sem)
            if s == 0:
                pump.steps(so_far, so_far + 1)

    pl.run_scoped(
        second_norms,
        pltpu.VMEM((shards, shard_rows, dims.inner_width), BF16),
        pltpu.VMEM((part, width), F32),
        pltpu.VMEM((part, width), BF16),
        pltpu.VMEM((part, width), BF16),
        pltpu.SemaphoreType.DMA((4,)),
    )
    ffn_swap = remote(ffn_term, ffn_other, ffn_sem.at[0], ffn_sem.at[1], other_half)
    ffn_swap.start()
    pump.steps(so_far + 1, so_far + 2)
    so_far += 2

    def back_move(j, s, peer):
        return remote(
            grads_out.at[j, peer, s], grads_in.at[j, me, s], back_send.at[j, s, peer], back_recv.at[j, s, me],
            {"ctx": peer},
        )

    def back_wait(j, s, peer):
        remote(
            grads_out.at[j, peer, s], grads_in.at[j, peer, s], back_send.at[j, s, peer], back_recv.at[j, s, peer],
            {"ctx": peer},
        ).wait_recv()

    def attention(pieces, lse, bias, sums, grad_k, grad_v, sem):
        @pl.loop(0, seqs * groups * n)
        def _(i):
            a, group, s = lax.rem(i, n), lax.rem(i // n, groups), i // (n * groups)
            at = pl.ds(pl.multiple_of(group * lanes, lanes), lanes)

            @pl.when((a == 0) & (group == 0))
            def _():
                here = [
                    pltpu.make_async_copy(pieces_from.at[:, :, s], pieces, sem.at[0]),
                    pltpu.make_async_copy(lse_from.at[s], lse, sem.at[1]),
                ]
                for copy in here:
                    copy.start()
                for copy in here:
                    copy.wait()
                for d in range(1, n):
                    head_wait(s, lax.rem(me + d, n))
                    head_move(s, lax.rem(me + d, n)).wait_send()

            @pl.when(a == 0)
            def _():
                for j in range(per):
                    bias_rows(table[pl.ds(group * per + j, 1), :], sums.at[j])
                bias[...] = sums[...].astype(BF16)
                sums[...] = jnp.zeros_like(sums)
                grad_k[...] = jnp.zeros_like(grad_k)
                grad_v[...] = jnp.zeros_like(grad_v)

            lane = lax.broadcasted_iota(jnp.int32, (part, lanes), 1)
            result = jnp.zeros((part, lanes), F32)
            for j in range(per):
                mask = (lane >= j * head_dim) & (lane < (j + 1) * head_dim)
                query = jnp.where(mask, pieces[0, a, :, at], 0)
                upstream = jnp.where(mask, grads[a, s, :, at], 0)
                log_total = jnp.sum(jnp.where(lane == group * per + j, lse[a], 0.0), axis=1, keepdims=True)
                windows = [pl.ds(pl.multiple_of((n + b - a) * part, part), part) for b in range(n)]
                probs, grad_probs = [], []
                for b in range(n):
                    scores = contract_cols(query, pieces[1, b, :, at]) + bias[j, :, windows[b]].astype(F32)
                    probs.append(jnp.exp(scores - log_total))
                    grad_probs.append(contract_cols(upstream, pieces[2, b, :, at]))
                delta = sum(jnp.sum(g * p, axis=1, keepdims=True) for g, p in zip(grad_probs, probs))
                summed = None
                for b in range(n):
                    grad_scores = (probs[b] * (grad_probs[b] - delta)).astype(BF16)
                    sums[j, :, windows[b]] += grad_scores.astype(F32)
                    product = dot(grad_scores, pieces[1, b, :, at])
                    summed = product if summed is None else summed + product
                    grad_k[b] += contract_rows(grad_scores, query)
                    grad_v[b] += contract_rows(probs[b].astype(BF16), upstream)
                result = jnp.where(mask, summed, result)
            grads_out[0, a, s, :, at] = result.astype(BF16)

            @pl.when(a == n - 1)
            def _():
                for b in range(n):
                    grads_out[1, b, s, :, at] = grad_k[b].astype(BF16)
                    grads_out[2, b, s, :, at] = grad_v[b].astype(BF16)
                for j in range(per):
                    table_out[pl.ds(group * per + j, 1), :] += diagonal_sums(sums.at[j])

            @pl.when((a == n - 1) & (group == groups - 1))
            def _():
                for j in range(3):
                    for d in range(1, n):
                        back_move(j, s, lax.rem(me + d, n)).start()
                    grads_in[j, me, s] = grads_out[j, me, s]

            @pl.when(a == n - 1)
            def _():
                pump.step(so_far + i // n)

    pl.run_scoped(
        attention,
        pltpu.VMEM((3, n, part, cols), BF16),
        pltpu.VMEM((n, part, lanes), F32),
        pltpu.VMEM((per, part, span), BF16),
        pltpu.VMEM((per, part, span), F32),
        pltpu.VMEM((n, part, lanes), F32),
        pltpu.VMEM((n, part, lanes), F32),
        pltpu.SemaphoreType.DMA((2,)),
    )
    so_far += seqs * groups
    lefts[2].start()
    lefts[2].wait()
    pump.steps(so_far, so_far + 1)
    so_far += 1
    assert so_far <= pump.early
    for s in range(seqs):
        for j in range(3):
            for d in range(1, n):
                back_wait(j, s, lax.rem(me + d, n))

    for copy in swaps:
        copy.wait_send()

    def first_norm_terms(weights, values, sem):
        def load(shard):
            return [
                pltpu.make_async_copy(w.at[shard], weights.at[shard % 2, j], sem.at[shard % 2, j])
                for j, w in enumerate((wq, wk, wv))
            ]

        for copy in load(0):
            copy.start()
        for j in range(3):
            for s in range(seqs):
                for k in range(n):
                    values[j, s * part : (s + 1) * part, k * cols : (k + 1) * cols] = grads_in[j, k, s]
        for shard in range(shards):
            if shard + 1 < shards:
                for copy in load(shard + 1):
                    copy.start()
            for copy in load(shard):
                copy.wait()
            total = contract_cols(values[0], weights[shard % 2, 0])
            total += contract_cols(values[1], weights[shard % 2, 1])
            total += contract_cols(values[2], weights[shard % 2, 2])
            for s in range(seqs):
                term[s, :, shard * shard_rows : (shard + 1) * shard_rows] = (
                    total[s * part : (s + 1) * part].astype(BF16)
                )

    pl.run_scoped(
        first_norm_terms,
        pltpu.VMEM((2, 3, shard_rows, dims.inner_width), BF16),
        pltpu.VMEM((3, seqs * part, dims.inner_width), BF16),
        pltpu.SemaphoreType.DMA((2, 3)),
    )
    ones = [
        remote(term.at[s], other_one.at[s], one_send.at[s], one_recv.at[s], other_half) for s in range(seqs)
    ]
    for swap in ones:
        swap.start()
    pump.steps(so_far, so_far + LAYER_STEPS)
    so_far += LAYER_STEPS
    ffn_swap.wait_recv()

    def layer_output(values, own, other, sem):
        for s in range(seqs):
            at = pl.ds(s * part, part)
            copies = [
                pltpu.make_async_copy(source.at[at, :], to, sem.at[i])
                for i, (source, to) in enumerate(((hidden, values), (ffn_term, own), (ffn_other, other)))
            ]
            for copy in copies:
                copy.start()
            for copy in copies:
                copy.wait()

            @pl.loop(0, part // 64)
            def _(i):
                here = pl.ds(pl.multiple_of(i * 64, 64), 64)
                total = own[here, :].astype(F32) + other[here, :].astype(F32)
                own[here, :] = (values[here, :] + total).astype(BF16)

            saved = pltpu.make_async_copy(own, layer_out.at[at, :], sem.at[0])
            saved.start()
            saved.wait()

    pl.run_scoped(
        layer_output,
        pltpu.VMEM((part, width), F32),
        pltpu.VMEM((part, width), BF16),
        pltpu.VMEM((part, width), BF16),
        pltpu.SemaphoreType.DMA((3,)),
    )
    pump.steps(so_far, so_far + INPUT_STEPS)
    so_far += INPUT_STEPS

    def first_norm_back(values, given, sem):
        for s in range(seqs):
            at = pl.ds(s * part, part)
            copies = [
                pltpu.make_async_copy(source.at[at, :], to, sem.at[i])
                for i, (source, to) in enumerate(((grad_hidden, values), (tokens, given)))
            ]
            for copy in copies:
                copy.start()
            for copy in copies:
                copy.wait()
            ones[s].wait_recv()

            @pl.loop(0, part // 64)
            def _(i):
                here = pl.ds(pl.multiple_of(i * 64, 64), 64)
                x = given[here, :].astype(F32)
                grad = term[s, here, :].astype(F32) + other_one[s, here, :].astype(F32)
                scale = rms_scale(x)
                norm_gain[...] += jnp.sum(grad * x * scale, axis=0, keepdims=True)
                values[here, :] += rms_back(x, scale, gains[0:1, :], grad)

            saved = pltpu.make_async_copy(values, input_grad.at[at, :], sem.at[0])
            saved.start()
            saved.wait()

    pl.run_scoped(
        first_norm_back,
        pltpu.VMEM((part, width), F32),
        pltpu.VMEM((part, width), BF16),
        pltpu.SemaphoreType.DMA((2,)),
    )

    lines, slots = width // 128, small.shape[1] - 2 * (width // 128)
    for i in range(lines):
        small[0, i : i + 1, :] = norm_gain[:, i * 128 : (i + 1) * 128]
        small[0, lines + i : lines + i + 1, :] = ffn_gain[:, i * 128 : (i + 1) * 128]
    hot = by_offset[...] == lax.broadcasted_iota(jnp.int32, (slots, span), 0).astype(F32)
    lane = lax.broadcasted_iota(jnp.int32, (slots, 128), 1)
    table_part = jnp.zeros((slots, 128), F32)
    for head in range(dims.own_heads):
        column = jnp.sum(jnp.where(hot, table_out[head : head + 1, :], 0.0), axis=1, keepdims=True)
        table_part = jnp.where(lane == me * dims.own_heads + head, column, table_part)
    small[0, 2 * lines :, :] = table_part
    partners = []
    for axis, at, count in (("shard", spot.shard, shards), ("ctx", me, n)):
        step = 1
        while step < count:
            partners.append({axis: at + step * (1 - 2 * lax.rem(at // step, 2))})
            step *= 2
    for i, partner in enumerate(partners):
        copy = remote(small.at[i], small_in.at[i], small_send.at[i], small_recv.at[i], partner)
        copy.start()
        pump.steps(so_far, so_far + 1)
        so_far += 1
        copy.wait_recv()
        copy.wait_send()
        small[i + 1] = small[i] + small_in[i]
    small_out[...] = small[len(partners)]
    pump.steps(so_far, pump.last)
    for copy in ones + [ffn_swap]:
        copy.wait_send()
    for s in range(seqs):
        for d in range(1, n):
            peer = lax.rem(me + d, n)
            for j in range(3):
                back_move(j, s, peer).wait_send()


def backward_call(dims):
    rows, width, n, part, seqs = dims.seqs * dims.part, dims.width, dims.n, dims.part, dims.seqs
    shards, shard_rows, inner, units, cols = dims.shards, dims.shard_rows, dims.inner_width, dims.units, dims.cols
    span, chips = 2 * n * part, dims.shards // 2
    vmem, anywhere = pl.BlockSpec(memory_space=pltpu.VMEM), pl.BlockSpec(memory_space=pl.ANY)
    shape, dma, regular = jax.ShapeDtypeStruct, pltpu.SemaphoreType.DMA, pltpu.SemaphoreType.REGULAR
    far = max(chips - 1, 1)
    stages = (shards * n).bit_length() - 1
    lines = 2 * (width // 128) + dims.slots
    block = (shard_rows, CHUNK)
    return pl.pallas_call(
        functools.partial(backward_kernel, dims),
        in_specs=[vmem] * 3 + [anywhere] * 17,
        out_specs=[anywhere] * 12 + [vmem],
        out_shape=[shape((shard_rows, units), BF16)] * 3
        + [shape((shard_rows, inner), BF16)] * 4
        + [
            shape((rows, width), BF16),
            shape((rows, width), F32),
            shape((rows, width), F32),
            shape((rows, width), BF16),
            shape((rows, width), BF16),
            shape((lines, 128), F32),
        ],
        scratch_shapes=[
            pltpu.VMEM((seqs, part, width), BF16),
            pltpu.VMEM((1, width), F32),
            pltpu.VMEM((1, width), F32),
            pltpu.VMEM((dims.own_heads, span), F32),
            pltpu.VMEM((stages + 1, lines, 128), F32),
            pltpu.VMEM((stages, lines, 128), F32),
            pltpu.VMEM((3, width, rows), BF16),
            pltpu.VMEM((SLOTS, rows, CHUNK), BF16),
            pltpu.VMEM((2, chips) + block, BF16),
            pltpu.VMEM((SLOTS, chips) + block, BF16),
            pltpu.VMEM((2, far) + block, BF16),
            pltpu.VMEM((SLOTS, far) + block, BF16),
            pltpu.VMEM((SLOTS,) + block, BF16),
            pltpu.VMEM((SLOTS,) + block, BF16),
            pltpu.VMEM((SLOTS,) + block, BF16),
            pltpu.VMEM((SLOTS,) + block, BF16),
            pltpu.VMEM((3, units // CHUNK, rows, CHUNK), BF16),
            pltpu.VMEM((seqs, part, width), BF16),
            pltpu.VMEM((seqs, part, width), BF16),
            pltpu.VMEM((n, seqs, part, cols), BF16),
            pltpu.VMEM((3, n, seqs, part, cols), BF16),
            pltpu.VMEM((3, n, seqs, part, cols), BF16),
            dma((SLOTS,)),
            dma((2,)),
            dma((SLOTS,)),
            dma((SLOTS, far)),
            dma((SLOTS, far)),
        ]
        + [dma((SLOTS,))] * 7
        + [dma((seqs,))] * 2
        + [dma((seqs, n))] * 2
        + [dma((3, seqs, n))] * 2
        + [dma((seqs,))] * 2
        + [dma((2,)), dma((4,)), dma((stages,)), dma((stages,))]
        + [regular, regular((far,)), regular, regular, regular],
        compiler_params=pltpu.CompilerParams(
            vmem_limit_bytes=62 * 2**20, collective_id=1, has_side_effects=True
        ),
        name="backward",
    )


TILE = 256


def finish_kernel(count, firsts, *refs):
    sources, outs = refs[:count], refs[count : 2 * count]
    taken, made = refs[2 * count : 3 * count], refs[3 * count : 4 * count]
    take_sem, save_sem = refs[4 * count :]
    sizes = [min(out.shape[0], TILE) for out in outs]
    tiles = [out.shape[0] // size for out, size in zip(outs, sizes)]

    def at(j, i, first=0):
        return pl.ds(pl.multiple_of(first + i * sizes[j], 16), sizes[j])

    def take(j, i):
        return pltpu.make_async_copy(sources[j].at[at(j, i, firsts[j])], taken[j].at[at(j, i)], take_sem.at[j, i])

    def save(j, i):
        return pltpu.make_async_copy(made[j].at[at(j, i)], outs[j].at[at(j, i)], save_sem.at[j, i])

    for j in range(count):
        @pl.loop(0, tiles[j])
        def _(i):
            take(j, i).start()

    for j in range(count):
        @pl.loop(0, tiles[j])
        def _(i):
            take(j, i).wait()
            if made[j].dtype != taken[j].dtype:
                made[j][at(j, i), :] = taken[j][at(j, i), :].astype(made[j].dtype)
            save(j, i).start()

    for j in range(count):
        @pl.loop(0, tiles[j])
        def _(i):
            save(j, i).wait()


def finish(jobs):
    count = len(jobs)
    sources, firsts, lengths, types = zip(*jobs)
    shapes = [(length, source.shape[1]) for source, length in zip(sources, lengths)]
    taken = [pltpu.VMEM(shape, source.dtype) for shape, source in zip(shapes, sources)]
    made = [pltpu.VMEM(shape, kind) for shape, kind in zip(shapes, types)]
    same = [source.dtype == kind for source, kind in zip(sources, types)]
    tiles = max(-(-length // TILE) for length in lengths)

    def kernel(*refs):
        refs = list(refs)
        made_at = iter(refs[3 * count : -2])
        full = [refs[2 * count + j] if same[j] else next(made_at) for j in range(count)]
        finish_kernel(count, firsts, *refs[: 3 * count], *full, *refs[-2:])

    return pl.pallas_call(
        kernel,
        in_specs=[pl.BlockSpec(memory_space=pl.ANY)] * count,
        out_specs=[pl.BlockSpec(memory_space=pl.ANY)] * count,
        out_shape=[jax.ShapeDtypeStruct(shape, kind) for shape, kind in zip(shapes, types)],
        scratch_shapes=taken
        + [m for m, keep in zip(made, same) if not keep]
        + [pltpu.SemaphoreType.DMA((count, tiles))] * 2,
        compiler_params=pltpu.CompilerParams(vmem_limit_bytes=56 * 2**20),
        name="finish",
    )(*sources)


def per_device(
    mesh,
    tokens,
    cotangent,
    buckets,
    query_weight,
    key_weight,
    value_weight,
    output_weight,
    gate_weight,
    up_weight,
    down_weight,
    norm_gain,
    ffn_gain,
    bucket_bias_table,
):
    seqs, part, width = tokens.shape
    rows, inner_width = seqs * part, query_weight.shape[1]
    slots, heads = bucket_bias_table.shape
    dims = Dims(mesh, seqs, part, width, inner_width, gate_weight.shape[1], heads, slots)
    token_rows, upstream = tokens.reshape(rows, width), cotangent.reshape(rows, width)
    gains = jnp.stack([norm_gain, ffn_gain]).astype(F32)
    hidden, normed_two, attended, lse, by_offset, bias_table, pieces, *lefts_and_weights = forward_call(dims)(
        token_rows, upstream, gains, bucket_bias_table.astype(F32), buckets,
        query_weight, key_weight, value_weight, output_weight, gate_weight, up_weight, down_weight,
    )
    left_g, left_one, left_two, wq, wk, wv, wo, wi0, wi1, wff = lefts_and_weights
    *weight_grads, result, grad_inputs, unused, unused_own, unused_other, small = backward_call(dims)(
        gains, bias_table, by_offset,
        token_rows, lse, pieces, left_g, left_two, left_one, normed_two, attended, hidden, upstream,
        wo, wq, wk, wv, wi0, wi1, wff,
    )
    lines = width // 128
    jobs = [(g, 0, g.shape[0], F32) for g in weight_grads]
    jobs += [(grad_inputs, 0, rows, F32), (result, 0, rows, BF16)]
    jobs += [(small, 0, lines, F32), (small, lines, lines, F32), (small, 2 * lines, slots, F32)]
    *weight_grads, grad_inputs, result, norm_gain_grad, ffn_gain_grad, table_grad = finish(jobs)
    grad_down_w, grad_gate_w, grad_up_w, grad_output_w, grad_query_w, grad_key_w, grad_value_w = weight_grads
    return (
        result.reshape(seqs, part, width),
        grad_inputs.reshape(seqs, part, width),
        grad_query_w,
        grad_key_w,
        grad_value_w,
        grad_output_w,
        grad_gate_w,
        grad_up_w,
        grad_down_w,
        norm_gain_grad.reshape(width),
        ffn_gain_grad.reshape(width),
        table_grad[:, :heads],
    )


def solution(mesh):
    rows, weights = P("shard", "ctx", None), P("shard", "tp")
    return jax.shard_map(
        functools.partial(per_device, mesh),
        mesh=mesh,
        in_specs=(rows, rows, P("ctx", None)) + (weights,) * 7 + (P(), P(), P(None, "tp")),
        out_specs=(rows, rows) + (weights,) * 7 + (P(), P(), P(None, "tp")),
        check_vma=False,
    )
```
